32 devices in a mesh: dp: 16 (over z, y, core), tensor: 2 (over x).
Axes of the slice: x: 2, y: 2, z: 4, core: 2. Of those that a mesh axis runs over, the one named last changes fastest.
Arguments:
- mixer_x: bfloat16 [2048, 8192], P(('dp', 'tensor')), may hold values from -6 to 6
- gate_z: bfloat16 [2048, 8192], P(('dp', 'tensor')), may hold values from -6 to 6
- b_matrix: bfloat16 [2048, 1024], P(('dp', 'tensor')), may hold values from -6 to 6
- c_matrix: bfloat16 [2048, 1024], P(('dp', 'tensor')), may hold values from -6 to 6
- raw_steps: bfloat16 [2048, 128], P(('dp', 'tensor')), may hold values from -3 to 11
- decay_log: float32 [128], P('tensor'), may hold values from -1 to 3
- skip_gain: float32 [128], P('tensor'), may hold values from 0.5 to 1.5
- step_bias: float32 [128], P('tensor'), may hold values from -14 to -3
- norm_gain: float32 [8192], P('tensor'), may hold values from 0.5 to 1.5
- out_grad: bfloat16 [2048, 8192], P(('dp', 'tensor')), may hold values from -12 to 12
Outputs:
- grad_mixer_x: bfloat16 [2048, 8192], P(('dp', 'tensor'))
- grad_gate_z: bfloat16 [2048, 8192], P(('dp', 'tensor'))
- grad_b_matrix: bfloat16 [2048, 1024], P(('dp', 'tensor'))
- grad_c_matrix: bfloat16 [2048, 1024], P(('dp', 'tensor'))
- grad_raw_steps: bfloat16 [2048, 128], P(('dp', 'tensor'))
- grad_decay_log: float32 [128], P('tensor')
- grad_skip_gain: float32 [128], P('tensor')
- grad_step_bias: float32 [128], P('tensor')
- grad_norm_gain: float32 [8192], P('tensor')
The draws below stay inside these ranges and needn't reach their ends.
All inputs are finite; a program needn't handle non-finite values.
Results may differ from the reference program's by a relative error of at most 0.013.
Values may be sent and summed in bfloat16 or wider, within the bound.
No kernel may reach another device: no remote copies, remote signals or barrier semaphores. Data moves between devices by JAX's collectives and lax.ppermute only.
A program may use at most 128 MiB of HBM per device.

```python
import math
import jax
import jax.numpy as jnp
from jax import lax

MIXER_HEADS = 128
HEAD_DIM = 64
STATE = 128
GROUPS = 8
SLAB = 128
CHANNELS = 8192
SEQUENCE_LENGTH = 2048


def head_kinds(key, fraction):
    key = jax.random.fold_in(key, 21)
    chooser, rate_key, level_key, bias_key, log_key = jax.random.split(key, 5)
    gradual_decay = jax.random.uniform(chooser, (MIXER_HEADS,)) < fraction
    slow_log = jax.random.uniform(rate_key, (MIXER_HEADS,), jnp.float32, math.log(4.0), math.log(16.0))
    levels = jax.random.uniform(level_key, (MIXER_HEADS,), jnp.float32, 0.25, 0.75)
    slow_bias = jnp.log(levels) - math.log(SEQUENCE_LENGTH) - slow_log
    fast_bias = jax.random.uniform(bias_key, (MIXER_HEADS,), jnp.float32, -4.5, -3.0)
    fast_log = jax.random.uniform(log_key, (MIXER_HEADS,), jnp.float32, -0.7, 0.7)
    return (gradual_decay, jnp.where(gradual_decay, slow_bias, fast_bias), jnp.where(gradual_decay, slow_log, fast_log))


def draw_step_bias(key, part):
    fraction = 0.5
    gradual_decay, per_head_bias, head_log = head_kinds(key, fraction)
    return per_head_bias.astype(jnp.float32)


def draw_decay_log(key, part):
    fraction = 0.5
    gradual_decay, per_head_bias, head_log = head_kinds(key, fraction)
    return head_log.astype(jnp.float32)


def draw_raw_steps(key, part):
    fraction = 0.5
    gradual_decay, per_head_bias, head_log = head_kinds(key, fraction)
    key = jax.random.fold_in(key, 12)
    noise_random_key, onset_random_key, length_random_key, spike_random_key, depth_random_key = jax.random.split(key, 5)
    random_jitter = jnp.clip(0.5 * jax.random.normal(noise_random_key, (SEQUENCE_LENGTH, MIXER_HEADS), jnp.float32), -3.0, 3.0)
    token_place = jnp.arange(SEQUENCE_LENGTH, dtype=jnp.int32)[:, None, None]
    stretch_length = jax.random.randint(length_random_key, (1, 3, MIXER_HEADS), SEQUENCE_LENGTH // 8, SEQUENCE_LENGTH // 4 + 1)
    stretch_start = jax.random.randint(onset_random_key, (1, 3, MIXER_HEADS), 0, SEQUENCE_LENGTH - SEQUENCE_LENGTH // 4)
    holding = jnp.any((token_place >= stretch_start) & (token_place < stretch_start + stretch_length), axis=1)
    holding = holding & jnp.logical_not(gradual_decay)[None, :]
    spike_location = jax.random.randint(spike_random_key, (1, 2, MIXER_HEADS), 0, SEQUENCE_LENGTH)
    spike_depth = jax.random.uniform(depth_random_key, (1, 2, MIXER_HEADS), jnp.float32, 0.25, 0.6)
    per_head_rates = jnp.exp(head_log)
    spike_unscaled = jnp.log(jnp.expm1(spike_depth / per_head_rates)) - per_head_bias
    spike_hit_index = (token_place == spike_location) & gradual_decay[None, None, :]
    spike_height = jnp.max(jnp.where(spike_hit_index, spike_unscaled, -100.0), axis=1)
    spike_hit = jnp.any(spike_hit_index, axis=1)
    draw_value_rows = jnp.where(holding, -3.0, random_jitter)
    draw_value_rows = jnp.where(spike_hit, spike_height, draw_value_rows)
    return draw_value_rows.astype(jnp.bfloat16)


def draw_out_grad(key, part):
    key = jax.random.fold_in(key, 13)
    token_place = lax_positions(SEQUENCE_LENGTH)
    scales = jnp.exp(math.log(3.0) * token_place)[:, None]
    random_jitter = jnp.clip(jax.random.normal(key, (SEQUENCE_LENGTH, CHANNELS), jnp.float32), -4.0, 4.0)
    return (random_jitter * scales).astype(jnp.bfloat16)


def lax_positions(count):
    return jnp.arange(count, dtype=jnp.float32) / count


def block_levels(own_key, shape, shards, smallest, largest):
    level = 1.0
    for dim, shards_of in shards:
        heights = jax.random.uniform(jax.random.fold_in(jax.random.fold_in(own_key, 6), dim), (shards_of,), jnp.float32, smallest / len(shards), largest / len(shards))
        level = level * jnp.repeat(jnp.exp(heights), shape[dim] // shards_of).reshape((-1,) + (1,) * (len(shape) - 1 - dim))
    return level


def centred(own_key, dims, width, reach, cuts=(), kind=jnp.bfloat16):
    drawn = jax.random.normal(own_key, dims, jnp.float32) * width
    if len(cuts) > 0:
        drawn = block_levels(own_key, dims, cuts, -0.22, 0.18) * drawn
    return jnp.clip(drawn, min=-reach, max=reach).astype(kind)


def setup_inputs(seed: int = 0) -> dict:
    streams_of = jax.random.split(jax.random.key(seed), 11)
    mixer_x = centred(streams_of[0], (SEQUENCE_LENGTH, CHANNELS), 1.0, 6.0, ((0, 32),))
    gate_z = centred(streams_of[1], (SEQUENCE_LENGTH, CHANNELS), 1.0, 6.0, ((0, 32),))
    b_matrix = centred(streams_of[2], (SEQUENCE_LENGTH, GROUPS * STATE), 1.0, 6.0, ((0, 32),))
    c_matrix = centred(streams_of[3], (SEQUENCE_LENGTH, GROUPS * STATE), 1.0, 6.0, ((0, 32),))
    raw_steps = draw_raw_steps(jax.random.fold_in(streams_of[10], 71), 0)
    decay_log = draw_decay_log(jax.random.fold_in(streams_of[10], 71), 0)
    skip_gain = jnp.clip(0.5 + 1.0 * jax.random.uniform(streams_of[6], (MIXER_HEADS,), jnp.float32) ** block_levels(streams_of[6], (MIXER_HEADS,), ((0, 2),), -0.2, 0.2), 0.5, 1.5)
    step_bias = draw_step_bias(jax.random.fold_in(streams_of[10], 71), 0)
    norm_gain = jnp.clip(1.0 + 0.1 * jax.random.normal(streams_of[8], (CHANNELS,), jnp.float32), 0.5, 1.5)
    out_grad = draw_out_grad(jax.random.fold_in(streams_of[10], 71), 0)
    return {"mixer_x": mixer_x, "gate_z": gate_z, "b_matrix": b_matrix, "c_matrix": c_matrix, "raw_steps": raw_steps, "decay_log": decay_log, "skip_gain": skip_gain, "step_bias": step_bias, "norm_gain": norm_gain, "out_grad": out_grad}


precise = lax.Precision.HIGHEST
epsilon = 1e-05

def decay_rates(raw_steps, decay_log, step_bias):
    stepsize = jax.nn.softplus(raw_steps.astype(jnp.float32) + step_bias)
    cumulative = jnp.cumsum(-jnp.exp(decay_log) * stepsize, axis=0)
    return (stepsize, cumulative)

def block_state(mixer_x, b_matrix, raw_steps, decay_log, step_bias):
    stepsize, cumulative = decay_rates(raw_steps, decay_log, step_bias)
    totals = cumulative[-1]
    weights = jnp.exp(totals[None] - cumulative) * stepsize
    scaled = mixer_x.astype(jnp.float32) * weights[..., None]
    states = jnp.einsum('lgkp,lgn->gkpn', scaled, b_matrix.astype(jnp.float32), precision=precise)
    return (states, totals)

def block_output(mixer_x, gate_z, b_matrix, c_matrix, raw_steps, decay_log, skip_gain, step_bias, norm_gain, inbound):
    stepsize, cumulative = decay_rates(raw_steps, decay_log, step_bias)
    value_rows = mixer_x.astype(jnp.float32)
    sources = b_matrix.astype(jnp.float32)
    readers = c_matrix.astype(jnp.float32)
    scores = jnp.einsum('tgn,sgn->gts', readers, sources, precision=precise)
    length = value_rows.shape[0]
    causal = lax.broadcasted_iota(jnp.int32, (length, length), 0) >= lax.broadcasted_iota(jnp.int32, (length, length), 1)
    by_head = jnp.transpose(cumulative, (1, 2, 0))
    spread = by_head[..., :, None] - by_head[..., None, :]
    decays = jnp.exp(jnp.where(causal, spread, -jnp.inf))
    weights = scores[:, None] * decays * jnp.transpose(stepsize, (1, 2, 0))[:, :, None, :]
    within = jnp.einsum('gkts,sgkp->tgkp', weights, value_rows, precision=precise)
    carried = jnp.einsum('tgn,gkpn->tgkp', readers, inbound, precision=precise) * jnp.exp(cumulative)[..., None]
    mixed = within + carried + skip_gain[None, :, :, None] * value_rows
    gated = mixed * jax.nn.silu(gate_z.astype(jnp.float32))
    power = lax.optimization_barrier(jnp.mean(gated * gated, axis=(2, 3), keepdims=True))
    return gated * lax.rsqrt(power + epsilon) * norm_gain[None]

def reference(mixer_x, gate_z, b_matrix, c_matrix, raw_steps, decay_log, skip_gain, step_bias, norm_gain, out_grad):
    blocks = SEQUENCE_LENGTH // SLAB
    per_group = MIXER_HEADS // GROUPS

    def channel_view(array):
        shaped = array.reshape(blocks, SLAB, GROUPS, 1, per_group, HEAD_DIM)
        return jnp.transpose(shaped, (2, 0, 1, 3, 4, 5))

    def state_view(array):
        shaped = array.reshape(blocks, SLAB, GROUPS, 1, STATE)
        return jnp.transpose(shaped, (2, 0, 1, 3, 4))

    def steps_view(array):
        shaped = array.reshape(blocks, SLAB, GROUPS, 1, per_group)
        return jnp.transpose(shaped, (2, 0, 1, 3, 4))

    def one_group(pieces):

        def forward(value_rows, gates, sources, readers, steps, logs, skips, biases, gains):
            states, totals = jax.vmap(block_state, in_axes=(0, 0, 0, None, None))(value_rows, sources, steps, logs, biases)

            def advance(carry, item):
                return (jnp.exp(item[1])[..., None, None] * carry + item[0], carry)
            unused, inbound = lax.scan(advance, jnp.zeros(states.shape[1:], jnp.float32), (states, totals))
            return jax.vmap(block_output, in_axes=(0, 0, 0, 0, 0, None, None, None, None, 0))(value_rows, gates, sources, readers, steps, logs, skips, biases, gains, inbound)
        normed, pullback = jax.vjp(forward, pieces[0], pieces[1], pieces[2], pieces[3], pieces[4], pieces[5], pieces[6], pieces[7], pieces[8])
        return pullback(pieces[9].astype(jnp.float32))
    grads = lax.map(one_group, (channel_view(mixer_x), channel_view(gate_z), state_view(b_matrix), state_view(c_matrix), steps_view(raw_steps), decay_log.reshape(GROUPS, 1, per_group), skip_gain.reshape(GROUPS, 1, per_group), step_bias.reshape(GROUPS, 1, per_group), norm_gain.reshape(GROUPS, 1, per_group, HEAD_DIM), channel_view(out_grad)))

    def channel_back(array):
        return jnp.transpose(array, (1, 2, 0, 3, 4, 5)).reshape(SEQUENCE_LENGTH, CHANNELS).astype(jnp.bfloat16)

    def state_back(array):
        return jnp.transpose(array, (1, 2, 0, 3, 4)).reshape(SEQUENCE_LENGTH, GROUPS * STATE).astype(jnp.bfloat16)

    def steps_back(array):
        return jnp.transpose(array, (1, 2, 0, 3, 4)).reshape(SEQUENCE_LENGTH, MIXER_HEADS).astype(jnp.bfloat16)
    return (channel_back(grads[0]), channel_back(grads[1]), state_back(grads[2]), state_back(grads[3]), steps_back(grads[4]), grads[5].reshape(MIXER_HEADS), grads[6].reshape(MIXER_HEADS), grads[7].reshape(MIXER_HEADS), grads[8].reshape(CHANNELS))
```

```python
import jax
import jax.numpy as jnp
from jax import lax
from jax.experimental import pallas as pl
from jax.experimental.pallas import tpu as pltpu
from jax.sharding import Mesh
from jax.sharding import PartitionSpec as P

MIXER_HEADS = 128
HEAD_DIM = 64
STATE = 128
GROUPS = 8
HEADS = MIXER_HEADS // GROUPS
WIDTH = HEADS * HEAD_DIM
PAIRS = HEADS // 2
CHUNK = 128
LANES = 128
epsilon = 1e-05
f32 = jnp.float32
bf16 = jnp.bfloat16

DT, CUM, WEIGHT, SHIFTED, ECUM, RATE, SIG = range(7)
X, B, C, STEPS = 0, WIDTH, WIDTH + STATE, WIDTH + 2 * STATE
FIRST = WIDTH + 2 * STATE + LANES
CLAMP = 80.0


def mm(a, b):
    return jnp.dot(a, b, preferred_element_type=f32)


def mm_nt(a, b):
    return lax.dot_general(a, b, (((1,), (1,)), ((), ())), preferred_element_type=f32)


def mm_tn(a, b):
    return lax.dot_general(a, b, (((0,), (0,)), ((), ())), preferred_element_type=f32)


def mm_exact(a, b):
    return jnp.dot(a, b, precision=lax.Precision.HIGHEST, preferred_element_type=f32)


def low_half(rows):
    return lax.broadcasted_iota(jnp.int32, (rows, LANES), 1) < HEAD_DIM


def spread_pair(values, kind, j):
    rows = values.shape[0]
    at = kind * HEADS + 2 * j
    return jnp.where(
        low_half(rows),
        jnp.broadcast_to(values[:, at : at + 1], (rows, LANES)),
        jnp.broadcast_to(values[:, at + 1 : at + 2], (rows, LANES)),
    )


def spread_row(row):
    rows = jnp.broadcast_to(row, (8, LANES))
    return jnp.concatenate([spread_pair(rows, 0, j) for j in range(PAIRS)], axis=1)


def head_matrix():
    channel = lax.broadcasted_iota(jnp.int32, (WIDTH, LANES), 0) // HEAD_DIM
    lane = lax.broadcasted_iota(jnp.int32, (WIDTH, LANES), 1) % HEADS
    return jnp.where(channel == lane, 1.0, 0.0).astype(bf16)


def head_sum(values, ones):
    high = values.astype(bf16)
    low = (values - high.astype(f32)).astype(bf16)
    return mm(high, ones) + mm(low, ones)


def split_pair(block):
    low = low_half(block.shape[0])
    zero = jnp.zeros_like(block)
    return jnp.concatenate(
        [jnp.where(low, block, zero), jnp.where(low, zero, block)], axis=0
    )


def blocks_of(sub_count, tensor_count):
    return [t * sub_count + s for s in range(sub_count) for t in range(tensor_count)]


def pack_first(owners, x_ref, b_ref, c_ref, steps_ref, out_ref):
    for j, g in enumerate(owners):
        out_ref[j, :, X : X + WIDTH] = x_ref[:, g * WIDTH : (g + 1) * WIDTH]
        out_ref[j, :, B : B + STATE] = b_ref[:, g * STATE : (g + 1) * STATE]
        out_ref[j, :, C : C + STATE] = c_ref[:, g * STATE : (g + 1) * STATE]
        out_ref[j, :, STEPS : STEPS + LANES] = steps_ref[...]


def pack_second(owners, z_ref, grad_ref, out_ref):
    for j, g in enumerate(owners):
        out_ref[j, :, :WIDTH] = z_ref[:, g * WIDTH : (g + 1) * WIDTH]
        out_ref[j, :, WIDTH:] = grad_ref[:, g * WIDTH : (g + 1) * WIDTH]


def unpack_gates(owners, in_ref, out_ref):
    for j, g in enumerate(owners):
        out_ref[:, g * WIDTH : (g + 1) * WIDTH] = in_ref[j]


def unpack_last(owners, in_ref, x_ref, b_ref, c_ref, steps_ref):
    steps = None
    for j, g in enumerate(owners):
        x_ref[:, g * WIDTH : (g + 1) * WIDTH] = in_ref[j, :, X : X + WIDTH]
        b_ref[:, g * STATE : (g + 1) * STATE] = in_ref[j, :, B : B + STATE]
        c_ref[:, g * STATE : (g + 1) * STATE] = in_ref[j, :, C : C + STATE]
        part = in_ref[j, :, STEPS : STEPS + LANES].astype(f32)
        steps = part if steps is None else steps + part
    steps_ref[...] = steps.astype(bf16)


def state_kernel(
    first_ref, pick_ref, heads_ref, sm_ref, smt_ref, own_ref, dec_ref, state_ref, whole_ref,
    carry, total,
):
    c = pl.program_id(0)

    @pl.when(c == 0)
    def _():
        carry[...] = jnp.zeros_like(carry)
        total[...] = jnp.zeros_like(total)

    raw = mm(first_ref[:, STEPS : STEPS + LANES], pick_ref[...]) + heads_ref[1:2, :]
    small = jnp.exp(-jnp.abs(raw))
    series = small * (1.0 - small * (0.5 - small * (1.0 / 3 - small * (0.25 - small * 0.2))))
    soft = jnp.maximum(raw, 0.0) + jnp.where(small < 0.015625, series, jnp.log(1.0 + small))
    sig = jnp.where(raw >= 0.0, 1.0, small) / (1.0 + small)
    rate = -jnp.exp(heads_ref[0:1, :]) * soft
    t = lax.broadcasted_iota(jnp.int32, (CHUNK, CHUNK), 0)
    s = lax.broadcasted_iota(jnp.int32, (CHUNK, CHUNK), 1)
    cum = mm_exact(jnp.where(t >= s, 1.0, 0.0), rate)
    after = mm_exact(jnp.where(t < s, 1.0, 0.0), rate)
    kind = lax.broadcasted_iota(jnp.int32, (CHUNK, LANES), 1) // HEADS
    sm = jnp.where(kind == DT, soft, jnp.zeros_like(soft))
    sm = jnp.where(kind == CUM, cum, sm)
    sm = jnp.where(kind == WEIGHT, soft * jnp.exp(after), sm)
    sm = jnp.where(kind == SHIFTED, cum - jnp.log(soft), sm)
    sm = jnp.where(kind == ECUM, jnp.exp(cum), sm)
    sm = jnp.where(kind == RATE, rate, sm)
    sm = jnp.where(kind == SIG, sig, sm)
    sm_ref[...] = sm
    smt_ref[...] = sm.T

    last = cum[CHUNK - 1 : CHUNK, :]
    total[...] += jnp.broadcast_to(last, total.shape)
    dec = spread_row(jnp.exp(last))
    dec_ref[0] = dec
    sources_t = first_ref[:, B : B + STATE].T
    for j in range(PAIRS):
        at = slice(j * LANES, (j + 1) * LANES)
        scaled = first_ref[:, at].astype(f32) * spread_pair(sm, WEIGHT, j)
        hi = scaled.astype(bf16)
        own = mm(sources_t, hi) + mm(sources_t, (scaled - hi.astype(f32)).astype(bf16))
        own_ref[0, :, at] = own
        new = dec[0:1, at] * carry[:, at] + own
        carry[:, at] = new
        state_ref[:, at] = new.astype(bf16)
    whole_ref[...] = spread_row(jnp.exp(total[0:1, :]))


def within_kernel(first_ref, sm_ref, smt_ref, out_ref):
    t = lax.broadcasted_iota(jnp.int32, (CHUNK, CHUNK), 0)
    s = lax.broadcasted_iota(jnp.int32, (CHUNK, CHUNK), 1)
    scores = mm_nt(first_ref[:, C : C + STATE], first_ref[:, B : B + STATE])
    scores = jnp.where(t >= s, scores, 0.0)
    for j in range(PAIRS):
        weights = []
        for h in (2 * j, 2 * j + 1):
            here = sm_ref[:, CUM * HEADS + h : CUM * HEADS + h + 1]
            there = smt_ref[SHIFTED * HEADS + h : SHIFTED * HEADS + h + 1, :]
            weights.append((scores * jnp.exp(jnp.minimum(here - there, CLAMP))).astype(bf16))
        at = slice(j * LANES, (j + 1) * LANES)
        out_ref[:, at] = mm(jnp.concatenate(weights, axis=1), split_pair(first_ref[:, at]))


def output_kernel(
    first_ref, second_ref, within_ref, sm_ref, inbound_ref, own_ref, dec_ref, gain_ref, skip_ref,
    gate_ref, mixed_ref, e_ref, back_ref, slab_ref, readers_ref, end_ref, param_ref,
    carry, pre, back_sum, gain_sum, skip_sum, ys, gated_s, high_s, low_s, scaled_s, wide_s,
):
    c = pl.program_id(0)

    @pl.when(c == 0)
    def _():
        carry[...] = inbound_ref[...].astype(f32)
        pre[...] = jnp.ones_like(pre)
        back_sum[...] = jnp.zeros_like(back_sum)
        gain_sum[...] = jnp.zeros_like(gain_sum)
        skip_sum[...] = jnp.zeros_like(skip_sum)

    sm = sm_ref[...]
    readers = first_ref[:, C : C + STATE]
    state = carry[...].astype(bf16)
    carried = mm(readers, state) + mm(readers, (carry[...]-state.astype(f32)).astype(bf16))
    power = jnp.zeros((CHUNK, LANES), f32)
    cross = jnp.zeros((CHUNK, LANES), f32)
    for j in range(PAIRS):
        at = slice(j * LANES, (j + 1) * LANES)
        values = first_ref[:, at].astype(f32)
        gates = second_ref[:, at].astype(f32)
        y = within_ref[:, at] + spread_pair(sm, ECUM, j) * carried[:, at]
        ys[:, at] = y
        mixed = y + skip_ref[0:1, at] * values
        gated = mixed * (gates / (1.0 + jnp.exp(-gates)))
        gated_s[:, at] = gated
        grad = second_ref[:, WIDTH + j * LANES : WIDTH + (j + 1) * LANES].astype(f32)
        power = power + gated * gated
        cross = cross + grad * gain_ref[0:1, at] * gated
    inverse = lax.rsqrt(jnp.sum(power, axis=1, keepdims=True) * (1.0 / WIDTH) + epsilon)
    pull = inverse * inverse * inverse * (jnp.sum(cross, axis=1, keepdims=True) * (1.0 / WIDTH))
    for j in range(PAIRS):
        at = slice(j * LANES, (j + 1) * LANES)
        values = first_ref[:, at].astype(f32)
        gates = second_ref[:, at].astype(f32)
        grad = second_ref[:, WIDTH + j * LANES : WIDTH + (j + 1) * LANES].astype(f32)
        y = ys[:, at]
        gated = gated_s[:, at]
        mixed = y + skip_ref[0:1, at] * values
        sig = 1.0 / (1.0 + jnp.exp(-gates))
        scaled = inverse * grad
        gain_sum[0:1, at] += jnp.sum(scaled * gated, axis=0, keepdims=True)
        d_gated = scaled * gain_ref[0:1, at] - pull * gated
        silu = gates * sig
        d_mixed = d_gated * silu
        gate_ref[:, at] = (d_gated * mixed * (sig + silu * (1.0 - sig))).astype(bf16)
        skip_sum[0:1, at] += jnp.sum(values * d_mixed, axis=0, keepdims=True)
        rounded = d_mixed.astype(bf16)
        mixed_ref[:, at] = rounded
        rounded = rounded.astype(f32)
        product = rounded * y
        high = product.astype(bf16)
        high_s[:, at] = high
        low_s[:, at] = (product - high.astype(f32)).astype(bf16)
        wide_s[:, at] = d_mixed * spread_pair(sm, ECUM, j)
    ones = head_matrix()
    e_ref[...] = mm(high_s[...], ones) + mm(low_s[...], ones)
    outgoing = wide_s[...].astype(bf16)
    lowg = (wide_s[...] - outgoing.astype(f32)).astype(bf16)
    readers_ref[...] = mm_nt(outgoing, state)
    back = mm(readers.T, outgoing) + mm(readers.T, lowg)
    back_ref[0] = back
    back_sum[...] += pre[0:1, :] * back
    slab_ref[...] = back_sum[...].astype(bf16)
    dec = dec_ref[0, 0:1, :]
    pre[...] = pre[...] * dec
    new = dec * carry[...] + own_ref[0]
    carry[...] = new
    end_ref[0] = new

    @pl.when(c == pl.num_programs(0) - 1)
    def _():
        for j in range(PAIRS):
            param_ref[j : j + 1, :] = gain_sum[0:1, j * LANES : (j + 1) * LANES]
        skips = head_sum(jnp.broadcast_to(skip_sum[0:1, :], (8, WIDTH)), ones)
        param_ref[PAIRS:, :] = skips


def local_kernel(
    first_ref, grad_ref, sm_ref, smt_ref, readers_ref, values_out, sources_out, readers_out
):
    s = lax.broadcasted_iota(jnp.int32, (CHUNK, CHUNK), 0)
    t = lax.broadcasted_iota(jnp.int32, (CHUNK, CHUNK), 1)
    causal = t >= s
    sources = first_ref[:, B : B + STATE]
    readers = first_ref[:, C : C + STATE]
    scores = jnp.where(causal, mm_nt(sources, readers), 0.0)
    total = jnp.zeros((CHUNK, CHUNK), f32)
    for j in range(PAIRS):
        at = slice(j * LANES, (j + 1) * LANES)
        grads = split_pair(grad_ref[:, at])
        weight_grads = mm_nt(first_ref[:, at], grads)
        weights = []
        for k, h in enumerate((2 * j, 2 * j + 1)):
            there = sm_ref[:, SHIFTED * HEADS + h : SHIFTED * HEADS + h + 1]
            here = smt_ref[CUM * HEADS + h : CUM * HEADS + h + 1, :]
            decay = jnp.exp(jnp.minimum(here - there, CLAMP))
            weights.append((scores * decay).astype(bf16))
            total = total + weight_grads[:, k * CHUNK : (k + 1) * CHUNK] * decay
        values_out[:, at] = mm(jnp.concatenate(weights, axis=1), grads)
    total = jnp.where(causal, total, 0.0).astype(bf16)
    sources_out[...] = mm(total, readers)
    readers_out[...] = (mm_tn(total, sources) + readers_ref[...]).astype(bf16)


def last_kernel(
    first_ref, within_ref, sources_ref, readers_ref, grad_ref, e_ref, sm_ref, outer_ref,
    back_ref, end_ref, dec_ref, skip_ref, heads_ref, place_ref,
    out_ref, param_ref,
    carry, high_s, low_s, scaled_s, flux_s,
):
    c = pl.program_id(0)

    @pl.when(c == 0)
    def _():
        carry[...] = outer_ref[...].astype(f32)
        param_ref[...] = jnp.zeros_like(param_ref)

    sm = sm_ref[...]
    state = carry[...]
    rounded = state.astype(bf16)
    arriving = mm(first_ref[:, B : B + STATE], rounded) + mm(first_ref[:, B : B + STATE], (state - rounded.astype(f32)).astype(bf16))
    for j in range(PAIRS):
        at = slice(j * LANES, (j + 1) * LANES)
        values = first_ref[:, at].astype(f32)
        weight = spread_pair(sm, WEIGHT, j)
        grad = within_ref[:, at] + weight * arriving[:, at]
        out_ref[:, at] = (grad + skip_ref[0:1, at] * grad_ref[:, at].astype(f32)).astype(bf16)
        product = values * grad
        high = product.astype(bf16)
        high_s[:, at] = high
        low_s[:, at] = (product - high.astype(f32)).astype(bf16)
        scaled_s[:, at] = (values * weight).astype(bf16)
        flux_s[:, at] = jnp.broadcast_to(
            jnp.sum(end_ref[0, :, at].astype(f32) * state[:, at], axis=0, keepdims=True), (8, LANES)
        )
    ones = head_matrix()
    g = mm(high_s[...], ones) + mm(low_s[...], ones)
    constant = head_sum(flux_s[...], ones)[0:1, :]
    sources = sources_ref[...] + mm_nt(scaled_s[...], rounded)
    out_ref[:, B : B + STATE] = sources.astype(bf16)
    out_ref[:, C : C + STATE] = readers_ref[...]
    s = lax.broadcasted_iota(jnp.int32, (CHUNK, CHUNK), 0)
    t = lax.broadcasted_iota(jnp.int32, (CHUNK, CHUNK), 1)
    flux = constant + mm_exact(jnp.where(t >= s, 1.0, 0.0), e_ref[...] - g)
    own_heads = lax.broadcasted_iota(jnp.int32, (CHUNK, LANES), 1) < HEADS
    steps = g / jnp.where(own_heads, sm, 1.0) - jnp.exp(heads_ref[0:1, :]) * flux
    steps = steps * pltpu.roll(sm, LANES - SIG * HEADS, 1)
    steps = jnp.where(own_heads, steps, 0.0)
    out_ref[:, STEPS : STEPS + LANES] = mm(steps.astype(bf16), place_ref[...]).astype(bf16)
    logs = jnp.where(own_heads, flux * pltpu.roll(sm, LANES - RATE * HEADS, 1), 0.0)
    param_ref[0:1, :] += jnp.sum(logs, axis=0, keepdims=True)
    param_ref[1:2, :] += jnp.sum(steps, axis=0, keepdims=True)
    carry[...] = dec_ref[0, 0:1, :] * state + back_ref[0]


def call(kernel, out_shape, flops, moved, grid=None, in_specs=None, out_specs=None, scratch=()):
    extra = {}
    if grid is not None:
        extra = dict(grid=grid, in_specs=in_specs, out_specs=out_specs)
    return pl.pallas_call(
        kernel,
        out_shape=out_shape,
        scratch_shapes=list(scratch),
        compiler_params=pltpu.CompilerParams(vmem_limit_bytes=40 * 1024 * 1024),
        cost_estimate=pl.CostEstimate(flops=flops, bytes_accessed=moved, transcendentals=0),
        **extra,
    )


def shifted(array, count, by):
    pairs = [(i, i + by) for i in range(count) if 0 <= i + by < count]
    return lax.ppermute(array, "slab", pairs)


def carry_over(state, decay, first_decay, count, sign):
    window, window_decay, step = state, decay, 1
    result = result_decay = None
    while step < count:
        arrived = shifted(window, count, sign * step)
        more = 2 * step < count
        if result is None:
            result, result_decay = arrived, first_decay
            if more:
                window = (state.astype(f32) + decay[0:1] * arrived.astype(f32)).astype(bf16)
                window_decay = decay * first_decay
        else:
            if more:
                arrived_decay = shifted(window_decay, count, sign * step)
                window = (window.astype(f32) + window_decay[0:1] * arrived.astype(f32)).astype(bf16)
                window_decay = window_decay * arrived_decay
            result = result.astype(f32) + result_decay[0:1] * arrived.astype(f32)
            if more:
                result_decay = result_decay * arrived_decay
        step *= 2
    return jnp.zeros_like(state) if result is None else result


def on_device(
    slab_count, sub_count, tensor_count,
    mixer_x, gate_z, b_matrix, c_matrix, raw_steps, decay_log, skip_gain, step_bias, norm_gain, out_grad,
):
    rows = mixer_x.shape[0]
    peers = sub_count * tensor_count
    tokens = rows * peers
    chunks = tokens // CHUNK
    owners = blocks_of(sub_count, tensor_count)
    sub = lax.axis_index("sub")
    group = lax.axis_index("tensor") * sub_count + sub

    def struct(shape, kind=f32):
        return jax.ShapeDtypeStruct(shape, kind)

    def exchange(array):
        return lax.all_to_all(array, ("sub", "tensor"), split_axis=0, concat_axis=0, tiled=True)

    own_logs = lax.dynamic_slice(decay_log, (sub * HEADS,), (HEADS,))
    own_bias = lax.dynamic_slice(step_bias, (sub * HEADS,), (HEADS,))
    own_skip = lax.dynamic_slice(skip_gain, (sub * HEADS,), (HEADS,))
    own_gain = lax.dynamic_slice(norm_gain, (sub * WIDTH,), (WIDTH,)).reshape(1, WIDTH)
    repeats = LANES // HEADS
    heads = jnp.stack([jnp.tile(own_logs, repeats), jnp.tile(own_bias, repeats)])
    skip_row = jnp.repeat(own_skip, HEAD_DIM).reshape(1, WIDTH)
    from_head = lax.broadcasted_iota(jnp.int32, (LANES, LANES), 0)
    to_lane = lax.broadcasted_iota(jnp.int32, (LANES, LANES), 1)
    pick = (from_head == group * HEADS + to_lane % HEADS).astype(bf16)
    place = ((to_lane == group * HEADS + from_head) & (from_head < HEADS)).astype(bf16)

    def packed(kernel, width, *arrays):
        size = peers * rows * width * 2
        out = struct((peers, rows, width), bf16)
        return call(lambda *refs: kernel(owners, *refs), out, 0, 2 * size)(*arrays)

    first = exchange(packed(pack_first, FIRST, mixer_x, b_matrix, c_matrix, raw_steps))
    first = first.reshape(tokens, FIRST)
    second = exchange(packed(pack_second, 2 * WIDTH, gate_z, out_grad))
    second = second.reshape(tokens, 2 * WIDTH)

    def row_block(width):
        return pl.BlockSpec((CHUNK, width), lambda c: (c, 0))

    def whole(*shape):
        return pl.BlockSpec(shape, lambda c: (0,) * len(shape))

    lane_block = pl.BlockSpec((LANES, CHUNK), lambda c: (0, c))
    state_block = pl.BlockSpec((1, STATE, WIDTH), lambda c: (c, 0, 0))
    dec_block = pl.BlockSpec((1, 8, WIDTH), lambda c: (c, 0, 0))
    grid = (chunks,)
    unit = 2 * tokens * CHUNK * WIDTH

    sm, smt, own, dec, state, decay = call(
        state_kernel,
        (
            struct((tokens, LANES)), struct((LANES, tokens)), struct((chunks, STATE, WIDTH)),
            struct((chunks, 8, WIDTH)), struct((STATE, WIDTH), bf16), struct((8, WIDTH)),
        ),
        unit, tokens * WIDTH * 8, grid,
        [row_block(FIRST), whole(LANES, LANES), whole(2, LANES)],
        (
            row_block(LANES), lane_block, state_block,
            dec_block, whole(STATE, WIDTH), whole(8, WIDTH),
        ),
        [pltpu.VMEM((STATE, WIDTH), f32), pltpu.VMEM((8, LANES), f32)],
    )(first, pick, heads)

    before = shifted(decay, slab_count, 1) if slab_count > 1 else None
    after = shifted(decay, slab_count, -1) if slab_count > 1 else None
    inbound = carry_over(state, decay, before, slab_count, 1)

    within = call(
        within_kernel,
        struct((tokens, WIDTH)),
        4 * unit, tokens * WIDTH * 8, grid,
        [row_block(FIRST), row_block(LANES), lane_block],
        row_block(WIDTH),
    )(first, sm, smt)

    d_gates, d_mixed, e, back, slab_back, readers_part, ends, params = call(
        output_kernel,
        (
            struct((tokens, WIDTH), bf16), struct((tokens, WIDTH), bf16), struct((tokens, LANES)),
            struct((chunks, STATE, WIDTH)), struct((STATE, WIDTH), bf16), struct((tokens, STATE)),
            struct((chunks, STATE, WIDTH)), struct((PAIRS + 8, LANES)),
        ),
        4 * unit, tokens * WIDTH * 20, grid,
        [
            row_block(FIRST), row_block(2 * WIDTH), row_block(WIDTH), row_block(LANES),
            whole(STATE, WIDTH), state_block, dec_block, whole(1, WIDTH), whole(1, WIDTH),
        ],
        (
            row_block(WIDTH), row_block(WIDTH), row_block(LANES),
            state_block, whole(STATE, WIDTH), row_block(STATE),
            state_block, whole(PAIRS + 8, LANES),
        ),
        [
            pltpu.VMEM((STATE, WIDTH), f32), pltpu.VMEM((8, WIDTH), f32),
            pltpu.VMEM((STATE, WIDTH), f32), pltpu.VMEM((8, WIDTH), f32),
            pltpu.VMEM((8, WIDTH), f32), pltpu.VMEM((CHUNK, WIDTH), f32),
            pltpu.VMEM((CHUNK, WIDTH), f32), pltpu.VMEM((CHUNK, WIDTH), bf16),
            pltpu.VMEM((CHUNK, WIDTH), bf16), pltpu.VMEM((CHUNK, WIDTH), bf16), pltpu.VMEM((CHUNK, WIDTH), f32),
        ],
    )(first, second, within, sm, inbound, own, dec, own_gain, skip_row)

    gates_back = exchange(d_gates.reshape(peers, rows, WIDTH))

    def gathered(array):
        copies = slab_count * sub_count
        sent = jnp.broadcast_to(array[None], (copies,) + array.shape)
        got = lax.all_to_all(sent, ("slab", "sub"), split_axis=0, concat_axis=0, tiled=True)
        return jnp.sum(got.reshape((slab_count, sub_count) + array.shape), axis=0)

    outer = carry_over(slab_back, decay, after, slab_count, -1)

    d_values, d_sources, d_readers = call(
        local_kernel,
        (
            struct((tokens, WIDTH)), struct((tokens, STATE)), struct((tokens, STATE), bf16),
        ),
        8 * unit, tokens * WIDTH * 8, grid,
        [row_block(FIRST), row_block(WIDTH), row_block(LANES), lane_block, row_block(STATE)],
        (row_block(WIDTH), row_block(STATE), row_block(STATE)),
    )(first, d_mixed, sm, smt, readers_part)

    def down(spec):
        def index(c):
            return tuple(spec.index_map(chunks - 1 - c))

        return pl.BlockSpec(spec.block_shape, index)

    rows_down = lambda width: down(row_block(width))
    last, last_params = call(
        last_kernel,
        (struct((tokens, FIRST), bf16), struct((8, LANES))),
        2 * unit, tokens * WIDTH * 16, grid,
        [
            rows_down(FIRST), rows_down(WIDTH), rows_down(STATE), rows_down(STATE),
            rows_down(WIDTH), rows_down(LANES), rows_down(LANES), whole(STATE, WIDTH),
            down(state_block), down(state_block), down(dec_block), whole(1, WIDTH),
            whole(2, LANES), whole(LANES, LANES),
        ],
        (rows_down(FIRST), whole(8, LANES)),
        [
            pltpu.VMEM((STATE, WIDTH), f32), pltpu.VMEM((CHUNK, WIDTH), bf16),
            pltpu.VMEM((CHUNK, WIDTH), bf16), pltpu.VMEM((CHUNK, WIDTH), bf16),
            pltpu.VMEM((8, WIDTH), f32),
        ],
    )(
        first, d_values, d_sources, d_readers, d_mixed, e, sm, outer, back, ends, dec,
        skip_row, heads, place,
    )

    last_back = exchange(last.reshape(peers, rows, FIRST))
    grad_gates = call(
        lambda *refs: unpack_gates(owners, *refs),
        struct((rows, GROUPS * WIDTH), bf16), 0, 4 * rows * GROUPS * WIDTH,
    )(gates_back)
    grad_x, grad_b, grad_c, grad_steps = call(
        lambda *refs: unpack_last(owners, *refs),
        (
            struct((rows, GROUPS * WIDTH), bf16), struct((rows, GROUPS * STATE), bf16),
            struct((rows, GROUPS * STATE), bf16), struct((rows, MIXER_HEADS), bf16),
        ),
        0, 4 * rows * GROUPS * FIRST,
    )(last_back)
    early = gathered(params)
    late = gathered(last_params)
    return (
        grad_x,
        grad_gates,
        grad_b,
        grad_c,
        grad_steps,
        late[:, 0, :HEADS].reshape(-1),
        early[:, PAIRS, :HEADS].reshape(-1),
        late[:, 1, :HEADS].reshape(-1),
        early[:, :PAIRS].reshape(-1),
    )


def solution(mesh):
    tensor_count = mesh.shape["tensor"]
    sub_count = GROUPS // tensor_count
    slab_count = mesh.shape["dp"] // sub_count
    devices = mesh.devices.reshape(slab_count, sub_count, tensor_count)
    split_mesh = Mesh(devices, ("slab", "sub", "tensor"))
    rows = P(("slab", "sub", "tensor"), None)
    param = P("tensor")

    def local(*arrays):
        return on_device(slab_count, sub_count, tensor_count, *arrays)

    return jax.shard_map(
        local,
        mesh=split_mesh,
        in_specs=(rows,) * 5 + (param,) * 4 + (rows,),
        out_specs=(rows,) * 5 + (param,) * 4,
        check_vma=False,
    )
```

```python
import jax
import jax.numpy as jnp
from jax import lax
from jax.experimental import pallas as pl
from jax.experimental.pallas import tpu as pltpu
from jax.sharding import Mesh
from jax.sharding import PartitionSpec as P

MIXER_HEADS = 128
HEAD_DIM = 64
STATE = 128
GROUPS = 8
CHANNELS = MIXER_HEADS * HEAD_DIM
HEADS = 8
WIDTH = HEADS * HEAD_DIM
GROUP_WIDTH = 2 * WIDTH
OWNERS = MIXER_HEADS // HEADS
LANES = 128
PAIRS = WIDTH // LANES
CHUNK = 128
STEP_ROWS = 16
epsilon = 1e-05
f32 = jnp.float32
bf16 = jnp.bfloat16

DT, CUM, WEIGHT, SHIFTED, ECUM, RATE, SIG = range(7)
KINDS = 8
CLAMP = 80.0


def mm(a, b):
    return jnp.dot(a, b, preferred_element_type=f32)


def mm_nt(a, b):
    return lax.dot_general(a, b, (((1,), (1,)), ((), ())), preferred_element_type=f32)


def mm_tn(a, b):
    return lax.dot_general(a, b, (((0,), (0,)), ((), ())), preferred_element_type=f32)


def mm_exact(a, b):
    return jnp.dot(a, b, precision=lax.Precision.HIGHEST, preferred_element_type=f32)


def two_terms(values):
    high = values.astype(bf16)
    return high, (values - high.astype(f32)).astype(bf16)


def mm_two(a, high, low):
    both = mm(a, jnp.concatenate([high, low], axis=1))
    width = high.shape[1]
    return both[:, :width] + both[:, width:]


def low_half(rows):
    return lax.broadcasted_iota(jnp.int32, (rows, LANES), 1) < HEAD_DIM


def spread_pair(values, kind, j):
    rows = values.shape[0]
    at = kind * HEADS + 2 * j
    return jnp.where(
        low_half(rows),
        jnp.broadcast_to(values[:, at : at + 1], (rows, LANES)),
        jnp.broadcast_to(values[:, at + 1 : at + 2], (rows, LANES)),
    )


def head_rows():
    row = lax.broadcasted_iota(jnp.int32, (16, WIDTH), 0)
    channel = lax.broadcasted_iota(jnp.int32, (16, WIDTH), 1) // HEAD_DIM
    return jnp.where(row == channel, 1.0, 0.0).astype(bf16)


def split_pair(block):
    low = low_half(block.shape[0])
    zero = jnp.zeros_like(block)
    return jnp.concatenate(
        [jnp.where(low, block, zero), jnp.where(low, zero, block)], axis=0
    )


def lanes(j):
    return slice(j * LANES, (j + 1) * LANES)


class Message:
    def __init__(self, rows):
        self.rows = rows
        self.per_chunk = CHUNK // rows

    def place(self, chunk, k):
        r = self.rows
        return (slice(chunk * self.per_chunk, (chunk + 1) * self.per_chunk), slice(k * r, (k + 1) * r))

    def get(self, ref, chunk, k):
        a, b = self.place(chunk, k)
        return ref[a, b, :].reshape(CHUNK, LANES)

    def put(self, ref, chunk, k, value):
        a, b = self.place(chunk, k)
        ref[a, b, :] = value.reshape(self.per_chunk, self.rows, LANES)


X, B = 0, PAIRS
FIRST = PAIRS + 1
Z, GRAD, C = 0, PAIRS, 2 * PAIRS
SECOND = 2 * PAIRS + 1
LAST_X, LAST_B, LAST_C = 0, PAIRS, PAIRS + 1
LAST = PAIRS + 2


def pack_first(owners, x_ref, b_ref, steps_ref, out_ref):
    r = x_ref.shape[0]
    steps = steps_ref[...].astype(f32)
    padded = jnp.concatenate([steps, jnp.zeros((LANES - r, LANES), f32)], axis=0)
    by_head = padded.T
    zero = jnp.zeros((STEP_ROWS - HEADS, LANES), f32)
    for peer, own in enumerate(owners):
        for j in range(PAIRS):
            out_ref[peer, j * r : (j + 1) * r, :] = x_ref[:, lanes(own * PAIRS + j)]
        out_ref[peer, B * r : (B + 1) * r, :] = b_ref[:, lanes(own // 2)]
        mine = jnp.concatenate([by_head[own * HEADS : (own + 1) * HEADS, :], zero], axis=0)
        out_ref[peer, FIRST * r :, :] = mine.astype(bf16)


def pack_second(owners, z_ref, grad_ref, c_ref, out_ref):
    r = z_ref.shape[0]
    for peer, own in enumerate(owners):
        for j in range(PAIRS):
            out_ref[peer, (Z + j) * r : (Z + j + 1) * r, :] = z_ref[:, lanes(own * PAIRS + j)]
            out_ref[peer, (GRAD + j) * r : (GRAD + j + 1) * r, :] = grad_ref[:, lanes(own * PAIRS + j)]
        out_ref[peer, C * r : (C + 1) * r, :] = c_ref[:, lanes(own // 2)]


def unpack_gates(owners, in_ref, out_ref):
    r = out_ref.shape[0]
    for peer, own in enumerate(owners):
        for j in range(PAIRS):
            out_ref[:, lanes(own * PAIRS + j)] = in_ref[peer, j * r : (j + 1) * r, :]


def unpack_last(owners, in_ref, x_ref, b_ref, c_ref, steps_ref):
    r = x_ref.shape[0]
    peer_of = {own: peer for peer, own in enumerate(owners)}
    for peer, own in enumerate(owners):
        for j in range(PAIRS):
            x_ref[:, lanes(own * PAIRS + j)] = in_ref[peer, j * r : (j + 1) * r, :]
    for g in range(GROUPS):
        for block, ref in ((LAST_B, b_ref), (LAST_C, c_ref)):
            at = slice(block * r, (block + 1) * r)
            halves = [in_ref[peer_of[2 * g + k], at, :].astype(f32) for k in range(2)]
            ref[:, lanes(g)] = (halves[0] + halves[1]).astype(bf16)
    by_head = jnp.concatenate(
        [in_ref[peer_of[own], LAST * r :, :].astype(f32)[:HEADS] for own in range(OWNERS)], axis=0
    )
    steps_ref[...] = by_head.T[:r, :].astype(bf16)


def state_kernel(
    message, per_step,
    first_ref, heads_ref, sm_ref, smt_ref, own_ref, dec_ref, state_ref, whole_ref,
    carry,
):
    @pl.when(pl.program_id(0) == 0)
    def _():
        carry[...] = jnp.zeros_like(carry)
        whole_ref[...] = jnp.ones_like(whole_ref)

    r = message.rows
    before = lax.broadcasted_iota(jnp.int32, (CHUNK, CHUNK), 0)
    after = lax.broadcasted_iota(jnp.int32, (CHUNK, CHUNK), 1)
    up_to = jnp.where(before <= after, 1.0, 0.0)
    beyond = jnp.where(before > after, 1.0, 0.0)
    for i in range(per_step):
        raw = None
        for p in range(message.per_chunk):
            part = first_ref[i * message.per_chunk + p, FIRST * r :, :].astype(f32)[:HEADS]
            part = part if p == 0 else pltpu.roll(part, p * r, 1)
            raw = part if raw is None else raw + part
        raw = raw + heads_ref[HEADS:, :]
        small = jnp.exp(-jnp.abs(raw))
        series = small * (
            1.0 - small * (0.5 - small * (1.0 / 3 - small * (0.25 - small * 0.2)))
        )
        soft = jnp.maximum(raw, 0.0) + jnp.where(small < 0.015625, series, jnp.log(1.0 + small))
        sig = jnp.where(raw >= 0.0, 1.0, small) / (1.0 + small)
        rate = -jnp.exp(heads_ref[:HEADS, :]) * soft
        cum = mm_exact(rate, up_to)
        rest = mm_exact(rate, beyond)
        rows = jnp.concatenate(
            [
                soft, cum, soft * jnp.exp(rest), cum - jnp.log(soft), jnp.exp(cum), rate, sig,
                jnp.zeros_like(soft),
            ],
            axis=0,
        )
        smt_ref[:, lanes(i)] = rows
        sm = jnp.concatenate([rows, jnp.zeros_like(rows)], axis=0).T
        sm_ref[i * CHUNK : (i + 1) * CHUNK, :] = sm
        last = jnp.broadcast_to(sm[CHUNK - 1 : CHUNK, :], (8, LANES))
        sources_t = message.get(first_ref, i, B).T
        for j in range(PAIRS):
            dec = spread_pair(last, ECUM, j)
            dec_ref[i, :, lanes(j)] = dec
            whole_ref[:, lanes(j)] = whole_ref[:, lanes(j)] * dec
            scaled = message.get(first_ref, i, X + j).astype(f32) * spread_pair(sm, WEIGHT, j)
            own = mm_two(sources_t, *two_terms(scaled))
            own_ref[i, :, lanes(j)] = own
            carry[:, lanes(j)] = dec[0:1] * carry[:, lanes(j)] + own
    state_ref[...] = carry[...].astype(bf16)


def within_kernel(message, per_step, first_ref, second_ref, sm_ref, smt_ref, out_ref):
    t = lax.broadcasted_iota(jnp.int32, (CHUNK, CHUNK), 0)
    s = lax.broadcasted_iota(jnp.int32, (CHUNK, CHUNK), 1)
    for i in range(per_step):
        rows = slice(i * CHUNK, (i + 1) * CHUNK)
        scores = mm_nt(message.get(second_ref, i, C), message.get(first_ref, i, B))
        scores = jnp.where(t >= s, scores, 0.0)
        for j in range(PAIRS):
            weights = []
            for h in (2 * j, 2 * j + 1):
                here = sm_ref[rows, CUM * HEADS + h : CUM * HEADS + h + 1]
                there = smt_ref[SHIFTED * HEADS + h : SHIFTED * HEADS + h + 1, lanes(i)]
                weights.append(
                    (scores * jnp.exp(jnp.minimum(here - there, CLAMP))).astype(bf16)
                )
            values = split_pair(message.get(first_ref, i, X + j))
            out_ref[rows, lanes(j)] = mm(jnp.concatenate(weights, axis=1), values)


def mix_kernel(
    message, per_step,
    first_ref, second_ref, within_ref, sm_ref, inbound_ref, own_ref, dec_ref, gain_ref, skip_ref,
    y_ref, start_ref, sums_ref,
    carry,
):
    @pl.when(pl.program_id(0) == 0)
    def _():
        carry[...] = inbound_ref[...].astype(f32)

    for i in range(per_step):
        rows = slice(i * CHUNK, (i + 1) * CHUNK)
        sm = sm_ref[rows, :]
        readers = message.get(second_ref, i, C)
        power = jnp.zeros((CHUNK, LANES), f32)
        cross = jnp.zeros((CHUNK, LANES), f32)
        for j in range(PAIRS):
            state = carry[:, lanes(j)]
            start_ref[i, :, lanes(j)] = state
            carried = mm_two(readers, *two_terms(state))
            carry[:, lanes(j)] = dec_ref[i, 0:1, lanes(j)] * state + own_ref[i, :, lanes(j)]
            y = within_ref[rows, lanes(j)] + spread_pair(sm, ECUM, j) * carried
            y_ref[rows, lanes(j)] = y
            values = message.get(first_ref, i, X + j).astype(f32)
            gates = message.get(second_ref, i, Z + j).astype(f32)
            grad = message.get(second_ref, i, GRAD + j).astype(f32)
            gated = (y + skip_ref[0:1, lanes(j)] * values) * (gates / (1.0 + jnp.exp(-gates)))
            power = power + gated * gated
            cross = cross + grad * gain_ref[0:1, lanes(j)] * gated
        sums_ref[i, 0:1, :] = jnp.sum(power.T, axis=0, keepdims=True)
        sums_ref[i, 1:2, :] = jnp.sum(cross.T, axis=0, keepdims=True)
        sums_ref[i, 2:, :] = jnp.zeros((6, LANES), f32)


def norm_kernel(
    message, per_step,
    first_ref, second_ref, y_ref, sm_ref, start_ref, dec_ref, sums_ref, other_ref, gain_ref, skip_ref,
    gate_ref, mixed_ref, e_ref, back_ref, slab_ref, readers_ref, param_ref,
    pre, back_sum, gain_sum, skip_sum, high_s, low_s, scaled_s,
):
    c = pl.program_id(0)

    @pl.when(c == 0)
    def _():
        pre[...] = jnp.ones_like(pre)
        back_sum[...] = jnp.zeros_like(back_sum)
        gain_sum[...] = jnp.zeros_like(gain_sum)
        skip_sum[...] = jnp.zeros_like(skip_sum)

    ones = head_rows()
    for i in range(per_step):
        rows = slice(i * CHUNK, (i + 1) * CHUNK)
        sm = sm_ref[rows, :]
        readers = message.get(second_ref, i, C)
        readers_t = readers.T
        sums = (sums_ref[i] + other_ref[i]) * (1.0 / GROUP_WIDTH)
        inverse_row = lax.rsqrt(sums[0:1] + epsilon)
        pull_row = inverse_row * inverse_row * inverse_row * sums[1:2]
        inverse = jnp.broadcast_to(inverse_row, (CHUNK, LANES)).T
        pull = jnp.broadcast_to(pull_row, (CHUNK, LANES)).T
        for j in range(PAIRS):
            at = lanes(j)
            values = message.get(first_ref, i, X + j).astype(f32)
            gates = message.get(second_ref, i, Z + j).astype(f32)
            grad = message.get(second_ref, i, GRAD + j).astype(f32)
            y = y_ref[rows, at]
            mixed = y + skip_ref[0:1, at] * values
            sig = 1.0 / (1.0 + jnp.exp(-gates))
            silu = gates * sig
            gated = mixed * silu
            scaled = inverse * grad
            gain_sum[0:1, at] += jnp.sum(scaled * gated, axis=0, keepdims=True)
            d_gated = scaled * gain_ref[0:1, at] - pull * gated
            d_mixed = d_gated * silu
            d_gate = d_gated * mixed * (sig + silu * (1.0 - sig))
            message.put(gate_ref, i, j, d_gate.astype(bf16))
            skip_sum[0:1, at] += jnp.sum(values * d_mixed, axis=0, keepdims=True)
            rounded = d_mixed.astype(bf16)
            mixed_ref[rows, at] = rounded
            high_s[:, at], low_s[:, at] = two_terms(rounded.astype(f32) * y)
            high, low = two_terms(d_mixed * spread_pair(sm, ECUM, j))
            scaled_s[:, at] = high
            back = mm_two(readers_t, high, low)
            back_ref[i, :, at] = back
            back_sum[:, at] += pre[0:1, at] * back
            pre[:, at] = pre[:, at] * dec_ref[i, :, at]
        e_ref[:, lanes(i)] = (mm_nt(ones, high_s[...]) + mm_nt(ones, low_s[...]))[:HEADS]
        readers_ref[rows, :] = mm_nt(scaled_s[...], start_ref[i].astype(bf16))
    slab_ref[...] = back_sum[...].astype(bf16)

    @pl.when(c == pl.num_programs(0) - 1)
    def _():
        for j in range(PAIRS):
            param_ref[j : j + 1, :] = gain_sum[0:1, lanes(j)]
        high, low = two_terms(jnp.broadcast_to(skip_sum[0:1, :], (LANES, WIDTH)))
        skips = (mm_nt(high, ones) + mm_nt(low, ones))[0:1]
        param_ref[PAIRS : PAIRS + 1, :] = jnp.concatenate(
            [skips, jnp.zeros((1, LANES - 16), f32)], axis=1
        )
        param_ref[PAIRS + 1 :, :] = jnp.zeros((8 - PAIRS - 1, LANES), f32)


def local_kernel(
    message, per_step,
    first_ref, second_ref, grad_ref, sm_ref, smt_ref, readers_ref,
    values_out, sources_out, readers_out,
):
    s = lax.broadcasted_iota(jnp.int32, (CHUNK, CHUNK), 0)
    t = lax.broadcasted_iota(jnp.int32, (CHUNK, CHUNK), 1)
    causal = t >= s
    for i in range(per_step):
        rows = slice(i * CHUNK, (i + 1) * CHUNK)
        sources = message.get(first_ref, i, B)
        readers = message.get(second_ref, i, C)
        scores = jnp.where(causal, mm_nt(sources, readers), 0.0)
        total = jnp.zeros((CHUNK, CHUNK), f32)
        for j in range(PAIRS):
            grads = split_pair(grad_ref[rows, lanes(j)])
            weight_grads = mm_nt(message.get(first_ref, i, X + j), grads)
            weights = []
            for k, h in enumerate((2 * j, 2 * j + 1)):
                there = sm_ref[rows, SHIFTED * HEADS + h : SHIFTED * HEADS + h + 1]
                here = smt_ref[CUM * HEADS + h : CUM * HEADS + h + 1, lanes(i)]
                decay = jnp.exp(jnp.minimum(here - there, CLAMP))
                weights.append((scores * decay).astype(bf16))
                total = total + weight_grads[:, lanes(k)] * decay
            values_out[rows, lanes(j)] = mm(jnp.concatenate(weights, axis=1), grads)
        total = jnp.where(causal, total, 0.0).astype(bf16)
        sources_out[rows, :] = mm(total, readers)
        readers_out[rows, :] = (mm_tn(total, sources) + readers_ref[rows, :]).astype(bf16)


def last_kernel(
    message, per_step,
    first_ref, within_ref, sources_ref, readers_ref, grad_ref, e_ref, sm_ref, smt_ref, outer_ref,
    back_ref, start_ref, dec_ref, skip_ref, heads_ref, early_ref,
    out_ref, param_ref,
    carry, sums, high_s, low_s, scaled_s, state_s, flux_s,
):
    c = pl.program_id(0)

    @pl.when(c == 0)
    def _():
        carry[...] = outer_ref[...].astype(f32)
        sums[...] = jnp.zeros_like(sums)

    r = message.rows
    ones = head_rows()
    before = lax.broadcasted_iota(jnp.int32, (CHUNK, CHUNK), 0)
    after = lax.broadcasted_iota(jnp.int32, (CHUNK, CHUNK), 1)
    earlier = jnp.where(before < after, 1.0, 0.0)
    decay_rate = jnp.exp(heads_ref[:HEADS, :])
    for i in reversed(range(per_step)):
        rows = slice(i * CHUNK, (i + 1) * CHUNK)
        sm = sm_ref[rows, :]
        sources = message.get(first_ref, i, B)
        for j in range(PAIRS):
            at = lanes(j)
            state = carry[:, at]
            high, low = two_terms(state)
            state_s[:, at] = high
            values = message.get(first_ref, i, X + j).astype(f32)
            weight = spread_pair(sm, WEIGHT, j)
            grad = within_ref[rows, at] + weight * mm_two(sources, high, low)
            skipped = skip_ref[0:1, at] * grad_ref[rows, at].astype(f32)
            message.put(out_ref, i, LAST_X + j, (grad + skipped).astype(bf16))
            high_s[:, at], low_s[:, at] = two_terms(values * grad)
            scaled_s[:, at] = (values * weight).astype(bf16)
            new = dec_ref[i, 0:1, at] * state + back_ref[i, :, at]
            carry[:, at] = new
            flux_s[:, at] = jnp.broadcast_to(
                jnp.sum(start_ref[i, :, at] * new, axis=0, keepdims=True), (16, LANES)
            )
        d_sources = sources_ref[rows, :] + mm_nt(scaled_s[...], state_s[...])
        message.put(out_ref, i, LAST_B, d_sources.astype(bf16))
        message.put(out_ref, i, LAST_C, readers_ref[rows, :])
        g = (mm_nt(ones, high_s[...]) + mm_nt(ones, low_s[...]))[:HEADS]
        high, low = two_terms(flux_s[...])
        constant = (mm_nt(ones, high) + mm_nt(ones, low))[:HEADS, 0:1]
        flux = constant + mm_exact(g - e_ref[:, lanes(i)], earlier)
        soft = smt_ref[DT * HEADS : (DT + 1) * HEADS, lanes(i)]
        rate = smt_ref[RATE * HEADS : (RATE + 1) * HEADS, lanes(i)]
        sig = smt_ref[SIG * HEADS : (SIG + 1) * HEADS, lanes(i)]
        steps = (g / soft - decay_rate * flux) * sig
        sums[:HEADS, :] += flux * rate
        sums[HEADS:, :] += steps
        steps = jnp.concatenate([steps, jnp.zeros_like(steps)], axis=0)
        for p in range(message.per_chunk):
            part = steps if p == 0 else pltpu.roll(steps, LANES - p * r, 1)
            out_ref[i * message.per_chunk + p, LAST * r :, :] = part.astype(bf16)

    @pl.when(c == pl.num_programs(0) - 1)
    def _():
        param_ref[...] = early_ref[...]
        for k in range(2):
            column = jnp.sum(sums[k * HEADS : (k + 1) * HEADS, :], axis=1, keepdims=True)
            block = jnp.broadcast_to(column, (HEADS, LANES))
            block = jnp.concatenate([block, jnp.zeros((LANES - HEADS, LANES), f32)], axis=0)
            param_ref[PAIRS + 1 + k : PAIRS + 2 + k, :] = block.T[0:1, :]


def call(kernel, out_shape, flops, moved, grid=None, in_specs=None, out_specs=None, scratch=()):
    extra = {}
    if grid is not None:
        extra = dict(grid=grid, in_specs=in_specs, out_specs=out_specs)
    return pl.pallas_call(
        kernel,
        out_shape=out_shape,
        scratch_shapes=list(scratch),
        compiler_params=pltpu.CompilerParams(vmem_limit_bytes=60 * 1024 * 1024),
        cost_estimate=pl.CostEstimate(flops=flops, bytes_accessed=moved, transcendentals=0),
        **extra,
    )


def shifted(array, count, by):
    pairs = [(i, i + by) for i in range(count) if 0 <= i + by < count]
    return lax.ppermute(array, "slab", pairs)


def carry_over(state, decay, first_decay, count, sign):
    window, window_decay, step = state, decay, 1
    result = result_decay = None
    while step < count:
        arrived = shifted(window, count, sign * step)
        more = 2 * step < count
        if result is None:
            result = arrived
            if more:
                result_decay = first_decay
                window = (state.astype(f32) + decay[0:1] * arrived.astype(f32)).astype(bf16)
                window_decay = decay * first_decay
        else:
            if more:
                arrived_decay = shifted(window_decay, count, sign * step)
                window = (window.astype(f32) + window_decay[0:1] * arrived.astype(f32)).astype(bf16)
                window_decay = window_decay * arrived_decay
            result = result.astype(f32) + result_decay[0:1] * arrived.astype(f32)
            if more:
                result_decay = result_decay * arrived_decay
        step *= 2
    return jnp.zeros_like(state) if result is None else result


def sum_over(array, axis, count):
    step = 1
    while step < count:
        array = array + lax.ppermute(array, axis, [(i, i ^ step) for i in range(count)])
        step *= 2
    return array


def on_device(
    slab_count, sub_count, tensor_count,
    mixer_x, gate_z, b_matrix, c_matrix, raw_steps, decay_log, skip_gain, step_bias, norm_gain, out_grad,
):
    rows = mixer_x.shape[0]
    peers = sub_count * tensor_count
    tokens = rows * peers
    chunks = tokens // CHUNK
    per_step = min(2, chunks)
    grid = (chunks // per_step,)
    message = Message(rows)
    owners = [t * sub_count + s for s in range(sub_count) for t in range(tensor_count)]
    sub = lax.axis_index("sub")

    def struct(shape, kind=f32):
        return jax.ShapeDtypeStruct(shape, kind)

    def exchange(array):
        return lax.all_to_all(array, ("sub", "tensor"), split_axis=0, concat_axis=0, tiled=True)

    own_logs = lax.dynamic_slice(decay_log, (sub * HEADS,), (HEADS,))
    own_bias = lax.dynamic_slice(step_bias, (sub * HEADS,), (HEADS,))
    own_skip = lax.dynamic_slice(skip_gain, (sub * HEADS,), (HEADS,))
    own_gain = lax.dynamic_slice(norm_gain, (sub * WIDTH,), (WIDTH,)).reshape(1, WIDTH)
    heads = jnp.broadcast_to(jnp.concatenate([own_logs, own_bias])[:, None], (2 * HEADS, LANES))
    skip_row = jnp.repeat(own_skip, HEAD_DIM).reshape(1, WIDTH)

    first_rows = FIRST * rows + STEP_ROWS
    second_rows = SECOND * rows
    last_rows = LAST * rows + STEP_ROWS

    def packed(kernel, height, *arrays):
        out = struct((peers, height, LANES), bf16)
        moved = 4 * peers * height * LANES
        return call(lambda *refs: kernel(owners, *refs), out, 0, moved)(*arrays)

    first = exchange(packed(pack_first, first_rows, mixer_x, b_matrix, raw_steps))
    second = exchange(packed(pack_second, second_rows, gate_z, out_grad, c_matrix))

    def flow(kernel, shape_specs, flops, moved, in_specs, scratch=()):
        def body(*refs):
            return kernel(message, per_step, *refs)

        shapes = tuple(shape for shape, _ in shape_specs)
        specs = tuple(spec for _, spec in shape_specs)
        return call(body, shapes, flops, moved, grid, in_specs, specs, scratch)

    def spec(block, axis, down=False):
        def index(c):
            at = grid[0] - 1 - c if down else c
            return tuple(at if k == axis else 0 for k in range(len(block)))

        return pl.BlockSpec(block, index)

    span = per_step * CHUNK

    def specs_of(down):
        return dict(
            message=lambda height: spec((per_step * message.per_chunk, height, LANES), 0, down),
            token=lambda width: spec((span, width), 0, down),
            lane=lambda height: spec((height, span), 1, down),
            chunk=lambda *shape: spec((per_step,) + shape, 0, down),
        )

    up, dn = specs_of(False), specs_of(True)

    def whole(*shape):
        return pl.BlockSpec(shape, lambda c: (0,) * len(shape))

    unit = 2 * tokens * CHUNK * WIDTH
    size = tokens * WIDTH

    sm, smt, own, dec, state, decay = flow(
        state_kernel,
        [
            (struct((tokens, LANES)), up["token"](LANES)),
            (struct((KINDS * HEADS, tokens)), up["lane"](KINDS * HEADS)),
            (struct((chunks, STATE, WIDTH)), up["chunk"](STATE, WIDTH)),
            (struct((chunks, 8, WIDTH)), up["chunk"](8, WIDTH)),
            (struct((STATE, WIDTH), bf16), whole(STATE, WIDTH)),
            (struct((8, WIDTH)), whole(8, WIDTH)),
        ],
        2 * unit, size * 8,
        [up["message"](first_rows), whole(2 * HEADS, LANES)],
        [pltpu.VMEM((STATE, WIDTH), f32)],
    )(first, heads)

    before = after = None
    if slab_count > 2:
        before, after = shifted(decay, slab_count, 1), shifted(decay, slab_count, -1)
    inbound = carry_over(state, decay, before, slab_count, 1)

    (within,) = flow(
        within_kernel,
        [(struct((tokens, WIDTH)), up["token"](WIDTH))],
        4 * unit, size * 8,
        [
            up["message"](first_rows), up["message"](second_rows),
            up["token"](LANES), up["lane"](KINDS * HEADS),
        ],
    )(first, second, sm, smt)

    y, starts, sums = flow(
        mix_kernel,
        [
            (struct((tokens, WIDTH)), up["token"](WIDTH)),
            (struct((chunks, STATE, WIDTH)), up["chunk"](STATE, WIDTH)),
            (struct((chunks, 8, LANES)), up["chunk"](8, LANES)),
        ],
        2 * unit, size * 20,
        [
            up["message"](first_rows), up["message"](second_rows), up["token"](WIDTH),
            up["token"](LANES), whole(STATE, WIDTH), up["chunk"](STATE, WIDTH),
            up["chunk"](8, WIDTH), whole(1, WIDTH), whole(1, WIDTH),
        ],
        [pltpu.VMEM((STATE, WIDTH), f32)],
    )(first, second, within, sm, inbound, own, dec, own_gain, skip_row)

    partner = lax.ppermute(sums, "sub", [(i, i ^ 1) for i in range(sub_count)])

    d_gates, d_mixed, e, back, slab_back, readers_part, params = flow(
        norm_kernel,
        [
            (struct((peers, PAIRS * rows, LANES), bf16), up["message"](PAIRS * rows)),
            (struct((tokens, WIDTH), bf16), up["token"](WIDTH)),
            (struct((HEADS, tokens)), up["lane"](HEADS)),
            (struct((chunks, STATE, WIDTH)), up["chunk"](STATE, WIDTH)),
            (struct((STATE, WIDTH), bf16), whole(STATE, WIDTH)),
            (struct((tokens, STATE)), up["token"](STATE)),
            (struct((8, LANES)), whole(8, LANES)),
        ],
        4 * unit, size * 20,
        [
            up["message"](first_rows), up["message"](second_rows), up["token"](WIDTH),
            up["token"](LANES), up["chunk"](STATE, WIDTH), up["chunk"](8, WIDTH),
            up["chunk"](8, LANES), up["chunk"](8, LANES), whole(1, WIDTH), whole(1, WIDTH),
        ],
        [
            pltpu.VMEM((8, WIDTH), f32), pltpu.VMEM((STATE, WIDTH), f32),
            pltpu.VMEM((8, WIDTH), f32), pltpu.VMEM((8, WIDTH), f32),
            pltpu.VMEM((CHUNK, WIDTH), bf16), pltpu.VMEM((CHUNK, WIDTH), bf16),
            pltpu.VMEM((CHUNK, WIDTH), bf16),
        ],
    )(first, second, y, sm, starts, dec, sums, partner, own_gain, skip_row)

    outer = carry_over(slab_back, decay, after, slab_count, -1)
    gates_back = exchange(d_gates)

    d_values, d_sources, d_readers = flow(
        local_kernel,
        [
            (struct((tokens, WIDTH)), up["token"](WIDTH)),
            (struct((tokens, STATE)), up["token"](STATE)),
            (struct((tokens, STATE), bf16), up["token"](STATE)),
        ],
        8 * unit, size * 8,
        [
            up["message"](first_rows), up["message"](second_rows), up["token"](WIDTH),
            up["token"](LANES), up["lane"](KINDS * HEADS), up["token"](STATE),
        ],
    )(first, second, d_mixed, sm, smt, readers_part)

    last, params = flow(
        last_kernel,
        [
            (struct((peers, last_rows, LANES), bf16), dn["message"](last_rows)),
            (struct((8, LANES)), whole(8, LANES)),
        ],
        4 * unit, size * 16,
        [
            dn["message"](first_rows), dn["token"](WIDTH), dn["token"](STATE), dn["token"](STATE),
            dn["token"](WIDTH), dn["lane"](HEADS), dn["token"](LANES), dn["lane"](KINDS * HEADS),
            whole(STATE, WIDTH), dn["chunk"](STATE, WIDTH), dn["chunk"](STATE, WIDTH),
            dn["chunk"](8, WIDTH), whole(1, WIDTH), whole(2 * HEADS, LANES), whole(8, LANES),
        ],
        [
            pltpu.VMEM((STATE, WIDTH), f32), pltpu.VMEM((2 * HEADS, LANES), f32),
            pltpu.VMEM((CHUNK, WIDTH), bf16), pltpu.VMEM((CHUNK, WIDTH), bf16),
            pltpu.VMEM((CHUNK, WIDTH), bf16), pltpu.VMEM((STATE, WIDTH), bf16),
            pltpu.VMEM((16, WIDTH), f32),
        ],
    )(
        first, d_values, d_sources, d_readers, d_mixed, e, sm, smt, outer, back, starts, dec,
        skip_row, heads, params,
    )

    last_back = exchange(last)
    params = sum_over(params, "slab", slab_count)
    mine = lax.broadcasted_iota(jnp.int32, (sub_count, 1, 1), 0) == sub
    params = sum_over(jnp.where(mine, params[None], 0.0), "sub", sub_count)
    grad_gates = call(
        lambda *refs: unpack_gates(owners, *refs),
        struct((rows, CHANNELS), bf16), 0, 4 * rows * CHANNELS,
    )(gates_back)
    grad_x, grad_b, grad_c, grad_steps = call(
        lambda *refs: unpack_last(owners, *refs),
        (
            struct((rows, CHANNELS), bf16), struct((rows, GROUPS * STATE), bf16),
            struct((rows, GROUPS * STATE), bf16), struct((rows, MIXER_HEADS), bf16),
        ),
        0, 6 * rows * CHANNELS,
    )(last_back)
    return (
        grad_x,
        grad_gates,
        grad_b,
        grad_c,
        grad_steps,
        params[:, PAIRS + 1, :HEADS].reshape(-1),
        params[:, PAIRS, :HEADS].reshape(-1),
        params[:, PAIRS + 2, :HEADS].reshape(-1),
        params[:, :PAIRS].reshape(-1),
    )


def solution(mesh):
    tensor_count = mesh.shape["tensor"]
    sub_count = OWNERS // tensor_count
    slab_count = mesh.shape["dp"] // sub_count
    devices = mesh.devices.reshape(slab_count, sub_count, tensor_count)
    split_mesh = Mesh(devices, ("slab", "sub", "tensor"))
    rows = P(("slab", "sub", "tensor"), None)
    param = P("tensor")

    def local(*arrays):
        return on_device(slab_count, sub_count, tensor_count, *arrays)

    return jax.shard_map(
        local,
        mesh=split_mesh,
        in_specs=(rows,) * 5 + (param,) * 4 + (rows,),
        out_specs=(rows,) * 5 + (param,) * 4,
        check_vma=False,
    )
```

```python
import jax
import jax.numpy as jnp
from jax import lax
from jax.experimental import pallas as pl
from jax.experimental.pallas import tpu as pltpu
from jax.sharding import Mesh
from jax.sharding import PartitionSpec as P

MIXER_HEADS = 128
HEAD_DIM = 64
STATE = 128
GROUPS = 8
CHANNELS = MIXER_HEADS * HEAD_DIM
HEADS = 8
WIDTH = HEADS * HEAD_DIM
GROUP_WIDTH = 2 * WIDTH
OWNERS = MIXER_HEADS // HEADS
LANES = 128
PAIRS = WIDTH // LANES
CHUNK = 128
STEP_ROWS = 16
epsilon = 1e-05
f32 = jnp.float32
bf16 = jnp.bfloat16

DT, CUM, WEIGHT, SHIFTED, ECUM, RATE, SIG = range(7)
KINDS = 8
CLAMP = 80.0


def mm(a, b):
    return jnp.dot(a, b, preferred_element_type=f32)


def mm_nt(a, b):
    return lax.dot_general(a, b, (((1,), (1,)), ((), ())), preferred_element_type=f32)


def mm_tn(a, b):
    return lax.dot_general(a, b, (((0,), (0,)), ((), ())), preferred_element_type=f32)


def mm_exact(a, b):
    return jnp.dot(a, b, precision=lax.Precision.HIGHEST, preferred_element_type=f32)


def two_terms(values):
    high = values.astype(bf16)
    return high, (values - high.astype(f32)).astype(bf16)


def mm_two(a, high, low):
    both = mm(a, jnp.concatenate([high, low], axis=1))
    width = high.shape[1]
    return both[:, :width] + both[:, width:]


def low_half(rows):
    return lax.broadcasted_iota(jnp.int32, (rows, LANES), 1) < HEAD_DIM


def spread_pair(values, kind, j):
    rows = values.shape[0]
    at = kind * HEADS + 2 * j
    return jnp.where(
        low_half(rows),
        jnp.broadcast_to(values[:, at : at + 1], (rows, LANES)),
        jnp.broadcast_to(values[:, at + 1 : at + 2], (rows, LANES)),
    )


def head_rows():
    row = lax.broadcasted_iota(jnp.int32, (16, WIDTH), 0)
    channel = lax.broadcasted_iota(jnp.int32, (16, WIDTH), 1) // HEAD_DIM
    return jnp.where(row == channel, 1.0, 0.0).astype(bf16)


def split_pair(block):
    low = low_half(block.shape[0])
    zero = jnp.zeros_like(block)
    return jnp.concatenate(
        [jnp.where(low, block, zero), jnp.where(low, zero, block)], axis=0
    )


def lanes(j):
    return slice(j * LANES, (j + 1) * LANES)


class Message:
    def __init__(self, rows):
        self.rows = rows
        self.per_chunk = CHUNK // rows

    def place(self, chunk, k):
        r = self.rows
        return (slice(chunk * self.per_chunk, (chunk + 1) * self.per_chunk), slice(k * r, (k + 1) * r))

    def get(self, ref, chunk, k):
        a, b = self.place(chunk, k)
        return ref[a, b, :].reshape(CHUNK, LANES)

    def put(self, ref, chunk, k, value):
        a, b = self.place(chunk, k)
        ref[a, b, :] = value.reshape(self.per_chunk, self.rows, LANES)


X, B, C = 0, PAIRS, PAIRS + 1
FIRST = PAIRS + 2
Z, GRAD = 0, PAIRS
SECOND = 2 * PAIRS
GATE_Z, GATE_C = 0, PAIRS
GATES = PAIRS + 1
LAST_X, LAST_B = 0, PAIRS
LAST = PAIRS + 1
TERMS = 3


def pack_first(owners, x_ref, b_ref, c_ref, steps_ref, out_ref):
    r = x_ref.shape[0]
    steps = steps_ref[...].astype(f32)
    padded = jnp.concatenate([steps, jnp.zeros((LANES - r, LANES), f32)], axis=0)
    by_head = padded.T
    zero = jnp.zeros((STEP_ROWS - HEADS, LANES), f32)
    for peer, own in enumerate(owners):
        for j in range(PAIRS):
            out_ref[peer, j * r : (j + 1) * r, :] = x_ref[:, lanes(own * PAIRS + j)]
        out_ref[peer, B * r : (B + 1) * r, :] = b_ref[:, lanes(own // 2)]
        out_ref[peer, C * r : (C + 1) * r, :] = c_ref[:, lanes(own // 2)]
        mine = jnp.concatenate([by_head[own * HEADS : (own + 1) * HEADS, :], zero], axis=0)
        out_ref[peer, FIRST * r :, :] = mine.astype(bf16)


def pack_second(owners, z_ref, grad_ref, out_ref):
    r = z_ref.shape[0]
    for peer, own in enumerate(owners):
        for j in range(PAIRS):
            out_ref[peer, (Z + j) * r : (Z + j + 1) * r, :] = z_ref[:, lanes(own * PAIRS + j)]
            out_ref[peer, (GRAD + j) * r : (GRAD + j + 1) * r, :] = grad_ref[:, lanes(own * PAIRS + j)]


def add_halves(owners, in_ref, block, out_ref):
    r = out_ref.shape[0]
    peer_of = {own: peer for peer, own in enumerate(owners)}
    for g in range(GROUPS):
        halves = [
            in_ref[peer_of[2 * g + k], block * r : (block + 1) * r, :].astype(f32) for k in range(2)
        ]
        out_ref[:, lanes(g)] = (halves[0] + halves[1]).astype(bf16)


def unpack_gates(owners, in_ref, out_ref, c_ref):
    r = out_ref.shape[0]
    for peer, own in enumerate(owners):
        for j in range(PAIRS):
            out_ref[:, lanes(own * PAIRS + j)] = in_ref[peer, j * r : (j + 1) * r, :]
    add_halves(owners, in_ref, GATE_C, c_ref)


def unpack_last(owners, in_ref, x_ref, b_ref, steps_ref):
    r = x_ref.shape[0]
    peer_of = {own: peer for peer, own in enumerate(owners)}
    for peer, own in enumerate(owners):
        for j in range(PAIRS):
            x_ref[:, lanes(own * PAIRS + j)] = in_ref[peer, j * r : (j + 1) * r, :]
    add_halves(owners, in_ref, LAST_B, b_ref)
    by_head = jnp.concatenate(
        [
            in_ref[peer_of[own], LAST * r : LAST * r + STEP_ROWS, :].astype(f32)[:HEADS]
            for own in range(OWNERS)
        ],
        axis=0,
    )
    steps_ref[...] = by_head.T[:r, :].astype(bf16)


def three_terms(values):
    high = values.astype(bf16).astype(f32)
    rest = values - high
    middle = rest.astype(bf16).astype(f32)
    return [high, middle, rest - middle]


def unpack_params(sub_count, tensor_count, late_ref, early_ref, mine_ref, late_out, gain_out, skip_out):
    lane = lax.broadcasted_iota(jnp.int32, (1, LANES), 1)
    late = [jnp.zeros((1, LANES), f32) for _ in range(2)]
    skip = jnp.zeros((1, LANES), f32)

    def placed(rows, at):
        total = rows[at : at + 1] + rows[at + 1 : at + 2] + rows[at + 2 : at + 3]
        return jnp.where(lane < HEADS, total, 0.0)

    for s in range(sub_count):
        late_rows = jnp.zeros((STEP_ROWS, LANES), f32)
        early_rows = jnp.zeros((STEP_ROWS, LANES), f32)
        for t in range(tensor_count):
            mine = mine_ref[t : t + 1, :] > 0.0
            peer = s * tensor_count + t
            late_rows = jnp.where(mine, late_ref[peer].astype(f32), late_rows)
            early_rows = jnp.where(mine, early_ref[peer].astype(f32), early_rows)
        for k in range(2):
            part = placed(late_rows, HEADS + k * TERMS)
            late[k] = late[k] + (part if s == 0 else pltpu.roll(part, s * HEADS, 1))
        part = placed(early_rows, TERMS * PAIRS)
        skip = skip + (part if s == 0 else pltpu.roll(part, s * HEADS, 1))
        gain = early_rows[:PAIRS] + early_rows[PAIRS : 2 * PAIRS] + early_rows[2 * PAIRS : 3 * PAIRS]
        gain_out[s * PAIRS : (s + 1) * PAIRS, :] = gain
    late_out[...] = jnp.concatenate(late + [jnp.zeros((6, LANES), f32)], axis=0)
    skip_out[...] = skip


def state_kernel(
    message, per_step,
    first_ref, heads_ref, sm_ref, smt_ref, own_ref, dec_ref, state_ref, whole_ref,
    carry,
):
    @pl.when(pl.program_id(0) == 0)
    def _():
        carry[...] = jnp.zeros_like(carry)
        whole_ref[...] = jnp.ones_like(whole_ref)

    r = message.rows
    before = lax.broadcasted_iota(jnp.int32, (CHUNK, CHUNK), 0)
    after = lax.broadcasted_iota(jnp.int32, (CHUNK, CHUNK), 1)
    up_to = jnp.where(before <= after, 1.0, 0.0)
    beyond = jnp.where(before > after, 1.0, 0.0)
    for i in range(per_step):
        raw = None
        for p in range(message.per_chunk):
            part = first_ref[i * message.per_chunk + p, FIRST * r :, :].astype(f32)[:HEADS]
            part = part if p == 0 else pltpu.roll(part, p * r, 1)
            raw = part if raw is None else raw + part
        raw = raw + heads_ref[HEADS:, :]
        small = jnp.exp(-jnp.abs(raw))
        series = small * (
            1.0 - small * (0.5 - small * (1.0 / 3 - small * (0.25 - small * 0.2)))
        )
        soft = jnp.maximum(raw, 0.0) + jnp.where(small < 0.015625, series, jnp.log(1.0 + small))
        sig = jnp.where(raw >= 0.0, 1.0, small) / (1.0 + small)
        rate = -jnp.exp(heads_ref[:HEADS, :]) * soft
        cum = mm_exact(rate, up_to)
        rest = mm_exact(rate, beyond)
        rows = jnp.concatenate(
            [
                soft, cum, soft * jnp.exp(rest), cum - jnp.log(soft), jnp.exp(cum), rate, sig,
                jnp.zeros_like(soft),
            ],
            axis=0,
        )
        smt_ref[:, lanes(i)] = rows
        sm = jnp.concatenate([rows, jnp.zeros_like(rows)], axis=0).T
        sm_ref[i * CHUNK : (i + 1) * CHUNK, :] = sm
        last = jnp.broadcast_to(sm[CHUNK - 1 : CHUNK, :], (8, LANES))
        sources_t = message.get(first_ref, i, B).T
        for j in range(PAIRS):
            dec = spread_pair(last, ECUM, j)
            dec_ref[i, :, lanes(j)] = dec
            whole_ref[:, lanes(j)] = whole_ref[:, lanes(j)] * dec
            scaled = message.get(first_ref, i, X + j).astype(f32) * spread_pair(sm, WEIGHT, j)
            own = mm_two(sources_t, *two_terms(scaled))
            own_ref[i, :, lanes(j)] = own
            carry[:, lanes(j)] = dec[0:1] * carry[:, lanes(j)] + own
    state_ref[...] = carry[...].astype(bf16)


def within_kernel(message, per_step, first_ref, sm_ref, smt_ref, out_ref):
    t = lax.broadcasted_iota(jnp.int32, (CHUNK, CHUNK), 0)
    s = lax.broadcasted_iota(jnp.int32, (CHUNK, CHUNK), 1)
    for i in range(per_step):
        rows = slice(i * CHUNK, (i + 1) * CHUNK)
        scores = mm_nt(message.get(first_ref, i, C), message.get(first_ref, i, B))
        scores = jnp.where(t >= s, scores, 0.0)
        for j in range(PAIRS):
            weights = []
            for h in (2 * j, 2 * j + 1):
                here = sm_ref[rows, CUM * HEADS + h : CUM * HEADS + h + 1]
                there = smt_ref[SHIFTED * HEADS + h : SHIFTED * HEADS + h + 1, lanes(i)]
                weights.append(
                    (scores * jnp.exp(jnp.minimum(here - there, CLAMP))).astype(bf16)
                )
            values = split_pair(message.get(first_ref, i, X + j))
            out_ref[rows, lanes(j)] = mm(jnp.concatenate(weights, axis=1), values)


def mix_kernel(
    message, per_step,
    first_ref, second_ref, within_ref, sm_ref, inbound_ref, own_ref, dec_ref, gain_ref, skip_ref,
    y_ref, start_ref, sums_ref,
    carry,
):
    @pl.when(pl.program_id(0) == 0)
    def _():
        carry[...] = inbound_ref[...].astype(f32)

    for i in range(per_step):
        rows = slice(i * CHUNK, (i + 1) * CHUNK)
        sm = sm_ref[rows, :]
        readers = message.get(first_ref, i, C)
        power = jnp.zeros((CHUNK, LANES), f32)
        cross = jnp.zeros((CHUNK, LANES), f32)
        for j in range(PAIRS):
            state = carry[:, lanes(j)]
            start_ref[i, :, lanes(j)] = state
            carried = mm_two(readers, *two_terms(state))
            carry[:, lanes(j)] = dec_ref[i, 0:1, lanes(j)] * state + own_ref[i, :, lanes(j)]
            y = within_ref[rows, lanes(j)] + spread_pair(sm, ECUM, j) * carried
            y_ref[rows, lanes(j)] = y
            values = message.get(first_ref, i, X + j).astype(f32)
            gates = message.get(second_ref, i, Z + j).astype(f32)
            grad = message.get(second_ref, i, GRAD + j).astype(f32)
            gated = (y + skip_ref[0:1, lanes(j)] * values) * (gates / (1.0 + jnp.exp(-gates)))
            power = power + gated * gated
            cross = cross + grad * gain_ref[0:1, lanes(j)] * gated
        sums_ref[i, 0:1, :] = jnp.sum(power.T, axis=0, keepdims=True)
        sums_ref[i, 1:2, :] = jnp.sum(cross.T, axis=0, keepdims=True)
        sums_ref[i, 2:, :] = jnp.zeros((6, LANES), f32)


def norm_kernel(
    message, per_step,
    first_ref, second_ref, y_ref, sm_ref, start_ref, dec_ref, sums_ref, other_ref, gain_ref, skip_ref,
    gate_ref, mixed_ref, e_ref, back_ref, slab_ref, readers_ref, param_ref,
    pre, back_sum, gain_sum, skip_sum, high_s, low_s, scaled_s,
):
    c = pl.program_id(0)

    @pl.when(c == 0)
    def _():
        pre[...] = jnp.ones_like(pre)
        back_sum[...] = jnp.zeros_like(back_sum)
        gain_sum[...] = jnp.zeros_like(gain_sum)
        skip_sum[...] = jnp.zeros_like(skip_sum)

    ones = head_rows()
    for i in range(per_step):
        rows = slice(i * CHUNK, (i + 1) * CHUNK)
        sm = sm_ref[rows, :]
        readers = message.get(first_ref, i, C)
        readers_t = readers.T
        sums = (sums_ref[i] + other_ref[i]) * (1.0 / GROUP_WIDTH)
        inverse_row = lax.rsqrt(sums[0:1] + epsilon)
        pull_row = inverse_row * inverse_row * inverse_row * sums[1:2]
        inverse = jnp.broadcast_to(inverse_row, (CHUNK, LANES)).T
        pull = jnp.broadcast_to(pull_row, (CHUNK, LANES)).T
        for j in range(PAIRS):
            at = lanes(j)
            values = message.get(first_ref, i, X + j).astype(f32)
            gates = message.get(second_ref, i, Z + j).astype(f32)
            grad = message.get(second_ref, i, GRAD + j).astype(f32)
            y = y_ref[rows, at]
            mixed = y + skip_ref[0:1, at] * values
            sig = 1.0 / (1.0 + jnp.exp(-gates))
            silu = gates * sig
            gated = mixed * silu
            scaled = inverse * grad
            gain_sum[0:1, at] += jnp.sum(scaled * gated, axis=0, keepdims=True)
            d_gated = scaled * gain_ref[0:1, at] - pull * gated
            d_mixed = d_gated * silu
            d_gate = d_gated * mixed * (sig + silu * (1.0 - sig))
            message.put(gate_ref, i, j, d_gate.astype(bf16))
            skip_sum[0:1, at] += jnp.sum(values * d_mixed, axis=0, keepdims=True)
            rounded = d_mixed.astype(bf16)
            mixed_ref[rows, at] = rounded
            high_s[:, at], low_s[:, at] = two_terms(rounded.astype(f32) * y)
            high, low = two_terms(d_mixed * spread_pair(sm, ECUM, j))
            scaled_s[:, at] = high
            back = mm_two(readers_t, high, low)
            back_ref[i, :, at] = back
            back_sum[:, at] += pre[0:1, at] * back
            pre[:, at] = pre[:, at] * dec_ref[i, :, at]
        e_ref[:, lanes(i)] = (mm_nt(ones, high_s[...]) + mm_nt(ones, low_s[...]))[:HEADS]
        readers_ref[rows, :] = mm_nt(scaled_s[...], start_ref[i].astype(bf16))
    slab_ref[...] = back_sum[...].astype(bf16)

    @pl.when(c == pl.num_programs(0) - 1)
    def _():
        for j in range(PAIRS):
            param_ref[j : j + 1, :] = gain_sum[0:1, lanes(j)]
        high, low = two_terms(jnp.broadcast_to(skip_sum[0:1, :], (LANES, WIDTH)))
        skips = (mm_nt(high, ones) + mm_nt(low, ones))[0:1]
        param_ref[PAIRS : PAIRS + 1, :] = jnp.concatenate(
            [skips, jnp.zeros((1, LANES - 16), f32)], axis=1
        )
        param_ref[PAIRS + 1 :, :] = jnp.zeros((8 - PAIRS - 1, LANES), f32)


def local_kernel(
    message, per_step,
    first_ref, grad_ref, sm_ref, smt_ref, readers_ref, gate_ref,
    values_out, sources_out, gates_out,
):
    s = lax.broadcasted_iota(jnp.int32, (CHUNK, CHUNK), 0)
    t = lax.broadcasted_iota(jnp.int32, (CHUNK, CHUNK), 1)
    causal = t >= s
    for i in range(per_step):
        rows = slice(i * CHUNK, (i + 1) * CHUNK)
        sources = message.get(first_ref, i, B)
        readers = message.get(first_ref, i, C)
        scores = jnp.where(causal, mm_nt(sources, readers), 0.0)
        total = jnp.zeros((CHUNK, CHUNK), f32)
        for j in range(PAIRS):
            grads = split_pair(grad_ref[rows, lanes(j)])
            weight_grads = mm_nt(message.get(first_ref, i, X + j), grads)
            weights = []
            for k, h in enumerate((2 * j, 2 * j + 1)):
                there = sm_ref[rows, SHIFTED * HEADS + h : SHIFTED * HEADS + h + 1]
                here = smt_ref[CUM * HEADS + h : CUM * HEADS + h + 1, lanes(i)]
                decay = jnp.exp(jnp.minimum(here - there, CLAMP))
                weights.append((scores * decay).astype(bf16))
                total = total + weight_grads[:, lanes(k)] * decay
            values_out[rows, lanes(j)] = mm(jnp.concatenate(weights, axis=1), grads)
        total = jnp.where(causal, total, 0.0).astype(bf16)
        sources_out[rows, :] = mm(total, readers)
        d_readers = mm_tn(total, sources) + readers_ref[rows, :]
        message.put(gates_out, i, GATE_C, d_readers.astype(bf16))
        for j in range(PAIRS):
            message.put(gates_out, i, GATE_Z + j, message.get(gate_ref, i, j))


def last_kernel(
    message, per_step,
    first_ref, within_ref, sources_ref, grad_ref, e_ref, sm_ref, smt_ref, outer_ref,
    back_ref, start_ref, dec_ref, skip_ref, heads_ref, early_ref,
    out_ref,
    carry, sums, high_s, low_s, scaled_s, state_s, flux_s,
):
    c = pl.program_id(0)

    @pl.when(c == 0)
    def _():
        carry[...] = outer_ref[...].astype(f32)
        sums[...] = jnp.zeros_like(sums)

    r = message.rows
    ones = head_rows()
    before = lax.broadcasted_iota(jnp.int32, (CHUNK, CHUNK), 0)
    after = lax.broadcasted_iota(jnp.int32, (CHUNK, CHUNK), 1)
    earlier = jnp.where(before < after, 1.0, 0.0)
    decay_rate = jnp.exp(heads_ref[:HEADS, :])
    first_peer = (pl.num_programs(0) - 1 - c) * per_step * message.per_chunk
    mine = out_ref.at[pl.ds(first_peer, per_step * message.per_chunk)]
    for i in reversed(range(per_step)):
        rows = slice(i * CHUNK, (i + 1) * CHUNK)
        sm = sm_ref[rows, :]
        sources = message.get(first_ref, i, B)
        for j in range(PAIRS):
            at = lanes(j)
            state = carry[:, at]
            high, low = two_terms(state)
            state_s[:, at] = high
            values = message.get(first_ref, i, X + j).astype(f32)
            weight = spread_pair(sm, WEIGHT, j)
            grad = within_ref[rows, at] + weight * mm_two(sources, high, low)
            skipped = skip_ref[0:1, at] * grad_ref[rows, at].astype(f32)
            message.put(mine, i, LAST_X + j, (grad + skipped).astype(bf16))
            high_s[:, at], low_s[:, at] = two_terms(values * grad)
            scaled_s[:, at] = (values * weight).astype(bf16)
            new = dec_ref[i, 0:1, at] * state + back_ref[i, :, at]
            carry[:, at] = new
            flux_s[:, at] = jnp.broadcast_to(
                jnp.sum(start_ref[i, :, at] * new, axis=0, keepdims=True), (16, LANES)
            )
        d_sources = sources_ref[rows, :] + mm_nt(scaled_s[...], state_s[...])
        message.put(mine, i, LAST_B, d_sources.astype(bf16))
        g = (mm_nt(ones, high_s[...]) + mm_nt(ones, low_s[...]))[:HEADS]
        high, low = two_terms(flux_s[...])
        constant = (mm_nt(ones, high) + mm_nt(ones, low))[:HEADS, 0:1]
        flux = constant + mm_exact(g - e_ref[:, lanes(i)], earlier)
        soft = smt_ref[DT * HEADS : (DT + 1) * HEADS, lanes(i)]
        rate = smt_ref[RATE * HEADS : (RATE + 1) * HEADS, lanes(i)]
        sig = smt_ref[SIG * HEADS : (SIG + 1) * HEADS, lanes(i)]
        steps = (g / soft - decay_rate * flux) * sig
        sums[:HEADS, :] += flux * rate
        sums[HEADS:, :] += steps
        steps = jnp.concatenate([steps, jnp.zeros_like(steps)], axis=0)
        for p in range(message.per_chunk):
            part = steps if p == 0 else pltpu.roll(steps, LANES - p * r, 1)
            mine[i * message.per_chunk + p, LAST * r : LAST * r + STEP_ROWS, :] = part.astype(bf16)

    @pl.when(c == pl.num_programs(0) - 1)
    def _():
        late = []
        for k in range(2):
            column = jnp.sum(sums[k * HEADS : (k + 1) * HEADS, :], axis=1, keepdims=True)
            block = jnp.broadcast_to(column, (HEADS, LANES))
            block = jnp.concatenate([block, jnp.zeros((LANES - HEADS, LANES), f32)], axis=0)
            late += three_terms(block.T[0:1, :])
        late += [jnp.zeros((HEADS - 2 * TERMS, LANES), f32)]
        late = jnp.concatenate([jnp.zeros((HEADS, LANES), f32)] + late, axis=0)
        late = late.astype(bf16)
        early = three_terms(early_ref[:PAIRS, :]) + three_terms(early_ref[PAIRS : PAIRS + 1, :])
        early += [jnp.zeros((STEP_ROWS - TERMS * (PAIRS + 1), LANES), f32)]
        early = jnp.concatenate(early, axis=0).astype(bf16)
        own_rows = lax.broadcasted_iota(jnp.int32, (STEP_ROWS, LANES), 0) < HEADS

        def fill(peer, unused):
            steps_at = slice(LAST * r, LAST * r + STEP_ROWS)
            out_ref[peer, steps_at, :] = jnp.where(own_rows, out_ref[peer, steps_at, :], late)
            out_ref[peer, LAST * r + STEP_ROWS :, :] = early
            return unused

        lax.fori_loop(0, out_ref.shape[0], fill, 0)


def call(kernel, out_shape, flops, moved, grid=None, in_specs=None, out_specs=None, scratch=()):
    extra = {}
    if grid is not None:
        extra = dict(grid=grid, in_specs=in_specs, out_specs=out_specs)
    return pl.pallas_call(
        kernel,
        out_shape=out_shape,
        scratch_shapes=list(scratch),
        compiler_params=pltpu.CompilerParams(vmem_limit_bytes=16 * 1024 * 1024),
        cost_estimate=pl.CostEstimate(flops=flops, bytes_accessed=moved, transcendentals=0),
        **extra,
    )


def shifted(array, count, by):
    pairs = [(i, i + by) for i in range(count) if 0 <= i + by < count]
    return lax.ppermute(array, "slab", pairs)


def carry_over(state, decay, first_decay, count, sign):
    window, window_decay, step = state, decay, 1
    result = result_decay = None
    while step < count:
        arrived = shifted(window, count, sign * step)
        more = 2 * step < count
        if result is None:
            result = arrived
            if more:
                result_decay = first_decay
                window = (state.astype(f32) + decay[0:1] * arrived.astype(f32)).astype(bf16)
                window_decay = decay * first_decay
        else:
            if more:
                arrived_decay = shifted(window_decay, count, sign * step)
                window = (window.astype(f32) + window_decay[0:1] * arrived.astype(f32)).astype(bf16)
                window_decay = window_decay * arrived_decay
            result = result.astype(f32) + result_decay[0:1] * arrived.astype(f32)
            if more:
                result_decay = result_decay * arrived_decay
        step *= 2
    return jnp.zeros_like(state) if result is None else result


def sum_over(array, axis, count):
    step = 1
    while step < count:
        array = array + lax.ppermute(array, axis, [(i, i ^ step) for i in range(count)])
        step *= 2
    return array


def on_device(
    slab_count, sub_count, tensor_count,
    mixer_x, gate_z, b_matrix, c_matrix, raw_steps, decay_log, skip_gain, step_bias, norm_gain, out_grad,
):
    rows = mixer_x.shape[0]
    peers = sub_count * tensor_count
    tokens = rows * peers
    chunks = tokens // CHUNK
    per_step = min(2, chunks)
    grid = (chunks // per_step,)
    message = Message(rows)
    owners = [t * sub_count + s for s in range(sub_count) for t in range(tensor_count)]
    sub = lax.axis_index("sub")

    def struct(shape, kind=f32):
        return jax.ShapeDtypeStruct(shape, kind)

    def exchange(array):
        return lax.all_to_all(array, ("sub", "tensor"), split_axis=0, concat_axis=0, tiled=True)

    own_logs = lax.dynamic_slice(decay_log, (sub * HEADS,), (HEADS,))
    own_bias = lax.dynamic_slice(step_bias, (sub * HEADS,), (HEADS,))
    own_skip = lax.dynamic_slice(skip_gain, (sub * HEADS,), (HEADS,))
    own_gain = lax.dynamic_slice(norm_gain, (sub * WIDTH,), (WIDTH,)).reshape(1, WIDTH)
    heads = jnp.broadcast_to(jnp.concatenate([own_logs, own_bias])[:, None], (2 * HEADS, LANES))
    skip_row = jnp.repeat(own_skip, HEAD_DIM).reshape(1, WIDTH)

    first_rows = FIRST * rows + STEP_ROWS
    second_rows = SECOND * rows
    gate_rows = GATES * rows
    last_rows = LAST * rows + 2 * STEP_ROWS

    def packed(kernel, height, *arrays):
        out = struct((peers, height, LANES), bf16)
        moved = 4 * peers * height * LANES
        return call(lambda *refs: kernel(owners, *refs), out, 0, moved)(*arrays)

    first = exchange(packed(pack_first, first_rows, mixer_x, b_matrix, c_matrix, raw_steps))
    second = exchange(packed(pack_second, second_rows, gate_z, out_grad))

    def flow(kernel, shape_specs, flops, moved, in_specs, scratch=()):
        def body(*refs):
            return kernel(message, per_step, *refs)

        shapes = tuple(shape for shape, _ in shape_specs)
        specs = tuple(spec for _, spec in shape_specs)
        return call(body, shapes, flops, moved, grid, in_specs, specs, scratch)

    def spec(block, axis, down=False):
        def index(c):
            at = grid[0] - 1 - c if down else c
            return tuple(at if k == axis else 0 for k in range(len(block)))

        return pl.BlockSpec(block, index)

    span = per_step * CHUNK

    def specs_of(down):
        return dict(
            message=lambda height: spec((per_step * message.per_chunk, height, LANES), 0, down),
            token=lambda width: spec((span, width), 0, down),
            lane=lambda height: spec((height, span), 1, down),
            chunk=lambda *shape: spec((per_step,) + shape, 0, down),
        )

    up, dn = specs_of(False), specs_of(True)

    def whole(*shape):
        return pl.BlockSpec(shape, lambda c: (0,) * len(shape))

    unit = 2 * tokens * CHUNK * WIDTH
    size = tokens * WIDTH

    sm, smt, own, dec, state, decay = flow(
        state_kernel,
        [
            (struct((tokens, LANES)), up["token"](LANES)),
            (struct((KINDS * HEADS, tokens)), up["lane"](KINDS * HEADS)),
            (struct((chunks, STATE, WIDTH)), up["chunk"](STATE, WIDTH)),
            (struct((chunks, 8, WIDTH)), up["chunk"](8, WIDTH)),
            (struct((STATE, WIDTH), bf16), whole(STATE, WIDTH)),
            (struct((8, WIDTH)), whole(8, WIDTH)),
        ],
        2 * unit, size * 8,
        [up["message"](first_rows), whole(2 * HEADS, LANES)],
        [pltpu.VMEM((STATE, WIDTH), f32)],
    )(first, heads)

    before = after = None
    if slab_count > 2:
        before, after = shifted(decay, slab_count, 1), shifted(decay, slab_count, -1)
    inbound = carry_over(state, decay, before, slab_count, 1)

    (within,) = flow(
        within_kernel,
        [(struct((tokens, WIDTH)), up["token"](WIDTH))],
        4 * unit, size * 8,
        [
            up["message"](first_rows), up["token"](LANES), up["lane"](KINDS * HEADS),
        ],
    )(first, sm, smt)

    y, starts, sums = flow(
        mix_kernel,
        [
            (struct((tokens, WIDTH)), up["token"](WIDTH)),
            (struct((chunks, STATE, WIDTH)), up["chunk"](STATE, WIDTH)),
            (struct((chunks, 8, LANES)), up["chunk"](8, LANES)),
        ],
        2 * unit, size * 20,
        [
            up["message"](first_rows), up["message"](second_rows), up["token"](WIDTH),
            up["token"](LANES), whole(STATE, WIDTH), up["chunk"](STATE, WIDTH),
            up["chunk"](8, WIDTH), whole(1, WIDTH), whole(1, WIDTH),
        ],
        [pltpu.VMEM((STATE, WIDTH), f32)],
    )(first, second, within, sm, inbound, own, dec, own_gain, skip_row)

    partner = lax.ppermute(sums, "sub", [(i, i ^ 1) for i in range(sub_count)])

    d_gates, d_mixed, e, back, slab_back, readers_part, params = flow(
        norm_kernel,
        [
            (struct((peers, PAIRS * rows, LANES), bf16), up["message"](PAIRS * rows)),
            (struct((tokens, WIDTH), bf16), up["token"](WIDTH)),
            (struct((HEADS, tokens)), up["lane"](HEADS)),
            (struct((chunks, STATE, WIDTH)), up["chunk"](STATE, WIDTH)),
            (struct((STATE, WIDTH), bf16), whole(STATE, WIDTH)),
            (struct((tokens, STATE)), up["token"](STATE)),
            (struct((8, LANES)), whole(8, LANES)),
        ],
        4 * unit, size * 20,
        [
            up["message"](first_rows), up["message"](second_rows), up["token"](WIDTH),
            up["token"](LANES), up["chunk"](STATE, WIDTH), up["chunk"](8, WIDTH),
            up["chunk"](8, LANES), up["chunk"](8, LANES), whole(1, WIDTH), whole(1, WIDTH),
        ],
        [
            pltpu.VMEM((8, WIDTH), f32), pltpu.VMEM((STATE, WIDTH), f32),
            pltpu.VMEM((8, WIDTH), f32), pltpu.VMEM((8, WIDTH), f32),
            pltpu.VMEM((CHUNK, WIDTH), bf16), pltpu.VMEM((CHUNK, WIDTH), bf16),
            pltpu.VMEM((CHUNK, WIDTH), bf16),
        ],
    )(first, second, y, sm, starts, dec, sums, partner, own_gain, skip_row)

    outer = carry_over(slab_back, decay, after, slab_count, -1)
    params = sum_over(params, "slab", slab_count)

    d_values, d_sources, gates_message = flow(
        local_kernel,
        [
            (struct((tokens, WIDTH)), up["token"](WIDTH)),
            (struct((tokens, STATE)), up["token"](STATE)),
            (struct((peers, gate_rows, LANES), bf16), up["message"](gate_rows)),
        ],
        8 * unit, size * 8,
        [
            up["message"](first_rows), up["token"](WIDTH), up["token"](LANES),
            up["lane"](KINDS * HEADS), up["token"](STATE), up["message"](PAIRS * rows),
        ],
    )(first, d_mixed, sm, smt, readers_part, d_gates)
    gates_back = exchange(gates_message)

    (last,) = flow(
        last_kernel,
        [(struct((peers, last_rows, LANES), bf16), whole(peers, last_rows, LANES))],
        4 * unit, size * 16,
        [
            dn["message"](first_rows), dn["token"](WIDTH), dn["token"](STATE),
            dn["token"](WIDTH), dn["lane"](HEADS), dn["token"](LANES), dn["lane"](KINDS * HEADS),
            whole(STATE, WIDTH), dn["chunk"](STATE, WIDTH), dn["chunk"](STATE, WIDTH),
            dn["chunk"](8, WIDTH), whole(1, WIDTH), whole(2 * HEADS, LANES), whole(8, LANES),
        ],
        [
            pltpu.VMEM((STATE, WIDTH), f32), pltpu.VMEM((2 * HEADS, LANES), f32),
            pltpu.VMEM((CHUNK, WIDTH), bf16), pltpu.VMEM((CHUNK, WIDTH), bf16),
            pltpu.VMEM((CHUNK, WIDTH), bf16), pltpu.VMEM((STATE, WIDTH), bf16),
            pltpu.VMEM((16, WIDTH), f32),
        ],
    )(
        first, d_values, d_sources, d_mixed, e, sm, smt, outer, back, starts, dec,
        skip_row, heads, params,
    )

    last_back = exchange(last)
    grad_gates, grad_c = call(
        lambda *refs: unpack_gates(owners, *refs),
        (struct((rows, CHANNELS), bf16), struct((rows, GROUPS * STATE), bf16)),
        0, 4 * rows * CHANNELS,
    )(gates_back)

    tile_at = LAST * rows // STEP_ROWS
    mine = lax.broadcasted_iota(jnp.int32, (tensor_count, LANES), 0) == lax.axis_index("tensor")

    def tile(at):
        return pl.BlockSpec((peers, STEP_ROWS, LANES), lambda c: (0, at, 0))

    late, gain, skip = call(
        lambda *refs: unpack_params(sub_count, tensor_count, *refs),
        (struct((8, LANES)), struct((sub_count * PAIRS, LANES)), struct((1, LANES))),
        0, 4 * peers * STEP_ROWS * LANES, (1,),
        [tile(tile_at), tile(tile_at + 1), whole(tensor_count, LANES)],
        (whole(8, LANES), whole(sub_count * PAIRS, LANES), whole(1, LANES)),
    )(last_back, last_back, mine.astype(f32))
    late = sum_over(late, "slab", slab_count)
    grad_x, grad_b, grad_steps = call(
        lambda *refs: unpack_last(owners, *refs),
        (
            struct((rows, CHANNELS), bf16), struct((rows, GROUPS * STATE), bf16),
            struct((rows, MIXER_HEADS), bf16),
        ),
        0, 6 * rows * CHANNELS,
    )(last_back)
    count = sub_count * HEADS
    return (
        grad_x,
        grad_gates,
        grad_b,
        grad_c,
        grad_steps,
        late[0, :count],
        skip[0, :count],
        late[1, :count],
        gain.reshape(-1),
    )


def solution(mesh):
    tensor_count = mesh.shape["tensor"]
    sub_count = OWNERS // tensor_count
    slab_count = mesh.shape["dp"] // sub_count
    devices = mesh.devices.reshape(slab_count, sub_count, tensor_count)
    split_mesh = Mesh(devices, ("slab", "sub", "tensor"))
    rows = P(("slab", "sub", "tensor"), None)
    param = P("tensor")

    def local(*arrays):
        return on_device(slab_count, sub_count, tensor_count, *arrays)

    return jax.shard_map(
        local,
        mesh=split_mesh,
        in_specs=(rows,) * 5 + (param,) * 4 + (rows,),
        out_specs=(rows,) * 5 + (param,) * 4,
        check_vma=False,
    )
```

```python
import jax
import jax.numpy as jnp
from jax import lax
from jax.experimental import pallas as pl
from jax.experimental.pallas import tpu as pltpu
from jax.sharding import Mesh
from jax.sharding import PartitionSpec as P

MIXER_HEADS = 128
HEAD_DIM = 64
STATE = 128
GROUPS = 8
CHANNELS = MIXER_HEADS * HEAD_DIM
HEADS = 8
WIDTH = HEADS * HEAD_DIM
GROUP_WIDTH = 2 * WIDTH
OWNERS = MIXER_HEADS // HEADS
LANES = 128
PAIRS = WIDTH // LANES
CHUNK = 128
STEP_ROWS = 16
epsilon = 1e-05
f32 = jnp.float32
bf16 = jnp.bfloat16

DT, CUM, WEIGHT, SHIFTED, ECUM, RATE, SIG = range(7)
KINDS = 8
CLAMP = 80.0


def mm(a, b):
    return jnp.dot(a, b, preferred_element_type=f32)


def mm_nt(a, b):
    return lax.dot_general(a, b, (((1,), (1,)), ((), ())), preferred_element_type=f32)


def mm_tn(a, b):
    return lax.dot_general(a, b, (((0,), (0,)), ((), ())), preferred_element_type=f32)


def mm_exact(a, b):
    return jnp.dot(a, b, precision=lax.Precision.HIGHEST, preferred_element_type=f32)


def two_terms(values):
    high = values.astype(bf16)
    return high, (values - high.astype(f32)).astype(bf16)


def mm_two(a, high, low):
    both = mm(a, jnp.concatenate([high, low], axis=1))
    width = high.shape[1]
    return both[:, :width] + both[:, width:]


def sigmoid(values):
    return 0.5 + 0.5 * jnp.tanh(0.5 * values)


def low_half(rows):
    return lax.broadcasted_iota(jnp.int32, (rows, LANES), 1) < HEAD_DIM


def spread_pair(values, kind, j):
    rows = values.shape[0]
    at = kind * HEADS + 2 * j
    return jnp.where(
        low_half(rows),
        jnp.broadcast_to(values[:, at : at + 1], (rows, LANES)),
        jnp.broadcast_to(values[:, at + 1 : at + 2], (rows, LANES)),
    )


def head_rows():
    row = lax.broadcasted_iota(jnp.int32, (16, WIDTH), 0)
    channel = lax.broadcasted_iota(jnp.int32, (16, WIDTH), 1) // HEAD_DIM
    return jnp.where(row == channel, 1.0, 0.0).astype(bf16)


def split_pair(block):
    low = low_half(block.shape[0])
    zero = jnp.zeros_like(block)
    return jnp.concatenate(
        [jnp.where(low, block, zero), jnp.where(low, zero, block)], axis=0
    )


def lanes(j):
    return slice(j * LANES, (j + 1) * LANES)


class Message:
    def __init__(self, rows):
        self.rows = rows
        self.per_chunk = CHUNK // rows

    def place(self, chunk, k):
        r = self.rows
        return (slice(chunk * self.per_chunk, (chunk + 1) * self.per_chunk), slice(k * r, (k + 1) * r))

    def get(self, ref, chunk, k):
        a, b = self.place(chunk, k)
        return ref[a, b, :].reshape(CHUNK, LANES)

    def put(self, ref, chunk, k, value):
        a, b = self.place(chunk, k)
        ref[a, b, :] = value.reshape(self.per_chunk, self.rows, LANES)


X, B, C = 0, PAIRS, PAIRS + 1
FIRST = PAIRS + 2
Z, GRAD = 0, PAIRS
SECOND = 2 * PAIRS
GATE_Z, GATE_C = 0, PAIRS
GATES = PAIRS + 1
LAST_X, LAST_B = 0, PAIRS
LAST = PAIRS + 1
TERMS = 3


def pack_first(x_ref, b_ref, c_ref, steps_ref, out_ref, by_head):
    r = x_ref.shape[0]
    step = pl.program_id(0)
    subs = out_ref.shape[0]

    @pl.when(step == 0)
    def _():
        steps = steps_ref[...].astype(f32)
        by_head[...] = jnp.concatenate([steps, jnp.zeros((LANES - r, LANES), f32)], axis=0).T

    zero = jnp.zeros((STEP_ROWS - HEADS, LANES), f32)
    for s in range(subs):
        for j in range(PAIRS):
            out_ref[s, 0, j * r : (j + 1) * r, :] = x_ref[:, lanes(s * PAIRS + j)]
        out_ref[s, 0, B * r : (B + 1) * r, :] = b_ref[:, lanes(s // 2)]
        out_ref[s, 0, C * r : (C + 1) * r, :] = c_ref[:, lanes(s // 2)]
        at = pl.multiple_of((step * subs + s) * HEADS, HEADS)
        mine = jnp.concatenate([by_head[pl.ds(at, HEADS), :], zero], axis=0)
        out_ref[s, 0, FIRST * r :, :] = mine.astype(bf16)


def pack_second(z_ref, grad_ref, out_ref):
    r = z_ref.shape[0]
    for s in range(out_ref.shape[0]):
        for j in range(PAIRS):
            at = lanes(s * PAIRS + j)
            out_ref[s, 0, (Z + j) * r : (Z + j + 1) * r, :] = z_ref[:, at]
            out_ref[s, 0, (GRAD + j) * r : (GRAD + j + 1) * r, :] = grad_ref[:, at]


def add_halves(owners, in_ref, block, out_ref):
    r = out_ref.shape[0]
    peer_of = {own: peer for peer, own in enumerate(owners)}
    for g in range(GROUPS):
        halves = [
            in_ref[peer_of[2 * g + k], block * r : (block + 1) * r, :].astype(f32) for k in range(2)
        ]
        out_ref[:, lanes(g)] = (halves[0] + halves[1]).astype(bf16)


def unpack_gates(owners, in_ref, out_ref, c_ref):
    r = out_ref.shape[0]
    for peer, own in enumerate(owners):
        for j in range(PAIRS):
            out_ref[:, lanes(own * PAIRS + j)] = in_ref[peer, j * r : (j + 1) * r, :]
    add_halves(owners, in_ref, GATE_C, c_ref)


def unpack_last(owners, in_ref, x_ref, b_ref, steps_ref):
    r = x_ref.shape[0]
    peer_of = {own: peer for peer, own in enumerate(owners)}
    for peer, own in enumerate(owners):
        for j in range(PAIRS):
            x_ref[:, lanes(own * PAIRS + j)] = in_ref[peer, j * r : (j + 1) * r, :]
    add_halves(owners, in_ref, LAST_B, b_ref)
    by_head = jnp.concatenate(
        [
            in_ref[peer_of[own], LAST * r : LAST * r + STEP_ROWS, :].astype(f32)[:HEADS]
            for own in range(OWNERS)
        ],
        axis=0,
    )
    steps_ref[...] = by_head.T[:r, :].astype(bf16)


def three_terms(values):
    high = values.astype(bf16).astype(f32)
    rest = values - high
    middle = rest.astype(bf16).astype(f32)
    return [high, middle, rest - middle]


def unpack_params(sub_count, tensor_count, late_ref, early_ref, mine_ref, out_ref):
    lane = lax.broadcasted_iota(jnp.int32, (1, LANES), 1)
    late = [jnp.zeros((1, LANES), f32) for _ in range(2)]
    skip = jnp.zeros((1, LANES), f32)

    def placed(rows, at):
        total = rows[at : at + 1] + rows[at + 1 : at + 2] + rows[at + 2 : at + 3]
        return jnp.where(lane < HEADS, total, 0.0)

    for s in range(sub_count):
        late_rows = jnp.zeros((STEP_ROWS, LANES), f32)
        early_rows = jnp.zeros((STEP_ROWS, LANES), f32)
        for t in range(tensor_count):
            mine = mine_ref[t : t + 1, :] > 0.0
            peer = s * tensor_count + t
            late_rows = jnp.where(mine, late_ref[peer].astype(f32), late_rows)
            early_rows = jnp.where(mine, early_ref[peer].astype(f32), early_rows)
        for k in range(2):
            part = placed(late_rows, HEADS + k * TERMS)
            late[k] = late[k] + (part if s == 0 else pltpu.roll(part, s * HEADS, 1))
        part = placed(early_rows, TERMS * PAIRS)
        skip = skip + (part if s == 0 else pltpu.roll(part, s * HEADS, 1))
        gain = early_rows[:PAIRS] + early_rows[PAIRS : 2 * PAIRS] + early_rows[2 * PAIRS : 3 * PAIRS]
        out_ref[8 + s * PAIRS : 8 + (s + 1) * PAIRS, :] = gain
    out_ref[:8, :] = jnp.concatenate(late + [skip, jnp.zeros((5, LANES), f32)], axis=0)


def state_kernel(
    message, per_step,
    first_ref, heads_ref, sm_ref, smt_ref, own_ref, dec_ref, state_ref, whole_ref,
    carry,
):
    @pl.when(pl.program_id(0) == 0)
    def _():
        carry[...] = jnp.zeros_like(carry)
        whole_ref[...] = jnp.ones_like(whole_ref)

    r = message.rows
    before = lax.broadcasted_iota(jnp.int32, (CHUNK, CHUNK), 0)
    after = lax.broadcasted_iota(jnp.int32, (CHUNK, CHUNK), 1)
    up_to = jnp.where(before <= after, 1.0, 0.0)
    beyond = jnp.where(before > after, 1.0, 0.0)
    for i in range(per_step):
        raw = None
        for p in range(message.per_chunk):
            part = first_ref[i * message.per_chunk + p, FIRST * r :, :].astype(f32)[:HEADS]
            part = part if p == 0 else pltpu.roll(part, p * r, 1)
            raw = part if raw is None else raw + part
        raw = raw + heads_ref[HEADS:, :]
        small = jnp.exp(-jnp.abs(raw))
        series = small * (
            1.0 - small * (0.5 - small * (1.0 / 3 - small * (0.25 - small * 0.2)))
        )
        soft = jnp.maximum(raw, 0.0) + jnp.where(small < 0.015625, series, jnp.log(1.0 + small))
        sig = jnp.where(raw >= 0.0, 1.0, small) / (1.0 + small)
        rate = -jnp.exp(heads_ref[:HEADS, :]) * soft
        cum = mm_exact(rate, up_to)
        rest = mm_exact(rate, beyond)
        rows = jnp.concatenate(
            [
                soft, cum, soft * jnp.exp(rest), cum - jnp.log(soft), jnp.exp(cum), rate, sig,
                jnp.zeros_like(soft),
            ],
            axis=0,
        )
        smt_ref[:, lanes(i)] = rows
        sm = jnp.concatenate([rows, jnp.zeros_like(rows)], axis=0).T
        sm_ref[i * CHUNK : (i + 1) * CHUNK, :] = sm
        last = jnp.broadcast_to(sm[CHUNK - 1 : CHUNK, :], (8, LANES))
        sources_t = message.get(first_ref, i, B).T
        for j in range(PAIRS):
            dec = spread_pair(last, ECUM, j)
            dec_ref[i, :, lanes(j)] = dec
            whole_ref[:, lanes(j)] = whole_ref[:, lanes(j)] * dec
            scaled = message.get(first_ref, i, X + j).astype(f32) * spread_pair(sm, WEIGHT, j)
            own = mm_two(sources_t, *two_terms(scaled))
            own_ref[i, :, lanes(j)] = own
            carry[:, lanes(j)] = dec[0:1] * carry[:, lanes(j)] + own
    state_ref[...] = carry[...].astype(bf16)


def forward_kernel(
    message, per_step,
    first_ref, sm_ref, smt_ref, inbound_ref, own_ref, dec_ref, y_ref, start_ref, carry,
):
    @pl.when(pl.program_id(0) == 0)
    def _():
        carry[...] = inbound_ref[...].astype(f32)

    t = lax.broadcasted_iota(jnp.int32, (CHUNK, CHUNK), 0)
    s = lax.broadcasted_iota(jnp.int32, (CHUNK, CHUNK), 1)
    for i in range(per_step):
        rows = slice(i * CHUNK, (i + 1) * CHUNK)
        sm = sm_ref[rows, :]
        readers = message.get(first_ref, i, C)
        scores = jnp.where(t >= s, mm_nt(readers, message.get(first_ref, i, B)), 0.0)
        for j in range(PAIRS):
            at = lanes(j)
            weights = []
            for h in (2 * j, 2 * j + 1):
                here = sm_ref[rows, CUM * HEADS + h : CUM * HEADS + h + 1]
                there = smt_ref[SHIFTED * HEADS + h : SHIFTED * HEADS + h + 1, lanes(i)]
                weights.append(
                    (scores * jnp.exp(jnp.minimum(here - there, CLAMP))).astype(bf16)
                )
            values = split_pair(message.get(first_ref, i, X + j))
            within = mm(jnp.concatenate(weights, axis=1), values)
            state = carry[:, at]
            start_ref[i, :, at] = state
            carried = mm_two(readers, *two_terms(state))
            carry[:, at] = dec_ref[i, 0:1, at] * state + own_ref[i, :, at]
            y_ref[rows, at] = within + spread_pair(sm, ECUM, j) * carried


def mix_kernel(message, per_step, first_ref, second_ref, y_ref, gain_ref, skip_ref, sums_ref):
    for i in range(per_step):
        rows = slice(i * CHUNK, (i + 1) * CHUNK)
        power = jnp.zeros((CHUNK, LANES), f32)
        cross = jnp.zeros((CHUNK, LANES), f32)
        for j in range(PAIRS):
            values = message.get(first_ref, i, X + j).astype(f32)
            gates = message.get(second_ref, i, Z + j).astype(f32)
            grad = message.get(second_ref, i, GRAD + j).astype(f32)
            mixed = y_ref[rows, lanes(j)] + skip_ref[0:1, lanes(j)] * values
            gated = mixed * (gates * sigmoid(gates))
            power = power + gated * gated
            cross = cross + grad * gain_ref[0:1, lanes(j)] * gated
        sums_ref[i, 0:1, :] = jnp.sum(power.T, axis=0, keepdims=True)
        sums_ref[i, 1:2, :] = jnp.sum(cross.T, axis=0, keepdims=True)
        sums_ref[i, 2:, :] = jnp.zeros((6, LANES), f32)


def norm_kernel(
    message, per_step,
    first_ref, second_ref, y_ref, sm_ref, start_ref, dec_ref, sums_ref, other_ref, gain_ref, skip_ref,
    gate_ref, mixed_ref, e_ref, back_ref, slab_ref, readers_ref, param_ref,
    pre, back_sum, gain_sum, skip_sum, high_s, low_s, scaled_s,
):
    c = pl.program_id(0)

    @pl.when(c == 0)
    def _():
        pre[...] = jnp.ones_like(pre)
        back_sum[...] = jnp.zeros_like(back_sum)
        gain_sum[...] = jnp.zeros_like(gain_sum)
        skip_sum[...] = jnp.zeros_like(skip_sum)

    ones = head_rows()
    for i in range(per_step):
        rows = slice(i * CHUNK, (i + 1) * CHUNK)
        sm = sm_ref[rows, :]
        readers = message.get(first_ref, i, C)
        readers_t = readers.T
        sums = (sums_ref[i] + other_ref[i]) * (1.0 / GROUP_WIDTH)
        inverse_row = lax.rsqrt(sums[0:1] + epsilon)
        pull_row = inverse_row * inverse_row * inverse_row * sums[1:2]
        inverse = jnp.broadcast_to(inverse_row, (CHUNK, LANES)).T
        pull = jnp.broadcast_to(pull_row, (CHUNK, LANES)).T
        for j in range(PAIRS):
            at = lanes(j)
            values = message.get(first_ref, i, X + j).astype(f32)
            gates = message.get(second_ref, i, Z + j).astype(f32)
            grad = message.get(second_ref, i, GRAD + j).astype(f32)
            y = y_ref[rows, at]
            mixed = y + skip_ref[0:1, at] * values
            sig = sigmoid(gates)
            silu = gates * sig
            gated = mixed * silu
            scaled = inverse * grad
            gain_sum[0:1, at] += jnp.sum(scaled * gated, axis=0, keepdims=True)
            d_gated = scaled * gain_ref[0:1, at] - pull * gated
            d_mixed = d_gated * silu
            d_gate = d_gated * mixed * (sig + silu * (1.0 - sig))
            message.put(gate_ref, i, j, d_gate.astype(bf16))
            skip_sum[0:1, at] += jnp.sum(values * d_mixed, axis=0, keepdims=True)
            rounded = d_mixed.astype(bf16)
            mixed_ref[rows, at] = rounded
            high_s[:, at], low_s[:, at] = two_terms(rounded.astype(f32) * y)
            high, low = two_terms(d_mixed * spread_pair(sm, ECUM, j))
            scaled_s[:, at] = high
            back = mm_two(readers_t, high, low)
            back_ref[i, :, at] = back
            back_sum[:, at] += pre[0:1, at] * back
            pre[:, at] = pre[:, at] * dec_ref[i, :, at]
        e_ref[:, lanes(i)] = (mm_nt(ones, high_s[...]) + mm_nt(ones, low_s[...]))[:HEADS]
        readers_ref[rows, :] = mm_nt(scaled_s[...], start_ref[i].astype(bf16))
    slab_ref[...] = back_sum[...].astype(bf16)

    @pl.when(c == pl.num_programs(0) - 1)
    def _():
        for j in range(PAIRS):
            param_ref[j : j + 1, :] = gain_sum[0:1, lanes(j)]
        high, low = two_terms(jnp.broadcast_to(skip_sum[0:1, :], (LANES, WIDTH)))
        skips = (mm_nt(high, ones) + mm_nt(low, ones))[0:1]
        param_ref[PAIRS : PAIRS + 1, :] = jnp.concatenate(
            [skips, jnp.zeros((1, LANES - 16), f32)], axis=1
        )
        param_ref[PAIRS + 1 :, :] = jnp.zeros((8 - PAIRS - 1, LANES), f32)


def local_kernel(
    message, per_step,
    first_ref, grad_ref, sm_ref, smt_ref, readers_ref, gate_ref,
    values_out, sources_out, gates_out,
):
    s = lax.broadcasted_iota(jnp.int32, (CHUNK, CHUNK), 0)
    t = lax.broadcasted_iota(jnp.int32, (CHUNK, CHUNK), 1)
    causal = t >= s
    for i in range(per_step):
        rows = slice(i * CHUNK, (i + 1) * CHUNK)
        sources = message.get(first_ref, i, B)
        readers = message.get(first_ref, i, C)
        scores = jnp.where(causal, mm_nt(sources, readers), 0.0)
        total = jnp.zeros((CHUNK, CHUNK), f32)
        for j in range(PAIRS):
            grads = split_pair(grad_ref[rows, lanes(j)])
            weight_grads = mm_nt(message.get(first_ref, i, X + j), grads)
            weights = []
            for k, h in enumerate((2 * j, 2 * j + 1)):
                there = sm_ref[rows, SHIFTED * HEADS + h : SHIFTED * HEADS + h + 1]
                here = smt_ref[CUM * HEADS + h : CUM * HEADS + h + 1, lanes(i)]
                decay = jnp.exp(jnp.minimum(here - there, CLAMP))
                weights.append((scores * decay).astype(bf16))
                total = total + weight_grads[:, lanes(k)] * decay
            values_out[rows, lanes(j)] = mm(jnp.concatenate(weights, axis=1), grads)
        total = jnp.where(causal, total, 0.0).astype(bf16)
        sources_out[rows, :] = mm(total, readers)
        d_readers = mm_tn(total, sources) + readers_ref[rows, :]
        message.put(gates_out, i, GATE_C, d_readers.astype(bf16))
        for j in range(PAIRS):
            message.put(gates_out, i, GATE_Z + j, message.get(gate_ref, i, j))


def last_kernel(
    message, per_step,
    first_ref, within_ref, sources_ref, grad_ref, e_ref, sm_ref, smt_ref, outer_ref,
    back_ref, start_ref, dec_ref, skip_ref, heads_ref, early_ref,
    out_ref,
    carry, sums, high_s, low_s, scaled_s, state_s, flux_s,
):
    c = pl.program_id(0)

    @pl.when(c == 0)
    def _():
        carry[...] = outer_ref[...].astype(f32)
        sums[...] = jnp.zeros_like(sums)

    r = message.rows
    ones = head_rows()
    before = lax.broadcasted_iota(jnp.int32, (CHUNK, CHUNK), 0)
    after = lax.broadcasted_iota(jnp.int32, (CHUNK, CHUNK), 1)
    earlier = jnp.where(before < after, 1.0, 0.0)
    decay_rate = jnp.exp(heads_ref[:HEADS, :])
    first_peer = (pl.num_programs(0) - 1 - c) * per_step * message.per_chunk
    mine = out_ref.at[pl.ds(first_peer, per_step * message.per_chunk)]
    for i in reversed(range(per_step)):
        rows = slice(i * CHUNK, (i + 1) * CHUNK)
        sm = sm_ref[rows, :]
        sources = message.get(first_ref, i, B)
        for j in range(PAIRS):
            at = lanes(j)
            state = carry[:, at]
            high, low = two_terms(state)
            state_s[:, at] = high
            values = message.get(first_ref, i, X + j).astype(f32)
            weight = spread_pair(sm, WEIGHT, j)
            grad = within_ref[rows, at] + weight * mm_two(sources, high, low)
            skipped = skip_ref[0:1, at] * grad_ref[rows, at].astype(f32)
            message.put(mine, i, LAST_X + j, (grad + skipped).astype(bf16))
            high_s[:, at], low_s[:, at] = two_terms(values * grad)
            scaled_s[:, at] = (values * weight).astype(bf16)
            new = dec_ref[i, 0:1, at] * state + back_ref[i, :, at]
            carry[:, at] = new
            flux_s[:, at] = jnp.broadcast_to(
                jnp.sum(start_ref[i, :, at] * new, axis=0, keepdims=True), (16, LANES)
            )
        d_sources = sources_ref[rows, :] + mm_nt(scaled_s[...], state_s[...])
        message.put(mine, i, LAST_B, d_sources.astype(bf16))
        g = (mm_nt(ones, high_s[...]) + mm_nt(ones, low_s[...]))[:HEADS]
        high, low = two_terms(flux_s[...])
        constant = (mm_nt(ones, high) + mm_nt(ones, low))[:HEADS, 0:1]
        flux = constant + mm_exact(g - e_ref[:, lanes(i)], earlier)
        soft = smt_ref[DT * HEADS : (DT + 1) * HEADS, lanes(i)]
        rate = smt_ref[RATE * HEADS : (RATE + 1) * HEADS, lanes(i)]
        sig = smt_ref[SIG * HEADS : (SIG + 1) * HEADS, lanes(i)]
        steps = (g / soft - decay_rate * flux) * sig
        sums[:HEADS, :] += flux * rate
        sums[HEADS:, :] += steps
        steps = jnp.concatenate([steps, jnp.zeros_like(steps)], axis=0)
        for p in range(message.per_chunk):
            part = steps if p == 0 else pltpu.roll(steps, LANES - p * r, 1)
            mine[i * message.per_chunk + p, LAST * r : LAST * r + STEP_ROWS, :] = part.astype(bf16)

    @pl.when(c == pl.num_programs(0) - 1)
    def _():
        late = []
        for k in range(2):
            column = jnp.sum(sums[k * HEADS : (k + 1) * HEADS, :], axis=1, keepdims=True)
            block = jnp.broadcast_to(column, (HEADS, LANES))
            block = jnp.concatenate([block, jnp.zeros((LANES - HEADS, LANES), f32)], axis=0)
            late += three_terms(block.T[0:1, :])
        late += [jnp.zeros((HEADS - 2 * TERMS, LANES), f32)]
        late = jnp.concatenate([jnp.zeros((HEADS, LANES), f32)] + late, axis=0)
        late = late.astype(bf16)
        early = three_terms(early_ref[:PAIRS, :]) + three_terms(early_ref[PAIRS : PAIRS + 1, :])
        early += [jnp.zeros((STEP_ROWS - TERMS * (PAIRS + 1), LANES), f32)]
        early = jnp.concatenate(early, axis=0).astype(bf16)
        own_rows = lax.broadcasted_iota(jnp.int32, (STEP_ROWS, LANES), 0) < HEADS

        def fill(peer, unused):
            steps_at = slice(LAST * r, LAST * r + STEP_ROWS)
            out_ref[peer, steps_at, :] = jnp.where(own_rows, out_ref[peer, steps_at, :], late)
            out_ref[peer, LAST * r + STEP_ROWS :, :] = early
            return unused

        lax.fori_loop(0, out_ref.shape[0], fill, 0)


def call(kernel, out_shape, flops, moved, grid=None, in_specs=None, out_specs=None, scratch=()):
    extra = {}
    if grid is not None:
        extra = dict(grid=grid, in_specs=in_specs, out_specs=out_specs)
    return pl.pallas_call(
        kernel,
        out_shape=out_shape,
        scratch_shapes=list(scratch),
        compiler_params=pltpu.CompilerParams(vmem_limit_bytes=16 * 1024 * 1024),
        cost_estimate=pl.CostEstimate(flops=flops, bytes_accessed=moved, transcendentals=0),
        **extra,
    )


def shifted(array, count, by):
    pairs = [(i, i + by) for i in range(count) if 0 <= i + by < count]
    return lax.ppermute(array, "slab", pairs)


def carry_over(state, decay, first_decay, count, sign):
    window, window_decay, step = state, decay, 1
    result = result_decay = None
    while step < count:
        arrived = shifted(window, count, sign * step)
        more = 2 * step < count
        if result is None:
            result = arrived
            if more:
                result_decay = first_decay
                window = (state.astype(f32) + decay[0:1] * arrived.astype(f32)).astype(bf16)
                window_decay = decay * first_decay
        else:
            if more:
                arrived_decay = shifted(window_decay, count, sign * step)
                window = (window.astype(f32) + window_decay[0:1] * arrived.astype(f32)).astype(bf16)
                window_decay = window_decay * arrived_decay
            result = result.astype(f32) + result_decay[0:1] * arrived.astype(f32)
            if more:
                result_decay = result_decay * arrived_decay
        step *= 2
    return jnp.zeros_like(state) if result is None else result


def sum_over(array, axis, count):
    step = 1
    while step < count:
        array = array + lax.ppermute(array, axis, [(i, i ^ step) for i in range(count)])
        step *= 2
    return array


def on_device(
    slab_count, sub_count, tensor_count,
    mixer_x, gate_z, b_matrix, c_matrix, raw_steps, decay_log, skip_gain, step_bias, norm_gain, out_grad,
):
    rows = mixer_x.shape[0]
    peers = sub_count * tensor_count
    tokens = rows * peers
    chunks = tokens // CHUNK
    per_step = min(2, chunks)
    grid = (chunks // per_step,)
    message = Message(rows)
    owners = [t * sub_count + s for s in range(sub_count) for t in range(tensor_count)]
    sub = lax.axis_index("sub")

    def struct(shape, kind=f32):
        return jax.ShapeDtypeStruct(shape, kind)

    def hbm(shape, kind=f32):
        return pltpu.HBM(shape, kind)

    def in_hbm(array):
        return pltpu.with_memory_space_constraint(array, pltpu.HBM)

    def exchange(array):
        return lax.all_to_all(array, ("sub", "tensor"), split_axis=0, concat_axis=0, tiled=True)

    own_logs = lax.dynamic_slice(decay_log, (sub * HEADS,), (HEADS,))
    own_bias = lax.dynamic_slice(step_bias, (sub * HEADS,), (HEADS,))
    own_skip = lax.dynamic_slice(skip_gain, (sub * HEADS,), (HEADS,))
    own_gain = lax.dynamic_slice(norm_gain, (sub * WIDTH,), (WIDTH,)).reshape(1, WIDTH)
    heads = jnp.broadcast_to(jnp.concatenate([own_logs, own_bias])[:, None], (2 * HEADS, LANES))
    skip_row = jnp.repeat(own_skip, HEAD_DIM).reshape(1, WIDTH)

    first_rows = FIRST * rows + STEP_ROWS
    second_rows = SECOND * rows
    gate_rows = GATES * rows
    last_rows = LAST * rows + 2 * STEP_ROWS

    def packed(kernel, height, arrays, whole_arrays=(), scratch=()):
        out = hbm((sub_count, tensor_count, height, LANES), bf16)
        moved = 4 * peers * height * LANES
        specs = [
            pl.BlockSpec((rows, a.shape[1] // tensor_count), lambda t: (0, t)) for a in arrays
        ] + [pl.BlockSpec(a.shape, lambda t: (0, 0)) for a in whole_arrays]
        out_spec = pl.BlockSpec((sub_count, 1, height, LANES), lambda t: (0, t, 0, 0))
        made = call(kernel, out, 0, moved, (tensor_count,), specs, out_spec, scratch)(
            *(in_hbm(a) for a in (*arrays, *whole_arrays))
        )
        return made.reshape(peers, height, LANES)

    first = exchange(
        packed(
            pack_first, first_rows, (mixer_x, b_matrix, c_matrix), (raw_steps,),
            [pltpu.VMEM((LANES, LANES), f32)],
        )
    )
    gate_z, heads, skip_row, own_gain = lax.optimization_barrier(
        (gate_z, heads, skip_row, own_gain)
    )
    second = exchange(packed(pack_second, second_rows, (gate_z, out_grad)))

    def flow(kernel, shape_specs, flops, moved, in_specs, scratch=()):
        def body(*refs):
            return kernel(message, per_step, *refs)

        shapes = tuple(shape for shape, _ in shape_specs)
        specs = tuple(spec for _, spec in shape_specs)
        return call(body, shapes, flops, moved, grid, in_specs, specs, scratch)

    def spec(block, axis, down=False):
        def index(c):
            at = grid[0] - 1 - c if down else c
            return tuple(at if k == axis else 0 for k in range(len(block)))

        return pl.BlockSpec(block, index)

    span = per_step * CHUNK

    def specs_of(down):
        return dict(
            message=lambda height: spec((per_step * message.per_chunk, height, LANES), 0, down),
            token=lambda width: spec((span, width), 0, down),
            lane=lambda height: spec((height, span), 1, down),
            chunk=lambda *shape: spec((per_step,) + shape, 0, down),
        )

    up, dn = specs_of(False), specs_of(True)

    def whole(*shape):
        return pl.BlockSpec(shape, lambda c: (0,) * len(shape))

    unit = 2 * tokens * CHUNK * WIDTH
    size = tokens * WIDTH

    sm, smt, own, dec, state, decay = flow(
        state_kernel,
        [
            (hbm((tokens, LANES)), up["token"](LANES)),
            (hbm((KINDS * HEADS, tokens)), up["lane"](KINDS * HEADS)),
            (hbm((chunks, STATE, WIDTH)), up["chunk"](STATE, WIDTH)),
            (hbm((chunks, 8, WIDTH)), up["chunk"](8, WIDTH)),
            (struct((STATE, WIDTH), bf16), whole(STATE, WIDTH)),
            (struct((8, WIDTH)), whole(8, WIDTH)),
        ],
        2 * unit, size * 8,
        [up["message"](first_rows), whole(2 * HEADS, LANES)],
        [pltpu.VMEM((STATE, WIDTH), f32)],
    )(first, heads)

    before = after = None
    if slab_count > 2:
        before, after = shifted(decay, slab_count, 1), shifted(decay, slab_count, -1)
    inbound = carry_over(state, decay, before, slab_count, 1)

    y, starts = flow(
        forward_kernel,
        [
            (hbm((tokens, WIDTH)), up["token"](WIDTH)),
            (hbm((chunks, STATE, WIDTH)), up["chunk"](STATE, WIDTH)),
        ],
        6 * unit, size * 16,
        [
            up["message"](first_rows), up["token"](LANES), up["lane"](KINDS * HEADS),
            whole(STATE, WIDTH), up["chunk"](STATE, WIDTH), up["chunk"](8, WIDTH),
        ],
        [pltpu.VMEM((STATE, WIDTH), f32)],
    )(first, in_hbm(sm), in_hbm(smt), inbound, in_hbm(own), in_hbm(dec))

    (sums,) = flow(
        mix_kernel,
        [(struct((chunks, 8, LANES)), up["chunk"](8, LANES))],
        0, size * 12,
        [
            up["message"](first_rows), up["message"](second_rows), up["token"](WIDTH),
            whole(1, WIDTH), whole(1, WIDTH),
        ],
    )(first, in_hbm(second), in_hbm(y), own_gain, skip_row)

    partner = lax.ppermute(sums, "sub", [(i, i ^ 1) for i in range(sub_count)])

    d_gates, d_mixed, e, back, slab_back, readers_part, params = flow(
        norm_kernel,
        [
            (struct((peers, PAIRS * rows, LANES), bf16), up["message"](PAIRS * rows)),
            (hbm((tokens, WIDTH), bf16), up["token"](WIDTH)),
            (hbm((HEADS, tokens)), up["lane"](HEADS)),
            (hbm((chunks, STATE, WIDTH)), up["chunk"](STATE, WIDTH)),
            (struct((STATE, WIDTH), bf16), whole(STATE, WIDTH)),
            (struct((tokens, STATE)), up["token"](STATE)),
            (struct((8, LANES)), whole(8, LANES)),
        ],
        4 * unit, size * 20,
        [
            up["message"](first_rows), up["message"](second_rows), up["token"](WIDTH),
            up["token"](LANES), up["chunk"](STATE, WIDTH), up["chunk"](8, WIDTH),
            up["chunk"](8, LANES), up["chunk"](8, LANES), whole(1, WIDTH), whole(1, WIDTH),
        ],
        [
            pltpu.VMEM((8, WIDTH), f32), pltpu.VMEM((STATE, WIDTH), f32),
            pltpu.VMEM((8, WIDTH), f32), pltpu.VMEM((8, WIDTH), f32),
            pltpu.VMEM((CHUNK, WIDTH), bf16), pltpu.VMEM((CHUNK, WIDTH), bf16),
            pltpu.VMEM((CHUNK, WIDTH), bf16),
        ],
    )(
        first, in_hbm(second), in_hbm(y), in_hbm(sm), in_hbm(starts), in_hbm(dec), sums, partner,
        own_gain, skip_row,
    )

    outer = carry_over(slab_back, decay, after, slab_count, -1)
    d_values, d_sources, gates_message = flow(
        local_kernel,
        [
            (hbm((tokens, WIDTH)), up["token"](WIDTH)),
            (hbm((tokens, STATE)), up["token"](STATE)),
            (hbm((peers, gate_rows, LANES), bf16), up["message"](gate_rows)),
        ],
        8 * unit, size * 8,
        [
            up["message"](first_rows), up["token"](WIDTH), up["token"](LANES),
            up["lane"](KINDS * HEADS), up["token"](STATE), up["message"](PAIRS * rows),
        ],
    )(first, in_hbm(d_mixed), in_hbm(sm), in_hbm(smt), readers_part, d_gates)
    gates_message, outer = lax.optimization_barrier((gates_message, outer))
    gates_back = exchange(gates_message)

    (last,) = flow(
        last_kernel,
        [(hbm((peers, last_rows, LANES), bf16), whole(peers, last_rows, LANES))],
        4 * unit, size * 16,
        [
            dn["message"](first_rows), dn["token"](WIDTH), dn["token"](STATE),
            dn["token"](WIDTH), dn["lane"](HEADS), dn["token"](LANES), dn["lane"](KINDS * HEADS),
            whole(STATE, WIDTH), dn["chunk"](STATE, WIDTH), dn["chunk"](STATE, WIDTH),
            dn["chunk"](8, WIDTH), whole(1, WIDTH), whole(2 * HEADS, LANES), whole(8, LANES),
        ],
        [
            pltpu.VMEM((STATE, WIDTH), f32), pltpu.VMEM((2 * HEADS, LANES), f32),
            pltpu.VMEM((CHUNK, WIDTH), bf16), pltpu.VMEM((CHUNK, WIDTH), bf16),
            pltpu.VMEM((CHUNK, WIDTH), bf16), pltpu.VMEM((STATE, WIDTH), bf16),
            pltpu.VMEM((16, WIDTH), f32),
        ],
    )(
        first, in_hbm(d_values), in_hbm(d_sources), in_hbm(d_mixed), in_hbm(e), in_hbm(sm),
        in_hbm(smt), outer, in_hbm(back), in_hbm(starts), in_hbm(dec), skip_row, heads, params,
    )

    last_back = exchange(last)
    grad_gates, grad_c = call(
        lambda *refs: unpack_gates(owners, *refs),
        (struct((rows, CHANNELS), bf16), struct((rows, GROUPS * STATE), bf16)),
        0, 4 * rows * CHANNELS,
    )(gates_back)

    tile_at = LAST * rows // STEP_ROWS
    mine = lax.broadcasted_iota(jnp.int32, (tensor_count, LANES), 0) == lax.axis_index("tensor")

    def tile(at):
        return pl.BlockSpec((peers, STEP_ROWS, LANES), lambda c: (0, at, 0))

    params = call(
        lambda *refs: unpack_params(sub_count, tensor_count, *refs),
        struct((8 + sub_count * PAIRS, LANES)),
        0, 4 * peers * STEP_ROWS * LANES, (1,),
        [tile(tile_at), tile(tile_at + 1), whole(tensor_count, LANES)],
        whole(8 + sub_count * PAIRS, LANES),
    )(last_back, last_back, mine.astype(f32))
    params = sum_over(params, "slab", slab_count)
    grad_x, grad_b, grad_steps = call(
        lambda *refs: unpack_last(owners, *refs),
        (
            struct((rows, CHANNELS), bf16), struct((rows, GROUPS * STATE), bf16),
            struct((rows, MIXER_HEADS), bf16),
        ),
        0, 6 * rows * CHANNELS,
    )(last_back)
    count = sub_count * HEADS
    return (
        grad_x,
        grad_gates,
        grad_b,
        grad_c,
        grad_steps,
        params[0, :count],
        params[2, :count],
        params[1, :count],
        params[8:].reshape(-1),
    )


def solution(mesh):
    tensor_count = mesh.shape["tensor"]
    sub_count = OWNERS // tensor_count
    slab_count = mesh.shape["dp"] // sub_count
    devices = mesh.devices.reshape(slab_count, sub_count, tensor_count)
    split_mesh = Mesh(devices, ("slab", "sub", "tensor"))
    rows = P(("slab", "sub", "tensor"), None)
    param = P("tensor")

    def local(*arrays):
        return on_device(slab_count, sub_count, tensor_count, *arrays)

    return jax.shard_map(
        local,
        mesh=split_mesh,
        in_specs=(rows,) * 5 + (param,) * 4 + (rows,),
        out_specs=(rows,) * 5 + (param,) * 4,
        check_vma=False,
    )
```

```python
import jax
import jax.numpy as jnp
from jax import lax
from jax.experimental import pallas as pl
from jax.experimental.pallas import tpu as pltpu
from jax.sharding import Mesh
from jax.sharding import PartitionSpec as P

MIXER_HEADS = 128
HEAD_DIM = 64
STATE = 128
GROUPS = 8
CHANNELS = MIXER_HEADS * HEAD_DIM
HEADS = 8
WIDTH = HEADS * HEAD_DIM
GROUP_WIDTH = 2 * WIDTH
OWNERS = MIXER_HEADS // HEADS
LANES = 128
PAIRS = WIDTH // LANES
CHUNK = 128
STEP_ROWS = 16
epsilon = 1e-05
f32 = jnp.float32
bf16 = jnp.bfloat16

DT, CUM, WEIGHT, SHIFTED, ECUM, RATE, SIG = range(7)
KINDS = 8
CLAMP = 80.0


def mm(a, b):
    return jnp.dot(a, b, preferred_element_type=f32)


def mm_nt(a, b):
    return lax.dot_general(a, b, (((1,), (1,)), ((), ())), preferred_element_type=f32)


def mm_tn(a, b):
    return lax.dot_general(a, b, (((0,), (0,)), ((), ())), preferred_element_type=f32)


def mm_exact(a, b):
    return jnp.dot(a, b, precision=lax.Precision.HIGHEST, preferred_element_type=f32)


def two_terms(values):
    high = values.astype(bf16)
    return high, (values - high.astype(f32)).astype(bf16)


def mm_two(a, high, low):
    both = mm(a, jnp.concatenate([high, low], axis=1))
    width = high.shape[1]
    return both[:, :width] + both[:, width:]


def sigmoid(values):
    return 0.5 + 0.5 * jnp.tanh(0.5 * values)


def low_half(rows):
    return lax.broadcasted_iota(jnp.int32, (rows, LANES), 1) < HEAD_DIM


def spread_pair(values, kind, j):
    rows = values.shape[0]
    at = kind * HEADS + 2 * j
    return jnp.where(
        low_half(rows),
        jnp.broadcast_to(values[:, at : at + 1], (rows, LANES)),
        jnp.broadcast_to(values[:, at + 1 : at + 2], (rows, LANES)),
    )


def head_rows():
    row = lax.broadcasted_iota(jnp.int32, (16, WIDTH), 0)
    channel = lax.broadcasted_iota(jnp.int32, (16, WIDTH), 1) // HEAD_DIM
    return jnp.where(row == channel, 1.0, 0.0).astype(bf16)


def split_pair(block):
    low = low_half(block.shape[0])
    zero = jnp.zeros_like(block)
    return jnp.concatenate(
        [jnp.where(low, block, zero), jnp.where(low, zero, block)], axis=0
    )


def lanes(j):
    return slice(j * LANES, (j + 1) * LANES)


class Message:
    def __init__(self, rows):
        self.rows = rows
        self.per_chunk = CHUNK // rows

    def place(self, chunk, k):
        r = self.rows
        return (slice(chunk * self.per_chunk, (chunk + 1) * self.per_chunk), slice(k * r, (k + 1) * r))

    def get(self, ref, chunk, k):
        a, b = self.place(chunk, k)
        return ref[a, b, :].reshape(CHUNK, LANES)

    def put(self, ref, chunk, k, value):
        a, b = self.place(chunk, k)
        ref[a, b, :] = value.reshape(self.per_chunk, self.rows, LANES)


X, B, C, Z, GRAD = 0, PAIRS, PAIRS + 1, PAIRS + 2, 2 * PAIRS + 2
SOURCES = PAIRS + 1
MIXER = PAIRS + 2
FIRST = 3 * PAIRS + 2
GATE_Z, GATE_C = 0, PAIRS
GATES = PAIRS + 1
LAST_X, LAST_B = 0, PAIRS
LAST = PAIRS + 1
TERMS = 3


def pack(x_ref, b_ref, c_ref, z_ref, grad_ref, steps_ref, out_ref, by_head):
    r = x_ref.shape[0]
    step = pl.program_id(0)
    subs = out_ref.shape[0]

    @pl.when(step == 0)
    def _():
        steps = steps_ref[...].astype(f32)
        by_head[...] = jnp.concatenate([steps, jnp.zeros((LANES - r, LANES), f32)], axis=0).T

    zero = jnp.zeros((STEP_ROWS - HEADS, LANES), f32)
    for s in range(subs):
        for j in range(PAIRS):
            for block, ref in ((X, x_ref), (Z, z_ref), (GRAD, grad_ref)):
                at = slice((block + j) * r, (block + j + 1) * r)
                out_ref[s, 0, at, :] = ref[:, lanes(s * PAIRS + j)]
        out_ref[s, 0, B * r : (B + 1) * r, :] = b_ref[:, lanes(s // 2)]
        out_ref[s, 0, C * r : (C + 1) * r, :] = c_ref[:, lanes(s // 2)]
        at = pl.multiple_of((step * subs + s) * HEADS, HEADS)
        mine = jnp.concatenate([by_head[pl.ds(at, HEADS), :], zero], axis=0)
        out_ref[s, 0, FIRST * r :, :] = mine.astype(bf16)


def add_halves(owners, in_ref, block, out_ref):
    r = out_ref.shape[0]
    peer_of = {own: peer for peer, own in enumerate(owners)}
    for g in range(GROUPS):
        halves = [
            in_ref[peer_of[2 * g + k], block * r : (block + 1) * r, :].astype(f32) for k in range(2)
        ]
        out_ref[:, lanes(g)] = (halves[0] + halves[1]).astype(bf16)


def unpack_gates(owners, in_ref, out_ref, c_ref):
    r = out_ref.shape[0]
    for peer, own in enumerate(owners):
        for j in range(PAIRS):
            out_ref[:, lanes(own * PAIRS + j)] = in_ref[peer, j * r : (j + 1) * r, :]
    add_halves(owners, in_ref, GATE_C, c_ref)


def unpack_last(owners, in_ref, x_ref, b_ref, steps_ref):
    r = x_ref.shape[0]
    peer_of = {own: peer for peer, own in enumerate(owners)}
    for peer, own in enumerate(owners):
        for j in range(PAIRS):
            x_ref[:, lanes(own * PAIRS + j)] = in_ref[peer, j * r : (j + 1) * r, :]
    add_halves(owners, in_ref, LAST_B, b_ref)
    by_head = jnp.concatenate(
        [
            in_ref[peer_of[own], LAST * r : LAST * r + STEP_ROWS, :].astype(f32)[:HEADS]
            for own in range(OWNERS)
        ],
        axis=0,
    )
    steps_ref[...] = by_head.T[:r, :].astype(bf16)


def three_terms(values):
    high = values.astype(bf16).astype(f32)
    rest = values - high
    middle = rest.astype(bf16).astype(f32)
    return [high, middle, rest - middle]


def unpack_params(sub_count, tensor_count, late_ref, early_ref, mine_ref, out_ref):
    lane = lax.broadcasted_iota(jnp.int32, (1, LANES), 1)
    late = [jnp.zeros((1, LANES), f32) for _ in range(2)]
    skip = jnp.zeros((1, LANES), f32)

    def placed(rows, at):
        total = rows[at : at + 1] + rows[at + 1 : at + 2] + rows[at + 2 : at + 3]
        return jnp.where(lane < HEADS, total, 0.0)

    for s in range(sub_count):
        late_rows = jnp.zeros((STEP_ROWS, LANES), f32)
        early_rows = jnp.zeros((STEP_ROWS, LANES), f32)
        for t in range(tensor_count):
            mine = mine_ref[t : t + 1, :] > 0.0
            peer = s * tensor_count + t
            late_rows = jnp.where(mine, late_ref[peer].astype(f32), late_rows)
            early_rows = jnp.where(mine, early_ref[peer].astype(f32), early_rows)
        for k in range(2):
            part = placed(late_rows, HEADS + k * TERMS)
            late[k] = late[k] + (part if s == 0 else pltpu.roll(part, s * HEADS, 1))
        part = placed(early_rows, TERMS * PAIRS)
        skip = skip + (part if s == 0 else pltpu.roll(part, s * HEADS, 1))
        gain = early_rows[:PAIRS] + early_rows[PAIRS : 2 * PAIRS] + early_rows[2 * PAIRS : 3 * PAIRS]
        out_ref[8 + s * PAIRS : 8 + (s + 1) * PAIRS, :] = gain
    out_ref[:8, :] = jnp.concatenate(late + [skip, jnp.zeros((5, LANES), f32)], axis=0)


def state_kernel(
    message, per_step,
    first_ref, steps_ref, heads_ref, sm_ref, smt_ref, own_ref, dec_ref, state_ref, whole_ref,
    carry, rows_s,
):
    c = pl.program_id(0)

    @pl.when(c == 0)
    def _():
        carry[...] = jnp.zeros_like(carry)
        whole_ref[...] = jnp.ones_like(whole_ref)
        chunks = rows_s.shape[0]
        before = lax.broadcasted_iota(jnp.int32, (CHUNK, CHUNK), 0)
        after = lax.broadcasted_iota(jnp.int32, (CHUNK, CHUNK), 1)
        raws = []
        for k in range(chunks):
            raw = heads_ref[HEADS:, :]
            for p in range(message.per_chunk):
                part = steps_ref[k * message.per_chunk + p].astype(f32)[:HEADS]
                raw = raw + (part if p == 0 else pltpu.roll(part, p * message.rows, 1))
            raws.append(raw)
        raw = jnp.concatenate(raws, axis=0)
        small = jnp.exp(-jnp.abs(raw))
        series = small * (
            1.0 - small * (0.5 - small * (1.0 / 3 - small * (0.25 - small * 0.2)))
        )
        soft = jnp.maximum(raw, 0.0) + jnp.where(small < 0.015625, series, jnp.log(1.0 + small))
        sig = jnp.where(raw >= 0.0, 1.0, small) / (1.0 + small)
        decay_rate = jnp.concatenate([jnp.exp(heads_ref[:HEADS, :])] * chunks, axis=0)
        rate = -decay_rate * soft
        cum = mm_exact(rate, jnp.where(before <= after, 1.0, 0.0))
        rest = mm_exact(rate, jnp.where(before > after, 1.0, 0.0))
        kinds = [
            soft, cum, soft * jnp.exp(rest), cum - jnp.log(soft), jnp.exp(cum), rate, sig,
            jnp.zeros_like(soft),
        ]
        for k in range(chunks):
            at = slice(k * HEADS, (k + 1) * HEADS)
            rows_s[k] = jnp.concatenate([kind[at] for kind in kinds], axis=0)

    for i in range(per_step):
        rows = rows_s[c * per_step + i]
        smt_ref[:, lanes(i)] = rows
        sm = jnp.concatenate([rows, jnp.zeros_like(rows)], axis=0).T
        sm_ref[i * CHUNK : (i + 1) * CHUNK, :] = sm
        last = jnp.broadcast_to(sm[CHUNK - 1 : CHUNK, :], (8, LANES))
        sources_t = message.get(first_ref, i, B).T
        for j in range(PAIRS):
            dec = spread_pair(last, ECUM, j)
            dec_ref[i, :, lanes(j)] = dec
            whole_ref[:, lanes(j)] = whole_ref[:, lanes(j)] * dec
            scaled = message.get(first_ref, i, X + j).astype(f32) * spread_pair(sm, WEIGHT, j)
            own = mm_two(sources_t, *two_terms(scaled))
            own_ref[i, :, lanes(j)] = own
            carry[:, lanes(j)] = dec[0:1] * carry[:, lanes(j)] + own
    state_ref[...] = carry[...].astype(bf16)


def within_kernel(message, per_step, first_ref, sm_ref, smt_ref, out_ref):
    t = lax.broadcasted_iota(jnp.int32, (CHUNK, CHUNK), 0)
    s = lax.broadcasted_iota(jnp.int32, (CHUNK, CHUNK), 1)
    for i in range(per_step):
        rows = slice(i * CHUNK, (i + 1) * CHUNK)
        scores = mm_nt(message.get(first_ref, i, C), message.get(first_ref, i, B))
        scores = jnp.where(t >= s, scores, 0.0)
        for j in range(PAIRS):
            weights = []
            for h in (2 * j, 2 * j + 1):
                here = sm_ref[rows, CUM * HEADS + h : CUM * HEADS + h + 1]
                there = smt_ref[SHIFTED * HEADS + h : SHIFTED * HEADS + h + 1, lanes(i)]
                weights.append(
                    (scores * jnp.exp(jnp.minimum(here - there, CLAMP))).astype(bf16)
                )
            values = split_pair(message.get(first_ref, i, X + j))
            out_ref[rows, lanes(j)] = mm(jnp.concatenate(weights, axis=1), values)


def mix_kernel(
    message, per_step,
    first_ref, within_ref, sm_ref, inbound_ref, own_ref, dec_ref, gain_ref, skip_ref,
    y_ref, start_ref, sums_ref,
    carry,
):
    @pl.when(pl.program_id(0) == 0)
    def _():
        carry[...] = inbound_ref[...].astype(f32)

    for i in range(per_step):
        rows = slice(i * CHUNK, (i + 1) * CHUNK)
        sm = sm_ref[rows, :]
        readers = message.get(first_ref, i, C)
        power = jnp.zeros((CHUNK, LANES), f32)
        cross = jnp.zeros((CHUNK, LANES), f32)
        for j in range(PAIRS):
            state = carry[:, lanes(j)]
            start_ref[i, :, lanes(j)] = state
            carried = mm_two(readers, *two_terms(state))
            carry[:, lanes(j)] = dec_ref[i, 0:1, lanes(j)] * state + own_ref[i, :, lanes(j)]
            y = within_ref[rows, lanes(j)] + spread_pair(sm, ECUM, j) * carried
            y_ref[rows, lanes(j)] = y
            values = message.get(first_ref, i, X + j).astype(f32)
            gates = message.get(first_ref, i, Z + j).astype(f32)
            grad = message.get(first_ref, i, GRAD + j).astype(f32)
            gated = (y + skip_ref[0:1, lanes(j)] * values) * (gates * sigmoid(gates))
            power = power + gated * gated
            cross = cross + grad * gain_ref[0:1, lanes(j)] * gated
        sums_ref[i, 0:1, :] = jnp.sum(power.T, axis=0, keepdims=True)
        sums_ref[i, 1:2, :] = jnp.sum(cross.T, axis=0, keepdims=True)
        sums_ref[i, 2:, :] = jnp.zeros((6, LANES), f32)


def norm_kernel(
    message, per_step,
    first_ref, y_ref, sm_ref, start_ref, dec_ref, sums_ref, other_ref, gain_ref, skip_ref,
    gate_ref, mixed_ref, e_ref, back_ref, slab_ref, readers_ref, param_ref,
    pre, back_sum, gain_sum, skip_sum, high_s, low_s, scaled_s,
):
    c = pl.program_id(0)

    @pl.when(c == 0)
    def _():
        pre[...] = jnp.ones_like(pre)
        back_sum[...] = jnp.zeros_like(back_sum)
        gain_sum[...] = jnp.zeros_like(gain_sum)
        skip_sum[...] = jnp.zeros_like(skip_sum)

    ones = head_rows()
    for i in range(per_step):
        rows = slice(i * CHUNK, (i + 1) * CHUNK)
        sm = sm_ref[rows, :]
        readers = message.get(first_ref, i, C)
        readers_t = readers.T
        sums = (sums_ref[i] + other_ref[i]) * (1.0 / GROUP_WIDTH)
        inverse_row = lax.rsqrt(sums[0:1] + epsilon)
        pull_row = inverse_row * inverse_row * inverse_row * sums[1:2]
        inverse = jnp.broadcast_to(inverse_row, (CHUNK, LANES)).T
        pull = jnp.broadcast_to(pull_row, (CHUNK, LANES)).T
        for j in range(PAIRS):
            at = lanes(j)
            values = message.get(first_ref, i, X + j).astype(f32)
            gates = message.get(first_ref, i, Z + j).astype(f32)
            grad = message.get(first_ref, i, GRAD + j).astype(f32)
            y = y_ref[rows, at]
            mixed = y + skip_ref[0:1, at] * values
            sig = sigmoid(gates)
            silu = gates * sig
            gated = mixed * silu
            scaled = inverse * grad
            gain_sum[0:1, at] += jnp.sum(scaled * gated, axis=0, keepdims=True)
            d_gated = scaled * gain_ref[0:1, at] - pull * gated
            d_mixed = d_gated * silu
            d_gate = d_gated * mixed * (sig + silu * (1.0 - sig))
            message.put(gate_ref, i, j, d_gate.astype(bf16))
            skip_sum[0:1, at] += jnp.sum(values * d_mixed, axis=0, keepdims=True)
            rounded = d_mixed.astype(bf16)
            mixed_ref[rows, at] = rounded
            high_s[:, at], low_s[:, at] = two_terms(rounded.astype(f32) * y)
            high, low = two_terms(d_mixed * spread_pair(sm, ECUM, j))
            scaled_s[:, at] = high
            back = mm_two(readers_t, high, low)
            back_ref[i, :, at] = back
            back_sum[:, at] += pre[0:1, at] * back
            pre[:, at] = pre[:, at] * dec_ref[i, :, at]
        e_ref[:, lanes(i)] = (mm_nt(ones, high_s[...]) + mm_nt(ones, low_s[...]))[:HEADS]
        readers_ref[rows, :] = mm_nt(scaled_s[...], start_ref[i].astype(bf16))
    slab_ref[...] = back_sum[...].astype(bf16)

    @pl.when(c == pl.num_programs(0) - 1)
    def _():
        for j in range(PAIRS):
            param_ref[j : j + 1, :] = gain_sum[0:1, lanes(j)]
        high, low = two_terms(jnp.broadcast_to(skip_sum[0:1, :], (LANES, WIDTH)))
        skips = (mm_nt(high, ones) + mm_nt(low, ones))[0:1]
        param_ref[PAIRS : PAIRS + 1, :] = jnp.concatenate(
            [skips, jnp.zeros((1, LANES - 16), f32)], axis=1
        )
        param_ref[PAIRS + 1 :, :] = jnp.zeros((8 - PAIRS - 1, LANES), f32)


def local_kernel(
    message, per_step,
    first_ref, grad_ref, sm_ref, smt_ref, readers_ref, gate_ref,
    values_out, sources_out, gates_out,
):
    s = lax.broadcasted_iota(jnp.int32, (CHUNK, CHUNK), 0)
    t = lax.broadcasted_iota(jnp.int32, (CHUNK, CHUNK), 1)
    causal = t >= s
    for i in range(per_step):
        rows = slice(i * CHUNK, (i + 1) * CHUNK)
        sources = message.get(first_ref, i, B)
        readers = message.get(first_ref, i, C)
        scores = jnp.where(causal, mm_nt(sources, readers), 0.0)
        total = jnp.zeros((CHUNK, CHUNK), f32)
        for j in range(PAIRS):
            grads = split_pair(grad_ref[rows, lanes(j)])
            weight_grads = mm_nt(message.get(first_ref, i, X + j), grads)
            weights = []
            for k, h in enumerate((2 * j, 2 * j + 1)):
                there = sm_ref[rows, SHIFTED * HEADS + h : SHIFTED * HEADS + h + 1]
                here = smt_ref[CUM * HEADS + h : CUM * HEADS + h + 1, lanes(i)]
                decay = jnp.exp(jnp.minimum(here - there, CLAMP))
                weights.append((scores * decay).astype(bf16))
                total = total + weight_grads[:, lanes(k)] * decay
            values_out[rows, lanes(j)] = mm(jnp.concatenate(weights, axis=1), grads)
        total = jnp.where(causal, total, 0.0).astype(bf16)
        sources_out[rows, :] = mm(total, readers)
        d_readers = mm_tn(total, sources) + readers_ref[rows, :]
        message.put(gates_out, i, GATE_C, d_readers.astype(bf16))
        for j in range(PAIRS):
            message.put(gates_out, i, GATE_Z + j, message.get(gate_ref, i, j))


def last_kernel(
    message, per_step,
    first_ref, within_ref, sources_ref, grad_ref, e_ref, sm_ref, smt_ref, outer_ref,
    back_ref, start_ref, dec_ref, skip_ref, heads_ref, early_ref,
    out_ref,
    carry, sums, high_s, low_s, scaled_s, state_s, flux_s,
):
    c = pl.program_id(0)

    @pl.when(c == 0)
    def _():
        carry[...] = outer_ref[...].astype(f32)
        sums[...] = jnp.zeros_like(sums)

    r = message.rows
    ones = head_rows()
    before = lax.broadcasted_iota(jnp.int32, (CHUNK, CHUNK), 0)
    after = lax.broadcasted_iota(jnp.int32, (CHUNK, CHUNK), 1)
    earlier = jnp.where(before < after, 1.0, 0.0)
    decay_rate = jnp.exp(heads_ref[:HEADS, :])
    first_peer = (pl.num_programs(0) - 1 - c) * per_step * message.per_chunk
    mine = out_ref.at[pl.ds(first_peer, per_step * message.per_chunk)]
    for i in reversed(range(per_step)):
        rows = slice(i * CHUNK, (i + 1) * CHUNK)
        sm = sm_ref[rows, :]
        sources = message.get(first_ref, i, B)
        for j in range(PAIRS):
            at = lanes(j)
            state = carry[:, at]
            high, low = two_terms(state)
            state_s[:, at] = high
            values = message.get(first_ref, i, X + j).astype(f32)
            weight = spread_pair(sm, WEIGHT, j)
            grad = within_ref[rows, at] + weight * mm_two(sources, high, low)
            skipped = skip_ref[0:1, at] * grad_ref[rows, at].astype(f32)
            message.put(mine, i, LAST_X + j, (grad + skipped).astype(bf16))
            high_s[:, at], low_s[:, at] = two_terms(values * grad)
            scaled_s[:, at] = (values * weight).astype(bf16)
            new = dec_ref[i, 0:1, at] * state + back_ref[i, :, at]
            carry[:, at] = new
            flux_s[:, at] = jnp.broadcast_to(
                jnp.sum(start_ref[i, :, at] * new, axis=0, keepdims=True), (16, LANES)
            )
        d_sources = sources_ref[rows, :] + mm_nt(scaled_s[...], state_s[...])
        message.put(mine, i, LAST_B, d_sources.astype(bf16))
        g = (mm_nt(ones, high_s[...]) + mm_nt(ones, low_s[...]))[:HEADS]
        high, low = two_terms(flux_s[...])
        constant = (mm_nt(ones, high) + mm_nt(ones, low))[:HEADS, 0:1]
        flux = constant + mm_exact(g - e_ref[:, lanes(i)], earlier)
        soft = smt_ref[DT * HEADS : (DT + 1) * HEADS, lanes(i)]
        rate = smt_ref[RATE * HEADS : (RATE + 1) * HEADS, lanes(i)]
        sig = smt_ref[SIG * HEADS : (SIG + 1) * HEADS, lanes(i)]
        steps = (g / soft - decay_rate * flux) * sig
        sums[:HEADS, :] += flux * rate
        sums[HEADS:, :] += steps
        steps = jnp.concatenate([steps, jnp.zeros_like(steps)], axis=0)
        for p in range(message.per_chunk):
            part = steps if p == 0 else pltpu.roll(steps, LANES - p * r, 1)
            mine[i * message.per_chunk + p, LAST * r : LAST * r + STEP_ROWS, :] = part.astype(bf16)

    @pl.when(c == pl.num_programs(0) - 1)
    def _():
        late = []
        for k in range(2):
            column = jnp.sum(sums[k * HEADS : (k + 1) * HEADS, :], axis=1, keepdims=True)
            block = jnp.broadcast_to(column, (HEADS, LANES))
            block = jnp.concatenate([block, jnp.zeros((LANES - HEADS, LANES), f32)], axis=0)
            late += three_terms(block.T[0:1, :])
        late += [jnp.zeros((HEADS - 2 * TERMS, LANES), f32)]
        late = jnp.concatenate([jnp.zeros((HEADS, LANES), f32)] + late, axis=0)
        late = late.astype(bf16)
        early = three_terms(early_ref[:PAIRS, :]) + three_terms(early_ref[PAIRS : PAIRS + 1, :])
        early += [jnp.zeros((STEP_ROWS - TERMS * (PAIRS + 1), LANES), f32)]
        early = jnp.concatenate(early, axis=0).astype(bf16)
        own_rows = lax.broadcasted_iota(jnp.int32, (STEP_ROWS, LANES), 0) < HEADS

        def fill(peer, unused):
            steps_at = slice(LAST * r, LAST * r + STEP_ROWS)
            out_ref[peer, steps_at, :] = jnp.where(own_rows, out_ref[peer, steps_at, :], late)
            out_ref[peer, LAST * r + STEP_ROWS :, :] = early
            return unused

        lax.fori_loop(0, out_ref.shape[0], fill, 0)


def call(kernel, out_shape, flops, moved, grid=None, in_specs=None, out_specs=None, scratch=()):
    extra = {}
    if grid is not None:
        extra = dict(grid=grid, in_specs=in_specs, out_specs=out_specs)
    return pl.pallas_call(
        kernel,
        out_shape=out_shape,
        scratch_shapes=list(scratch),
        compiler_params=pltpu.CompilerParams(vmem_limit_bytes=16 * 1024 * 1024),
        cost_estimate=pl.CostEstimate(flops=flops, bytes_accessed=moved, transcendentals=0),
        **extra,
    )


def shifted(array, count, by):
    pairs = [(i, i + by) for i in range(count) if 0 <= i + by < count]
    return lax.ppermute(array, "slab", pairs)


def carry_over(state, decay, first_decay, count, sign):
    window, window_decay, step = state, decay, 1
    result = result_decay = None
    while step < count:
        arrived = shifted(window, count, sign * step)
        more = 2 * step < count
        if result is None:
            result = arrived
            if more:
                result_decay = first_decay
                window = (state.astype(f32) + decay[0:1] * arrived.astype(f32)).astype(bf16)
                window_decay = decay * first_decay
        else:
            if more:
                arrived_decay = shifted(window_decay, count, sign * step)
                window = (window.astype(f32) + window_decay[0:1] * arrived.astype(f32)).astype(bf16)
                window_decay = window_decay * arrived_decay
            result = result.astype(f32) + result_decay[0:1] * arrived.astype(f32)
            if more:
                result_decay = result_decay * arrived_decay
        step *= 2
    return jnp.zeros_like(state) if result is None else result


def sum_over(array, axis, count):
    step = 1
    while step < count:
        array = array + lax.ppermute(array, axis, [(i, i ^ step) for i in range(count)])
        step *= 2
    return array


def on_device(
    slab_count, sub_count, tensor_count,
    mixer_x, gate_z, b_matrix, c_matrix, raw_steps, decay_log, skip_gain, step_bias, norm_gain, out_grad,
):
    rows = mixer_x.shape[0]
    peers = sub_count * tensor_count
    tokens = rows * peers
    chunks = tokens // CHUNK
    per_step = min(2, chunks)
    grid = (chunks // per_step,)
    message = Message(rows)
    owners = [t * sub_count + s for s in range(sub_count) for t in range(tensor_count)]
    sub = lax.axis_index("sub")

    def struct(shape, kind=f32):
        return jax.ShapeDtypeStruct(shape, kind)

    def hbm(shape, kind=f32):
        return pltpu.HBM(shape, kind)

    def in_hbm(array):
        return pltpu.with_memory_space_constraint(array, pltpu.HBM)

    def exchange(array):
        return lax.all_to_all(array, ("sub", "tensor"), split_axis=0, concat_axis=0, tiled=True)

    own_logs = lax.dynamic_slice(decay_log, (sub * HEADS,), (HEADS,))
    own_bias = lax.dynamic_slice(step_bias, (sub * HEADS,), (HEADS,))
    own_skip = lax.dynamic_slice(skip_gain, (sub * HEADS,), (HEADS,))
    own_gain = lax.dynamic_slice(norm_gain, (sub * WIDTH,), (WIDTH,)).reshape(1, WIDTH)
    heads = jnp.broadcast_to(jnp.concatenate([own_logs, own_bias])[:, None], (2 * HEADS, LANES))
    skip_row = jnp.repeat(own_skip, HEAD_DIM).reshape(1, WIDTH)

    first_rows = FIRST * rows + STEP_ROWS
    gate_rows = GATES * rows
    last_rows = LAST * rows + 2 * STEP_ROWS

    def packed(arrays, steps):
        specs = [
            pl.BlockSpec((rows, a.shape[1] // tensor_count), lambda t: (0, t)) for a in arrays
        ] + [pl.BlockSpec(steps.shape, lambda t: (0, 0))]
        made = call(
            pack, hbm((sub_count, tensor_count, first_rows, LANES), bf16),
            0, 4 * peers * first_rows * LANES, (tensor_count,), specs,
            pl.BlockSpec((sub_count, 1, first_rows, LANES), lambda t: (0, t, 0, 0)),
            [pltpu.VMEM((LANES, LANES), f32)],
        )(*(in_hbm(a) for a in (*arrays, steps)))
        return made.reshape(peers, first_rows, LANES)

    first = exchange(packed((mixer_x, b_matrix, c_matrix, gate_z, out_grad), raw_steps))

    def flow(kernel, shape_specs, flops, moved, in_specs, scratch=()):
        def body(*refs):
            return kernel(message, per_step, *refs)

        shapes = tuple(shape for shape, _ in shape_specs)
        specs = tuple(spec for _, spec in shape_specs)
        return call(body, shapes, flops, moved, grid, in_specs, specs, scratch)

    def spec(block, axis, down=False):
        def index(c):
            at = grid[0] - 1 - c if down else c
            return tuple(at if k == axis else 0 for k in range(len(block)))

        return pl.BlockSpec(block, index)

    span = per_step * CHUNK

    def specs_of(down):
        return dict(
            message=lambda height: spec((per_step * message.per_chunk, height, LANES), 0, down),
            token=lambda width: spec((span, width), 0, down),
            lane=lambda height: spec((height, span), 1, down),
            chunk=lambda *shape: spec((per_step,) + shape, 0, down),
        )

    up, dn = specs_of(False), specs_of(True)

    def whole(*shape):
        return pl.BlockSpec(shape, lambda c: (0,) * len(shape))

    unit = 2 * tokens * CHUNK * WIDTH
    size = tokens * WIDTH

    first, heads, skip_row, own_gain = lax.optimization_barrier((first, heads, skip_row, own_gain))
    first = in_hbm(first)
    sm, smt, own, dec, state, decay = flow(
        state_kernel,
        [
            (struct((tokens, LANES)), up["token"](LANES)),
            (struct((KINDS * HEADS, tokens)), up["lane"](KINDS * HEADS)),
            (struct((chunks, STATE, WIDTH)), up["chunk"](STATE, WIDTH)),
            (struct((chunks, 8, WIDTH)), up["chunk"](8, WIDTH)),
            (struct((STATE, WIDTH), bf16), whole(STATE, WIDTH)),
            (struct((8, WIDTH)), whole(8, WIDTH)),
        ],
        2 * unit, size * 8,
        [
            up["message"](SOURCES * rows),
            pl.BlockSpec((peers, STEP_ROWS, LANES), lambda c: (0, FIRST * rows // STEP_ROWS, 0)),
            whole(2 * HEADS, LANES),
        ],
        [pltpu.VMEM((STATE, WIDTH), f32), pltpu.VMEM((chunks, KINDS * HEADS, LANES), f32)],
    )(first, first, heads)

    before = after = None
    if slab_count > 2:
        before, after = shifted(decay, slab_count, 1), shifted(decay, slab_count, -1)
    inbound = carry_over(state, decay, before, slab_count, 1)

    (within,) = flow(
        within_kernel,
        [(struct((tokens, WIDTH)), up["token"](WIDTH))],
        4 * unit, size * 8,
        [up["message"](MIXER * rows), up["token"](LANES), up["lane"](KINDS * HEADS)],
    )(first, sm, smt)

    y, starts, sums = flow(
        mix_kernel,
        [
            (struct((tokens, WIDTH)), up["token"](WIDTH)),
            (hbm((chunks, STATE, WIDTH)), up["chunk"](STATE, WIDTH)),
            (struct((chunks, 8, LANES)), up["chunk"](8, LANES)),
        ],
        2 * unit, size * 20,
        [
            up["message"](FIRST * rows), up["token"](WIDTH), up["token"](LANES),
            whole(STATE, WIDTH), up["chunk"](STATE, WIDTH), up["chunk"](8, WIDTH),
            whole(1, WIDTH), whole(1, WIDTH),
        ],
        [pltpu.VMEM((STATE, WIDTH), f32)],
    )(first, within, sm, inbound, own, dec, own_gain, skip_row)

    partner = lax.ppermute(sums, "sub", [(i, i ^ 1) for i in range(sub_count)])

    d_gates, d_mixed, e, back, slab_back, readers_part, params = flow(
        norm_kernel,
        [
            (struct((peers, PAIRS * rows, LANES), bf16), up["message"](PAIRS * rows)),
            (hbm((tokens, WIDTH), bf16), up["token"](WIDTH)),
            (hbm((HEADS, tokens)), up["lane"](HEADS)),
            (hbm((chunks, STATE, WIDTH)), up["chunk"](STATE, WIDTH)),
            (struct((STATE, WIDTH), bf16), whole(STATE, WIDTH)),
            (struct((tokens, STATE)), up["token"](STATE)),
            (struct((8, LANES)), whole(8, LANES)),
        ],
        4 * unit, size * 20,
        [
            up["message"](FIRST * rows), up["token"](WIDTH),
            up["token"](LANES), up["chunk"](STATE, WIDTH), up["chunk"](8, WIDTH),
            up["chunk"](8, LANES), up["chunk"](8, LANES), whole(1, WIDTH), whole(1, WIDTH),
        ],
        [
            pltpu.VMEM((8, WIDTH), f32), pltpu.VMEM((STATE, WIDTH), f32),
            pltpu.VMEM((8, WIDTH), f32), pltpu.VMEM((8, WIDTH), f32),
            pltpu.VMEM((CHUNK, WIDTH), bf16), pltpu.VMEM((CHUNK, WIDTH), bf16),
            pltpu.VMEM((CHUNK, WIDTH), bf16),
        ],
    )(
        first, y, sm, in_hbm(starts), dec, sums, partner, own_gain, skip_row,
    )

    outer = carry_over(slab_back, decay, after, slab_count, -1)
    d_values, d_sources, gates_message = flow(
        local_kernel,
        [
            (hbm((tokens, WIDTH)), up["token"](WIDTH)),
            (hbm((tokens, STATE)), up["token"](STATE)),
            (hbm((peers, gate_rows, LANES), bf16), up["message"](gate_rows)),
        ],
        8 * unit, size * 8,
        [
            up["message"](MIXER * rows), up["token"](WIDTH), up["token"](LANES),
            up["lane"](KINDS * HEADS), up["token"](STATE), up["message"](PAIRS * rows),
        ],
    )(first, in_hbm(d_mixed), sm, smt, readers_part, d_gates)
    gates_message, outer = lax.optimization_barrier((gates_message, outer))
    gates_back = exchange(gates_message)

    (last,) = flow(
        last_kernel,
        [(hbm((peers, last_rows, LANES), bf16), whole(peers, last_rows, LANES))],
        4 * unit, size * 16,
        [
            dn["message"](SOURCES * rows), dn["token"](WIDTH), dn["token"](STATE),
            dn["token"](WIDTH), dn["lane"](HEADS), dn["token"](LANES), dn["lane"](KINDS * HEADS),
            whole(STATE, WIDTH), dn["chunk"](STATE, WIDTH), dn["chunk"](STATE, WIDTH),
            dn["chunk"](8, WIDTH), whole(1, WIDTH), whole(2 * HEADS, LANES), whole(8, LANES),
        ],
        [
            pltpu.VMEM((STATE, WIDTH), f32), pltpu.VMEM((2 * HEADS, LANES), f32),
            pltpu.VMEM((CHUNK, WIDTH), bf16), pltpu.VMEM((CHUNK, WIDTH), bf16),
            pltpu.VMEM((CHUNK, WIDTH), bf16), pltpu.VMEM((STATE, WIDTH), bf16),
            pltpu.VMEM((16, WIDTH), f32),
        ],
    )(
        first, in_hbm(d_values), in_hbm(d_sources), in_hbm(d_mixed), in_hbm(e), sm, smt, outer,
        in_hbm(back), in_hbm(starts), dec, skip_row, heads, params,
    )

    last, gates_back = lax.optimization_barrier((last, gates_back))
    last_back = exchange(last)
    grad_gates, grad_c = call(
        lambda *refs: unpack_gates(owners, *refs),
        (struct((rows, CHANNELS), bf16), struct((rows, GROUPS * STATE), bf16)),
        0, 4 * rows * CHANNELS,
    )(gates_back)

    tile_at = LAST * rows // STEP_ROWS
    mine = lax.broadcasted_iota(jnp.int32, (tensor_count, LANES), 0) == lax.axis_index("tensor")

    def tile(at):
        return pl.BlockSpec((peers, STEP_ROWS, LANES), lambda c: (0, at, 0))

    params = call(
        lambda *refs: unpack_params(sub_count, tensor_count, *refs),
        struct((8 + sub_count * PAIRS, LANES)),
        0, 4 * peers * STEP_ROWS * LANES, (1,),
        [tile(tile_at), tile(tile_at + 1), whole(tensor_count, LANES)],
        whole(8 + sub_count * PAIRS, LANES),
    )(last_back, last_back, mine.astype(f32))
    params = sum_over(params, "slab", slab_count)
    grad_x, grad_b, grad_steps = call(
        lambda *refs: unpack_last(owners, *refs),
        (
            struct((rows, CHANNELS), bf16), struct((rows, GROUPS * STATE), bf16),
            struct((rows, MIXER_HEADS), bf16),
        ),
        0, 6 * rows * CHANNELS,
    )(last_back)
    count = sub_count * HEADS
    return (
        grad_x,
        grad_gates,
        grad_b,
        grad_c,
        grad_steps,
        params[0, :count],
        params[2, :count],
        params[1, :count],
        params[8:].reshape(-1),
    )


def solution(mesh):
    tensor_count = mesh.shape["tensor"]
    sub_count = OWNERS // tensor_count
    slab_count = mesh.shape["dp"] // sub_count
    devices = mesh.devices.reshape(slab_count, sub_count, tensor_count)
    split_mesh = Mesh(devices, ("slab", "sub", "tensor"))
    rows = P(("slab", "sub", "tensor"), None)
    param = P("tensor")

    def local(*arrays):
        return on_device(slab_count, sub_count, tensor_count, *arrays)

    return jax.shard_map(
        local,
        mesh=split_mesh,
        in_specs=(rows,) * 5 + (param,) * 4 + (rows,),
        out_specs=(rows,) * 5 + (param,) * 4,
        check_vma=False,
    )
```

```python
import jax
import jax.numpy as jnp
from jax import lax
from jax.experimental import pallas as pl
from jax.experimental.pallas import tpu as pltpu
from jax.sharding import Mesh
from jax.sharding import PartitionSpec as P

MIXER_HEADS = 128
HEAD_DIM = 64
STATE = 128
GROUPS = 8
CHANNELS = MIXER_HEADS * HEAD_DIM
HEADS = 8
WIDTH = HEADS * HEAD_DIM
GROUP_WIDTH = 2 * WIDTH
OWNERS = MIXER_HEADS // HEADS
LANES = 128
PAIRS = WIDTH // LANES
CHUNK = 128
STEP_ROWS = 16
epsilon = 1e-05
f32 = jnp.float32
bf16 = jnp.bfloat16

DT, CUM, WEIGHT, SHIFTED, ECUM, RATE, SIG = range(7)
KINDS = 8
CLAMP = 80.0


def mm(a, b):
    return jnp.dot(a, b, preferred_element_type=f32)


def mm_nt(a, b):
    return lax.dot_general(a, b, (((1,), (1,)), ((), ())), preferred_element_type=f32)


def mm_tn(a, b):
    return lax.dot_general(a, b, (((0,), (0,)), ((), ())), preferred_element_type=f32)


def mm_exact(a, b):
    return jnp.dot(a, b, precision=lax.Precision.HIGHEST, preferred_element_type=f32)


def two_terms(values):
    high = values.astype(bf16)
    return high, (values - high.astype(f32)).astype(bf16)


def mm_two(a, high, low):
    both = mm(a, jnp.concatenate([high, low], axis=1))
    width = high.shape[1]
    return both[:, :width] + both[:, width:]


def sigmoid(values):
    return 0.5 + 0.5 * jnp.tanh(0.5 * values)


def low_half(rows):
    return lax.broadcasted_iota(jnp.int32, (rows, LANES), 1) < HEAD_DIM


def spread_pair(values, kind, j):
    rows = values.shape[0]
    at = kind * HEADS + 2 * j
    return jnp.where(
        low_half(rows),
        jnp.broadcast_to(values[:, at : at + 1], (rows, LANES)),
        jnp.broadcast_to(values[:, at + 1 : at + 2], (rows, LANES)),
    )


def head_rows():
    row = lax.broadcasted_iota(jnp.int32, (16, WIDTH), 0)
    channel = lax.broadcasted_iota(jnp.int32, (16, WIDTH), 1) // HEAD_DIM
    return jnp.where(row == channel, 1.0, 0.0).astype(bf16)


def split_pair(block):
    low = low_half(block.shape[0])
    zero = jnp.zeros_like(block)
    return jnp.concatenate(
        [jnp.where(low, block, zero), jnp.where(low, zero, block)], axis=0
    )


def lanes(j):
    return slice(j * LANES, (j + 1) * LANES)


class Message:
    def __init__(self, rows):
        self.rows = rows
        self.per_chunk = CHUNK // rows

    def place(self, chunk, k):
        r = self.rows
        return (slice(chunk * self.per_chunk, (chunk + 1) * self.per_chunk), slice(k * r, (k + 1) * r))

    def get(self, ref, chunk, k):
        a, b = self.place(chunk, k)
        return ref[a, b, :].reshape(CHUNK, LANES)

    def put(self, ref, chunk, k, value):
        a, b = self.place(chunk, k)
        ref[a, b, :] = value.reshape(self.per_chunk, self.rows, LANES)


X, B, C = 0, PAIRS, PAIRS + 1
SOURCES = PAIRS + 1
FIRST = PAIRS + 2
Z, GRAD = 0, PAIRS
SECOND = 2 * PAIRS
LAST_X, LAST_Z, LAST_B, LAST_C = 0, PAIRS, 2 * PAIRS, 2 * PAIRS + 1
LAST = 2 * PAIRS + 2
TERMS = 3


def pack_first(x_ref, b_ref, c_ref, steps_ref, out_ref, by_head):
    r = x_ref.shape[0]
    step = pl.program_id(0)
    subs = out_ref.shape[0]

    @pl.when(step == 0)
    def _():
        steps = steps_ref[...].astype(f32)
        by_head[...] = jnp.concatenate([steps, jnp.zeros((LANES - r, LANES), f32)], axis=0).T

    zero = jnp.zeros((STEP_ROWS - HEADS, LANES), f32)
    for s in range(subs):
        for j in range(PAIRS):
            out_ref[s, 0, j * r : (j + 1) * r, :] = x_ref[:, lanes(s * PAIRS + j)]
        out_ref[s, 0, B * r : (B + 1) * r, :] = b_ref[:, lanes(s // 2)]
        out_ref[s, 0, C * r : (C + 1) * r, :] = c_ref[:, lanes(s // 2)]
        at = pl.multiple_of((step * subs + s) * HEADS, HEADS)
        mine = jnp.concatenate([by_head[pl.ds(at, HEADS), :], zero], axis=0)
        out_ref[s, 0, FIRST * r :, :] = mine.astype(bf16)


def pack_second(z_ref, grad_ref, out_ref):
    r = z_ref.shape[0]
    for s in range(out_ref.shape[0]):
        for j in range(PAIRS):
            at = lanes(s * PAIRS + j)
            out_ref[s, 0, (Z + j) * r : (Z + j + 1) * r, :] = z_ref[:, at]
            out_ref[s, 0, (GRAD + j) * r : (GRAD + j + 1) * r, :] = grad_ref[:, at]


def add_halves(owners, in_ref, block, out_ref):
    r = out_ref.shape[0]
    peer_of = {own: peer for peer, own in enumerate(owners)}
    for g in range(GROUPS):
        halves = [
            in_ref[peer_of[2 * g + k], block * r : (block + 1) * r, :].astype(f32) for k in range(2)
        ]
        out_ref[:, lanes(g)] = (halves[0] + halves[1]).astype(bf16)


def unpack(owners, in_ref, x_ref, z_ref, b_ref, c_ref, steps_ref):
    r = x_ref.shape[0]
    peer_of = {own: peer for peer, own in enumerate(owners)}
    for peer, own in enumerate(owners):
        for j in range(PAIRS):
            for block, ref in ((LAST_X, x_ref), (LAST_Z, z_ref)):
                at = slice((block + j) * r, (block + j + 1) * r)
                ref[:, lanes(own * PAIRS + j)] = in_ref[peer, at, :]
    add_halves(owners, in_ref, LAST_B, b_ref)
    add_halves(owners, in_ref, LAST_C, c_ref)
    by_head = jnp.concatenate(
        [
            in_ref[peer_of[own], LAST * r : LAST * r + STEP_ROWS, :].astype(f32)[:HEADS]
            for own in range(OWNERS)
        ],
        axis=0,
    )
    steps_ref[...] = by_head.T[:r, :].astype(bf16)


def three_terms(values):
    high = values.astype(bf16).astype(f32)
    rest = values - high
    middle = rest.astype(bf16).astype(f32)
    return [high, middle, rest - middle]


def unpack_params(sub_count, tensor_count, late_ref, early_ref, mine_ref, out_ref):
    lane = lax.broadcasted_iota(jnp.int32, (1, LANES), 1)
    late = [jnp.zeros((1, LANES), f32) for _ in range(2)]
    skip = jnp.zeros((1, LANES), f32)

    def placed(rows, at):
        total = rows[at : at + 1] + rows[at + 1 : at + 2] + rows[at + 2 : at + 3]
        return jnp.where(lane < HEADS, total, 0.0)

    for s in range(sub_count):
        late_rows = jnp.zeros((STEP_ROWS, LANES), f32)
        early_rows = jnp.zeros((STEP_ROWS, LANES), f32)
        for t in range(tensor_count):
            mine = mine_ref[t : t + 1, :] > 0.0
            peer = s * tensor_count + t
            late_rows = jnp.where(mine, late_ref[peer].astype(f32), late_rows)
            early_rows = jnp.where(mine, early_ref[peer].astype(f32), early_rows)
        for k in range(2):
            part = placed(late_rows, HEADS + k * TERMS)
            late[k] = late[k] + (part if s == 0 else pltpu.roll(part, s * HEADS, 1))
        part = placed(early_rows, TERMS * PAIRS)
        skip = skip + (part if s == 0 else pltpu.roll(part, s * HEADS, 1))
        gain = early_rows[:PAIRS] + early_rows[PAIRS : 2 * PAIRS] + early_rows[2 * PAIRS : 3 * PAIRS]
        out_ref[8 + s * PAIRS : 8 + (s + 1) * PAIRS, :] = gain
    out_ref[:8, :] = jnp.concatenate(late + [skip, jnp.zeros((5, LANES), f32)], axis=0)


def state_kernel(
    message, per_step,
    first_ref, steps_ref, heads_ref, sm_ref, smt_ref, own_ref, dec_ref, state_ref, whole_ref,
    carry, rows_s,
):
    c = pl.program_id(0)

    @pl.when(c == 0)
    def _():
        carry[...] = jnp.zeros_like(carry)
        whole_ref[...] = jnp.ones_like(whole_ref)
        chunks = rows_s.shape[0]
        before = lax.broadcasted_iota(jnp.int32, (CHUNK, CHUNK), 0)
        after = lax.broadcasted_iota(jnp.int32, (CHUNK, CHUNK), 1)
        raws = []
        for k in range(chunks):
            raw = heads_ref[HEADS:, :]
            for p in range(message.per_chunk):
                part = steps_ref[k * message.per_chunk + p].astype(f32)[:HEADS]
                raw = raw + (part if p == 0 else pltpu.roll(part, p * message.rows, 1))
            raws.append(raw)
        raw = jnp.concatenate(raws, axis=0)
        small = jnp.exp(-jnp.abs(raw))
        series = small * (
            1.0 - small * (0.5 - small * (1.0 / 3 - small * (0.25 - small * 0.2)))
        )
        soft = jnp.maximum(raw, 0.0) + jnp.where(small < 0.015625, series, jnp.log(1.0 + small))
        sig = jnp.where(raw >= 0.0, 1.0, small) / (1.0 + small)
        decay_rate = jnp.concatenate([jnp.exp(heads_ref[:HEADS, :])] * chunks, axis=0)
        rate = -decay_rate * soft
        cum = mm_exact(rate, jnp.where(before <= after, 1.0, 0.0))
        rest = mm_exact(rate, jnp.where(before > after, 1.0, 0.0))
        kinds = [
            soft, cum, soft * jnp.exp(rest), cum - jnp.log(soft), jnp.exp(cum), rate, sig,
            jnp.zeros_like(soft),
        ]
        for k in range(chunks):
            at = slice(k * HEADS, (k + 1) * HEADS)
            rows_s[k] = jnp.concatenate([kind[at] for kind in kinds], axis=0)

    for i in range(per_step):
        rows = rows_s[c * per_step + i]
        smt_ref[:, lanes(i)] = rows
        sm = jnp.concatenate([rows, jnp.zeros_like(rows)], axis=0).T
        sm_ref[i * CHUNK : (i + 1) * CHUNK, :] = sm
        last = jnp.broadcast_to(sm[CHUNK - 1 : CHUNK, :], (8, LANES))
        sources_t = message.get(first_ref, i, B).T
        for j in range(PAIRS):
            dec = spread_pair(last, ECUM, j)
            dec_ref[i, :, lanes(j)] = dec
            whole_ref[:, lanes(j)] = whole_ref[:, lanes(j)] * dec
            scaled = message.get(first_ref, i, X + j).astype(f32) * spread_pair(sm, WEIGHT, j)
            own = mm_two(sources_t, *two_terms(scaled))
            own_ref[i, :, lanes(j)] = own
            carry[:, lanes(j)] = dec[0:1] * carry[:, lanes(j)] + own
    state_ref[...] = carry[...].astype(bf16)


def within_kernel(message, per_step, first_ref, sm_ref, smt_ref, out_ref):
    t = lax.broadcasted_iota(jnp.int32, (CHUNK, CHUNK), 0)
    s = lax.broadcasted_iota(jnp.int32, (CHUNK, CHUNK), 1)
    for i in range(per_step):
        rows = slice(i * CHUNK, (i + 1) * CHUNK)
        scores = mm_nt(message.get(first_ref, i, C), message.get(first_ref, i, B))
        scores = jnp.where(t >= s, scores, 0.0)
        for j in range(PAIRS):
            weights = []
            for h in (2 * j, 2 * j + 1):
                here = sm_ref[rows, CUM * HEADS + h : CUM * HEADS + h + 1]
                there = smt_ref[SHIFTED * HEADS + h : SHIFTED * HEADS + h + 1, lanes(i)]
                weights.append(
                    (scores * jnp.exp(jnp.minimum(here - there, CLAMP))).astype(bf16)
                )
            values = split_pair(message.get(first_ref, i, X + j))
            out_ref[rows, lanes(j)] = mm(jnp.concatenate(weights, axis=1), values)


def mix_kernel(
    message, per_step,
    first_ref, second_ref, within_ref, sm_ref, inbound_ref, own_ref, dec_ref, gain_ref, skip_ref,
    y_ref, start_ref, sums_ref,
    carry,
):
    @pl.when(pl.program_id(0) == 0)
    def _():
        carry[...] = inbound_ref[...].astype(f32)

    for i in range(per_step):
        rows = slice(i * CHUNK, (i + 1) * CHUNK)
        sm = sm_ref[rows, :]
        readers = message.get(first_ref, i, C)
        power = jnp.zeros((CHUNK, LANES), f32)
        cross = jnp.zeros((CHUNK, LANES), f32)
        for j in range(PAIRS):
            state = carry[:, lanes(j)]
            start_ref[i, :, lanes(j)] = state
            carried = mm_two(readers, *two_terms(state))
            carry[:, lanes(j)] = dec_ref[i, 0:1, lanes(j)] * state + own_ref[i, :, lanes(j)]
            y = within_ref[rows, lanes(j)] + spread_pair(sm, ECUM, j) * carried
            y_ref[rows, lanes(j)] = y
            values = message.get(first_ref, i, X + j).astype(f32)
            gates = message.get(second_ref, i, Z + j).astype(f32)
            grad = message.get(second_ref, i, GRAD + j).astype(f32)
            gated = (y + skip_ref[0:1, lanes(j)] * values) * (gates * sigmoid(gates))
            power = power + gated * gated
            cross = cross + grad * gain_ref[0:1, lanes(j)] * gated
        sums_ref[i, 0:1, :] = jnp.sum(power.T, axis=0, keepdims=True)
        sums_ref[i, 1:2, :] = jnp.sum(cross.T, axis=0, keepdims=True)
        sums_ref[i, 2:, :] = jnp.zeros((6, LANES), f32)


def norm_kernel(
    message, per_step,
    first_ref, second_ref, y_ref, sm_ref, start_ref, dec_ref, sums_ref, other_ref, gain_ref, skip_ref,
    gate_ref, mixed_ref, e_ref, back_ref, slab_ref, readers_ref, param_ref,
    pre, back_sum, gain_sum, skip_sum, high_s, low_s, scaled_s,
):
    c = pl.program_id(0)

    @pl.when(c == 0)
    def _():
        pre[...] = jnp.ones_like(pre)
        back_sum[...] = jnp.zeros_like(back_sum)
        gain_sum[...] = jnp.zeros_like(gain_sum)
        skip_sum[...] = jnp.zeros_like(skip_sum)

    ones = head_rows()
    for i in range(per_step):
        rows = slice(i * CHUNK, (i + 1) * CHUNK)
        sm = sm_ref[rows, :]
        readers = message.get(first_ref, i, C)
        readers_t = readers.T
        sums = (sums_ref[i] + other_ref[i]) * (1.0 / GROUP_WIDTH)
        inverse_row = lax.rsqrt(sums[0:1] + epsilon)
        pull_row = inverse_row * inverse_row * inverse_row * sums[1:2]
        inverse = jnp.broadcast_to(inverse_row, (CHUNK, LANES)).T
        pull = jnp.broadcast_to(pull_row, (CHUNK, LANES)).T
        for j in range(PAIRS):
            at = lanes(j)
            values = message.get(first_ref, i, X + j).astype(f32)
            gates = message.get(second_ref, i, Z + j).astype(f32)
            grad = message.get(second_ref, i, GRAD + j).astype(f32)
            y = y_ref[rows, at]
            mixed = y + skip_ref[0:1, at] * values
            sig = sigmoid(gates)
            silu = gates * sig
            gated = mixed * silu
            scaled = inverse * grad
            gain_sum[0:1, at] += jnp.sum(scaled * gated, axis=0, keepdims=True)
            d_gated = scaled * gain_ref[0:1, at] - pull * gated
            d_mixed = d_gated * silu
            d_gate = d_gated * mixed * (sig + silu * (1.0 - sig))
            message.put(gate_ref, i, j, d_gate.astype(bf16))
            skip_sum[0:1, at] += jnp.sum(values * d_mixed, axis=0, keepdims=True)
            rounded = d_mixed.astype(bf16)
            mixed_ref[rows, at] = rounded
            high_s[:, at], low_s[:, at] = two_terms(rounded.astype(f32) * y)
            high, low = two_terms(d_mixed * spread_pair(sm, ECUM, j))
            scaled_s[:, at] = high
            back = mm_two(readers_t, high, low)
            back_ref[i, :, at] = back
            back_sum[:, at] += pre[0:1, at] * back
            pre[:, at] = pre[:, at] * dec_ref[i, :, at]
        e_ref[:, lanes(i)] = (mm_nt(ones, high_s[...]) + mm_nt(ones, low_s[...]))[:HEADS]
        readers_ref[rows, :] = mm_nt(scaled_s[...], start_ref[i].astype(bf16))
    slab_ref[...] = back_sum[...].astype(bf16)

    @pl.when(c == pl.num_programs(0) - 1)
    def _():
        for j in range(PAIRS):
            param_ref[j : j + 1, :] = gain_sum[0:1, lanes(j)]
        high, low = two_terms(jnp.broadcast_to(skip_sum[0:1, :], (LANES, WIDTH)))
        skips = (mm_nt(high, ones) + mm_nt(low, ones))[0:1]
        param_ref[PAIRS : PAIRS + 1, :] = jnp.concatenate(
            [skips, jnp.zeros((1, LANES - 16), f32)], axis=1
        )
        param_ref[PAIRS + 1 :, :] = jnp.zeros((8 - PAIRS - 1, LANES), f32)


def local_kernel(
    message, per_step,
    first_ref, grad_ref, sm_ref, smt_ref, readers_ref, values_out, sources_out, readers_out,
):
    s = lax.broadcasted_iota(jnp.int32, (CHUNK, CHUNK), 0)
    t = lax.broadcasted_iota(jnp.int32, (CHUNK, CHUNK), 1)
    causal = t >= s
    for i in range(per_step):
        rows = slice(i * CHUNK, (i + 1) * CHUNK)
        sources = message.get(first_ref, i, B)
        readers = message.get(first_ref, i, C)
        scores = jnp.where(causal, mm_nt(sources, readers), 0.0)
        total = jnp.zeros((CHUNK, CHUNK), f32)
        for j in range(PAIRS):
            grads = split_pair(grad_ref[rows, lanes(j)])
            weight_grads = mm_nt(message.get(first_ref, i, X + j), grads)
            weights = []
            for k, h in enumerate((2 * j, 2 * j + 1)):
                there = sm_ref[rows, SHIFTED * HEADS + h : SHIFTED * HEADS + h + 1]
                here = smt_ref[CUM * HEADS + h : CUM * HEADS + h + 1, lanes(i)]
                decay = jnp.exp(jnp.minimum(here - there, CLAMP))
                weights.append((scores * decay).astype(bf16))
                total = total + weight_grads[:, lanes(k)] * decay
            values_out[rows, lanes(j)] = mm(jnp.concatenate(weights, axis=1), grads)
        total = jnp.where(causal, total, 0.0).astype(bf16)
        sources_out[rows, :] = mm(total, readers)
        d_readers = mm_tn(total, sources) + readers_ref[rows, :]
        message.put(readers_out, i, 0, d_readers.astype(bf16))


def last_kernel(
    message, per_step,
    first_ref, within_ref, sources_ref, readers_ref, gate_ref, grad_ref, e_ref, sm_ref, smt_ref, outer_ref,
    back_ref, start_ref, dec_ref, skip_ref, heads_ref, early_ref,
    out_ref,
    carry, sums, high_s, low_s, scaled_s, state_s, flux_s,
):
    c = pl.program_id(0)

    @pl.when(c == 0)
    def _():
        carry[...] = outer_ref[...].astype(f32)
        sums[...] = jnp.zeros_like(sums)

    r = message.rows
    ones = head_rows()
    before = lax.broadcasted_iota(jnp.int32, (CHUNK, CHUNK), 0)
    after = lax.broadcasted_iota(jnp.int32, (CHUNK, CHUNK), 1)
    earlier = jnp.where(before < after, 1.0, 0.0)
    decay_rate = jnp.exp(heads_ref[:HEADS, :])
    first_peer = (pl.num_programs(0) - 1 - c) * per_step * message.per_chunk
    mine = out_ref.at[pl.ds(first_peer, per_step * message.per_chunk)]
    for i in reversed(range(per_step)):
        rows = slice(i * CHUNK, (i + 1) * CHUNK)
        sm = sm_ref[rows, :]
        sources = message.get(first_ref, i, B)
        for j in range(PAIRS):
            at = lanes(j)
            state = carry[:, at]
            high, low = two_terms(state)
            state_s[:, at] = high
            values = message.get(first_ref, i, X + j).astype(f32)
            weight = spread_pair(sm, WEIGHT, j)
            grad = within_ref[rows, at] + weight * mm_two(sources, high, low)
            skipped = skip_ref[0:1, at] * grad_ref[rows, at].astype(f32)
            message.put(mine, i, LAST_X + j, (grad + skipped).astype(bf16))
            high_s[:, at], low_s[:, at] = two_terms(values * grad)
            scaled_s[:, at] = (values * weight).astype(bf16)
            new = dec_ref[i, 0:1, at] * state + back_ref[i, :, at]
            carry[:, at] = new
            flux_s[:, at] = jnp.broadcast_to(
                jnp.sum(start_ref[i, :, at] * new, axis=0, keepdims=True), (16, LANES)
            )
        d_sources = sources_ref[rows, :] + mm_nt(scaled_s[...], state_s[...])
        message.put(mine, i, LAST_B, d_sources.astype(bf16))
        message.put(mine, i, LAST_C, message.get(readers_ref, i, 0))
        for j in range(PAIRS):
            message.put(mine, i, LAST_Z + j, message.get(gate_ref, i, j))
        g = (mm_nt(ones, high_s[...]) + mm_nt(ones, low_s[...]))[:HEADS]
        high, low = two_terms(flux_s[...])
        constant = (mm_nt(ones, high) + mm_nt(ones, low))[:HEADS, 0:1]
        flux = constant + mm_exact(g - e_ref[:, lanes(i)], earlier)
        soft = smt_ref[DT * HEADS : (DT + 1) * HEADS, lanes(i)]
        rate = smt_ref[RATE * HEADS : (RATE + 1) * HEADS, lanes(i)]
        sig = smt_ref[SIG * HEADS : (SIG + 1) * HEADS, lanes(i)]
        steps = (g / soft - decay_rate * flux) * sig
        sums[:HEADS, :] += flux * rate
        sums[HEADS:, :] += steps
        steps = jnp.concatenate([steps, jnp.zeros_like(steps)], axis=0)
        for p in range(message.per_chunk):
            part = steps if p == 0 else pltpu.roll(steps, LANES - p * r, 1)
            mine[i * message.per_chunk + p, LAST * r : LAST * r + STEP_ROWS, :] = part.astype(bf16)

    @pl.when(c == pl.num_programs(0) - 1)
    def _():
        late = []
        for k in range(2):
            column = jnp.sum(sums[k * HEADS : (k + 1) * HEADS, :], axis=1, keepdims=True)
            block = jnp.broadcast_to(column, (HEADS, LANES))
            block = jnp.concatenate([block, jnp.zeros((LANES - HEADS, LANES), f32)], axis=0)
            late += three_terms(block.T[0:1, :])
        late += [jnp.zeros((HEADS - 2 * TERMS, LANES), f32)]
        late = jnp.concatenate([jnp.zeros((HEADS, LANES), f32)] + late, axis=0)
        late = late.astype(bf16)
        early = three_terms(early_ref[:PAIRS, :]) + three_terms(early_ref[PAIRS : PAIRS + 1, :])
        early += [jnp.zeros((STEP_ROWS - TERMS * (PAIRS + 1), LANES), f32)]
        early = jnp.concatenate(early, axis=0).astype(bf16)
        own_rows = lax.broadcasted_iota(jnp.int32, (STEP_ROWS, LANES), 0) < HEADS

        def fill(peer, unused):
            steps_at = slice(LAST * r, LAST * r + STEP_ROWS)
            out_ref[peer, steps_at, :] = jnp.where(own_rows, out_ref[peer, steps_at, :], late)
            out_ref[peer, LAST * r + STEP_ROWS :, :] = early
            return unused

        lax.fori_loop(0, out_ref.shape[0], fill, 0)


def call(kernel, out_shape, flops, moved, grid=None, in_specs=None, out_specs=None, scratch=()):
    extra = {}
    if grid is not None:
        extra = dict(grid=grid, in_specs=in_specs, out_specs=out_specs)
    return pl.pallas_call(
        kernel,
        out_shape=out_shape,
        scratch_shapes=list(scratch),
        compiler_params=pltpu.CompilerParams(vmem_limit_bytes=16 * 1024 * 1024),
        cost_estimate=pl.CostEstimate(flops=flops, bytes_accessed=moved, transcendentals=0),
        **extra,
    )


def shifted(array, count, by):
    pairs = [(i, i + by) for i in range(count) if 0 <= i + by < count]
    return lax.ppermute(array, "slab", pairs)


def carry_over(state, decay, first_decay, count, sign):
    window, window_decay, step = state, decay, 1
    result = result_decay = None
    while step < count:
        arrived = shifted(window, count, sign * step)
        more = 2 * step < count
        if result is None:
            result = arrived
            if more:
                result_decay = first_decay
                window = (state.astype(f32) + decay[0:1] * arrived.astype(f32)).astype(bf16)
                window_decay = decay * first_decay
        else:
            if more:
                arrived_decay = shifted(window_decay, count, sign * step)
                window = (window.astype(f32) + window_decay[0:1] * arrived.astype(f32)).astype(bf16)
                window_decay = window_decay * arrived_decay
            result = result.astype(f32) + result_decay[0:1] * arrived.astype(f32)
            if more:
                result_decay = result_decay * arrived_decay
        step *= 2
    return jnp.zeros_like(state) if result is None else result


def sum_over(array, axis, count):
    step = 1
    while step < count:
        array = array + lax.ppermute(array, axis, [(i, i ^ step) for i in range(count)])
        step *= 2
    return array


def on_device(
    slab_count, sub_count, tensor_count,
    mixer_x, gate_z, b_matrix, c_matrix, raw_steps, decay_log, skip_gain, step_bias, norm_gain, out_grad,
):
    rows = mixer_x.shape[0]
    peers = sub_count * tensor_count
    tokens = rows * peers
    chunks = tokens // CHUNK
    per_step = min(2, chunks)
    grid = (chunks // per_step,)
    message = Message(rows)
    owners = [t * sub_count + s for s in range(sub_count) for t in range(tensor_count)]
    sub = lax.axis_index("sub")

    def struct(shape, kind=f32):
        return jax.ShapeDtypeStruct(shape, kind)

    def hbm(shape, kind=f32):
        return pltpu.HBM(shape, kind)

    def in_hbm(array):
        return pltpu.with_memory_space_constraint(array, pltpu.HBM)

    def exchange(array):
        return lax.all_to_all(array, ("sub", "tensor"), split_axis=0, concat_axis=0, tiled=True)

    own_logs = lax.dynamic_slice(decay_log, (sub * HEADS,), (HEADS,))
    own_bias = lax.dynamic_slice(step_bias, (sub * HEADS,), (HEADS,))
    own_skip = lax.dynamic_slice(skip_gain, (sub * HEADS,), (HEADS,))
    own_gain = lax.dynamic_slice(norm_gain, (sub * WIDTH,), (WIDTH,)).reshape(1, WIDTH)
    heads = jnp.broadcast_to(jnp.concatenate([own_logs, own_bias])[:, None], (2 * HEADS, LANES))
    skip_row = jnp.repeat(own_skip, HEAD_DIM).reshape(1, WIDTH)

    first_rows = FIRST * rows + STEP_ROWS
    second_rows = SECOND * rows
    last_rows = LAST * rows + 2 * STEP_ROWS

    def packed(kernel, height, arrays, whole_arrays=(), scratch=()):
        out = hbm((sub_count, tensor_count, height, LANES), bf16)
        moved = 4 * peers * height * LANES
        specs = [
            pl.BlockSpec((rows, a.shape[1] // tensor_count), lambda t: (0, t)) for a in arrays
        ] + [pl.BlockSpec(a.shape, lambda t: (0, 0)) for a in whole_arrays]
        out_spec = pl.BlockSpec((sub_count, 1, height, LANES), lambda t: (0, t, 0, 0))
        made = call(kernel, out, 0, moved, (tensor_count,), specs, out_spec, scratch)(
            *(in_hbm(a) for a in (*arrays, *whole_arrays))
        )
        return made.reshape(peers, height, LANES)

    first = exchange(
        packed(
            pack_first, first_rows, (mixer_x, b_matrix, c_matrix), (raw_steps,),
            [pltpu.VMEM((LANES, LANES), f32)],
        )
    )
    tensor_rows = lax.broadcasted_iota(jnp.int32, (tensor_count, LANES), 0)
    mine = (tensor_rows == lax.axis_index("tensor")).astype(f32)
    gate_z, heads, skip_row, own_gain, mine = lax.optimization_barrier(
        (gate_z, heads, skip_row, own_gain, mine)
    )
    second = exchange(packed(pack_second, second_rows, (gate_z, out_grad)))

    def flow(kernel, shape_specs, flops, moved, in_specs, scratch=()):
        def body(*refs):
            return kernel(message, per_step, *refs)

        shapes = tuple(shape for shape, _ in shape_specs)
        specs = tuple(spec for _, spec in shape_specs)
        return call(body, shapes, flops, moved, grid, in_specs, specs, scratch)

    def spec(block, axis, down=False):
        def index(c):
            at = grid[0] - 1 - c if down else c
            return tuple(at if k == axis else 0 for k in range(len(block)))

        return pl.BlockSpec(block, index)

    span = per_step * CHUNK

    def specs_of(down):
        return dict(
            message=lambda height: spec((per_step * message.per_chunk, height, LANES), 0, down),
            token=lambda width: spec((span, width), 0, down),
            lane=lambda height: spec((height, span), 1, down),
            chunk=lambda *shape: spec((per_step,) + shape, 0, down),
        )

    up, dn = specs_of(False), specs_of(True)

    def whole(*shape):
        return pl.BlockSpec(shape, lambda c: (0,) * len(shape))

    unit = 2 * tokens * CHUNK * WIDTH
    size = tokens * WIDTH

    sm, smt, own, dec, state, decay = flow(
        state_kernel,
        [
            (hbm((tokens, LANES)), up["token"](LANES)),
            (hbm((KINDS * HEADS, tokens)), up["lane"](KINDS * HEADS)),
            (hbm((chunks, STATE, WIDTH)), up["chunk"](STATE, WIDTH)),
            (hbm((chunks, 8, WIDTH)), up["chunk"](8, WIDTH)),
            (struct((STATE, WIDTH), bf16), whole(STATE, WIDTH)),
            (struct((8, WIDTH)), whole(8, WIDTH)),
        ],
        2 * unit, size * 8,
        [
            up["message"](SOURCES * rows),
            pl.BlockSpec((peers, STEP_ROWS, LANES), lambda c: (0, FIRST * rows // STEP_ROWS, 0)),
            whole(2 * HEADS, LANES),
        ],
        [pltpu.VMEM((STATE, WIDTH), f32), pltpu.VMEM((chunks, KINDS * HEADS, LANES), f32)],
    )(first, first, heads)

    before = after = None
    if slab_count > 2:
        before, after = shifted(decay, slab_count, 1), shifted(decay, slab_count, -1)
    inbound = carry_over(state, decay, before, slab_count, 1)

    (within,) = flow(
        within_kernel,
        [(hbm((tokens, WIDTH)), up["token"](WIDTH))],
        4 * unit, size * 8,
        [up["message"](FIRST * rows), up["token"](LANES), up["lane"](KINDS * HEADS)],
    )(first, sm, smt)

    y, starts, sums = flow(
        mix_kernel,
        [
            (struct((tokens, WIDTH)), up["token"](WIDTH)),
            (struct((chunks, STATE, WIDTH)), up["chunk"](STATE, WIDTH)),
            (struct((chunks, 8, LANES)), up["chunk"](8, LANES)),
        ],
        2 * unit, size * 20,
        [
            up["message"](FIRST * rows), up["message"](second_rows), up["token"](WIDTH),
            up["token"](LANES), whole(STATE, WIDTH), up["chunk"](STATE, WIDTH), up["chunk"](8, WIDTH),
            whole(1, WIDTH), whole(1, WIDTH),
        ],
        [pltpu.VMEM((STATE, WIDTH), f32)],
    )(
        first, in_hbm(second), in_hbm(within), in_hbm(sm), inbound, in_hbm(own), in_hbm(dec),
        own_gain, skip_row,
    )

    partner = lax.ppermute(sums, "sub", [(i, i ^ 1) for i in range(sub_count)])

    d_gates, d_mixed, e, back, slab_back, readers_part, params = flow(
        norm_kernel,
        [
            (struct((peers, PAIRS * rows, LANES), bf16), up["message"](PAIRS * rows)),
            (struct((tokens, WIDTH), bf16), up["token"](WIDTH)),
            (struct((HEADS, tokens)), up["lane"](HEADS)),
            (struct((chunks, STATE, WIDTH)), up["chunk"](STATE, WIDTH)),
            (struct((STATE, WIDTH), bf16), whole(STATE, WIDTH)),
            (struct((tokens, STATE)), up["token"](STATE)),
            (struct((8, LANES)), whole(8, LANES)),
        ],
        4 * unit, size * 20,
        [
            up["message"](FIRST * rows), up["message"](second_rows), up["token"](WIDTH),
            up["token"](LANES), up["chunk"](STATE, WIDTH), up["chunk"](8, WIDTH),
            up["chunk"](8, LANES), up["chunk"](8, LANES), whole(1, WIDTH), whole(1, WIDTH),
        ],
        [
            pltpu.VMEM((8, WIDTH), f32), pltpu.VMEM((STATE, WIDTH), f32),
            pltpu.VMEM((8, WIDTH), f32), pltpu.VMEM((8, WIDTH), f32),
            pltpu.VMEM((CHUNK, WIDTH), bf16), pltpu.VMEM((CHUNK, WIDTH), bf16),
            pltpu.VMEM((CHUNK, WIDTH), bf16),
        ],
    )(
        first, in_hbm(second), y, sm, starts, dec, sums, partner, own_gain, skip_row,
    )

    outer = carry_over(slab_back, decay, after, slab_count, -1)
    d_values, d_sources, d_readers = flow(
        local_kernel,
        [
            (struct((tokens, WIDTH)), up["token"](WIDTH)),
            (struct((tokens, STATE)), up["token"](STATE)),
            (struct((peers, rows, LANES), bf16), up["message"](rows)),
        ],
        8 * unit, size * 8,
        [
            up["message"](FIRST * rows), up["token"](WIDTH), up["token"](LANES),
            up["lane"](KINDS * HEADS), up["token"](STATE),
        ],
    )(first, d_mixed, sm, smt, readers_part)

    (last,) = flow(
        last_kernel,
        [(hbm((peers, last_rows, LANES), bf16), whole(peers, last_rows, LANES))],
        4 * unit, size * 16,
        [
            dn["message"](SOURCES * rows), dn["token"](WIDTH), dn["token"](STATE),
            dn["message"](rows), dn["message"](PAIRS * rows),
            dn["token"](WIDTH), dn["lane"](HEADS), dn["token"](LANES), dn["lane"](KINDS * HEADS),
            whole(STATE, WIDTH), dn["chunk"](STATE, WIDTH), dn["chunk"](STATE, WIDTH),
            dn["chunk"](8, WIDTH), whole(1, WIDTH), whole(2 * HEADS, LANES), whole(8, LANES),
        ],
        [
            pltpu.VMEM((STATE, WIDTH), f32), pltpu.VMEM((2 * HEADS, LANES), f32),
            pltpu.VMEM((CHUNK, WIDTH), bf16), pltpu.VMEM((CHUNK, WIDTH), bf16),
            pltpu.VMEM((CHUNK, WIDTH), bf16), pltpu.VMEM((STATE, WIDTH), bf16),
            pltpu.VMEM((16, WIDTH), f32),
        ],
    )(
        first, d_values, d_sources, d_readers, d_gates, d_mixed, e, sm, smt, outer, back, starts,
        dec, skip_row, heads, params,
    )

    last_back = exchange(last)
    tile_at = LAST * rows // STEP_ROWS
    def tile(at):
        return pl.BlockSpec((peers, STEP_ROWS, LANES), lambda c: (0, at, 0))

    params = call(
        lambda *refs: unpack_params(sub_count, tensor_count, *refs),
        struct((8 + sub_count * PAIRS, LANES)),
        0, 4 * peers * STEP_ROWS * LANES, (1,),
        [tile(tile_at), tile(tile_at + 1), whole(tensor_count, LANES)],
        whole(8 + sub_count * PAIRS, LANES),
    )(last_back, last_back, mine)
    params = sum_over(params, "slab", slab_count)
    wide, narrow = struct((rows, CHANNELS), bf16), struct((rows, GROUPS * STATE), bf16)
    grad_x, grad_gates, grad_b, grad_c, grad_steps = call(
        lambda *refs: unpack(owners, *refs),
        (wide, wide, narrow, narrow, struct((rows, MIXER_HEADS), bf16)),
        0, 10 * rows * CHANNELS,
    )(last_back)
    count = sub_count * HEADS
    return (
        grad_x,
        grad_gates,
        grad_b,
        grad_c,
        grad_steps,
        params[0, :count],
        params[2, :count],
        params[1, :count],
        params[8:].reshape(-1),
    )


def solution(mesh):
    tensor_count = mesh.shape["tensor"]
    sub_count = OWNERS // tensor_count
    slab_count = mesh.shape["dp"] // sub_count
    devices = mesh.devices.reshape(slab_count, sub_count, tensor_count)
    split_mesh = Mesh(devices, ("slab", "sub", "tensor"))
    rows = P(("slab", "sub", "tensor"), None)
    param = P("tensor")

    def local(*arrays):
        return on_device(slab_count, sub_count, tensor_count, *arrays)

    return jax.shard_map(
        local,
        mesh=split_mesh,
        in_specs=(rows,) * 5 + (param,) * 4 + (rows,),
        out_specs=(rows,) * 5 + (param,) * 4,
        check_vma=False,
    )
```

```python
import jax
import jax.numpy as jnp
from jax import lax
from jax.experimental import pallas as pl
from jax.experimental.pallas import tpu as pltpu
from jax.sharding import Mesh
from jax.sharding import PartitionSpec as P

MIXER_HEADS = 128
HEAD_DIM = 64
STATE = 128
GROUPS = 8
CHANNELS = MIXER_HEADS * HEAD_DIM
HEADS = 8
WIDTH = HEADS * HEAD_DIM
GROUP_WIDTH = 2 * WIDTH
OWNERS = MIXER_HEADS // HEADS
LANES = 128
PAIRS = WIDTH // LANES
CHUNK = 128
STEP_ROWS = 16
epsilon = 1e-05
f32 = jnp.float32
bf16 = jnp.bfloat16

DT, CUM, WEIGHT, SHIFTED, ECUM, RATE, SIG = range(7)
KINDS = 8
CLAMP = 80.0


def mm(a, b):
    return jnp.dot(a, b, preferred_element_type=f32)


def mm_nt(a, b):
    return lax.dot_general(a, b, (((1,), (1,)), ((), ())), preferred_element_type=f32)


def mm_tn(a, b):
    return lax.dot_general(a, b, (((0,), (0,)), ((), ())), preferred_element_type=f32)


def mm_exact(a, b):
    return jnp.dot(a, b, precision=lax.Precision.HIGHEST, preferred_element_type=f32)


def two_terms(values):
    high = values.astype(bf16)
    return high, (values - high.astype(f32)).astype(bf16)


def mm_two(a, high, low):
    both = mm(a, jnp.concatenate([high, low], axis=1))
    width = high.shape[1]
    return both[:, :width] + both[:, width:]


def sigmoid(values):
    return 0.5 + 0.5 * jnp.tanh(0.5 * values)


def low_half(rows):
    return lax.broadcasted_iota(jnp.int32, (rows, LANES), 1) < HEAD_DIM


def spread_pair(values, kind, j):
    rows = values.shape[0]
    at = kind * HEADS + 2 * j
    return jnp.where(
        low_half(rows),
        jnp.broadcast_to(values[:, at : at + 1], (rows, LANES)),
        jnp.broadcast_to(values[:, at + 1 : at + 2], (rows, LANES)),
    )


def head_rows():
    row = lax.broadcasted_iota(jnp.int32, (16, WIDTH), 0)
    channel = lax.broadcasted_iota(jnp.int32, (16, WIDTH), 1) // HEAD_DIM
    return jnp.where(row == channel, 1.0, 0.0).astype(bf16)


def split_pair(block):
    low = low_half(block.shape[0])
    zero = jnp.zeros_like(block)
    return jnp.concatenate(
        [jnp.where(low, block, zero), jnp.where(low, zero, block)], axis=0
    )


def lanes(j):
    return slice(j * LANES, (j + 1) * LANES)


class Message:
    def __init__(self, rows):
        self.rows = rows
        self.per_chunk = CHUNK // rows

    def place(self, chunk, k):
        r = self.rows
        return (slice(chunk * self.per_chunk, (chunk + 1) * self.per_chunk), slice(k * r, (k + 1) * r))

    def get(self, ref, chunk, k):
        a, b = self.place(chunk, k)
        return ref[a, b, :].reshape(CHUNK, LANES)

    def put(self, ref, chunk, k, value):
        a, b = self.place(chunk, k)
        ref[a, b, :] = value.reshape(self.per_chunk, self.rows, LANES)


X, B, C = 0, PAIRS, PAIRS + 1
SOURCES = PAIRS + 1
FIRST = PAIRS + 2
Z, GRAD = 0, PAIRS
SECOND = 2 * PAIRS
LAST_X, LAST_Z, LAST_B, LAST_C = 0, PAIRS, 2 * PAIRS, 2 * PAIRS + 1
LAST = 2 * PAIRS + 2
TERMS = 3


def pack_first(x_ref, b_ref, c_ref, steps_ref, out_ref, by_head):
    r = x_ref.shape[0]
    step = pl.program_id(0) * pl.num_programs(1) + pl.program_id(1)
    subs = out_ref.shape[0]

    @pl.when(step == 0)
    def _():
        steps = steps_ref[...].astype(f32)
        by_head[...] = jnp.concatenate([steps, jnp.zeros((LANES - r, LANES), f32)], axis=0).T

    zero = jnp.zeros((STEP_ROWS - HEADS, LANES), f32)
    for s in range(subs):
        for j in range(PAIRS):
            out_ref[s, 0, j * r : (j + 1) * r, :] = x_ref[:, lanes(s * PAIRS + j)]
        out_ref[s, 0, B * r : (B + 1) * r, :] = b_ref[:, lanes(s // 2)]
        out_ref[s, 0, C * r : (C + 1) * r, :] = c_ref[:, lanes(s // 2)]
        at = pl.multiple_of((step * subs + s) * HEADS, HEADS)
        mine = jnp.concatenate([by_head[pl.ds(at, HEADS), :], zero], axis=0)
        out_ref[s, 0, FIRST * r :, :] = mine.astype(bf16)


def pack_second(z_ref, grad_ref, out_ref):
    r = z_ref.shape[0]
    for s in range(out_ref.shape[0]):
        for j in range(PAIRS):
            at = lanes(s * PAIRS + j)
            out_ref[s, 0, (Z + j) * r : (Z + j + 1) * r, :] = z_ref[:, at]
            out_ref[s, 0, (GRAD + j) * r : (GRAD + j + 1) * r, :] = grad_ref[:, at]


def add_halves(owners, in_ref, block, out_ref):
    r = out_ref.shape[0]
    peer_of = {own: peer for peer, own in enumerate(owners)}
    for g in range(GROUPS):
        halves = [
            in_ref[peer_of[2 * g + k], block * r : (block + 1) * r, :].astype(f32) for k in range(2)
        ]
        out_ref[:, lanes(g)] = (halves[0] + halves[1]).astype(bf16)


def unpack(owners, in_ref, x_ref, z_ref, b_ref, c_ref, steps_ref):
    r = x_ref.shape[0]
    peer_of = {own: peer for peer, own in enumerate(owners)}
    for peer, own in enumerate(owners):
        for j in range(PAIRS):
            for block, ref in ((LAST_X, x_ref), (LAST_Z, z_ref)):
                at = slice((block + j) * r, (block + j + 1) * r)
                ref[:, lanes(own * PAIRS + j)] = in_ref[peer, at, :]
    add_halves(owners, in_ref, LAST_B, b_ref)
    add_halves(owners, in_ref, LAST_C, c_ref)
    by_head = jnp.concatenate(
        [
            in_ref[peer_of[own], LAST * r : LAST * r + STEP_ROWS, :].astype(f32)[:HEADS]
            for own in range(OWNERS)
        ],
        axis=0,
    )
    steps_ref[...] = by_head.T[:r, :].astype(bf16)


def three_terms(values):
    high = values.astype(bf16).astype(f32)
    rest = values - high
    middle = rest.astype(bf16).astype(f32)
    return [high, middle, rest - middle]


def unpack_params(sub_count, tensor_count, late_ref, early_ref, mine_ref, out_ref):
    lane = lax.broadcasted_iota(jnp.int32, (1, LANES), 1)
    late = [jnp.zeros((1, LANES), f32) for _ in range(2)]
    skip = jnp.zeros((1, LANES), f32)

    def placed(rows, at):
        total = rows[at : at + 1] + rows[at + 1 : at + 2] + rows[at + 2 : at + 3]
        return jnp.where(lane < HEADS, total, 0.0)

    for s in range(sub_count):
        late_rows = jnp.zeros((STEP_ROWS, LANES), f32)
        early_rows = jnp.zeros((STEP_ROWS, LANES), f32)
        for t in range(tensor_count):
            mine = mine_ref[t : t + 1, :] > 0.0
            peer = s * tensor_count + t
            late_rows = jnp.where(mine, late_ref[peer].astype(f32), late_rows)
            early_rows = jnp.where(mine, early_ref[peer].astype(f32), early_rows)
        for k in range(2):
            part = placed(late_rows, HEADS + k * TERMS)
            late[k] = late[k] + (part if s == 0 else pltpu.roll(part, s * HEADS, 1))
        part = placed(early_rows, TERMS * PAIRS)
        skip = skip + (part if s == 0 else pltpu.roll(part, s * HEADS, 1))
        gain = early_rows[:PAIRS] + early_rows[PAIRS : 2 * PAIRS] + early_rows[2 * PAIRS : 3 * PAIRS]
        out_ref[8 + s * PAIRS : 8 + (s + 1) * PAIRS, :] = gain
    out_ref[:8, :] = jnp.concatenate(late + [skip, jnp.zeros((5, LANES), f32)], axis=0)


def state_kernel(
    message, per_step,
    first_ref, steps_ref, heads_ref, sm_ref, smt_ref, own_ref, dec_ref, state_ref, whole_ref,
    carry, rows_s,
):
    c = pl.program_id(0)

    @pl.when(c == 0)
    def _():
        carry[...] = jnp.zeros_like(carry)
        whole_ref[...] = jnp.ones_like(whole_ref)
        chunks = rows_s.shape[0]
        before = lax.broadcasted_iota(jnp.int32, (CHUNK, CHUNK), 0)
        after = lax.broadcasted_iota(jnp.int32, (CHUNK, CHUNK), 1)
        raws = []
        for k in range(chunks):
            raw = heads_ref[HEADS:, :]
            for p in range(message.per_chunk):
                part = steps_ref[k * message.per_chunk + p].astype(f32)[:HEADS]
                raw = raw + (part if p == 0 else pltpu.roll(part, p * message.rows, 1))
            raws.append(raw)
        raw = jnp.concatenate(raws, axis=0)
        small = jnp.exp(-jnp.abs(raw))
        series = small * (
            1.0 - small * (0.5 - small * (1.0 / 3 - small * (0.25 - small * 0.2)))
        )
        soft = jnp.maximum(raw, 0.0) + jnp.where(small < 0.015625, series, jnp.log(1.0 + small))
        sig = jnp.where(raw >= 0.0, 1.0, small) / (1.0 + small)
        decay_rate = jnp.concatenate([jnp.exp(heads_ref[:HEADS, :])] * chunks, axis=0)
        rate = -decay_rate * soft
        cum = mm_exact(rate, jnp.where(before <= after, 1.0, 0.0))
        rest = mm_exact(rate, jnp.where(before > after, 1.0, 0.0))
        kinds = [
            soft, cum, soft * jnp.exp(rest), cum - jnp.log(soft), jnp.exp(cum), rate, sig,
            jnp.zeros_like(soft),
        ]
        for k in range(chunks):
            at = slice(k * HEADS, (k + 1) * HEADS)
            rows_s[k] = jnp.concatenate([kind[at] for kind in kinds], axis=0)

    for i in range(per_step):
        rows = rows_s[c * per_step + i]
        smt_ref[:, lanes(i)] = rows
        sm = jnp.concatenate([rows, jnp.zeros_like(rows)], axis=0).T
        sm_ref[i * CHUNK : (i + 1) * CHUNK, :] = sm
        last = jnp.broadcast_to(sm[CHUNK - 1 : CHUNK, :], (8, LANES))
        sources_t = message.get(first_ref, i, B).T
        for j in range(PAIRS):
            dec = spread_pair(last, ECUM, j)
            dec_ref[i, :, lanes(j)] = dec
            whole_ref[:, lanes(j)] = whole_ref[:, lanes(j)] * dec
            scaled = message.get(first_ref, i, X + j).astype(f32) * spread_pair(sm, WEIGHT, j)
            own = mm_two(sources_t, *two_terms(scaled))
            own_ref[i, :, lanes(j)] = own
            carry[:, lanes(j)] = dec[0:1] * carry[:, lanes(j)] + own
    state_ref[...] = carry[...].astype(bf16)


def within_kernel(message, per_step, first_ref, sm_ref, smt_ref, out_ref):
    t = lax.broadcasted_iota(jnp.int32, (CHUNK, CHUNK), 0)
    s = lax.broadcasted_iota(jnp.int32, (CHUNK, CHUNK), 1)
    for i in range(per_step):
        rows = slice(i * CHUNK, (i + 1) * CHUNK)
        scores = mm_nt(message.get(first_ref, i, C), message.get(first_ref, i, B))
        scores = jnp.where(t >= s, scores, 0.0)
        for j in range(PAIRS):
            weights = []
            for h in (2 * j, 2 * j + 1):
                here = sm_ref[rows, CUM * HEADS + h : CUM * HEADS + h + 1]
                there = smt_ref[SHIFTED * HEADS + h : SHIFTED * HEADS + h + 1, lanes(i)]
                weights.append(
                    (scores * jnp.exp(jnp.minimum(here - there, CLAMP))).astype(bf16)
                )
            values = split_pair(message.get(first_ref, i, X + j))
            out_ref[rows, lanes(j)] = mm(jnp.concatenate(weights, axis=1), values)


def mix_kernel(
    message, per_step,
    first_ref, second_ref, within_ref, sm_ref, inbound_ref, own_ref, dec_ref, gain_ref, skip_ref,
    y_ref, start_ref, sums_ref,
    carry,
):
    @pl.when(pl.program_id(0) == 0)
    def _():
        carry[...] = inbound_ref[...].astype(f32)

    for i in range(per_step):
        rows = slice(i * CHUNK, (i + 1) * CHUNK)
        sm = sm_ref[rows, :]
        readers = message.get(first_ref, i, C)
        power = jnp.zeros((CHUNK, LANES), f32)
        cross = jnp.zeros((CHUNK, LANES), f32)
        for j in range(PAIRS):
            state = carry[:, lanes(j)]
            start_ref[i, :, lanes(j)] = state
            carried = mm_two(readers, *two_terms(state))
            carry[:, lanes(j)] = dec_ref[i, 0:1, lanes(j)] * state + own_ref[i, :, lanes(j)]
            y = within_ref[rows, lanes(j)] + spread_pair(sm, ECUM, j) * carried
            y_ref[rows, lanes(j)] = y
            values = message.get(first_ref, i, X + j).astype(f32)
            gates = message.get(second_ref, i, Z + j).astype(f32)
            grad = message.get(second_ref, i, GRAD + j).astype(f32)
            gated = (y + skip_ref[0:1, lanes(j)] * values) * (gates * sigmoid(gates))
            power = power + gated * gated
            cross = cross + grad * gain_ref[0:1, lanes(j)] * gated
        sums_ref[i, 0:1, :] = jnp.sum(power.T, axis=0, keepdims=True)
        sums_ref[i, 1:2, :] = jnp.sum(cross.T, axis=0, keepdims=True)
        sums_ref[i, 2:, :] = jnp.zeros((6, LANES), f32)


def norm_kernel(
    message, per_step,
    first_ref, second_ref, y_ref, sm_ref, start_ref, dec_ref, sums_ref, other_ref, gain_ref, skip_ref,
    gate_ref, mixed_ref, e_ref, back_ref, slab_ref, readers_ref, param_ref,
    pre, back_sum, gain_sum, skip_sum, high_s, low_s, scaled_s,
):
    c = pl.program_id(0)

    @pl.when(c == 0)
    def _():
        pre[...] = jnp.ones_like(pre)
        back_sum[...] = jnp.zeros_like(back_sum)
        gain_sum[...] = jnp.zeros_like(gain_sum)
        skip_sum[...] = jnp.zeros_like(skip_sum)

    ones = head_rows()
    for i in range(per_step):
        rows = slice(i * CHUNK, (i + 1) * CHUNK)
        sm = sm_ref[rows, :]
        readers = message.get(first_ref, i, C)
        readers_t = readers.T
        sums = (sums_ref[i] + other_ref[i]) * (1.0 / GROUP_WIDTH)
        inverse_row = lax.rsqrt(sums[0:1] + epsilon)
        pull_row = inverse_row * inverse_row * inverse_row * sums[1:2]
        inverse = jnp.broadcast_to(inverse_row, (CHUNK, LANES)).T
        pull = jnp.broadcast_to(pull_row, (CHUNK, LANES)).T
        for j in range(PAIRS):
            at = lanes(j)
            values = message.get(first_ref, i, X + j).astype(f32)
            gates = message.get(second_ref, i, Z + j).astype(f32)
            grad = message.get(second_ref, i, GRAD + j).astype(f32)
            y = y_ref[rows, at]
            mixed = y + skip_ref[0:1, at] * values
            sig = sigmoid(gates)
            silu = gates * sig
            gated = mixed * silu
            scaled = inverse * grad
            gain_sum[0:1, at] += jnp.sum(scaled * gated, axis=0, keepdims=True)
            d_gated = scaled * gain_ref[0:1, at] - pull * gated
            d_mixed = d_gated * silu
            d_gate = d_gated * mixed * (sig + silu * (1.0 - sig))
            message.put(gate_ref, i, j, d_gate.astype(bf16))
            skip_sum[0:1, at] += jnp.sum(values * d_mixed, axis=0, keepdims=True)
            rounded = d_mixed.astype(bf16)
            mixed_ref[rows, at] = rounded
            high_s[:, at], low_s[:, at] = two_terms(rounded.astype(f32) * y)
            high, low = two_terms(d_mixed * spread_pair(sm, ECUM, j))
            scaled_s[:, at] = high
            back = mm_two(readers_t, high, low)
            back_ref[i, :, at] = back
            back_sum[:, at] += pre[0:1, at] * back
            pre[:, at] = pre[:, at] * dec_ref[i, :, at]
        e_ref[:, lanes(i)] = (mm_nt(ones, high_s[...]) + mm_nt(ones, low_s[...]))[:HEADS]
        readers_ref[rows, :] = mm_nt(scaled_s[...], start_ref[i].astype(bf16))
    slab_ref[...] = back_sum[...].astype(bf16)

    @pl.when(c == pl.num_programs(0) - 1)
    def _():
        for j in range(PAIRS):
            param_ref[j : j + 1, :] = gain_sum[0:1, lanes(j)]
        high, low = two_terms(jnp.broadcast_to(skip_sum[0:1, :], (LANES, WIDTH)))
        skips = (mm_nt(high, ones) + mm_nt(low, ones))[0:1]
        param_ref[PAIRS : PAIRS + 1, :] = jnp.concatenate(
            [skips, jnp.zeros((1, LANES - 16), f32)], axis=1
        )
        param_ref[PAIRS + 1 :, :] = jnp.zeros((8 - PAIRS - 1, LANES), f32)


def local_kernel(
    message, per_step,
    first_ref, grad_ref, sm_ref, smt_ref, readers_ref, values_out, sources_out, readers_out,
):
    s = lax.broadcasted_iota(jnp.int32, (CHUNK, CHUNK), 0)
    t = lax.broadcasted_iota(jnp.int32, (CHUNK, CHUNK), 1)
    causal = t >= s
    for i in range(per_step):
        rows = slice(i * CHUNK, (i + 1) * CHUNK)
        sources = message.get(first_ref, i, B)
        readers = message.get(first_ref, i, C)
        scores = jnp.where(causal, mm_nt(sources, readers), 0.0)
        total = jnp.zeros((CHUNK, CHUNK), f32)
        for j in range(PAIRS):
            grads = split_pair(grad_ref[rows, lanes(j)])
            weight_grads = mm_nt(message.get(first_ref, i, X + j), grads)
            weights = []
            for k, h in enumerate((2 * j, 2 * j + 1)):
                there = sm_ref[rows, SHIFTED * HEADS + h : SHIFTED * HEADS + h + 1]
                here = smt_ref[CUM * HEADS + h : CUM * HEADS + h + 1, lanes(i)]
                decay = jnp.exp(jnp.minimum(here - there, CLAMP))
                weights.append((scores * decay).astype(bf16))
                total = total + weight_grads[:, lanes(k)] * decay
            values_out[rows, lanes(j)] = mm(jnp.concatenate(weights, axis=1), grads)
        total = jnp.where(causal, total, 0.0).astype(bf16)
        sources_out[rows, :] = mm(total, readers)
        d_readers = mm_tn(total, sources) + readers_ref[rows, :]
        message.put(readers_out, i, 0, d_readers.astype(bf16))


def last_kernel(
    message, per_step,
    first_ref, within_ref, sources_ref, readers_ref, gate_ref, grad_ref, e_ref, sm_ref, smt_ref, outer_ref,
    back_ref, start_ref, dec_ref, skip_ref, heads_ref, early_ref,
    out_ref,
    carry, sums, high_s, low_s, scaled_s, state_s, flux_s, message_s, sent,
):
    c = pl.program_id(0)

    @pl.when(c == 0)
    def _():
        carry[...] = outer_ref[...].astype(f32)
        sums[...] = jnp.zeros_like(sums)

    r = message.rows
    ones = head_rows()
    before = lax.broadcasted_iota(jnp.int32, (CHUNK, CHUNK), 0)
    after = lax.broadcasted_iota(jnp.int32, (CHUNK, CHUNK), 1)
    earlier = jnp.where(before < after, 1.0, 0.0)
    decay_rate = jnp.exp(heads_ref[:HEADS, :])
    first_peer = (pl.num_programs(0) - 1 - c) * per_step * message.per_chunk
    span = per_step * message.per_chunk
    mine = message_s.at[pl.ds(first_peer, span)]

    def body_copy(step):
        peer = (pl.num_programs(0) - 1 - step) * span
        at = (pl.ds(peer, span), pl.ds(0, LAST * r))
        return pltpu.make_async_copy(message_s.at[at], out_ref.at[at], sent.at[step])

    for i in reversed(range(per_step)):
        rows = slice(i * CHUNK, (i + 1) * CHUNK)
        sm = sm_ref[rows, :]
        sources = message.get(first_ref, i, B)
        for j in range(PAIRS):
            at = lanes(j)
            state = carry[:, at]
            high, low = two_terms(state)
            state_s[:, at] = high
            values = message.get(first_ref, i, X + j).astype(f32)
            weight = spread_pair(sm, WEIGHT, j)
            grad = within_ref[rows, at] + weight * mm_two(sources, high, low)
            skipped = skip_ref[0:1, at] * grad_ref[rows, at].astype(f32)
            message.put(mine, i, LAST_X + j, (grad + skipped).astype(bf16))
            high_s[:, at], low_s[:, at] = two_terms(values * grad)
            scaled_s[:, at] = (values * weight).astype(bf16)
            new = dec_ref[i, 0:1, at] * state + back_ref[i, :, at]
            carry[:, at] = new
            flux_s[:, at] = jnp.broadcast_to(
                jnp.sum(start_ref[i, :, at] * new, axis=0, keepdims=True), (16, LANES)
            )
        d_sources = sources_ref[rows, :] + mm_nt(scaled_s[...], state_s[...])
        message.put(mine, i, LAST_B, d_sources.astype(bf16))
        message.put(mine, i, LAST_C, message.get(readers_ref, i, 0))
        for j in range(PAIRS):
            message.put(mine, i, LAST_Z + j, message.get(gate_ref, i, j))
        g = (mm_nt(ones, high_s[...]) + mm_nt(ones, low_s[...]))[:HEADS]
        high, low = two_terms(flux_s[...])
        constant = (mm_nt(ones, high) + mm_nt(ones, low))[:HEADS, 0:1]
        flux = constant + mm_exact(g - e_ref[:, lanes(i)], earlier)
        soft = smt_ref[DT * HEADS : (DT + 1) * HEADS, lanes(i)]
        rate = smt_ref[RATE * HEADS : (RATE + 1) * HEADS, lanes(i)]
        sig = smt_ref[SIG * HEADS : (SIG + 1) * HEADS, lanes(i)]
        steps = (g / soft - decay_rate * flux) * sig
        sums[:HEADS, :] += flux * rate
        sums[HEADS:, :] += steps
        steps = jnp.concatenate([steps, jnp.zeros_like(steps)], axis=0)
        for p in range(message.per_chunk):
            part = steps if p == 0 else pltpu.roll(steps, LANES - p * r, 1)
            mine[i * message.per_chunk + p, LAST * r : LAST * r + STEP_ROWS, :] = part.astype(bf16)
    body_copy(c).start()

    @pl.when(c == pl.num_programs(0) - 1)
    def _():
        late = []
        for k in range(2):
            column = jnp.sum(sums[k * HEADS : (k + 1) * HEADS, :], axis=1, keepdims=True)
            block = jnp.broadcast_to(column, (HEADS, LANES))
            block = jnp.concatenate([block, jnp.zeros((LANES - HEADS, LANES), f32)], axis=0)
            late += three_terms(block.T[0:1, :])
        late += [jnp.zeros((HEADS - 2 * TERMS, LANES), f32)]
        late = jnp.concatenate([jnp.zeros((HEADS, LANES), f32)] + late, axis=0)
        late = late.astype(bf16)
        early = three_terms(early_ref[:PAIRS, :]) + three_terms(early_ref[PAIRS : PAIRS + 1, :])
        early += [jnp.zeros((STEP_ROWS - TERMS * (PAIRS + 1), LANES), f32)]
        early = jnp.concatenate(early, axis=0).astype(bf16)
        own_rows = lax.broadcasted_iota(jnp.int32, (STEP_ROWS, LANES), 0) < HEADS

        def fill(peer, unused):
            steps_at = slice(LAST * r, LAST * r + STEP_ROWS)
            message_s[peer, steps_at, :] = jnp.where(own_rows, message_s[peer, steps_at, :], late)
            message_s[peer, LAST * r + STEP_ROWS :, :] = early
            return unused

        lax.fori_loop(0, message_s.shape[0], fill, 0)
        at = (slice(None), pl.ds(LAST * r, 2 * STEP_ROWS))
        steps = sent.shape[0] - 1
        tiles = pltpu.make_async_copy(message_s.at[at], out_ref.at[at], sent.at[steps])
        tiles.start()
        for step in range(steps):
            body_copy(step).wait()
        tiles.wait()


def finish(own_ref, other_ref, logs_ref, skip_ref, bias_ref, gain_ref):
    total = own_ref[...] + other_ref[...]
    count = logs_ref.shape[1]
    logs_ref[...] = total[0:1, :count]
    bias_ref[...] = total[1:2, :count]
    skip_ref[...] = total[2:3, :count]
    gain_ref[...] = total[8:]


def call(kernel, out_shape, flops, moved, grid=None, in_specs=None, out_specs=None, scratch=()):
    extra = {}
    if grid is not None:
        extra = dict(grid=grid, in_specs=in_specs, out_specs=out_specs)
    return pl.pallas_call(
        kernel,
        out_shape=out_shape,
        scratch_shapes=list(scratch),
        compiler_params=pltpu.CompilerParams(vmem_limit_bytes=16 * 1024 * 1024),
        cost_estimate=pl.CostEstimate(flops=flops, bytes_accessed=moved, transcendentals=0),
        **extra,
    )


def shifted(array, count, by):
    pairs = [(i, i + by) for i in range(count) if 0 <= i + by < count]
    return lax.ppermute(array, "slab", pairs)


def carry_over(state, decay, first_decay, count, sign):
    window, window_decay, step = state, decay, 1
    result = result_decay = None
    while step < count:
        arrived = shifted(window, count, sign * step)
        more = 2 * step < count
        if result is None:
            result = arrived
            if more:
                result_decay = first_decay
                window = (state.astype(f32) + decay[0:1] * arrived.astype(f32)).astype(bf16)
                window_decay = decay * first_decay
        else:
            if more:
                arrived_decay = shifted(window_decay, count, sign * step)
                window = (window.astype(f32) + window_decay[0:1] * arrived.astype(f32)).astype(bf16)
                window_decay = window_decay * arrived_decay
            result = result.astype(f32) + result_decay[0:1] * arrived.astype(f32)
            if more:
                result_decay = result_decay * arrived_decay
        step *= 2
    return jnp.zeros_like(state) if result is None else result


def two_parts(array, axis, count):
    step, other = 1, jnp.zeros_like(array)
    while step < count:
        array = array if step == 1 else array + other
        other = lax.ppermute(array, axis, [(i, i ^ step) for i in range(count)])
        step *= 2
    return array, other


def on_device(
    slab_count, sub_count, tensor_count,
    mixer_x, gate_z, b_matrix, c_matrix, raw_steps, decay_log, skip_gain, step_bias, norm_gain, out_grad,
):
    rows = mixer_x.shape[0]
    peers = sub_count * tensor_count
    tokens = rows * peers
    chunks = tokens // CHUNK
    per_step = min(2, chunks)
    grid = (chunks // per_step,)
    message = Message(rows)
    owners = [t * sub_count + s for s in range(sub_count) for t in range(tensor_count)]
    sub = lax.axis_index("sub")

    def struct(shape, kind=f32):
        return jax.ShapeDtypeStruct(shape, kind)

    def hbm(shape, kind=f32):
        return pltpu.HBM(shape, kind)

    def in_hbm(array):
        return pltpu.with_memory_space_constraint(array, pltpu.HBM)

    def exchange(array):
        return lax.all_to_all(array, ("sub", "tensor"), split_axis=0, concat_axis=0, tiled=True)

    own_logs = lax.dynamic_slice(decay_log, (sub * HEADS,), (HEADS,))
    own_bias = lax.dynamic_slice(step_bias, (sub * HEADS,), (HEADS,))
    own_skip = lax.dynamic_slice(skip_gain, (sub * HEADS,), (HEADS,))
    own_gain = lax.dynamic_slice(norm_gain, (sub * WIDTH,), (WIDTH,)).reshape(1, WIDTH)
    heads = jnp.broadcast_to(jnp.concatenate([own_logs, own_bias])[:, None], (2 * HEADS, LANES))
    skip_row = jnp.repeat(own_skip, HEAD_DIM).reshape(1, WIDTH)

    first_rows = FIRST * rows + STEP_ROWS
    second_rows = SECOND * rows
    last_rows = LAST * rows + 2 * STEP_ROWS

    def packed(kernel, height, arrays, whole_arrays=(), scratch=()):
        out = hbm((sub_count, tensor_count, height, LANES), bf16)
        moved = 4 * peers * height * LANES
        runs = 2 if sub_count >= 4 else 1
        parts = tensor_count * runs
        specs = [
            pl.BlockSpec((rows, a.shape[1] // parts), lambda t, k: (0, t * runs + k)) for a in arrays
        ] + [pl.BlockSpec(a.shape, lambda t, k: (0, 0)) for a in whole_arrays]
        out_spec = pl.BlockSpec((sub_count // runs, 1, height, LANES), lambda t, k: (k, t, 0, 0))
        made = call(kernel, out, 0, moved, (tensor_count, runs), specs, out_spec, scratch)(
            *(in_hbm(a) for a in (*arrays, *whole_arrays))
        )
        return made.reshape(peers, height, LANES)

    first = exchange(
        packed(
            pack_first, first_rows, (mixer_x, b_matrix, c_matrix), (raw_steps,),
            [pltpu.VMEM((LANES, LANES), f32)],
        )
    )
    tensor_rows = lax.broadcasted_iota(jnp.int32, (tensor_count, LANES), 0)
    mine = (tensor_rows == lax.axis_index("tensor")).astype(f32)
    gate_z, heads, skip_row, own_gain, mine = lax.optimization_barrier(
        (gate_z, heads, skip_row, own_gain, mine)
    )
    second = exchange(packed(pack_second, second_rows, (gate_z, out_grad)))

    def flow(kernel, shape_specs, flops, moved, in_specs, scratch=()):
        def body(*refs):
            return kernel(message, per_step, *refs)

        shapes = tuple(shape for shape, _ in shape_specs)
        specs = tuple(spec for _, spec in shape_specs)
        return call(body, shapes, flops, moved, grid, in_specs, specs, scratch)

    def spec(block, axis, down=False):
        def index(c):
            at = grid[0] - 1 - c if down else c
            return tuple(at if k == axis else 0 for k in range(len(block)))

        return pl.BlockSpec(block, index)

    span = per_step * CHUNK

    def specs_of(down):
        return dict(
            message=lambda height: spec((per_step * message.per_chunk, height, LANES), 0, down),
            token=lambda width: spec((span, width), 0, down),
            lane=lambda height: spec((height, span), 1, down),
            chunk=lambda *shape: spec((per_step,) + shape, 0, down),
        )

    up, dn = specs_of(False), specs_of(True)

    def whole(*shape):
        return pl.BlockSpec(shape, lambda c: (0,) * len(shape))

    unit = 2 * tokens * CHUNK * WIDTH
    size = tokens * WIDTH

    sm, smt, own, dec, state, decay = flow(
        state_kernel,
        [
            (hbm((tokens, LANES)), up["token"](LANES)),
            (hbm((KINDS * HEADS, tokens)), up["lane"](KINDS * HEADS)),
            (hbm((chunks, STATE, WIDTH)), up["chunk"](STATE, WIDTH)),
            (hbm((chunks, 8, WIDTH)), up["chunk"](8, WIDTH)),
            (struct((STATE, WIDTH), bf16), whole(STATE, WIDTH)),
            (struct((8, WIDTH)), whole(8, WIDTH)),
        ],
        2 * unit, size * 8,
        [
            up["message"](SOURCES * rows),
            pl.BlockSpec((peers, STEP_ROWS, LANES), lambda c: (0, FIRST * rows // STEP_ROWS, 0)),
            whole(2 * HEADS, LANES),
        ],
        [pltpu.VMEM((STATE, WIDTH), f32), pltpu.VMEM((chunks, KINDS * HEADS, LANES), f32)],
    )(first, first, heads)

    before = after = None
    if slab_count > 2:
        before, after = shifted(decay, slab_count, 1), shifted(decay, slab_count, -1)
    inbound = carry_over(state, decay, before, slab_count, 1)

    (within,) = flow(
        within_kernel,
        [(hbm((tokens, WIDTH)), up["token"](WIDTH))],
        4 * unit, size * 8,
        [up["message"](FIRST * rows), up["token"](LANES), up["lane"](KINDS * HEADS)],
    )(first, sm, smt)

    y, starts, sums = flow(
        mix_kernel,
        [
            (struct((tokens, WIDTH)), up["token"](WIDTH)),
            (struct((chunks, STATE, WIDTH)), up["chunk"](STATE, WIDTH)),
            (struct((chunks, 8, LANES)), up["chunk"](8, LANES)),
        ],
        2 * unit, size * 20,
        [
            up["message"](FIRST * rows), up["message"](second_rows), up["token"](WIDTH),
            up["token"](LANES), whole(STATE, WIDTH), up["chunk"](STATE, WIDTH), up["chunk"](8, WIDTH),
            whole(1, WIDTH), whole(1, WIDTH),
        ],
        [pltpu.VMEM((STATE, WIDTH), f32)],
    )(
        first, in_hbm(second), in_hbm(within), in_hbm(sm), inbound, in_hbm(own), in_hbm(dec),
        own_gain, skip_row,
    )

    partner = lax.ppermute(sums, "sub", [(i, i ^ 1) for i in range(sub_count)])

    d_gates, d_mixed, e, back, slab_back, readers_part, params = flow(
        norm_kernel,
        [
            (struct((peers, PAIRS * rows, LANES), bf16), up["message"](PAIRS * rows)),
            (struct((tokens, WIDTH), bf16), up["token"](WIDTH)),
            (struct((HEADS, tokens)), up["lane"](HEADS)),
            (struct((chunks, STATE, WIDTH)), up["chunk"](STATE, WIDTH)),
            (struct((STATE, WIDTH), bf16), whole(STATE, WIDTH)),
            (struct((tokens, STATE)), up["token"](STATE)),
            (struct((8, LANES)), whole(8, LANES)),
        ],
        4 * unit, size * 20,
        [
            up["message"](FIRST * rows), up["message"](second_rows), up["token"](WIDTH),
            up["token"](LANES), up["chunk"](STATE, WIDTH), up["chunk"](8, WIDTH),
            up["chunk"](8, LANES), up["chunk"](8, LANES), whole(1, WIDTH), whole(1, WIDTH),
        ],
        [
            pltpu.VMEM((8, WIDTH), f32), pltpu.VMEM((STATE, WIDTH), f32),
            pltpu.VMEM((8, WIDTH), f32), pltpu.VMEM((8, WIDTH), f32),
            pltpu.VMEM((CHUNK, WIDTH), bf16), pltpu.VMEM((CHUNK, WIDTH), bf16),
            pltpu.VMEM((CHUNK, WIDTH), bf16),
        ],
    )(
        first, in_hbm(second), y, sm, starts, dec, sums, partner, own_gain, skip_row,
    )

    outer = carry_over(slab_back, decay, after, slab_count, -1)
    d_values, d_sources, d_readers = flow(
        local_kernel,
        [
            (struct((tokens, WIDTH)), up["token"](WIDTH)),
            (struct((tokens, STATE)), up["token"](STATE)),
            (struct((peers, rows, LANES), bf16), up["message"](rows)),
        ],
        8 * unit, size * 8,
        [
            up["message"](FIRST * rows), up["token"](WIDTH), up["token"](LANES),
            up["lane"](KINDS * HEADS), up["token"](STATE),
        ],
    )(first, d_mixed, sm, smt, readers_part)

    (last,) = flow(
        last_kernel,
        [(hbm((peers, last_rows, LANES), bf16), pl.BlockSpec(memory_space=pl.ANY))],
        4 * unit, size * 16,
        [
            dn["message"](SOURCES * rows), dn["token"](WIDTH), dn["token"](STATE),
            dn["message"](rows), dn["message"](PAIRS * rows),
            dn["token"](WIDTH), dn["lane"](HEADS), dn["token"](LANES), dn["lane"](KINDS * HEADS),
            whole(STATE, WIDTH), dn["chunk"](STATE, WIDTH), dn["chunk"](STATE, WIDTH),
            dn["chunk"](8, WIDTH), whole(1, WIDTH), whole(2 * HEADS, LANES), whole(8, LANES),
        ],
        [
            pltpu.VMEM((STATE, WIDTH), f32), pltpu.VMEM((2 * HEADS, LANES), f32),
            pltpu.VMEM((CHUNK, WIDTH), bf16), pltpu.VMEM((CHUNK, WIDTH), bf16),
            pltpu.VMEM((CHUNK, WIDTH), bf16), pltpu.VMEM((STATE, WIDTH), bf16),
            pltpu.VMEM((16, WIDTH), f32), pltpu.VMEM((peers, last_rows, LANES), bf16),
            pltpu.SemaphoreType.DMA((grid[0] + 1,)),
        ],
    )(
        first, d_values, d_sources, d_readers, d_gates, d_mixed, e, sm, smt, outer, back, starts,
        dec, skip_row, heads, params,
    )

    last_back = exchange(last)
    tile_at = LAST * rows // STEP_ROWS
    def tile(at):
        return pl.BlockSpec((peers, STEP_ROWS, LANES), lambda c: (0, at, 0))

    params = call(
        lambda *refs: unpack_params(sub_count, tensor_count, *refs),
        struct((8 + sub_count * PAIRS, LANES)),
        0, 4 * peers * STEP_ROWS * LANES, (1,),
        [tile(tile_at), tile(tile_at + 1), whole(tensor_count, LANES)],
        whole(8 + sub_count * PAIRS, LANES),
    )(last_back, last_back, mine)
    own_params, other_params = two_parts(params, "slab", slab_count)
    wide, narrow = struct((rows, CHANNELS), bf16), struct((rows, GROUPS * STATE), bf16)
    grad_x, grad_gates, grad_b, grad_c, grad_steps = call(
        lambda *refs: unpack(owners, *refs),
        (wide, wide, narrow, narrow, struct((rows, MIXER_HEADS), bf16)),
        0, 10 * rows * CHANNELS,
    )(last_back)
    row = struct((1, sub_count * HEADS))
    grad_logs, grad_skip, grad_bias, grad_gain = call(
        finish, (row, row, row, struct((sub_count * PAIRS, LANES))), 0, 1 << 16,
    )(own_params, other_params)
    return (
        grad_x,
        grad_gates,
        grad_b,
        grad_c,
        grad_steps,
        grad_logs.reshape(-1),
        grad_skip.reshape(-1),
        grad_bias.reshape(-1),
        grad_gain.reshape(-1),
    )


def solution(mesh):
    tensor_count = mesh.shape["tensor"]
    sub_count = OWNERS // tensor_count
    slab_count = mesh.shape["dp"] // sub_count
    devices = mesh.devices.reshape(slab_count, sub_count, tensor_count)
    split_mesh = Mesh(devices, ("slab", "sub", "tensor"))
    rows = P(("slab", "sub", "tensor"), None)
    param = P("tensor")

    def local(*arrays):
        return on_device(slab_count, sub_count, tensor_count, *arrays)

    return jax.shard_map(
        local,
        mesh=split_mesh,
        in_specs=(rows,) * 5 + (param,) * 4 + (rows,),
        out_specs=(rows,) * 5 + (param,) * 4,
        check_vma=False,
    )
```

```python
import jax
import jax.numpy as jnp
from jax import lax
from jax.experimental import pallas as pl
from jax.experimental.pallas import tpu as pltpu
from jax.sharding import Mesh
from jax.sharding import PartitionSpec as P

MIXER_HEADS = 128
HEAD_DIM = 64
STATE = 128
GROUPS = 8
CHANNELS = MIXER_HEADS * HEAD_DIM
HEADS = 8
WIDTH = HEADS * HEAD_DIM
GROUP_WIDTH = 2 * WIDTH
OWNERS = MIXER_HEADS // HEADS
LANES = 128
PAIRS = WIDTH // LANES
CHUNK = 128
STEP_ROWS = 16
epsilon = 1e-05
f32 = jnp.float32
bf16 = jnp.bfloat16

DT, CUM, WEIGHT, SHIFTED, ECUM, RATE, SIG = range(7)
KINDS = 8
CLAMP = 80.0


def mm(a, b):
    return jnp.dot(a, b, preferred_element_type=f32)


def mm_nt(a, b):
    return lax.dot_general(a, b, (((1,), (1,)), ((), ())), preferred_element_type=f32)


def mm_tn(a, b):
    return lax.dot_general(a, b, (((0,), (0,)), ((), ())), preferred_element_type=f32)


def mm_exact(a, b):
    return jnp.dot(a, b, precision=lax.Precision.HIGHEST, preferred_element_type=f32)


def two_terms(values):
    high = values.astype(bf16)
    return high, (values - high.astype(f32)).astype(bf16)


def mm_two(a, high, low):
    both = mm(a, jnp.concatenate([high, low], axis=1))
    width = high.shape[1]
    return both[:, :width] + both[:, width:]


def sigmoid(values):
    return 0.5 + 0.5 * jnp.tanh(0.5 * values)


def low_half(rows):
    return lax.broadcasted_iota(jnp.int32, (rows, LANES), 1) < HEAD_DIM


def spread_pair(values, kind, j):
    rows = values.shape[0]
    at = kind * HEADS + 2 * j
    return jnp.where(
        low_half(rows),
        jnp.broadcast_to(values[:, at : at + 1], (rows, LANES)),
        jnp.broadcast_to(values[:, at + 1 : at + 2], (rows, LANES)),
    )


def head_rows():
    row = lax.broadcasted_iota(jnp.int32, (16, WIDTH), 0)
    channel = lax.broadcasted_iota(jnp.int32, (16, WIDTH), 1) // HEAD_DIM
    return jnp.where(row == channel, 1.0, 0.0).astype(bf16)


def split_pair(block):
    low = low_half(block.shape[0])
    zero = jnp.zeros_like(block)
    return jnp.concatenate(
        [jnp.where(low, block, zero), jnp.where(low, zero, block)], axis=0
    )


def lanes(j):
    return slice(j * LANES, (j + 1) * LANES)


class Message:
    def __init__(self, rows):
        self.rows = rows
        self.per_chunk = CHUNK // rows

    def place(self, chunk, k):
        r = self.rows
        return (slice(chunk * self.per_chunk, (chunk + 1) * self.per_chunk), slice(k * r, (k + 1) * r))

    def get(self, ref, chunk, k):
        a, b = self.place(chunk, k)
        return ref[a, b, :].reshape(CHUNK, LANES)

    def put(self, ref, chunk, k, value):
        a, b = self.place(chunk, k)
        ref[a, b, :] = value.reshape(self.per_chunk, self.rows, LANES)


X, B, C = 0, PAIRS, PAIRS + 1
SOURCES = PAIRS + 1
FIRST = PAIRS + 2
Z, GRAD = 0, PAIRS
SECOND = 2 * PAIRS
LAST_X, LAST_Z, LAST_B, LAST_C = 0, PAIRS, 2 * PAIRS, 2 * PAIRS + 1
LAST = 2 * PAIRS + 2
TERMS = 3


def pack_first(x_ref, b_ref, c_ref, steps_ref, out_ref, by_head):
    r = x_ref.shape[0]
    step = pl.program_id(0) * pl.num_programs(1) + pl.program_id(1)
    subs = out_ref.shape[0]

    @pl.when(step == 0)
    def _():
        steps = steps_ref[...].astype(f32)
        by_head[...] = jnp.concatenate([steps, jnp.zeros((LANES - r, LANES), f32)], axis=0).T

    zero = jnp.zeros((STEP_ROWS - HEADS, LANES), f32)
    for s in range(subs):
        for j in range(PAIRS):
            out_ref[s, 0, j * r : (j + 1) * r, :] = x_ref[:, lanes(s * PAIRS + j)]
        out_ref[s, 0, B * r : (B + 1) * r, :] = b_ref[:, lanes(s // 2)]
        out_ref[s, 0, C * r : (C + 1) * r, :] = c_ref[:, lanes(s // 2)]
        at = pl.multiple_of((step * subs + s) * HEADS, HEADS)
        mine = jnp.concatenate([by_head[pl.ds(at, HEADS), :], zero], axis=0)
        out_ref[s, 0, FIRST * r :, :] = mine.astype(bf16)


def pack_second(z_ref, grad_ref, out_ref):
    r = z_ref.shape[0]
    for s in range(out_ref.shape[0]):
        for j in range(PAIRS):
            at = lanes(s * PAIRS + j)
            out_ref[s, 0, (Z + j) * r : (Z + j + 1) * r, :] = z_ref[:, at]
            out_ref[s, 0, (GRAD + j) * r : (GRAD + j + 1) * r, :] = grad_ref[:, at]


def add_halves(owners, in_ref, block, out_ref):
    r = out_ref.shape[0]
    peer_of = {own: peer for peer, own in enumerate(owners)}
    for g in range(GROUPS):
        halves = [
            in_ref[peer_of[2 * g + k], block * r : (block + 1) * r, :].astype(f32) for k in range(2)
        ]
        out_ref[:, lanes(g)] = (halves[0] + halves[1]).astype(bf16)


def unpack(owners, in_ref, x_ref, z_ref, b_ref, c_ref, steps_ref):
    r = x_ref.shape[0]
    peer_of = {own: peer for peer, own in enumerate(owners)}
    for peer, own in enumerate(owners):
        for j in range(PAIRS):
            for block, ref in ((LAST_X, x_ref), (LAST_Z, z_ref)):
                at = slice((block + j) * r, (block + j + 1) * r)
                ref[:, lanes(own * PAIRS + j)] = in_ref[peer, at, :]
    add_halves(owners, in_ref, LAST_B, b_ref)
    add_halves(owners, in_ref, LAST_C, c_ref)
    by_head = jnp.concatenate(
        [
            in_ref[peer_of[own], LAST * r : LAST * r + STEP_ROWS, :].astype(f32)[:HEADS]
            for own in range(OWNERS)
        ],
        axis=0,
    )
    steps_ref[...] = by_head.T[:r, :].astype(bf16)


def three_terms(values):
    high = values.astype(bf16).astype(f32)
    rest = values - high
    middle = rest.astype(bf16).astype(f32)
    return [high, middle, rest - middle]


def unpack_params(sub_count, tensor_count, late_ref, early_ref, mine_ref, out_ref):
    lane = lax.broadcasted_iota(jnp.int32, (1, LANES), 1)
    late = [jnp.zeros((1, LANES), f32) for _ in range(2)]
    skip = jnp.zeros((1, LANES), f32)

    def placed(rows, at):
        total = rows[at : at + 1] + rows[at + 1 : at + 2] + rows[at + 2 : at + 3]
        return jnp.where(lane < HEADS, total, 0.0)

    for s in range(sub_count):
        late_rows = jnp.zeros((STEP_ROWS, LANES), f32)
        early_rows = jnp.zeros((STEP_ROWS, LANES), f32)
        for t in range(tensor_count):
            mine = mine_ref[t : t + 1, :] > 0.0
            peer = s * tensor_count + t
            late_rows = jnp.where(mine, late_ref[peer].astype(f32), late_rows)
            early_rows = jnp.where(mine, early_ref[peer].astype(f32), early_rows)
        for k in range(2):
            part = placed(late_rows, HEADS + k * TERMS)
            late[k] = late[k] + (part if s == 0 else pltpu.roll(part, s * HEADS, 1))
        part = placed(early_rows, TERMS * PAIRS)
        skip = skip + (part if s == 0 else pltpu.roll(part, s * HEADS, 1))
        gain = early_rows[:PAIRS] + early_rows[PAIRS : 2 * PAIRS] + early_rows[2 * PAIRS : 3 * PAIRS]
        out_ref[8 + s * PAIRS : 8 + (s + 1) * PAIRS, :] = gain
    out_ref[:8, :] = jnp.concatenate(late + [skip, jnp.zeros((5, LANES), f32)], axis=0)


def state_kernel(
    message, per_step,
    first_ref, steps_ref, heads_ref, sm_ref, smt_ref, own_ref, dec_ref, state_ref, whole_ref,
    carry, rows_s,
):
    c = pl.program_id(0)

    @pl.when(c == 0)
    def _():
        carry[...] = jnp.zeros_like(carry)
        whole_ref[...] = jnp.ones_like(whole_ref)
        chunks = rows_s.shape[0]
        before = lax.broadcasted_iota(jnp.int32, (CHUNK, CHUNK), 0)
        after = lax.broadcasted_iota(jnp.int32, (CHUNK, CHUNK), 1)
        raws = []
        for k in range(chunks):
            raw = heads_ref[HEADS:, :]
            for p in range(message.per_chunk):
                part = steps_ref[k * message.per_chunk + p].astype(f32)[:HEADS]
                raw = raw + (part if p == 0 else pltpu.roll(part, p * message.rows, 1))
            raws.append(raw)
        raw = jnp.concatenate(raws, axis=0)
        small = jnp.exp(-jnp.abs(raw))
        series = small * (
            1.0 - small * (0.5 - small * (1.0 / 3 - small * (0.25 - small * 0.2)))
        )
        soft = jnp.maximum(raw, 0.0) + jnp.where(small < 0.015625, series, jnp.log(1.0 + small))
        sig = jnp.where(raw >= 0.0, 1.0, small) / (1.0 + small)
        decay_rate = jnp.concatenate([jnp.exp(heads_ref[:HEADS, :])] * chunks, axis=0)
        rate = -decay_rate * soft
        cum = mm_exact(rate, jnp.where(before <= after, 1.0, 0.0))
        rest = mm_exact(rate, jnp.where(before > after, 1.0, 0.0))
        kinds = [
            soft, cum, soft * jnp.exp(rest), cum - jnp.log(soft), jnp.exp(cum), rate, sig,
            jnp.zeros_like(soft),
        ]
        for k in range(chunks):
            at = slice(k * HEADS, (k + 1) * HEADS)
            rows_s[k] = jnp.concatenate([kind[at] for kind in kinds], axis=0)

    for i in range(per_step):
        rows = rows_s[c * per_step + i]
        smt_ref[:, lanes(i)] = rows
        sm = jnp.concatenate([rows, jnp.zeros_like(rows)], axis=0).T
        sm_ref[i * CHUNK : (i + 1) * CHUNK, :] = sm
        last = jnp.broadcast_to(sm[CHUNK - 1 : CHUNK, :], (8, LANES))
        sources_t = message.get(first_ref, i, B).T
        for j in range(PAIRS):
            dec = spread_pair(last, ECUM, j)
            dec_ref[i, :, lanes(j)] = dec
            whole_ref[:, lanes(j)] = whole_ref[:, lanes(j)] * dec
            scaled = message.get(first_ref, i, X + j).astype(f32) * spread_pair(sm, WEIGHT, j)
            own = mm_two(sources_t, *two_terms(scaled))
            own_ref[i, :, lanes(j)] = own
            carry[:, lanes(j)] = dec[0:1] * carry[:, lanes(j)] + own
    state_ref[...] = carry[...].astype(bf16)


def within_kernel(
    message, per_step,
    first_ref, sm_ref, smt_ref, own_ref, dec_ref, y_ref, start_ref, pre_ref, carry, pre,
):
    @pl.when(pl.program_id(0) == 0)
    def _():
        carry[...] = jnp.zeros_like(carry)
        pre[...] = jnp.ones_like(pre)

    t = lax.broadcasted_iota(jnp.int32, (CHUNK, CHUNK), 0)
    s = lax.broadcasted_iota(jnp.int32, (CHUNK, CHUNK), 1)
    for i in range(per_step):
        rows = slice(i * CHUNK, (i + 1) * CHUNK)
        sm = sm_ref[rows, :]
        readers = message.get(first_ref, i, C)
        scores = jnp.where(t >= s, mm_nt(readers, message.get(first_ref, i, B)), 0.0)
        pre_ref[i] = pre[...]
        pre[...] = pre[...] * dec_ref[i]
        for j in range(PAIRS):
            at = lanes(j)
            weights = []
            for h in (2 * j, 2 * j + 1):
                here = sm_ref[rows, CUM * HEADS + h : CUM * HEADS + h + 1]
                there = smt_ref[SHIFTED * HEADS + h : SHIFTED * HEADS + h + 1, lanes(i)]
                weights.append(
                    (scores * jnp.exp(jnp.minimum(here - there, CLAMP))).astype(bf16)
                )
            values = split_pair(message.get(first_ref, i, X + j))
            within = mm(jnp.concatenate(weights, axis=1), values)
            state = carry[:, at]
            start_ref[i, :, at] = state
            carried = mm_two(readers, *two_terms(state))
            y_ref[rows, at] = within + spread_pair(sm, ECUM, j) * carried
            carry[:, at] = dec_ref[i, 0:1, at] * state + own_ref[i, :, at]


def mix_kernel(
    message, per_step,
    first_ref, second_ref, within_ref, sm_ref, inbound_ref, pre_ref, gain_ref, skip_ref,
    y_ref, sums_ref,
):
    for i in range(per_step):
        rows = slice(i * CHUNK, (i + 1) * CHUNK)
        sm = sm_ref[rows, :]
        carried = mm(message.get(first_ref, i, C), inbound_ref[...].astype(bf16))
        power = jnp.zeros((CHUNK, LANES), f32)
        cross = jnp.zeros((CHUNK, LANES), f32)
        for j in range(PAIRS):
            at = lanes(j)
            decay = spread_pair(sm, ECUM, j) * pre_ref[i, 0:1, at]
            y = within_ref[rows, at] + decay * carried[:, at]
            y_ref[rows, at] = y
            values = message.get(first_ref, i, X + j).astype(f32)
            gates = message.get(second_ref, i, Z + j).astype(f32)
            grad = message.get(second_ref, i, GRAD + j).astype(f32)
            gated = (y + skip_ref[0:1, at] * values) * (gates * sigmoid(gates))
            power = power + gated * gated
            cross = cross + grad * gain_ref[0:1, at] * gated
        sums_ref[i, 0:1, :] = jnp.sum(power.T, axis=0, keepdims=True)
        sums_ref[i, 1:2, :] = jnp.sum(cross.T, axis=0, keepdims=True)
        sums_ref[i, 2:, :] = jnp.zeros((6, LANES), f32)


def norm_factors(sums):
    sums = sums * (1.0 / GROUP_WIDTH)
    inverse = lax.rsqrt(sums[0:1] + epsilon)
    pull = inverse * inverse * inverse * sums[1:2]
    return (
        jnp.broadcast_to(inverse, (CHUNK, LANES)).T,
        jnp.broadcast_to(pull, (CHUNK, LANES)).T,
    )


def norm_kernel(
    message, per_step,
    first_ref, second_ref, y_ref, sm_ref, pre_ref, sums_ref, other_ref, gain_ref, skip_ref,
    mixed_ref, back_ref, slab_ref,
    back_sum,
):
    @pl.when(pl.program_id(0) == 0)
    def _():
        back_sum[...] = jnp.zeros_like(back_sum)

    for i in range(per_step):
        rows = slice(i * CHUNK, (i + 1) * CHUNK)
        sm = sm_ref[rows, :]
        readers_t = message.get(first_ref, i, C).T
        inverse, pull = norm_factors(sums_ref[i] + other_ref[i])
        for j in range(PAIRS):
            at = lanes(j)
            values = message.get(first_ref, i, X + j).astype(f32)
            gates = message.get(second_ref, i, Z + j).astype(f32)
            grad = message.get(second_ref, i, GRAD + j).astype(f32)
            silu = gates * sigmoid(gates)
            gated = (y_ref[rows, at] + skip_ref[0:1, at] * values) * silu
            d_mixed = (inverse * grad * gain_ref[0:1, at] - pull * gated) * silu
            mixed_ref[rows, at] = d_mixed.astype(bf16)
            back = mm_two(readers_t, *two_terms(d_mixed * spread_pair(sm, ECUM, j)))
            back_ref[i, :, at] = back
            back_sum[:, at] += pre_ref[i, 0:1, at] * back
    slab_ref[...] = back_sum[...].astype(bf16)


def local_kernel(
    message, per_step,
    first_ref, second_ref, y_ref, grad_ref, sm_ref, smt_ref, start_ref, pre_ref, inbound_ref,
    sums_ref, other_ref, gain_ref, skip_ref,
    values_out, sources_out, readers_out, gate_ref, e_ref, param_ref,
    gain_sum, skip_sum, high_s, low_s, scaled_s,
):
    c = pl.program_id(0)

    @pl.when(c == 0)
    def _():
        gain_sum[...] = jnp.zeros_like(gain_sum)
        skip_sum[...] = jnp.zeros_like(skip_sum)

    s = lax.broadcasted_iota(jnp.int32, (CHUNK, CHUNK), 0)
    t = lax.broadcasted_iota(jnp.int32, (CHUNK, CHUNK), 1)
    causal = t >= s
    ones = head_rows()
    inbound = inbound_ref[...].astype(f32)
    for i in range(per_step):
        rows = slice(i * CHUNK, (i + 1) * CHUNK)
        sm = sm_ref[rows, :]
        sources = message.get(first_ref, i, B)
        readers = message.get(first_ref, i, C)
        inverse, pull = norm_factors(sums_ref[i] + other_ref[i])
        scores = jnp.where(causal, mm_nt(sources, readers), 0.0)
        total = jnp.zeros((CHUNK, CHUNK), f32)
        for j in range(PAIRS):
            at = lanes(j)
            rounded = grad_ref[rows, at]
            grads = split_pair(rounded)
            x = message.get(first_ref, i, X + j)
            weight_grads = mm_nt(x, grads)
            weights = []
            for k, h in enumerate((2 * j, 2 * j + 1)):
                there = sm_ref[rows, SHIFTED * HEADS + h : SHIFTED * HEADS + h + 1]
                here = smt_ref[CUM * HEADS + h : CUM * HEADS + h + 1, lanes(i)]
                decay = jnp.exp(jnp.minimum(here - there, CLAMP))
                weights.append((scores * decay).astype(bf16))
                total = total + weight_grads[:, lanes(k)] * decay
            values_out[rows, at] = mm(jnp.concatenate(weights, axis=1), grads)

            values = x.astype(f32)
            gates = message.get(second_ref, i, Z + j).astype(f32)
            grad = message.get(second_ref, i, GRAD + j).astype(f32)
            y = y_ref[rows, at]
            mixed = y + skip_ref[0:1, at] * values
            sig = sigmoid(gates)
            silu = gates * sig
            gated = mixed * silu
            scaled = inverse * grad
            gain_sum[0:1, at] += jnp.sum(scaled * gated, axis=0, keepdims=True)
            d_gated = scaled * gain_ref[0:1, at] - pull * gated
            d_gate = d_gated * mixed * (sig + silu * (1.0 - sig))
            message.put(gate_ref, i, j, d_gate.astype(bf16))
            skip_sum[0:1, at] += jnp.sum(values * (d_gated * silu), axis=0, keepdims=True)
            d_mixed = rounded.astype(f32)
            high_s[:, at], low_s[:, at] = two_terms(d_mixed * y)
            scaled_s[:, at] = (d_mixed * spread_pair(sm, ECUM, j)).astype(bf16)
        e_ref[:, lanes(i)] = (mm_nt(ones, high_s[...]) + mm_nt(ones, low_s[...]))[:HEADS]
        total = jnp.where(causal, total, 0.0).astype(bf16)
        sources_out[rows, :] = mm(total, readers)
        start = (start_ref[i] + pre_ref[i, 0:1, :] * inbound).astype(bf16)
        d_readers = mm_tn(total, sources) + mm_nt(scaled_s[...], start)
        message.put(readers_out, i, 0, d_readers.astype(bf16))

    @pl.when(c == pl.num_programs(0) - 1)
    def _():
        for j in range(PAIRS):
            param_ref[j : j + 1, :] = gain_sum[0:1, lanes(j)]
        high, low = two_terms(jnp.broadcast_to(skip_sum[0:1, :], (LANES, WIDTH)))
        skips = (mm_nt(high, ones) + mm_nt(low, ones))[0:1]
        param_ref[PAIRS : PAIRS + 1, :] = jnp.concatenate(
            [skips, jnp.zeros((1, LANES - 16), f32)], axis=1
        )
        param_ref[PAIRS + 1 :, :] = jnp.zeros((8 - PAIRS - 1, LANES), f32)


def last_kernel(
    message, per_step,
    first_ref, within_ref, sources_ref, readers_ref, gate_ref, grad_ref, e_ref, sm_ref, smt_ref, outer_ref,
    back_ref, start_ref, pre_ref, inbound_ref, dec_ref, skip_ref, heads_ref, early_ref,
    out_ref,
    carry, sums, high_s, low_s, scaled_s, state_s, flux_s, message_s, sent,
):
    c = pl.program_id(0)

    @pl.when(c == 0)
    def _():
        carry[...] = outer_ref[...].astype(f32)
        sums[...] = jnp.zeros_like(sums)

    r = message.rows
    ones = head_rows()
    before = lax.broadcasted_iota(jnp.int32, (CHUNK, CHUNK), 0)
    after = lax.broadcasted_iota(jnp.int32, (CHUNK, CHUNK), 1)
    earlier = jnp.where(before < after, 1.0, 0.0)
    decay_rate = jnp.exp(heads_ref[:HEADS, :])
    first_peer = (pl.num_programs(0) - 1 - c) * per_step * message.per_chunk
    span = per_step * message.per_chunk
    mine = message_s.at[pl.ds(first_peer, span)]

    def body_copy(step):
        peer = (pl.num_programs(0) - 1 - step) * span
        at = (pl.ds(peer, span), pl.ds(0, LAST * r))
        return pltpu.make_async_copy(message_s.at[at], out_ref.at[at], sent.at[step])

    for i in reversed(range(per_step)):
        rows = slice(i * CHUNK, (i + 1) * CHUNK)
        sm = sm_ref[rows, :]
        sources = message.get(first_ref, i, B)
        for j in range(PAIRS):
            at = lanes(j)
            state = carry[:, at]
            high, low = two_terms(state)
            state_s[:, at] = high
            values = message.get(first_ref, i, X + j).astype(f32)
            weight = spread_pair(sm, WEIGHT, j)
            grad = within_ref[rows, at] + weight * mm_two(sources, high, low)
            skipped = skip_ref[0:1, at] * grad_ref[rows, at].astype(f32)
            message.put(mine, i, LAST_X + j, (grad + skipped).astype(bf16))
            high_s[:, at], low_s[:, at] = two_terms(values * grad)
            scaled_s[:, at] = (values * weight).astype(bf16)
            new = dec_ref[i, 0:1, at] * state + back_ref[i, :, at]
            carry[:, at] = new
            start = start_ref[i, :, at] + pre_ref[i, 0:1, at] * inbound_ref[:, at].astype(f32)
            flux_s[:, at] = jnp.broadcast_to(
                jnp.sum(start * new, axis=0, keepdims=True), (16, LANES)
            )
        d_sources = sources_ref[rows, :] + mm_nt(scaled_s[...], state_s[...])
        message.put(mine, i, LAST_B, d_sources.astype(bf16))
        message.put(mine, i, LAST_C, message.get(readers_ref, i, 0))
        for j in range(PAIRS):
            message.put(mine, i, LAST_Z + j, message.get(gate_ref, i, j))
        g = (mm_nt(ones, high_s[...]) + mm_nt(ones, low_s[...]))[:HEADS]
        high, low = two_terms(flux_s[...])
        constant = (mm_nt(ones, high) + mm_nt(ones, low))[:HEADS, 0:1]
        flux = constant + mm_exact(g - e_ref[:, lanes(i)], earlier)
        soft = smt_ref[DT * HEADS : (DT + 1) * HEADS, lanes(i)]
        rate = smt_ref[RATE * HEADS : (RATE + 1) * HEADS, lanes(i)]
        sig = smt_ref[SIG * HEADS : (SIG + 1) * HEADS, lanes(i)]
        steps = (g / soft - decay_rate * flux) * sig
        sums[:HEADS, :] += flux * rate
        sums[HEADS:, :] += steps
        steps = jnp.concatenate([steps, jnp.zeros_like(steps)], axis=0)
        for p in range(message.per_chunk):
            part = steps if p == 0 else pltpu.roll(steps, LANES - p * r, 1)
            mine[i * message.per_chunk + p, LAST * r : LAST * r + STEP_ROWS, :] = part.astype(bf16)
    body_copy(c).start()

    @pl.when(c == pl.num_programs(0) - 1)
    def _():
        late = []
        for k in range(2):
            column = jnp.sum(sums[k * HEADS : (k + 1) * HEADS, :], axis=1, keepdims=True)
            block = jnp.broadcast_to(column, (HEADS, LANES))
            block = jnp.concatenate([block, jnp.zeros((LANES - HEADS, LANES), f32)], axis=0)
            late += three_terms(block.T[0:1, :])
        late += [jnp.zeros((HEADS - 2 * TERMS, LANES), f32)]
        late = jnp.concatenate([jnp.zeros((HEADS, LANES), f32)] + late, axis=0)
        late = late.astype(bf16)
        early = three_terms(early_ref[:PAIRS, :]) + three_terms(early_ref[PAIRS : PAIRS + 1, :])
        early += [jnp.zeros((STEP_ROWS - TERMS * (PAIRS + 1), LANES), f32)]
        early = jnp.concatenate(early, axis=0).astype(bf16)
        own_rows = lax.broadcasted_iota(jnp.int32, (STEP_ROWS, LANES), 0) < HEADS

        def fill(peer, unused):
            steps_at = slice(LAST * r, LAST * r + STEP_ROWS)
            message_s[peer, steps_at, :] = jnp.where(own_rows, message_s[peer, steps_at, :], late)
            message_s[peer, LAST * r + STEP_ROWS :, :] = early
            return unused

        lax.fori_loop(0, message_s.shape[0], fill, 0)
        at = (slice(None), pl.ds(LAST * r, 2 * STEP_ROWS))
        steps = sent.shape[0] - 1
        tiles = pltpu.make_async_copy(message_s.at[at], out_ref.at[at], sent.at[steps])
        tiles.start()
        for step in range(steps):
            body_copy(step).wait()
        tiles.wait()


def finish(own_ref, other_ref, logs_ref, skip_ref, bias_ref, gain_ref):
    total = own_ref[...] + other_ref[...]
    count = logs_ref.shape[1]
    logs_ref[...] = total[0:1, :count]
    bias_ref[...] = total[1:2, :count]
    skip_ref[...] = total[2:3, :count]
    gain_ref[...] = total[8:]


def call(kernel, out_shape, flops, moved, grid=None, in_specs=None, out_specs=None, scratch=()):
    extra = {}
    if grid is not None:
        extra = dict(grid=grid, in_specs=in_specs, out_specs=out_specs)
    return pl.pallas_call(
        kernel,
        out_shape=out_shape,
        scratch_shapes=list(scratch),
        compiler_params=pltpu.CompilerParams(vmem_limit_bytes=16 * 1024 * 1024),
        cost_estimate=pl.CostEstimate(flops=flops, bytes_accessed=moved, transcendentals=0),
        **extra,
    )


def shifted(array, count, by):
    pairs = [(i, i + by) for i in range(count) if 0 <= i + by < count]
    return lax.ppermute(array, "slab", pairs)


def carry_over(state, decay, first_decay, count, sign):
    window, window_decay, step = state, decay, 1
    result = result_decay = None
    while step < count:
        arrived = shifted(window, count, sign * step)
        more = 2 * step < count
        if result is None:
            result = arrived
            if more:
                result_decay = first_decay
                window = (state.astype(f32) + decay[0:1] * arrived.astype(f32)).astype(bf16)
                window_decay = decay * first_decay
        else:
            if more:
                arrived_decay = shifted(window_decay, count, sign * step)
                window = (window.astype(f32) + window_decay[0:1] * arrived.astype(f32)).astype(bf16)
                window_decay = window_decay * arrived_decay
            result = result.astype(f32) + result_decay[0:1] * arrived.astype(f32)
            if more:
                result_decay = result_decay * arrived_decay
        step *= 2
    return jnp.zeros_like(state) if result is None else result


def two_parts(array, axis, count):
    step, other = 1, jnp.zeros_like(array)
    while step < count:
        array = array if step == 1 else array + other
        other = lax.ppermute(array, axis, [(i, i ^ step) for i in range(count)])
        step *= 2
    return array, other


def on_device(
    slab_count, sub_count, tensor_count,
    mixer_x, gate_z, b_matrix, c_matrix, raw_steps, decay_log, skip_gain, step_bias, norm_gain, out_grad,
):
    rows = mixer_x.shape[0]
    peers = sub_count * tensor_count
    tokens = rows * peers
    chunks = tokens // CHUNK
    per_step = min(2, chunks)
    grid = (chunks // per_step,)
    message = Message(rows)
    owners = [t * sub_count + s for s in range(sub_count) for t in range(tensor_count)]
    sub = lax.axis_index("sub")

    def struct(shape, kind=f32):
        return jax.ShapeDtypeStruct(shape, kind)

    def hbm(shape, kind=f32):
        return pltpu.HBM(shape, kind)

    def in_hbm(array):
        return pltpu.with_memory_space_constraint(array, pltpu.HBM)

    def exchange(array):
        return lax.all_to_all(array, ("sub", "tensor"), split_axis=0, concat_axis=0, tiled=True)

    own_logs = lax.dynamic_slice(decay_log, (sub * HEADS,), (HEADS,))
    own_bias = lax.dynamic_slice(step_bias, (sub * HEADS,), (HEADS,))
    own_skip = lax.dynamic_slice(skip_gain, (sub * HEADS,), (HEADS,))
    own_gain = lax.dynamic_slice(norm_gain, (sub * WIDTH,), (WIDTH,)).reshape(1, WIDTH)
    heads = jnp.broadcast_to(jnp.concatenate([own_logs, own_bias])[:, None], (2 * HEADS, LANES))
    skip_row = jnp.repeat(own_skip, HEAD_DIM).reshape(1, WIDTH)

    first_rows = FIRST * rows + STEP_ROWS
    second_rows = SECOND * rows
    last_rows = LAST * rows + 2 * STEP_ROWS

    def packed(kernel, height, arrays, whole_arrays=(), scratch=()):
        out = hbm((sub_count, tensor_count, height, LANES), bf16)
        moved = 4 * peers * height * LANES
        runs = 1
        parts = tensor_count * runs
        specs = [
            pl.BlockSpec((rows, a.shape[1] // parts), lambda t, k: (0, t * runs + k)) for a in arrays
        ] + [pl.BlockSpec(a.shape, lambda t, k: (0, 0)) for a in whole_arrays]
        out_spec = pl.BlockSpec((sub_count // runs, 1, height, LANES), lambda t, k: (k, t, 0, 0))
        made = call(kernel, out, 0, moved, (tensor_count, runs), specs, out_spec, scratch)(
            *(in_hbm(a) for a in (*arrays, *whole_arrays))
        )
        return made.reshape(peers, height, LANES)

    first = exchange(
        packed(
            pack_first, first_rows, (mixer_x, b_matrix, c_matrix), (raw_steps,),
            [pltpu.VMEM((LANES, LANES), f32)],
        )
    )
    tensor_rows = lax.broadcasted_iota(jnp.int32, (tensor_count, LANES), 0)
    mine = (tensor_rows == lax.axis_index("tensor")).astype(f32)
    gate_z, heads, skip_row, own_gain, mine = lax.optimization_barrier(
        (gate_z, heads, skip_row, own_gain, mine)
    )
    second = exchange(packed(pack_second, second_rows, (gate_z, out_grad)))

    def flow(kernel, shape_specs, flops, moved, in_specs, scratch=()):
        def body(*refs):
            return kernel(message, per_step, *refs)

        shapes = tuple(shape for shape, _ in shape_specs)
        specs = tuple(spec for _, spec in shape_specs)
        return call(body, shapes, flops, moved, grid, in_specs, specs, scratch)

    def spec(block, axis, down=False):
        def index(c):
            at = grid[0] - 1 - c if down else c
            return tuple(at if k == axis else 0 for k in range(len(block)))

        return pl.BlockSpec(block, index)

    span = per_step * CHUNK

    def specs_of(down):
        return dict(
            message=lambda height: spec((per_step * message.per_chunk, height, LANES), 0, down),
            token=lambda width: spec((span, width), 0, down),
            lane=lambda height: spec((height, span), 1, down),
            chunk=lambda *shape: spec((per_step,) + shape, 0, down),
        )

    up, dn = specs_of(False), specs_of(True)

    def whole(*shape):
        return pl.BlockSpec(shape, lambda c: (0,) * len(shape))

    unit = 2 * tokens * CHUNK * WIDTH
    size = tokens * WIDTH

    sm, smt, own, dec, state, decay = flow(
        state_kernel,
        [
            (hbm((tokens, LANES)), up["token"](LANES)),
            (hbm((KINDS * HEADS, tokens)), up["lane"](KINDS * HEADS)),
            (hbm((chunks, STATE, WIDTH)), up["chunk"](STATE, WIDTH)),
            (hbm((chunks, 8, WIDTH)), up["chunk"](8, WIDTH)),
            (struct((STATE, WIDTH), bf16), whole(STATE, WIDTH)),
            (struct((8, WIDTH)), whole(8, WIDTH)),
        ],
        2 * unit, size * 8,
        [
            up["message"](SOURCES * rows),
            pl.BlockSpec((peers, STEP_ROWS, LANES), lambda c: (0, FIRST * rows // STEP_ROWS, 0)),
            whole(2 * HEADS, LANES),
        ],
        [pltpu.VMEM((STATE, WIDTH), f32), pltpu.VMEM((chunks, KINDS * HEADS, LANES), f32)],
    )(first, first, heads)

    before = after = None
    if slab_count > 2:
        before, after = shifted(decay, slab_count, 1), shifted(decay, slab_count, -1)
    inbound = carry_over(state, decay, before, slab_count, 1)

    within, starts, pre = flow(
        within_kernel,
        [
            (hbm((tokens, WIDTH)), up["token"](WIDTH)),
            (hbm((chunks, STATE, WIDTH)), up["chunk"](STATE, WIDTH)),
            (hbm((chunks, 8, WIDTH)), up["chunk"](8, WIDTH)),
        ],
        6 * unit, size * 16,
        [
            up["message"](FIRST * rows), up["token"](LANES), up["lane"](KINDS * HEADS),
            up["chunk"](STATE, WIDTH), up["chunk"](8, WIDTH),
        ],
        [pltpu.VMEM((STATE, WIDTH), f32), pltpu.VMEM((8, WIDTH), f32)],
    )(first, in_hbm(sm), in_hbm(smt), in_hbm(own), in_hbm(dec))

    y, sums = flow(
        mix_kernel,
        [
            (struct((tokens, WIDTH)), up["token"](WIDTH)),
            (struct((chunks, 8, LANES)), up["chunk"](8, LANES)),
        ],
        unit, size * 16,
        [
            up["message"](FIRST * rows), up["message"](second_rows), up["token"](WIDTH),
            up["token"](LANES), whole(STATE, WIDTH), up["chunk"](8, WIDTH),
            whole(1, WIDTH), whole(1, WIDTH),
        ],
    )(
        first, in_hbm(second), in_hbm(within), in_hbm(sm), inbound, in_hbm(pre), own_gain, skip_row,
    )

    partner = lax.ppermute(sums, "sub", [(i, i ^ 1) for i in range(sub_count)])

    d_mixed, back, slab_back = flow(
        norm_kernel,
        [
            (struct((tokens, WIDTH), bf16), up["token"](WIDTH)),
            (struct((chunks, STATE, WIDTH)), up["chunk"](STATE, WIDTH)),
            (struct((STATE, WIDTH), bf16), whole(STATE, WIDTH)),
        ],
        2 * unit, size * 12,
        [
            up["message"](FIRST * rows), up["message"](second_rows), up["token"](WIDTH),
            up["token"](LANES), up["chunk"](8, WIDTH), up["chunk"](8, LANES),
            up["chunk"](8, LANES), whole(1, WIDTH), whole(1, WIDTH),
        ],
        [pltpu.VMEM((STATE, WIDTH), f32)],
    )(first, in_hbm(second), y, sm, in_hbm(pre), sums, partner, own_gain, skip_row)

    outer = carry_over(slab_back, decay, after, slab_count, -1)

    d_values, d_sources, d_readers, d_gates, e, params = flow(
        local_kernel,
        [
            (struct((tokens, WIDTH)), up["token"](WIDTH)),
            (struct((tokens, STATE)), up["token"](STATE)),
            (struct((peers, rows, LANES), bf16), up["message"](rows)),
            (struct((peers, PAIRS * rows, LANES), bf16), up["message"](PAIRS * rows)),
            (struct((HEADS, tokens)), up["lane"](HEADS)),
            (struct((8, LANES)), whole(8, LANES)),
        ],
        10 * unit, size * 16,
        [
            up["message"](FIRST * rows), up["message"](second_rows), up["token"](WIDTH),
            up["token"](WIDTH), up["token"](LANES), up["lane"](KINDS * HEADS),
            up["chunk"](STATE, WIDTH), up["chunk"](8, WIDTH), whole(STATE, WIDTH),
            up["chunk"](8, LANES), up["chunk"](8, LANES), whole(1, WIDTH), whole(1, WIDTH),
        ],
        [
            pltpu.VMEM((8, WIDTH), f32), pltpu.VMEM((8, WIDTH), f32),
            pltpu.VMEM((CHUNK, WIDTH), bf16), pltpu.VMEM((CHUNK, WIDTH), bf16),
            pltpu.VMEM((CHUNK, WIDTH), bf16),
        ],
    )(
        first, in_hbm(second), y, d_mixed, sm, smt, in_hbm(starts), in_hbm(pre), inbound,
        sums, partner, own_gain, skip_row,
    )

    (last,) = flow(
        last_kernel,
        [(hbm((peers, last_rows, LANES), bf16), pl.BlockSpec(memory_space=pl.ANY))],
        4 * unit, size * 16,
        [
            dn["message"](SOURCES * rows), dn["token"](WIDTH), dn["token"](STATE),
            dn["message"](rows), dn["message"](PAIRS * rows),
            dn["token"](WIDTH), dn["lane"](HEADS), dn["token"](LANES), dn["lane"](KINDS * HEADS),
            whole(STATE, WIDTH), dn["chunk"](STATE, WIDTH), dn["chunk"](STATE, WIDTH),
            dn["chunk"](8, WIDTH), whole(STATE, WIDTH), dn["chunk"](8, WIDTH), whole(1, WIDTH), whole(2 * HEADS, LANES), whole(8, LANES),
        ],
        [
            pltpu.VMEM((STATE, WIDTH), f32), pltpu.VMEM((2 * HEADS, LANES), f32),
            pltpu.VMEM((CHUNK, WIDTH), bf16), pltpu.VMEM((CHUNK, WIDTH), bf16),
            pltpu.VMEM((CHUNK, WIDTH), bf16), pltpu.VMEM((STATE, WIDTH), bf16),
            pltpu.VMEM((16, WIDTH), f32), pltpu.VMEM((peers, last_rows, LANES), bf16),
            pltpu.SemaphoreType.DMA((grid[0] + 1,)),
        ],
    )(
        first, d_values, d_sources, d_readers, d_gates, d_mixed, e, sm, smt, outer, back,
        in_hbm(starts), in_hbm(pre), inbound, in_hbm(dec), skip_row, heads, params,
    )

    last_back = exchange(last)
    tile_at = LAST * rows // STEP_ROWS
    def tile(at):
        return pl.BlockSpec((peers, STEP_ROWS, LANES), lambda c: (0, at, 0))

    params = call(
        lambda *refs: unpack_params(sub_count, tensor_count, *refs),
        struct((8 + sub_count * PAIRS, LANES)),
        0, 4 * peers * STEP_ROWS * LANES, (1,),
        [tile(tile_at), tile(tile_at + 1), whole(tensor_count, LANES)],
        whole(8 + sub_count * PAIRS, LANES),
    )(last_back, last_back, mine)
    own_params, other_params = two_parts(params, "slab", slab_count)
    wide, narrow = struct((rows, CHANNELS), bf16), struct((rows, GROUPS * STATE), bf16)
    grad_x, grad_gates, grad_b, grad_c, grad_steps = call(
        lambda *refs: unpack(owners, *refs),
        (wide, wide, narrow, narrow, struct((rows, MIXER_HEADS), bf16)),
        0, 10 * rows * CHANNELS,
    )(last_back)
    row = struct((1, sub_count * HEADS))
    grad_logs, grad_skip, grad_bias, grad_gain = call(
        finish, (row, row, row, struct((sub_count * PAIRS, LANES))), 0, 1 << 16,
    )(own_params, other_params)
    return (
        grad_x,
        grad_gates,
        grad_b,
        grad_c,
        grad_steps,
        grad_logs.reshape(-1),
        grad_skip.reshape(-1),
        grad_bias.reshape(-1),
        grad_gain.reshape(-1),
    )


def solution(mesh):
    tensor_count = mesh.shape["tensor"]
    sub_count = OWNERS // tensor_count
    slab_count = mesh.shape["dp"] // sub_count
    devices = mesh.devices.reshape(slab_count, sub_count, tensor_count)
    split_mesh = Mesh(devices, ("slab", "sub", "tensor"))
    rows = P(("slab", "sub", "tensor"), None)
    param = P("tensor")

    def local(*arrays):
        return on_device(slab_count, sub_count, tensor_count, *arrays)

    return jax.shard_map(
        local,
        mesh=split_mesh,
        in_specs=(rows,) * 5 + (param,) * 4 + (rows,),
        out_specs=(rows,) * 5 + (param,) * 4,
        check_vma=False,
    )
```

```python
import jax
import jax.numpy as jnp
from jax import lax
from jax.experimental import pallas as pl
from jax.experimental.pallas import tpu as pltpu
from jax.sharding import Mesh
from jax.sharding import PartitionSpec as P

MIXER_HEADS = 128
HEAD_DIM = 64
STATE = 128
GROUPS = 8
CHANNELS = MIXER_HEADS * HEAD_DIM
HEADS = 8
WIDTH = HEADS * HEAD_DIM
GROUP_WIDTH = 2 * WIDTH
OWNERS = MIXER_HEADS // HEADS
LANES = 128
PAIRS = WIDTH // LANES
CHUNK = 128
STEP_ROWS = 16
epsilon = 1e-05
f32 = jnp.float32
bf16 = jnp.bfloat16

DT, CUM, WEIGHT, SHIFTED, ECUM, RATE, SIG = range(7)
KINDS = 8
CLAMP = 80.0


def mm(a, b):
    return jnp.dot(a, b, preferred_element_type=f32)


def mm_nt(a, b):
    return lax.dot_general(a, b, (((1,), (1,)), ((), ())), preferred_element_type=f32)


def mm_tn(a, b):
    return lax.dot_general(a, b, (((0,), (0,)), ((), ())), preferred_element_type=f32)


def mm_exact(a, b):
    return jnp.dot(a, b, precision=lax.Precision.HIGHEST, preferred_element_type=f32)


def two_terms(values):
    high = values.astype(bf16)
    return high, (values - high.astype(f32)).astype(bf16)


def mm_two(a, high, low):
    both = mm(a, jnp.concatenate([high, low], axis=1))
    width = high.shape[1]
    return both[:, :width] + both[:, width:]


def sigmoid(values):
    return 0.5 + 0.5 * jnp.tanh(0.5 * values)


def low_half(rows):
    return lax.broadcasted_iota(jnp.int32, (rows, LANES), 1) < HEAD_DIM


def spread_pair(values, kind, j):
    rows = values.shape[0]
    at = kind * HEADS + 2 * j
    return jnp.where(
        low_half(rows),
        jnp.broadcast_to(values[:, at : at + 1], (rows, LANES)),
        jnp.broadcast_to(values[:, at + 1 : at + 2], (rows, LANES)),
    )


def head_rows():
    row = lax.broadcasted_iota(jnp.int32, (16, WIDTH), 0)
    channel = lax.broadcasted_iota(jnp.int32, (16, WIDTH), 1) // HEAD_DIM
    return jnp.where(row == channel, 1.0, 0.0).astype(bf16)


def split_pair(block):
    low = low_half(block.shape[0])
    zero = jnp.zeros_like(block)
    return jnp.concatenate(
        [jnp.where(low, block, zero), jnp.where(low, zero, block)], axis=0
    )


def lanes(j):
    return slice(j * LANES, (j + 1) * LANES)


class Message:
    def __init__(self, rows):
        self.rows = rows
        self.per_chunk = CHUNK // rows

    def place(self, chunk, k):
        r = self.rows
        return (slice(chunk * self.per_chunk, (chunk + 1) * self.per_chunk), slice(k * r, (k + 1) * r))

    def get(self, ref, chunk, k):
        a, b = self.place(chunk, k)
        return ref[a, b, :].reshape(CHUNK, LANES)

    def put(self, ref, chunk, k, value):
        a, b = self.place(chunk, k)
        ref[a, b, :] = value.reshape(self.per_chunk, self.rows, LANES)


X, B, C = 0, PAIRS, PAIRS + 1
SOURCES = PAIRS + 1
FIRST = PAIRS + 2
Z, GRAD = 0, PAIRS
SECOND = 2 * PAIRS
LAST_X, LAST_Z, LAST_B, LAST_C = 0, PAIRS, 2 * PAIRS, 2 * PAIRS + 1
LAST = 2 * PAIRS + 2
TERMS = 3


def pack_first(x_ref, b_ref, c_ref, steps_ref, out_ref, by_head):
    r = x_ref.shape[0]
    step = pl.program_id(0) * pl.num_programs(1) + pl.program_id(1)
    subs = out_ref.shape[0]

    @pl.when(step == 0)
    def _():
        steps = steps_ref[...].astype(f32)
        by_head[...] = jnp.concatenate([steps, jnp.zeros((LANES - r, LANES), f32)], axis=0).T

    zero = jnp.zeros((STEP_ROWS - HEADS, LANES), f32)
    for s in range(subs):
        for j in range(PAIRS):
            out_ref[s, 0, j * r : (j + 1) * r, :] = x_ref[:, lanes(s * PAIRS + j)]
        out_ref[s, 0, B * r : (B + 1) * r, :] = b_ref[:, lanes(s // 2)]
        out_ref[s, 0, C * r : (C + 1) * r, :] = c_ref[:, lanes(s // 2)]
        at = pl.multiple_of((step * subs + s) * HEADS, HEADS)
        mine = jnp.concatenate([by_head[pl.ds(at, HEADS), :], zero], axis=0)
        out_ref[s, 0, FIRST * r :, :] = mine.astype(bf16)


def pack_second(z_ref, grad_ref, out_ref):
    r = z_ref.shape[0]
    for s in range(out_ref.shape[0]):
        for j in range(PAIRS):
            at = lanes(s * PAIRS + j)
            out_ref[s, 0, (Z + j) * r : (Z + j + 1) * r, :] = z_ref[:, at]
            out_ref[s, 0, (GRAD + j) * r : (GRAD + j + 1) * r, :] = grad_ref[:, at]


def add_halves(owners, in_ref, block, out_ref):
    r = out_ref.shape[0]
    peer_of = {own: peer for peer, own in enumerate(owners)}
    for g in range(GROUPS):
        halves = [
            in_ref[peer_of[2 * g + k], block * r : (block + 1) * r, :].astype(f32) for k in range(2)
        ]
        out_ref[:, lanes(g)] = (halves[0] + halves[1]).astype(bf16)


def unpack(owners, in_ref, x_ref, z_ref, b_ref, c_ref, steps_ref):
    r = x_ref.shape[0]
    peer_of = {own: peer for peer, own in enumerate(owners)}
    for peer, own in enumerate(owners):
        for j in range(PAIRS):
            for block, ref in ((LAST_X, x_ref), (LAST_Z, z_ref)):
                at = slice((block + j) * r, (block + j + 1) * r)
                ref[:, lanes(own * PAIRS + j)] = in_ref[peer, at, :]
    add_halves(owners, in_ref, LAST_B, b_ref)
    add_halves(owners, in_ref, LAST_C, c_ref)
    by_head = jnp.concatenate(
        [
            in_ref[peer_of[own], LAST * r : LAST * r + STEP_ROWS, :].astype(f32)[:HEADS]
            for own in range(OWNERS)
        ],
        axis=0,
    )
    steps_ref[...] = by_head.T[:r, :].astype(bf16)


def three_terms(values):
    high = values.astype(bf16).astype(f32)
    rest = values - high
    middle = rest.astype(bf16).astype(f32)
    return [high, middle, rest - middle]


def unpack_params(sub_count, tensor_count, late_ref, early_ref, mine_ref, out_ref):
    lane = lax.broadcasted_iota(jnp.int32, (1, LANES), 1)
    late = [jnp.zeros((1, LANES), f32) for _ in range(2)]
    skip = jnp.zeros((1, LANES), f32)

    def placed(rows, at):
        total = rows[at : at + 1] + rows[at + 1 : at + 2] + rows[at + 2 : at + 3]
        return jnp.where(lane < HEADS, total, 0.0)

    for s in range(sub_count):
        late_rows = jnp.zeros((STEP_ROWS, LANES), f32)
        early_rows = jnp.zeros((STEP_ROWS, LANES), f32)
        for t in range(tensor_count):
            mine = mine_ref[t : t + 1, :] > 0.0
            peer = s * tensor_count + t
            late_rows = jnp.where(mine, late_ref[peer].astype(f32), late_rows)
            early_rows = jnp.where(mine, early_ref[peer].astype(f32), early_rows)
        for k in range(2):
            part = placed(late_rows, HEADS + k * TERMS)
            late[k] = late[k] + (part if s == 0 else pltpu.roll(part, s * HEADS, 1))
        part = placed(early_rows, TERMS * PAIRS)
        skip = skip + (part if s == 0 else pltpu.roll(part, s * HEADS, 1))
        gain = early_rows[:PAIRS] + early_rows[PAIRS : 2 * PAIRS] + early_rows[2 * PAIRS : 3 * PAIRS]
        out_ref[8 + s * PAIRS : 8 + (s + 1) * PAIRS, :] = gain
    out_ref[:8, :] = jnp.concatenate(late + [skip, jnp.zeros((5, LANES), f32)], axis=0)


def state_kernel(
    message, per_step,
    first_ref, steps_ref, heads_ref, sm_ref, smt_ref, own_ref, dec_ref, state_ref, whole_ref,
    carry, rows_s,
):
    c = pl.program_id(0)

    @pl.when(c == 0)
    def _():
        carry[...] = jnp.zeros_like(carry)
        whole_ref[...] = jnp.ones_like(whole_ref)
        chunks = rows_s.shape[0]
        before = lax.broadcasted_iota(jnp.int32, (CHUNK, CHUNK), 0)
        after = lax.broadcasted_iota(jnp.int32, (CHUNK, CHUNK), 1)
        raws = []
        for k in range(chunks):
            raw = heads_ref[HEADS:, :]
            for p in range(message.per_chunk):
                part = steps_ref[k * message.per_chunk + p].astype(f32)[:HEADS]
                raw = raw + (part if p == 0 else pltpu.roll(part, p * message.rows, 1))
            raws.append(raw)
        raw = jnp.concatenate(raws, axis=0)
        small = jnp.exp(-jnp.abs(raw))
        series = small * (
            1.0 - small * (0.5 - small * (1.0 / 3 - small * (0.25 - small * 0.2)))
        )
        soft = jnp.maximum(raw, 0.0) + jnp.where(small < 0.015625, series, jnp.log(1.0 + small))
        sig = jnp.where(raw >= 0.0, 1.0, small) / (1.0 + small)
        decay_rate = jnp.concatenate([jnp.exp(heads_ref[:HEADS, :])] * chunks, axis=0)
        rate = -decay_rate * soft
        cum = mm_exact(rate, jnp.where(before <= after, 1.0, 0.0))
        rest = mm_exact(rate, jnp.where(before > after, 1.0, 0.0))
        kinds = [
            soft, cum, soft * jnp.exp(rest), cum - jnp.log(soft), jnp.exp(cum), rate, sig,
            jnp.zeros_like(soft),
        ]
        for k in range(chunks):
            at = slice(k * HEADS, (k + 1) * HEADS)
            rows_s[k] = jnp.concatenate([kind[at] for kind in kinds], axis=0)

    made = []
    state = [carry[:, lanes(j)] for j in range(PAIRS)]
    decays = [whole_ref[:, lanes(j)] for j in range(PAIRS)]
    for i in range(per_step):
        rows = rows_s[c * per_step + i]
        sm = jnp.concatenate([rows, jnp.zeros_like(rows)], axis=0).T
        last = jnp.broadcast_to(sm[CHUNK - 1 : CHUNK, :], (8, LANES))
        sources_t = message.get(first_ref, i, B).T
        decs, owns = [], []
        for j in range(PAIRS):
            dec = spread_pair(last, ECUM, j)
            scaled = message.get(first_ref, i, X + j).astype(f32) * spread_pair(sm, WEIGHT, j)
            own = mm_two(sources_t, *two_terms(scaled))
            state[j] = dec[0:1] * state[j] + own
            decays[j] = decays[j] * dec
            decs.append(dec)
            owns.append(own)
        made.append((rows, sm, decs, owns))
    for i, (rows, sm, decs, owns) in enumerate(made):
        smt_ref[:, lanes(i)] = rows
        sm_ref[i * CHUNK : (i + 1) * CHUNK, :] = sm
        for j in range(PAIRS):
            dec_ref[i, :, lanes(j)] = decs[j]
            own_ref[i, :, lanes(j)] = owns[j]
    for j in range(PAIRS):
        carry[:, lanes(j)] = state[j]
        whole_ref[:, lanes(j)] = decays[j]
        state_ref[:, lanes(j)] = state[j].astype(bf16)


def within_kernel(
    message, per_step,
    first_ref, sm_ref, smt_ref, own_ref, dec_ref, y_ref, start_ref, pre_ref, carry, pre,
):
    @pl.when(pl.program_id(0) == 0)
    def _():
        carry[...] = jnp.zeros_like(carry)
        pre[...] = jnp.ones_like(pre)

    t = lax.broadcasted_iota(jnp.int32, (CHUNK, CHUNK), 0)
    s = lax.broadcasted_iota(jnp.int32, (CHUNK, CHUNK), 1)
    made = []
    states = [carry[:, lanes(j)] for j in range(PAIRS)]
    before = pre[...]
    for i in range(per_step):
        rows = slice(i * CHUNK, (i + 1) * CHUNK)
        sm = sm_ref[rows, :]
        smt = smt_ref[:, lanes(i)]
        readers = message.get(first_ref, i, C)
        scores = jnp.where(t >= s, mm_nt(readers, message.get(first_ref, i, B)), 0.0)
        ys = []
        for j in range(PAIRS):
            weights = []
            for h in (2 * j, 2 * j + 1):
                here = sm[:, CUM * HEADS + h : CUM * HEADS + h + 1]
                there = smt[SHIFTED * HEADS + h : SHIFTED * HEADS + h + 1, :]
                weights.append(
                    (scores * jnp.exp(jnp.minimum(here - there, CLAMP))).astype(bf16)
                )
            values = split_pair(message.get(first_ref, i, X + j))
            within = mm(jnp.concatenate(weights, axis=1), values)
            carried = mm_two(readers, *two_terms(states[j]))
            ys.append(within + spread_pair(sm, ECUM, j) * carried)
        made.append((ys, list(states), before))
        for j in range(PAIRS):
            states[j] = dec_ref[i, 0:1, lanes(j)] * states[j] + own_ref[i, :, lanes(j)]
        before = before * dec_ref[i]
    for i, (ys, starts, prefix) in enumerate(made):
        pre_ref[i] = prefix
        for j in range(PAIRS):
            y_ref[i * CHUNK : (i + 1) * CHUNK, lanes(j)] = ys[j]
            start_ref[i, :, lanes(j)] = starts[j]
    pre[...] = before
    for j in range(PAIRS):
        carry[:, lanes(j)] = states[j]


def mix_kernel(
    message, per_step,
    first_ref, second_ref, within_ref, sm_ref, inbound_ref, pre_ref, gain_ref, skip_ref,
    y_ref, sums_ref,
):
    made = []
    inbound = inbound_ref[...].astype(bf16)
    for i in range(per_step):
        rows = slice(i * CHUNK, (i + 1) * CHUNK)
        sm = sm_ref[rows, :]
        carried = mm(message.get(first_ref, i, C), inbound)
        power = jnp.zeros((CHUNK, LANES), f32)
        cross = jnp.zeros((CHUNK, LANES), f32)
        ys = []
        for j in range(PAIRS):
            at = lanes(j)
            decay = spread_pair(sm, ECUM, j) * pre_ref[i, 0:1, at]
            y = within_ref[rows, at] + decay * carried[:, at]
            ys.append(y)
            values = message.get(first_ref, i, X + j).astype(f32)
            gates = message.get(second_ref, i, Z + j).astype(f32)
            grad = message.get(second_ref, i, GRAD + j).astype(f32)
            gated = (y + skip_ref[0:1, at] * values) * (gates * sigmoid(gates))
            power = power + gated * gated
            cross = cross + grad * gain_ref[0:1, at] * gated
        made.append(
            (ys, jnp.sum(power.T, axis=0, keepdims=True), jnp.sum(cross.T, axis=0, keepdims=True))
        )
    for i, (ys, power, cross) in enumerate(made):
        for j in range(PAIRS):
            y_ref[i * CHUNK : (i + 1) * CHUNK, lanes(j)] = ys[j]
        sums_ref[i] = jnp.concatenate([power, cross, jnp.zeros((6, LANES), f32)], axis=0)


def norm_factors(sums):
    sums = sums * (1.0 / GROUP_WIDTH)
    inverse = lax.rsqrt(sums[0:1] + epsilon)
    pull = inverse * inverse * inverse * sums[1:2]
    return (
        jnp.broadcast_to(inverse, (CHUNK, LANES)).T,
        jnp.broadcast_to(pull, (CHUNK, LANES)).T,
    )


def norm_kernel(
    message, per_step,
    first_ref, second_ref, y_ref, sm_ref, pre_ref, sums_ref, other_ref, gain_ref, skip_ref,
    mixed_ref, back_ref, slab_ref,
    back_sum,
):
    @pl.when(pl.program_id(0) == 0)
    def _():
        back_sum[...] = jnp.zeros_like(back_sum)

    made = []
    sums = [back_sum[:, lanes(j)] for j in range(PAIRS)]
    for i in range(per_step):
        rows = slice(i * CHUNK, (i + 1) * CHUNK)
        sm = sm_ref[rows, :]
        readers_t = message.get(first_ref, i, C).T
        inverse, pull = norm_factors(sums_ref[i] + other_ref[i])
        for j in range(PAIRS):
            at = lanes(j)
            values = message.get(first_ref, i, X + j).astype(f32)
            gates = message.get(second_ref, i, Z + j).astype(f32)
            grad = message.get(second_ref, i, GRAD + j).astype(f32)
            silu = gates * sigmoid(gates)
            gated = (y_ref[rows, at] + skip_ref[0:1, at] * values) * silu
            d_mixed = (inverse * grad * gain_ref[0:1, at] - pull * gated) * silu
            back = mm_two(readers_t, *two_terms(d_mixed * spread_pair(sm, ECUM, j)))
            sums[j] = sums[j] + pre_ref[i, 0:1, at] * back
            made.append((i, j, d_mixed.astype(bf16), back))
    for i, j, d_mixed, back in made:
        mixed_ref[i * CHUNK : (i + 1) * CHUNK, lanes(j)] = d_mixed
        back_ref[i, :, lanes(j)] = back
    for j in range(PAIRS):
        back_sum[:, lanes(j)] = sums[j]
        slab_ref[:, lanes(j)] = sums[j].astype(bf16)


def local_kernel(
    message, per_step,
    first_ref, second_ref, y_ref, grad_ref, sm_ref, smt_ref, start_ref, pre_ref, inbound_ref,
    sums_ref, other_ref, gain_ref, skip_ref,
    values_out, sources_out, readers_out, gate_ref, e_ref, start_out, param_ref,
    gain_sum, skip_sum,
):
    c = pl.program_id(0)

    @pl.when(c == 0)
    def _():
        gain_sum[...] = jnp.zeros_like(gain_sum)
        skip_sum[...] = jnp.zeros_like(skip_sum)

    s = lax.broadcasted_iota(jnp.int32, (CHUNK, CHUNK), 0)
    t = lax.broadcasted_iota(jnp.int32, (CHUNK, CHUNK), 1)
    causal = t >= s
    ones = head_rows()
    made = []
    gains = [gain_sum[0:1, lanes(j)] for j in range(PAIRS)]
    skips = [skip_sum[0:1, lanes(j)] for j in range(PAIRS)]
    for i in range(per_step):
        rows = slice(i * CHUNK, (i + 1) * CHUNK)
        sm = sm_ref[rows, :]
        smt = smt_ref[:, lanes(i)]
        sources = message.get(first_ref, i, B)
        readers = message.get(first_ref, i, C)
        inverse, pull = norm_factors(sums_ref[i] + other_ref[i])
        scores = jnp.where(causal, mm_nt(sources, readers), 0.0)
        total = jnp.zeros((CHUNK, CHUNK), f32)
        d_values, d_gates, highs, lows, scaleds, starts = [], [], [], [], [], []
        for j in range(PAIRS):
            at = lanes(j)
            rounded = grad_ref[rows, at]
            grads = split_pair(rounded)
            x = message.get(first_ref, i, X + j)
            weight_grads = mm_nt(x, grads)
            weights = []
            for k, h in enumerate((2 * j, 2 * j + 1)):
                there = sm[:, SHIFTED * HEADS + h : SHIFTED * HEADS + h + 1]
                here = smt[CUM * HEADS + h : CUM * HEADS + h + 1, :]
                decay = jnp.exp(jnp.minimum(here - there, CLAMP))
                weights.append((scores * decay).astype(bf16))
                total = total + weight_grads[:, lanes(k)] * decay
            d_values.append(mm(jnp.concatenate(weights, axis=1), grads))

            values = x.astype(f32)
            gates = message.get(second_ref, i, Z + j).astype(f32)
            grad = message.get(second_ref, i, GRAD + j).astype(f32)
            y = y_ref[rows, at]
            mixed = y + skip_ref[0:1, at] * values
            sig = sigmoid(gates)
            silu = gates * sig
            gated = mixed * silu
            scaled = inverse * grad
            gains[j] = gains[j] + jnp.sum(scaled * gated, axis=0, keepdims=True)
            d_gated = scaled * gain_ref[0:1, at] - pull * gated
            d_gate = d_gated * mixed * (sig + silu * (1.0 - sig))
            d_gates.append(d_gate.astype(bf16))
            skips[j] = skips[j] + jnp.sum(values * (d_gated * silu), axis=0, keepdims=True)
            d_mixed = rounded.astype(f32)
            high, low = two_terms(d_mixed * y)
            highs.append(high)
            lows.append(low)
            scaleds.append((d_mixed * spread_pair(sm, ECUM, j)).astype(bf16))
            starts.append(
                start_ref[i, :, at] + pre_ref[i, 0:1, at] * inbound_ref[:, at].astype(f32)
            )
        e = mm_nt(ones, jnp.concatenate(highs, axis=1)) + mm_nt(ones, jnp.concatenate(lows, axis=1))
        total = jnp.where(causal, total, 0.0).astype(bf16)
        start = jnp.concatenate([part.astype(bf16) for part in starts], axis=1)
        d_readers = mm_tn(total, sources) + mm_nt(jnp.concatenate(scaleds, axis=1), start)
        made.append(
            (d_values, d_gates, starts, e[:HEADS], mm(total, readers), d_readers.astype(bf16))
        )
    for i, (d_values, d_gates, starts, e, d_sources, d_readers) in enumerate(made):
        rows = slice(i * CHUNK, (i + 1) * CHUNK)
        for j in range(PAIRS):
            values_out[rows, lanes(j)] = d_values[j]
            message.put(gate_ref, i, j, d_gates[j])
            start_out[i, :, lanes(j)] = starts[j]
        e_ref[:, lanes(i)] = e
        sources_out[rows, :] = d_sources
        message.put(readers_out, i, 0, d_readers)
    for j in range(PAIRS):
        gain_sum[0:1, lanes(j)] = gains[j]
        skip_sum[0:1, lanes(j)] = skips[j]

    @pl.when(c == pl.num_programs(0) - 1)
    def _():
        for j in range(PAIRS):
            param_ref[j : j + 1, :] = gain_sum[0:1, lanes(j)]
        high, low = two_terms(jnp.broadcast_to(skip_sum[0:1, :], (LANES, WIDTH)))
        skips = (mm_nt(high, ones) + mm_nt(low, ones))[0:1]
        param_ref[PAIRS : PAIRS + 1, :] = jnp.concatenate(
            [skips, jnp.zeros((1, LANES - 16), f32)], axis=1
        )
        param_ref[PAIRS + 1 :, :] = jnp.zeros((8 - PAIRS - 1, LANES), f32)


def last_kernel(
    message, per_step,
    first_ref, within_ref, sources_ref, readers_ref, gate_ref, grad_ref, e_ref, sm_ref, smt_ref, outer_ref,
    back_ref, start_ref, dec_ref, skip_ref, heads_ref, early_ref,
    out_ref,
    carry, sums, message_s, sent,
):
    c = pl.program_id(0)

    @pl.when(c == 0)
    def _():
        carry[...] = outer_ref[...].astype(f32)
        sums[...] = jnp.zeros_like(sums)

    r = message.rows
    ones = head_rows()
    before = lax.broadcasted_iota(jnp.int32, (CHUNK, CHUNK), 0)
    after = lax.broadcasted_iota(jnp.int32, (CHUNK, CHUNK), 1)
    earlier = jnp.where(before < after, 1.0, 0.0)
    decay_rate = jnp.exp(heads_ref[:HEADS, :])
    first_peer = (pl.num_programs(0) - 1 - c) * per_step * message.per_chunk
    span = per_step * message.per_chunk
    mine = message_s.at[pl.ds(first_peer, span)]

    def body_copy(step):
        peer = (pl.num_programs(0) - 1 - step) * span
        at = (pl.ds(peer, span), pl.ds(0, LAST * r))
        return pltpu.make_async_copy(message_s.at[at], out_ref.at[at], sent.at[step])

    made = []
    states = [carry[:, lanes(j)] for j in range(PAIRS)]
    logs_sum, steps_sum = sums[:HEADS, :], sums[HEADS:, :]
    for i in reversed(range(per_step)):
        rows = slice(i * CHUNK, (i + 1) * CHUNK)
        sm = sm_ref[rows, :]
        sources = message.get(first_ref, i, B)
        d_values, highs, lows, scaleds, rounded, fluxes = [], [], [], [], [], []
        for j in range(PAIRS):
            at = lanes(j)
            high, low = two_terms(states[j])
            rounded.append(high)
            values = message.get(first_ref, i, X + j).astype(f32)
            weight = spread_pair(sm, WEIGHT, j)
            grad = within_ref[rows, at] + weight * mm_two(sources, high, low)
            skipped = skip_ref[0:1, at] * grad_ref[rows, at].astype(f32)
            d_values.append((grad + skipped).astype(bf16))
            high, low = two_terms(values * grad)
            highs.append(high)
            lows.append(low)
            scaleds.append((values * weight).astype(bf16))
            states[j] = dec_ref[i, 0:1, at] * states[j] + back_ref[i, :, at]
            fluxes.append(
                jnp.broadcast_to(
                    jnp.sum(start_ref[i, :, at] * states[j], axis=0, keepdims=True), (16, LANES)
                )
            )
        d_sources = sources_ref[rows, :] + mm_nt(
            jnp.concatenate(scaleds, axis=1), jnp.concatenate(rounded, axis=1)
        )
        g = mm_nt(ones, jnp.concatenate(highs, axis=1)) + mm_nt(ones, jnp.concatenate(lows, axis=1))
        g = g[:HEADS]
        high, low = two_terms(jnp.concatenate(fluxes, axis=1))
        constant = (mm_nt(ones, high) + mm_nt(ones, low))[:HEADS, 0:1]
        flux = constant + mm_exact(g - e_ref[:, lanes(i)], earlier)
        soft = smt_ref[DT * HEADS : (DT + 1) * HEADS, lanes(i)]
        rate = smt_ref[RATE * HEADS : (RATE + 1) * HEADS, lanes(i)]
        sig = smt_ref[SIG * HEADS : (SIG + 1) * HEADS, lanes(i)]
        steps = (g / soft - decay_rate * flux) * sig
        logs_sum = logs_sum + flux * rate
        steps_sum = steps_sum + steps
        steps = jnp.concatenate([steps, jnp.zeros_like(steps)], axis=0)
        made.append((i, d_values, d_sources.astype(bf16), steps))
    for i, d_values, d_sources, steps in made:
        for j in range(PAIRS):
            message.put(mine, i, LAST_X + j, d_values[j])
            message.put(mine, i, LAST_Z + j, message.get(gate_ref, i, j))
        message.put(mine, i, LAST_B, d_sources)
        message.put(mine, i, LAST_C, message.get(readers_ref, i, 0))
        for p in range(message.per_chunk):
            part = steps if p == 0 else pltpu.roll(steps, LANES - p * r, 1)
            mine[i * message.per_chunk + p, LAST * r : LAST * r + STEP_ROWS, :] = part.astype(bf16)
    for j in range(PAIRS):
        carry[:, lanes(j)] = states[j]
    sums[:HEADS, :] = logs_sum
    sums[HEADS:, :] = steps_sum
    body_copy(c).start()

    @pl.when(c == pl.num_programs(0) - 1)
    def _():
        late = []
        for k in range(2):
            column = jnp.sum(sums[k * HEADS : (k + 1) * HEADS, :], axis=1, keepdims=True)
            block = jnp.broadcast_to(column, (HEADS, LANES))
            block = jnp.concatenate([block, jnp.zeros((LANES - HEADS, LANES), f32)], axis=0)
            late += three_terms(block.T[0:1, :])
        late += [jnp.zeros((HEADS - 2 * TERMS, LANES), f32)]
        late = jnp.concatenate([jnp.zeros((HEADS, LANES), f32)] + late, axis=0)
        late = late.astype(bf16)
        early = three_terms(early_ref[:PAIRS, :]) + three_terms(early_ref[PAIRS : PAIRS + 1, :])
        early += [jnp.zeros((STEP_ROWS - TERMS * (PAIRS + 1), LANES), f32)]
        early = jnp.concatenate(early, axis=0).astype(bf16)
        own_rows = lax.broadcasted_iota(jnp.int32, (STEP_ROWS, LANES), 0) < HEADS

        def fill(peer, unused):
            steps_at = slice(LAST * r, LAST * r + STEP_ROWS)
            message_s[peer, steps_at, :] = jnp.where(own_rows, message_s[peer, steps_at, :], late)
            message_s[peer, LAST * r + STEP_ROWS :, :] = early
            return unused

        lax.fori_loop(0, message_s.shape[0], fill, 0)
        at = (slice(None), pl.ds(LAST * r, 2 * STEP_ROWS))
        steps = sent.shape[0] - 1
        tiles = pltpu.make_async_copy(message_s.at[at], out_ref.at[at], sent.at[steps])
        tiles.start()
        for step in range(steps):
            body_copy(step).wait()
        tiles.wait()


def finish(own_ref, other_ref, logs_ref, skip_ref, bias_ref, gain_ref):
    total = own_ref[...] + other_ref[...]
    count = logs_ref.shape[1]
    logs_ref[...] = total[0:1, :count]
    bias_ref[...] = total[1:2, :count]
    skip_ref[...] = total[2:3, :count]
    gain_ref[...] = total[8:]


def call(kernel, out_shape, flops, moved, grid=None, in_specs=None, out_specs=None, scratch=()):
    extra = {}
    if grid is not None:
        extra = dict(grid=grid, in_specs=in_specs, out_specs=out_specs)
    return pl.pallas_call(
        kernel,
        out_shape=out_shape,
        scratch_shapes=list(scratch),
        compiler_params=pltpu.CompilerParams(vmem_limit_bytes=16 * 1024 * 1024),
        cost_estimate=pl.CostEstimate(flops=flops, bytes_accessed=moved, transcendentals=0),
        **extra,
    )


def shifted(array, count, by):
    pairs = [(i, i + by) for i in range(count) if 0 <= i + by < count]
    return lax.ppermute(array, "slab", pairs)


def carry_over(state, decay, first_decay, count, sign):
    window, window_decay, step = state, decay, 1
    result = result_decay = None
    while step < count:
        arrived = shifted(window, count, sign * step)
        more = 2 * step < count
        if result is None:
            result = arrived
            if more:
                result_decay = first_decay
                window = (state.astype(f32) + decay[0:1] * arrived.astype(f32)).astype(bf16)
                window_decay = decay * first_decay
        else:
            if more:
                arrived_decay = shifted(window_decay, count, sign * step)
                window = (window.astype(f32) + window_decay[0:1] * arrived.astype(f32)).astype(bf16)
                window_decay = window_decay * arrived_decay
            result = result.astype(f32) + result_decay[0:1] * arrived.astype(f32)
            if more:
                result_decay = result_decay * arrived_decay
        step *= 2
    return jnp.zeros_like(state) if result is None else result


def two_parts(array, axis, count):
    step, other = 1, jnp.zeros_like(array)
    while step < count:
        array = array if step == 1 else array + other
        other = lax.ppermute(array, axis, [(i, i ^ step) for i in range(count)])
        step *= 2
    return array, other


def on_device(
    slab_count, sub_count, tensor_count,
    mixer_x, gate_z, b_matrix, c_matrix, raw_steps, decay_log, skip_gain, step_bias, norm_gain, out_grad,
):
    rows = mixer_x.shape[0]
    peers = sub_count * tensor_count
    tokens = rows * peers
    chunks = tokens // CHUNK
    per_step = min(2, chunks)
    grid = (chunks // per_step,)
    message = Message(rows)
    owners = [t * sub_count + s for s in range(sub_count) for t in range(tensor_count)]
    sub = lax.axis_index("sub")

    def struct(shape, kind=f32):
        return jax.ShapeDtypeStruct(shape, kind)

    def hbm(shape, kind=f32):
        return pltpu.HBM(shape, kind)

    def in_hbm(array):
        return pltpu.with_memory_space_constraint(array, pltpu.HBM)

    def exchange(array):
        return lax.all_to_all(array, ("sub", "tensor"), split_axis=0, concat_axis=0, tiled=True)

    own_logs = lax.dynamic_slice(decay_log, (sub * HEADS,), (HEADS,))
    own_bias = lax.dynamic_slice(step_bias, (sub * HEADS,), (HEADS,))
    own_skip = lax.dynamic_slice(skip_gain, (sub * HEADS,), (HEADS,))
    own_gain = lax.dynamic_slice(norm_gain, (sub * WIDTH,), (WIDTH,)).reshape(1, WIDTH)
    heads = jnp.broadcast_to(jnp.concatenate([own_logs, own_bias])[:, None], (2 * HEADS, LANES))
    skip_row = jnp.repeat(own_skip, HEAD_DIM).reshape(1, WIDTH)

    first_rows = FIRST * rows + STEP_ROWS
    second_rows = SECOND * rows
    last_rows = LAST * rows + 2 * STEP_ROWS

    def packed(kernel, height, arrays, whole_arrays=(), scratch=()):
        out = hbm((sub_count, tensor_count, height, LANES), bf16)
        moved = 4 * peers * height * LANES
        runs = 1
        parts = tensor_count * runs
        specs = [
            pl.BlockSpec((rows, a.shape[1] // parts), lambda t, k: (0, t * runs + k)) for a in arrays
        ] + [pl.BlockSpec(a.shape, lambda t, k: (0, 0)) for a in whole_arrays]
        out_spec = pl.BlockSpec((sub_count // runs, 1, height, LANES), lambda t, k: (k, t, 0, 0))
        made = call(kernel, out, 0, moved, (tensor_count, runs), specs, out_spec, scratch)(
            *(in_hbm(a) for a in (*arrays, *whole_arrays))
        )
        return made.reshape(peers, height, LANES)

    first = exchange(
        packed(
            pack_first, first_rows, (mixer_x, b_matrix, c_matrix), (raw_steps,),
            [pltpu.VMEM((LANES, LANES), f32)],
        )
    )
    tensor_rows = lax.broadcasted_iota(jnp.int32, (tensor_count, LANES), 0)
    mine = (tensor_rows == lax.axis_index("tensor")).astype(f32)
    gate_z, heads, skip_row, own_gain, mine = lax.optimization_barrier(
        (gate_z, heads, skip_row, own_gain, mine)
    )
    second = exchange(packed(pack_second, second_rows, (gate_z, out_grad)))

    def flow(kernel, shape_specs, flops, moved, in_specs, scratch=()):
        def body(*refs):
            return kernel(message, per_step, *refs)

        shapes = tuple(shape for shape, _ in shape_specs)
        specs = tuple(spec for _, spec in shape_specs)
        return call(body, shapes, flops, moved, grid, in_specs, specs, scratch)

    def spec(block, axis, down=False):
        def index(c):
            at = grid[0] - 1 - c if down else c
            return tuple(at if k == axis else 0 for k in range(len(block)))

        return pl.BlockSpec(block, index)

    span = per_step * CHUNK

    def specs_of(down):
        return dict(
            message=lambda height: spec((per_step * message.per_chunk, height, LANES), 0, down),
            token=lambda width: spec((span, width), 0, down),
            lane=lambda height: spec((height, span), 1, down),
            chunk=lambda *shape: spec((per_step,) + shape, 0, down),
        )

    up, dn = specs_of(False), specs_of(True)

    def whole(*shape):
        return pl.BlockSpec(shape, lambda c: (0,) * len(shape))

    unit = 2 * tokens * CHUNK * WIDTH
    size = tokens * WIDTH

    sm, smt, own, dec, state, decay = flow(
        state_kernel,
        [
            (hbm((tokens, LANES)), up["token"](LANES)),
            (hbm((KINDS * HEADS, tokens)), up["lane"](KINDS * HEADS)),
            (hbm((chunks, STATE, WIDTH)), up["chunk"](STATE, WIDTH)),
            (hbm((chunks, 8, WIDTH)), up["chunk"](8, WIDTH)),
            (struct((STATE, WIDTH), bf16), whole(STATE, WIDTH)),
            (struct((8, WIDTH)), whole(8, WIDTH)),
        ],
        2 * unit, size * 8,
        [
            up["message"](SOURCES * rows),
            pl.BlockSpec((peers, STEP_ROWS, LANES), lambda c: (0, FIRST * rows // STEP_ROWS, 0)),
            whole(2 * HEADS, LANES),
        ],
        [pltpu.VMEM((STATE, WIDTH), f32), pltpu.VMEM((chunks, KINDS * HEADS, LANES), f32)],
    )(first, first, heads)

    before = after = None
    if slab_count > 2:
        before, after = shifted(decay, slab_count, 1), shifted(decay, slab_count, -1)
    inbound = carry_over(state, decay, before, slab_count, 1)

    within, starts, pre = flow(
        within_kernel,
        [
            (hbm((tokens, WIDTH)), up["token"](WIDTH)),
            (hbm((chunks, STATE, WIDTH)), up["chunk"](STATE, WIDTH)),
            (hbm((chunks, 8, WIDTH)), up["chunk"](8, WIDTH)),
        ],
        6 * unit, size * 16,
        [
            up["message"](FIRST * rows), up["token"](LANES), up["lane"](KINDS * HEADS),
            up["chunk"](STATE, WIDTH), up["chunk"](8, WIDTH),
        ],
        [pltpu.VMEM((STATE, WIDTH), f32), pltpu.VMEM((8, WIDTH), f32)],
    )(first, in_hbm(sm), in_hbm(smt), in_hbm(own), in_hbm(dec))

    y, sums = flow(
        mix_kernel,
        [
            (struct((tokens, WIDTH)), up["token"](WIDTH)),
            (struct((chunks, 8, LANES)), up["chunk"](8, LANES)),
        ],
        unit, size * 16,
        [
            up["message"](FIRST * rows), up["message"](second_rows), up["token"](WIDTH),
            up["token"](LANES), whole(STATE, WIDTH), up["chunk"](8, WIDTH),
            whole(1, WIDTH), whole(1, WIDTH),
        ],
    )(
        first, in_hbm(second), in_hbm(within), in_hbm(sm), inbound, in_hbm(pre), own_gain, skip_row,
    )

    partner = lax.ppermute(sums, "sub", [(i, i ^ 1) for i in range(sub_count)])

    d_mixed, back, slab_back = flow(
        norm_kernel,
        [
            (struct((tokens, WIDTH), bf16), up["token"](WIDTH)),
            (struct((chunks, STATE, WIDTH)), up["chunk"](STATE, WIDTH)),
            (struct((STATE, WIDTH), bf16), whole(STATE, WIDTH)),
        ],
        2 * unit, size * 12,
        [
            up["message"](FIRST * rows), up["message"](second_rows), up["token"](WIDTH),
            up["token"](LANES), up["chunk"](8, WIDTH), up["chunk"](8, LANES),
            up["chunk"](8, LANES), whole(1, WIDTH), whole(1, WIDTH),
        ],
        [pltpu.VMEM((STATE, WIDTH), f32)],
    )(first, in_hbm(second), y, sm, in_hbm(pre), sums, partner, own_gain, skip_row)

    outer = carry_over(slab_back, decay, after, slab_count, -1)

    d_values, d_sources, d_readers, d_gates, e, starts, params = flow(
        local_kernel,
        [
            (struct((tokens, WIDTH)), up["token"](WIDTH)),
            (struct((tokens, STATE)), up["token"](STATE)),
            (struct((peers, rows, LANES), bf16), up["message"](rows)),
            (struct((peers, PAIRS * rows, LANES), bf16), up["message"](PAIRS * rows)),
            (struct((HEADS, tokens)), up["lane"](HEADS)),
            (struct((chunks, STATE, WIDTH)), up["chunk"](STATE, WIDTH)),
            (struct((8, LANES)), whole(8, LANES)),
        ],
        10 * unit, size * 16,
        [
            up["message"](FIRST * rows), up["message"](second_rows), up["token"](WIDTH),
            up["token"](WIDTH), up["token"](LANES), up["lane"](KINDS * HEADS),
            up["chunk"](STATE, WIDTH), up["chunk"](8, WIDTH), whole(STATE, WIDTH),
            up["chunk"](8, LANES), up["chunk"](8, LANES), whole(1, WIDTH), whole(1, WIDTH),
        ],
        [pltpu.VMEM((8, WIDTH), f32), pltpu.VMEM((8, WIDTH), f32)],
    )(
        first, in_hbm(second), y, d_mixed, sm, smt, in_hbm(starts), in_hbm(pre), inbound,
        sums, partner, own_gain, skip_row,
    )

    (last,) = flow(
        last_kernel,
        [(hbm((peers, last_rows, LANES), bf16), pl.BlockSpec(memory_space=pl.ANY))],
        4 * unit, size * 16,
        [
            dn["message"](SOURCES * rows), dn["token"](WIDTH), dn["token"](STATE),
            dn["message"](rows), dn["message"](PAIRS * rows),
            dn["token"](WIDTH), dn["lane"](HEADS), dn["token"](LANES), dn["lane"](KINDS * HEADS),
            whole(STATE, WIDTH), dn["chunk"](STATE, WIDTH), dn["chunk"](STATE, WIDTH),
            dn["chunk"](8, WIDTH), whole(1, WIDTH), whole(2 * HEADS, LANES), whole(8, LANES),
        ],
        [
            pltpu.VMEM((STATE, WIDTH), f32), pltpu.VMEM((2 * HEADS, LANES), f32),
            pltpu.VMEM((peers, last_rows, LANES), bf16),
            pltpu.SemaphoreType.DMA((grid[0] + 1,)),
        ],
    )(
        first, d_values, d_sources, d_readers, d_gates, d_mixed, e, sm, smt, outer, back,
        starts, in_hbm(dec), skip_row, heads, params,
    )

    last_back = exchange(last)
    tile_at = LAST * rows // STEP_ROWS
    def tile(at):
        return pl.BlockSpec((peers, STEP_ROWS, LANES), lambda c: (0, at, 0))

    params = call(
        lambda *refs: unpack_params(sub_count, tensor_count, *refs),
        struct((8 + sub_count * PAIRS, LANES)),
        0, 4 * peers * STEP_ROWS * LANES, (1,),
        [tile(tile_at), tile(tile_at + 1), whole(tensor_count, LANES)],
        whole(8 + sub_count * PAIRS, LANES),
    )(last_back, last_back, mine)
    own_params, other_params = two_parts(params, "slab", slab_count)
    wide, narrow = struct((rows, CHANNELS), bf16), struct((rows, GROUPS * STATE), bf16)
    grad_x, grad_gates, grad_b, grad_c, grad_steps = call(
        lambda *refs: unpack(owners, *refs),
        (wide, wide, narrow, narrow, struct((rows, MIXER_HEADS), bf16)),
        0, 10 * rows * CHANNELS,
    )(last_back)
    row = struct((1, sub_count * HEADS))
    grad_logs, grad_skip, grad_bias, grad_gain = call(
        finish, (row, row, row, struct((sub_count * PAIRS, LANES))), 0, 1 << 16,
    )(own_params, other_params)
    return (
        grad_x,
        grad_gates,
        grad_b,
        grad_c,
        grad_steps,
        grad_logs.reshape(-1),
        grad_skip.reshape(-1),
        grad_bias.reshape(-1),
        grad_gain.reshape(-1),
    )


def solution(mesh):
    tensor_count = mesh.shape["tensor"]
    sub_count = OWNERS // tensor_count
    slab_count = mesh.shape["dp"] // sub_count
    devices = mesh.devices.reshape(slab_count, sub_count, tensor_count)
    split_mesh = Mesh(devices, ("slab", "sub", "tensor"))
    rows = P(("slab", "sub", "tensor"), None)
    param = P("tensor")

    def local(*arrays):
        return on_device(slab_count, sub_count, tensor_count, *arrays)

    return jax.shard_map(
        local,
        mesh=split_mesh,
        in_specs=(rows,) * 5 + (param,) * 4 + (rows,),
        out_specs=(rows,) * 5 + (param,) * 4,
        check_vma=False,
    )
```

```python
import jax
import jax.numpy as jnp
from jax import lax
from jax.experimental import pallas as pl
from jax.experimental.pallas import tpu as pltpu
from jax.sharding import Mesh
from jax.sharding import PartitionSpec as P

MIXER_HEADS = 128
HEAD_DIM = 64
STATE = 128
GROUPS = 8
CHANNELS = MIXER_HEADS * HEAD_DIM
HEADS = 8
WIDTH = HEADS * HEAD_DIM
GROUP_WIDTH = 2 * WIDTH
OWNERS = MIXER_HEADS // HEADS
LANES = 128
PAIRS = WIDTH // LANES
CHUNK = 128
STEP_ROWS = 16
epsilon = 1e-05
f32 = jnp.float32
bf16 = jnp.bfloat16

DT, CUM, WEIGHT, SHIFTED, ECUM, RATE, SIG = range(7)
KINDS = 8
CLAMP = 80.0


def mm(a, b):
    return jnp.dot(a, b, preferred_element_type=f32)


def mm_nt(a, b):
    return lax.dot_general(a, b, (((1,), (1,)), ((), ())), preferred_element_type=f32)


def mm_tn(a, b):
    return lax.dot_general(a, b, (((0,), (0,)), ((), ())), preferred_element_type=f32)


def mm_exact(a, b):
    return jnp.dot(a, b, precision=lax.Precision.HIGHEST, preferred_element_type=f32)


def two_terms(values):
    high = values.astype(bf16)
    return high, (values - high.astype(f32)).astype(bf16)


def two_terms_each(tiles):
    return zip(*(two_terms(tile) for tile in tiles))


def twice(a):
    return jnp.concatenate([a, a], axis=1)


def mm_two(a_twice, high, low):
    return mm(a_twice, jnp.concatenate([high, low], axis=0))


def sum_heads(ones_twice, highs, lows):
    return mm_nt(ones_twice, jnp.concatenate([*highs, *lows], axis=1))


def sigmoid(values):
    return 0.5 + 0.5 * jnp.tanh(0.5 * values)


def low_half(rows):
    return lax.broadcasted_iota(jnp.int32, (rows, LANES), 1) < HEAD_DIM


def spread_pair(values, kind, j):
    rows = values.shape[0]
    at = kind * HEADS + 2 * j
    return jnp.where(
        low_half(rows),
        jnp.broadcast_to(values[:, at : at + 1], (rows, LANES)),
        jnp.broadcast_to(values[:, at + 1 : at + 2], (rows, LANES)),
    )


def head_rows():
    row = lax.broadcasted_iota(jnp.int32, (16, WIDTH), 0)
    channel = lax.broadcasted_iota(jnp.int32, (16, WIDTH), 1) // HEAD_DIM
    return jnp.where(row == channel, 1.0, 0.0).astype(bf16)


def split_pair(block):
    low = low_half(block.shape[0])
    zero = jnp.zeros_like(block)
    return jnp.concatenate(
        [jnp.where(low, block, zero), jnp.where(low, zero, block)], axis=0
    )


def lanes(j):
    return slice(j * LANES, (j + 1) * LANES)


class Message:
    def __init__(self, rows):
        self.rows = rows
        self.per_chunk = CHUNK // rows

    def place(self, chunk, k):
        r = self.rows
        return (slice(chunk * self.per_chunk, (chunk + 1) * self.per_chunk), slice(k * r, (k + 1) * r))

    def get(self, ref, chunk, k):
        a, b = self.place(chunk, k)
        return ref[a, b, :].reshape(CHUNK, LANES)

    def put(self, ref, chunk, k, value):
        a, b = self.place(chunk, k)
        ref[a, b, :] = value.reshape(self.per_chunk, self.rows, LANES)


X, HALF = 0, PAIRS
FIRST = PAIRS + 1
Z, GRAD = 0, PAIRS
SECOND = 2 * PAIRS
LAST_X, LAST_Z, LAST_B, LAST_C = 0, PAIRS, 2 * PAIRS, 2 * PAIRS + 1
LAST = 2 * PAIRS + 2
TERMS = 3


def pack_first(x_ref, b_ref, c_ref, steps_ref, out_ref, by_head):
    r = x_ref.shape[0]
    step = pl.program_id(0) * pl.num_programs(1) + pl.program_id(1)
    subs = out_ref.shape[0]

    @pl.when(step == 0)
    def _():
        steps = steps_ref[...].astype(f32)
        by_head[...] = jnp.concatenate([steps, jnp.zeros((LANES - r, LANES), f32)], axis=0).T

    zero = jnp.zeros((STEP_ROWS - HEADS, LANES), f32)
    for s in range(subs):
        for j in range(PAIRS):
            out_ref[s, 0, j * r : (j + 1) * r, :] = x_ref[:, lanes(s * PAIRS + j)]
        half = b_ref if s % 2 == 0 else c_ref
        out_ref[s, 0, HALF * r : (HALF + 1) * r, :] = half[:, lanes(s // 2)]
        at = pl.multiple_of((step * subs + s) * HEADS, HEADS)
        mine = jnp.concatenate([by_head[pl.ds(at, HEADS), :], zero], axis=0)
        out_ref[s, 0, FIRST * r :, :] = mine.astype(bf16)


def pack_second(z_ref, grad_ref, out_ref):
    r = z_ref.shape[0]
    for s in range(out_ref.shape[0]):
        for j in range(PAIRS):
            at = lanes(s * PAIRS + j)
            out_ref[s, 0, (Z + j) * r : (Z + j + 1) * r, :] = z_ref[:, at]
            out_ref[s, 0, (GRAD + j) * r : (GRAD + j + 1) * r, :] = grad_ref[:, at]


def add_halves(owners, in_ref, block, out_ref):
    r = out_ref.shape[0]
    peer_of = {own: peer for peer, own in enumerate(owners)}
    for g in range(GROUPS):
        halves = [
            in_ref[peer_of[2 * g + k], block * r : (block + 1) * r, :].astype(f32) for k in range(2)
        ]
        out_ref[:, lanes(g)] = (halves[0] + halves[1]).astype(bf16)


def unpack(owners, in_ref, x_ref, z_ref, b_ref, c_ref, steps_ref):
    r = x_ref.shape[0]
    peer_of = {own: peer for peer, own in enumerate(owners)}
    for peer, own in enumerate(owners):
        for j in range(PAIRS):
            for block, ref in ((LAST_X, x_ref), (LAST_Z, z_ref)):
                at = slice((block + j) * r, (block + j + 1) * r)
                ref[:, lanes(own * PAIRS + j)] = in_ref[peer, at, :]
    add_halves(owners, in_ref, LAST_B, b_ref)
    add_halves(owners, in_ref, LAST_C, c_ref)
    by_head = jnp.concatenate(
        [
            in_ref[peer_of[own], LAST * r : LAST * r + STEP_ROWS, :].astype(f32)[:HEADS]
            for own in range(OWNERS)
        ],
        axis=0,
    )
    steps_ref[...] = by_head.T[:r, :].astype(bf16)


def three_terms(values):
    high = values.astype(bf16).astype(f32)
    rest = values - high
    middle = rest.astype(bf16).astype(f32)
    return [high, middle, rest - middle]


def unpack_params(sub_count, tensor_count, late_ref, early_ref, mine_ref, out_ref):
    lane = lax.broadcasted_iota(jnp.int32, (1, LANES), 1)
    late = [jnp.zeros((1, LANES), f32) for _ in range(2)]
    skip = jnp.zeros((1, LANES), f32)

    def placed(rows, at):
        total = rows[at : at + 1] + rows[at + 1 : at + 2] + rows[at + 2 : at + 3]
        return jnp.where(lane < HEADS, total, 0.0)

    for s in range(sub_count):
        late_rows = jnp.zeros((STEP_ROWS, LANES), f32)
        early_rows = jnp.zeros((STEP_ROWS, LANES), f32)
        for t in range(tensor_count):
            mine = mine_ref[t : t + 1, :] > 0.0
            peer = s * tensor_count + t
            late_rows = jnp.where(mine, late_ref[peer].astype(f32), late_rows)
            early_rows = jnp.where(mine, early_ref[peer].astype(f32), early_rows)
        for k in range(2):
            part = placed(late_rows, HEADS + k * TERMS)
            late[k] = late[k] + (part if s == 0 else pltpu.roll(part, s * HEADS, 1))
        part = placed(early_rows, TERMS * PAIRS)
        skip = skip + (part if s == 0 else pltpu.roll(part, s * HEADS, 1))
        gain = early_rows[:PAIRS] + early_rows[PAIRS : 2 * PAIRS] + early_rows[2 * PAIRS : 3 * PAIRS]
        out_ref[8 + s * PAIRS : 8 + (s + 1) * PAIRS, :] = gain
    out_ref[:8, :] = jnp.concatenate(late + [skip, jnp.zeros((5, LANES), f32)], axis=0)


def state_kernel(
    message, per_step,
    first_ref, sources_ref, steps_ref, heads_ref, sm_ref, smt_ref, own_ref, dec_ref, state_ref, whole_ref,
    carry, rows_s,
):
    c = pl.program_id(0)

    @pl.when(c == 0)
    def _():
        carry[...] = jnp.zeros_like(carry)
        whole_ref[...] = jnp.ones_like(whole_ref)
        chunks = rows_s.shape[0]
        before = lax.broadcasted_iota(jnp.int32, (CHUNK, CHUNK), 0)
        after = lax.broadcasted_iota(jnp.int32, (CHUNK, CHUNK), 1)
        raws = []
        for k in range(chunks):
            raw = heads_ref[HEADS:, :]
            for p in range(message.per_chunk):
                part = steps_ref[k * message.per_chunk + p].astype(f32)[:HEADS]
                raw = raw + (part if p == 0 else pltpu.roll(part, p * message.rows, 1))
            raws.append(raw)
        raw = jnp.concatenate(raws, axis=0)
        small = jnp.exp(-jnp.abs(raw))
        series = small * (
            1.0 - small * (0.5 - small * (1.0 / 3 - small * (0.25 - small * 0.2)))
        )
        soft = jnp.maximum(raw, 0.0) + jnp.where(small < 0.015625, series, jnp.log(1.0 + small))
        sig = jnp.where(raw >= 0.0, 1.0, small) / (1.0 + small)
        decay_rate = jnp.concatenate([jnp.exp(heads_ref[:HEADS, :])] * chunks, axis=0)
        rate = -decay_rate * soft
        cum = mm_exact(rate, jnp.where(before <= after, 1.0, 0.0))
        rest = mm_exact(rate, jnp.where(before > after, 1.0, 0.0))
        kinds = [
            soft, cum, soft * jnp.exp(rest), cum - jnp.log(soft), jnp.exp(cum), rate, sig,
            jnp.zeros_like(soft),
        ]
        for k in range(chunks):
            at = slice(k * HEADS, (k + 1) * HEADS)
            rows_s[k] = jnp.concatenate([kind[at] for kind in kinds], axis=0)

    made = []
    state = [carry[:, lanes(j)] for j in range(PAIRS)]
    decays = [whole_ref[:, lanes(j)] for j in range(PAIRS)]
    for i in range(per_step):
        rows = rows_s[c * per_step + i]
        sm = jnp.concatenate([rows, jnp.zeros_like(rows)], axis=0).T
        last = jnp.broadcast_to(sm[CHUNK - 1 : CHUNK, :], (8, LANES))
        sources_t = twice(message.get(sources_ref, i, 0).T)
        decs, owns = [], []
        for j in range(PAIRS):
            dec = spread_pair(last, ECUM, j)
            scaled = message.get(first_ref, i, X + j).astype(f32) * spread_pair(sm, WEIGHT, j)
            own = mm_two(sources_t, *two_terms(scaled))
            state[j] = dec[0:1] * state[j] + own
            decays[j] = decays[j] * dec
            decs.append(dec)
            owns.append(own)
        made.append((rows, sm, decs, owns))
    for i, (rows, sm, decs, owns) in enumerate(made):
        smt_ref[:, lanes(i)] = rows
        sm_ref[i * CHUNK : (i + 1) * CHUNK, :] = sm
        for j in range(PAIRS):
            dec_ref[i, :, lanes(j)] = decs[j]
            own_ref[i, :, lanes(j)] = owns[j]
    for j in range(PAIRS):
        carry[:, lanes(j)] = state[j]
        whole_ref[:, lanes(j)] = decays[j]
        state_ref[:, lanes(j)] = state[j].astype(bf16)


def within_kernel(
    message, per_step,
    first_ref, sources_ref, readers_ref, sm_ref, smt_ref, own_ref, dec_ref, y_ref, start_ref, pre_ref, carry, pre,
):
    @pl.when(pl.program_id(0) == 0)
    def _():
        carry[...] = jnp.zeros_like(carry)
        pre[...] = jnp.ones_like(pre)

    t = lax.broadcasted_iota(jnp.int32, (CHUNK, CHUNK), 0)
    s = lax.broadcasted_iota(jnp.int32, (CHUNK, CHUNK), 1)
    made = []
    states = [carry[:, lanes(j)] for j in range(PAIRS)]
    before = pre[...]
    for i in range(per_step):
        rows = slice(i * CHUNK, (i + 1) * CHUNK)
        sm = sm_ref[rows, :]
        smt = smt_ref[:, lanes(i)]
        readers = message.get(readers_ref, i, 0)
        readers_twice = twice(readers)
        scores = jnp.where(t >= s, mm_nt(readers, message.get(sources_ref, i, 0)), 0.0)
        ys = []
        for j in range(PAIRS):
            weights = []
            for h in (2 * j, 2 * j + 1):
                here = sm[:, CUM * HEADS + h : CUM * HEADS + h + 1]
                there = smt[SHIFTED * HEADS + h : SHIFTED * HEADS + h + 1, :]
                weights.append(
                    (scores * jnp.exp(jnp.minimum(here - there, CLAMP))).astype(bf16)
                )
            values = split_pair(message.get(first_ref, i, X + j))
            within = mm(jnp.concatenate(weights, axis=1), values)
            carried = mm_two(readers_twice, *two_terms(states[j]))
            ys.append(within + spread_pair(sm, ECUM, j) * carried)
        made.append((ys, list(states), before))
        for j in range(PAIRS):
            states[j] = dec_ref[i, 0:1, lanes(j)] * states[j] + own_ref[i, :, lanes(j)]
        before = before * dec_ref[i]
    for i, (ys, starts, prefix) in enumerate(made):
        pre_ref[i] = prefix
        for j in range(PAIRS):
            y_ref[i * CHUNK : (i + 1) * CHUNK, lanes(j)] = ys[j]
            start_ref[i, :, lanes(j)] = starts[j]
    pre[...] = before
    for j in range(PAIRS):
        carry[:, lanes(j)] = states[j]


def mix_kernel(
    message, per_step,
    first_ref, readers_ref, second_ref, within_ref, sm_ref, inbound_ref, pre_ref, gain_ref, skip_ref,
    y_ref, sums_ref,
):
    made = []
    inbound = inbound_ref[...].astype(bf16)
    for i in range(per_step):
        rows = slice(i * CHUNK, (i + 1) * CHUNK)
        sm = sm_ref[rows, :]
        carried = mm(message.get(readers_ref, i, 0), inbound)
        power = jnp.zeros((CHUNK, LANES), f32)
        cross = jnp.zeros((CHUNK, LANES), f32)
        ys = []
        for j in range(PAIRS):
            at = lanes(j)
            decay = spread_pair(sm, ECUM, j) * pre_ref[i, 0:1, at]
            y = within_ref[rows, at] + decay * carried[:, at]
            ys.append(y)
            values = message.get(first_ref, i, X + j).astype(f32)
            gates = message.get(second_ref, i, Z + j).astype(f32)
            grad = message.get(second_ref, i, GRAD + j).astype(f32)
            gated = (y + skip_ref[0:1, at] * values) * (gates * sigmoid(gates))
            power = power + gated * gated
            cross = cross + grad * gain_ref[0:1, at] * gated
        made.append(
            (ys, jnp.sum(power.T, axis=0, keepdims=True), jnp.sum(cross.T, axis=0, keepdims=True))
        )
    for i, (ys, power, cross) in enumerate(made):
        for j in range(PAIRS):
            y_ref[i * CHUNK : (i + 1) * CHUNK, lanes(j)] = ys[j]
        sums_ref[i] = jnp.concatenate([power, cross, jnp.zeros((6, LANES), f32)], axis=0)


def norm_factors(sums):
    sums = sums * (1.0 / GROUP_WIDTH)
    inverse = lax.rsqrt(sums[0:1] + epsilon)
    pull = inverse * inverse * inverse * sums[1:2]
    return (
        jnp.broadcast_to(inverse, (CHUNK, LANES)).T,
        jnp.broadcast_to(pull, (CHUNK, LANES)).T,
    )


def norm_kernel(
    message, per_step,
    first_ref, readers_ref, second_ref, y_ref, sm_ref, pre_ref, sums_ref, other_ref, gain_ref, skip_ref,
    mixed_ref, back_ref, slab_ref,
    back_sum,
):
    @pl.when(pl.program_id(0) == 0)
    def _():
        back_sum[...] = jnp.zeros_like(back_sum)

    made = []
    sums = [back_sum[:, lanes(j)] for j in range(PAIRS)]
    for i in range(per_step):
        rows = slice(i * CHUNK, (i + 1) * CHUNK)
        sm = sm_ref[rows, :]
        readers_t = twice(message.get(readers_ref, i, 0).T)
        inverse, pull = norm_factors(sums_ref[i] + other_ref[i])
        for j in range(PAIRS):
            at = lanes(j)
            values = message.get(first_ref, i, X + j).astype(f32)
            gates = message.get(second_ref, i, Z + j).astype(f32)
            grad = message.get(second_ref, i, GRAD + j).astype(f32)
            silu = gates * sigmoid(gates)
            gated = (y_ref[rows, at] + skip_ref[0:1, at] * values) * silu
            d_mixed = (inverse * grad * gain_ref[0:1, at] - pull * gated) * silu
            back = mm_two(readers_t, *two_terms(d_mixed * spread_pair(sm, ECUM, j)))
            sums[j] = sums[j] + pre_ref[i, 0:1, at] * back
            made.append((i, j, d_mixed.astype(bf16), back))
    for i, j, d_mixed, back in made:
        mixed_ref[i * CHUNK : (i + 1) * CHUNK, lanes(j)] = d_mixed
        back_ref[i, :, lanes(j)] = back
    for j in range(PAIRS):
        back_sum[:, lanes(j)] = sums[j]
        slab_ref[:, lanes(j)] = sums[j].astype(bf16)


def local_kernel(
    message, per_step,
    first_ref, sources_ref, readers_ref, second_ref, y_ref, grad_ref, sm_ref, smt_ref, start_ref, pre_ref, inbound_ref,
    sums_ref, other_ref, gain_ref, skip_ref,
    values_out, sources_out, readers_out, gate_ref, e_ref, start_out, param_ref,
    gain_sum, skip_sum,
):
    c = pl.program_id(0)

    @pl.when(c == 0)
    def _():
        gain_sum[...] = jnp.zeros_like(gain_sum)
        skip_sum[...] = jnp.zeros_like(skip_sum)

    s = lax.broadcasted_iota(jnp.int32, (CHUNK, CHUNK), 0)
    t = lax.broadcasted_iota(jnp.int32, (CHUNK, CHUNK), 1)
    causal = t >= s
    ones = head_rows()
    ones_twice = twice(ones)
    made = []
    gains = [gain_sum[0:1, lanes(j)] for j in range(PAIRS)]
    skips = [skip_sum[0:1, lanes(j)] for j in range(PAIRS)]
    for i in range(per_step):
        rows = slice(i * CHUNK, (i + 1) * CHUNK)
        sm = sm_ref[rows, :]
        smt = smt_ref[:, lanes(i)]
        sources = message.get(sources_ref, i, 0)
        readers = message.get(readers_ref, i, 0)
        inverse, pull = norm_factors(sums_ref[i] + other_ref[i])
        scores = jnp.where(causal, mm_nt(sources, readers), 0.0)
        total = jnp.zeros((CHUNK, CHUNK), f32)
        d_values, d_gates, highs, lows, scaleds, starts = [], [], [], [], [], []
        for j in range(PAIRS):
            at = lanes(j)
            rounded = grad_ref[rows, at]
            grads = split_pair(rounded)
            x = message.get(first_ref, i, X + j)
            weight_grads = mm_nt(x, grads)
            weights = []
            for k, h in enumerate((2 * j, 2 * j + 1)):
                there = sm[:, SHIFTED * HEADS + h : SHIFTED * HEADS + h + 1]
                here = smt[CUM * HEADS + h : CUM * HEADS + h + 1, :]
                decay = jnp.exp(jnp.minimum(here - there, CLAMP))
                weights.append((scores * decay).astype(bf16))
                total = total + weight_grads[:, lanes(k)] * decay
            d_values.append(mm(jnp.concatenate(weights, axis=1), grads))

            values = x.astype(f32)
            gates = message.get(second_ref, i, Z + j).astype(f32)
            grad = message.get(second_ref, i, GRAD + j).astype(f32)
            y = y_ref[rows, at]
            mixed = y + skip_ref[0:1, at] * values
            sig = sigmoid(gates)
            silu = gates * sig
            gated = mixed * silu
            scaled = inverse * grad
            gains[j] = gains[j] + jnp.sum(scaled * gated, axis=0, keepdims=True)
            d_gated = scaled * gain_ref[0:1, at] - pull * gated
            d_gate = d_gated * mixed * (sig + silu * (1.0 - sig))
            d_gates.append(d_gate.astype(bf16))
            skips[j] = skips[j] + jnp.sum(values * (d_gated * silu), axis=0, keepdims=True)
            d_mixed = rounded.astype(f32)
            high, low = two_terms(d_mixed * y)
            highs.append(high)
            lows.append(low)
            scaleds.append((d_mixed * spread_pair(sm, ECUM, j)).astype(bf16))
            starts.append(
                start_ref[i, :, at] + pre_ref[i, 0:1, at] * inbound_ref[:, at].astype(f32)
            )
        e = sum_heads(ones_twice, highs, lows)
        total = jnp.where(causal, total, 0.0).astype(bf16)
        start = jnp.concatenate([part.astype(bf16) for part in starts], axis=1)
        d_readers = mm_tn(total, sources) + mm_nt(jnp.concatenate(scaleds, axis=1), start)
        made.append(
            (d_values, d_gates, starts, e[:HEADS], mm(total, readers), d_readers.astype(bf16))
        )
    for i, (d_values, d_gates, starts, e, d_sources, d_readers) in enumerate(made):
        rows = slice(i * CHUNK, (i + 1) * CHUNK)
        for j in range(PAIRS):
            values_out[rows, lanes(j)] = d_values[j]
            message.put(gate_ref, i, j, d_gates[j])
            start_out[i, :, lanes(j)] = starts[j]
        e_ref[:, lanes(i)] = e
        sources_out[rows, :] = d_sources
        message.put(readers_out, i, 0, d_readers)
    for j in range(PAIRS):
        gain_sum[0:1, lanes(j)] = gains[j]
        skip_sum[0:1, lanes(j)] = skips[j]

    @pl.when(c == pl.num_programs(0) - 1)
    def _():
        for j in range(PAIRS):
            param_ref[j : j + 1, :] = gain_sum[0:1, lanes(j)]
        high, low = two_terms(jnp.broadcast_to(skip_sum[0:1, :], (LANES, WIDTH)))
        skips = (mm_nt(high, ones) + mm_nt(low, ones))[0:1]
        param_ref[PAIRS : PAIRS + 1, :] = jnp.concatenate(
            [skips, jnp.zeros((1, LANES - 16), f32)], axis=1
        )
        param_ref[PAIRS + 1 :, :] = jnp.zeros((8 - PAIRS - 1, LANES), f32)


def last_kernel(
    message, per_step,
    first_ref, sources_ref, within_ref, d_sources_ref, d_readers_ref, gate_ref, grad_ref, e_ref, sm_ref, smt_ref, outer_ref,
    back_ref, start_ref, dec_ref, skip_ref, heads_ref, early_ref,
    out_ref,
    carry, sums, message_s, sent,
):
    c = pl.program_id(0)

    @pl.when(c == 0)
    def _():
        carry[...] = outer_ref[...].astype(f32)
        sums[...] = jnp.zeros_like(sums)

    r = message.rows
    ones = head_rows()
    ones_twice = twice(ones)
    before = lax.broadcasted_iota(jnp.int32, (CHUNK, CHUNK), 0)
    after = lax.broadcasted_iota(jnp.int32, (CHUNK, CHUNK), 1)
    earlier = jnp.where(before < after, 1.0, 0.0)
    decay_rate = jnp.exp(heads_ref[:HEADS, :])
    first_peer = (pl.num_programs(0) - 1 - c) * per_step * message.per_chunk
    span = per_step * message.per_chunk
    mine = message_s.at[pl.ds(first_peer, span)]

    def body_copy(step):
        peer = (pl.num_programs(0) - 1 - step) * span
        at = (pl.ds(peer, span), pl.ds(0, LAST * r))
        return pltpu.make_async_copy(message_s.at[at], out_ref.at[at], sent.at[step])

    made = []
    states = [carry[:, lanes(j)] for j in range(PAIRS)]
    logs_sum, steps_sum = sums[:HEADS, :], sums[HEADS:, :]
    for i in reversed(range(per_step)):
        rows = slice(i * CHUNK, (i + 1) * CHUNK)
        sm = sm_ref[rows, :]
        sources_twice = twice(message.get(sources_ref, i, 0))
        d_values, highs, lows, scaleds, rounded, fluxes = [], [], [], [], [], []
        for j in range(PAIRS):
            at = lanes(j)
            high, low = two_terms(states[j])
            rounded.append(high)
            values = message.get(first_ref, i, X + j).astype(f32)
            weight = spread_pair(sm, WEIGHT, j)
            grad = within_ref[rows, at] + weight * mm_two(sources_twice, high, low)
            skipped = skip_ref[0:1, at] * grad_ref[rows, at].astype(f32)
            d_values.append((grad + skipped).astype(bf16))
            high, low = two_terms(values * grad)
            highs.append(high)
            lows.append(low)
            scaleds.append((values * weight).astype(bf16))
            states[j] = dec_ref[i, 0:1, at] * states[j] + back_ref[i, :, at]
            fluxes.append(
                jnp.broadcast_to(
                    jnp.sum(start_ref[i, :, at] * states[j], axis=0, keepdims=True), (16, LANES)
                )
            )
        d_sources = d_sources_ref[rows, :] + mm_nt(
            jnp.concatenate(scaleds, axis=1), jnp.concatenate(rounded, axis=1)
        )
        g = sum_heads(ones_twice, highs, lows)[:HEADS]
        constant = sum_heads(ones_twice, *two_terms_each(fluxes))[:HEADS, 0:1]
        flux = constant + mm_exact(g - e_ref[:, lanes(i)], earlier)
        soft = smt_ref[DT * HEADS : (DT + 1) * HEADS, lanes(i)]
        rate = smt_ref[RATE * HEADS : (RATE + 1) * HEADS, lanes(i)]
        sig = smt_ref[SIG * HEADS : (SIG + 1) * HEADS, lanes(i)]
        steps = (g / soft - decay_rate * flux) * sig
        logs_sum = logs_sum + flux * rate
        steps_sum = steps_sum + steps
        steps = jnp.concatenate([steps, jnp.zeros_like(steps)], axis=0)
        made.append((i, d_values, d_sources.astype(bf16), steps))
    for i, d_values, d_sources, steps in made:
        for j in range(PAIRS):
            message.put(mine, i, LAST_X + j, d_values[j])
            message.put(mine, i, LAST_Z + j, message.get(gate_ref, i, j))
        message.put(mine, i, LAST_B, d_sources)
        message.put(mine, i, LAST_C, message.get(d_readers_ref, i, 0))
        for p in range(message.per_chunk):
            part = steps if p == 0 else pltpu.roll(steps, LANES - p * r, 1)
            mine[i * message.per_chunk + p, LAST * r : LAST * r + STEP_ROWS, :] = part.astype(bf16)
    for j in range(PAIRS):
        carry[:, lanes(j)] = states[j]
    sums[:HEADS, :] = logs_sum
    sums[HEADS:, :] = steps_sum
    body_copy(c).start()

    @pl.when(c == pl.num_programs(0) - 1)
    def _():
        late = []
        for k in range(2):
            column = jnp.sum(sums[k * HEADS : (k + 1) * HEADS, :], axis=1, keepdims=True)
            block = jnp.broadcast_to(column, (HEADS, LANES))
            block = jnp.concatenate([block, jnp.zeros((LANES - HEADS, LANES), f32)], axis=0)
            late += three_terms(block.T[0:1, :])
        late += [jnp.zeros((HEADS - 2 * TERMS, LANES), f32)]
        late = jnp.concatenate([jnp.zeros((HEADS, LANES), f32)] + late, axis=0)
        late = late.astype(bf16)
        early = three_terms(early_ref[:PAIRS, :]) + three_terms(early_ref[PAIRS : PAIRS + 1, :])
        early += [jnp.zeros((STEP_ROWS - TERMS * (PAIRS + 1), LANES), f32)]
        early = jnp.concatenate(early, axis=0).astype(bf16)
        own_rows = lax.broadcasted_iota(jnp.int32, (STEP_ROWS, LANES), 0) < HEADS

        def fill(peer, unused):
            steps_at = slice(LAST * r, LAST * r + STEP_ROWS)
            message_s[peer, steps_at, :] = jnp.where(own_rows, message_s[peer, steps_at, :], late)
            message_s[peer, LAST * r + STEP_ROWS :, :] = early
            return unused

        lax.fori_loop(0, message_s.shape[0], fill, 0)
        at = (slice(None), pl.ds(LAST * r, 2 * STEP_ROWS))
        steps = sent.shape[0] - 1
        tiles = pltpu.make_async_copy(message_s.at[at], out_ref.at[at], sent.at[steps])
        tiles.start()
        for step in range(steps):
            body_copy(step).wait()
        tiles.wait()


def finish(own_ref, other_ref, logs_ref, skip_ref, bias_ref, gain_ref):
    total = own_ref[...] + other_ref[...]
    count = logs_ref.shape[1]
    logs_ref[...] = total[0:1, :count]
    bias_ref[...] = total[1:2, :count]
    skip_ref[...] = total[2:3, :count]
    gain_ref[...] = total[8:]


def call(kernel, out_shape, flops, moved, grid=None, in_specs=None, out_specs=None, scratch=()):
    extra = {}
    if grid is not None:
        extra = dict(grid=grid, in_specs=in_specs, out_specs=out_specs)
    return pl.pallas_call(
        kernel,
        out_shape=out_shape,
        scratch_shapes=list(scratch),
        compiler_params=pltpu.CompilerParams(vmem_limit_bytes=16 * 1024 * 1024),
        cost_estimate=pl.CostEstimate(flops=flops, bytes_accessed=moved, transcendentals=0),
        **extra,
    )


def shifted(array, count, by):
    pairs = [(i, i + by) for i in range(count) if 0 <= i + by < count]
    return lax.ppermute(array, "slab", pairs)


def carry_over(state, decay, first_decay, count, sign):
    window, window_decay, step = state, decay, 1
    result = result_decay = None
    while step < count:
        arrived = shifted(window, count, sign * step)
        more = 2 * step < count
        if result is None:
            result = arrived
            if more:
                result_decay = first_decay
                window = (state.astype(f32) + decay[0:1] * arrived.astype(f32)).astype(bf16)
                window_decay = decay * first_decay
        else:
            if more:
                arrived_decay = shifted(window_decay, count, sign * step)
                window = (window.astype(f32) + window_decay[0:1] * arrived.astype(f32)).astype(bf16)
                window_decay = window_decay * arrived_decay
            result = result.astype(f32) + result_decay[0:1] * arrived.astype(f32)
            if more:
                result_decay = result_decay * arrived_decay
        step *= 2
    return jnp.zeros_like(state) if result is None else result


def two_parts(array, axis, count):
    step, other = 1, jnp.zeros_like(array)
    while step < count:
        array = array if step == 1 else array + other
        other = lax.ppermute(array, axis, [(i, i ^ step) for i in range(count)])
        step *= 2
    return array, other


def on_device(
    slab_count, sub_count, tensor_count,
    mixer_x, gate_z, b_matrix, c_matrix, raw_steps, decay_log, skip_gain, step_bias, norm_gain, out_grad,
):
    rows = mixer_x.shape[0]
    peers = sub_count * tensor_count
    tokens = rows * peers
    chunks = tokens // CHUNK
    per_step = min(2, chunks)
    grid = (chunks // per_step,)
    message = Message(rows)
    owners = [t * sub_count + s for s in range(sub_count) for t in range(tensor_count)]
    sub = lax.axis_index("sub")

    def struct(shape, kind=f32):
        return jax.ShapeDtypeStruct(shape, kind)

    def hbm(shape, kind=f32):
        return pltpu.HBM(shape, kind)

    def in_hbm(array):
        return pltpu.with_memory_space_constraint(array, pltpu.HBM)

    def exchange(array):
        return lax.all_to_all(array, ("sub", "tensor"), split_axis=0, concat_axis=0, tiled=True)

    own_logs = lax.dynamic_slice(decay_log, (sub * HEADS,), (HEADS,))
    own_bias = lax.dynamic_slice(step_bias, (sub * HEADS,), (HEADS,))
    own_skip = lax.dynamic_slice(skip_gain, (sub * HEADS,), (HEADS,))
    own_gain = lax.dynamic_slice(norm_gain, (sub * WIDTH,), (WIDTH,)).reshape(1, WIDTH)
    heads = jnp.broadcast_to(jnp.concatenate([own_logs, own_bias])[:, None], (2 * HEADS, LANES))
    skip_row = jnp.repeat(own_skip, HEAD_DIM).reshape(1, WIDTH)

    first_rows = FIRST * rows + STEP_ROWS
    second_rows = SECOND * rows
    last_rows = LAST * rows + 2 * STEP_ROWS

    def packed(kernel, height, arrays, whole_arrays=(), scratch=()):
        out = hbm((sub_count, tensor_count, height, LANES), bf16)
        moved = 4 * peers * height * LANES
        runs = 1
        parts = tensor_count * runs
        specs = [
            pl.BlockSpec((rows, a.shape[1] // parts), lambda t, k: (0, t * runs + k)) for a in arrays
        ] + [pl.BlockSpec(a.shape, lambda t, k: (0, 0)) for a in whole_arrays]
        out_spec = pl.BlockSpec((sub_count // runs, 1, height, LANES), lambda t, k: (k, t, 0, 0))
        made = call(kernel, out, 0, moved, (tensor_count, runs), specs, out_spec, scratch)(
            *(in_hbm(a) for a in (*arrays, *whole_arrays))
        )
        return made.reshape(peers, height, LANES)

    first = exchange(
        packed(
            pack_first, first_rows, (mixer_x, b_matrix, c_matrix), (raw_steps,),
            [pltpu.VMEM((LANES, LANES), f32)],
        )
    )
    tensor_rows = lax.broadcasted_iota(jnp.int32, (tensor_count, LANES), 0)
    mine = (tensor_rows == lax.axis_index("tensor")).astype(f32)
    half = first[:, HALF * rows : (HALF + 1) * rows, :]
    other_half = lax.ppermute(half, "sub", [(i, i ^ 1) for i in range(sub_count)])
    even = sub % 2 == 0
    sources, readers = jnp.where(even, half, other_half), jnp.where(even, other_half, half)
    gate_z, heads, skip_row, own_gain, mine = lax.optimization_barrier(
        (gate_z, heads, skip_row, own_gain, mine)
    )
    second = exchange(packed(pack_second, second_rows, (gate_z, out_grad)))

    def flow(kernel, shape_specs, flops, moved, in_specs, scratch=()):
        def body(*refs):
            return kernel(message, per_step, *refs)

        shapes = tuple(shape for shape, _ in shape_specs)
        specs = tuple(spec for _, spec in shape_specs)
        return call(body, shapes, flops, moved, grid, in_specs, specs, scratch)

    def spec(block, axis, down=False):
        def index(c):
            at = grid[0] - 1 - c if down else c
            return tuple(at if k == axis else 0 for k in range(len(block)))

        return pl.BlockSpec(block, index)

    span = per_step * CHUNK

    def specs_of(down):
        return dict(
            message=lambda height: spec((per_step * message.per_chunk, height, LANES), 0, down),
            token=lambda width: spec((span, width), 0, down),
            lane=lambda height: spec((height, span), 1, down),
            chunk=lambda *shape: spec((per_step,) + shape, 0, down),
        )

    up, dn = specs_of(False), specs_of(True)

    def whole(*shape):
        return pl.BlockSpec(shape, lambda c: (0,) * len(shape))

    unit = 2 * tokens * CHUNK * WIDTH
    size = tokens * WIDTH

    sm, smt, own, dec, state, decay = flow(
        state_kernel,
        [
            (hbm((tokens, LANES)), up["token"](LANES)),
            (hbm((KINDS * HEADS, tokens)), up["lane"](KINDS * HEADS)),
            (hbm((chunks, STATE, WIDTH)), up["chunk"](STATE, WIDTH)),
            (hbm((chunks, 8, WIDTH)), up["chunk"](8, WIDTH)),
            (struct((STATE, WIDTH), bf16), whole(STATE, WIDTH)),
            (struct((8, WIDTH)), whole(8, WIDTH)),
        ],
        2 * unit, size * 8,
        [
            up["message"](PAIRS * rows), up["message"](rows),
            pl.BlockSpec((peers, STEP_ROWS, LANES), lambda c: (0, FIRST * rows // STEP_ROWS, 0)),
            whole(2 * HEADS, LANES),
        ],
        [pltpu.VMEM((STATE, WIDTH), f32), pltpu.VMEM((chunks, KINDS * HEADS, LANES), f32)],
    )(first, sources, first, heads)

    before = after = None
    if slab_count > 2:
        before, after = shifted(decay, slab_count, 1), shifted(decay, slab_count, -1)
    inbound = carry_over(state, decay, before, slab_count, 1)

    within, starts, pre = flow(
        within_kernel,
        [
            (hbm((tokens, WIDTH)), up["token"](WIDTH)),
            (hbm((chunks, STATE, WIDTH)), up["chunk"](STATE, WIDTH)),
            (hbm((chunks, 8, WIDTH)), up["chunk"](8, WIDTH)),
        ],
        6 * unit, size * 16,
        [
            up["message"](PAIRS * rows), up["message"](rows), up["message"](rows),
            up["token"](LANES), up["lane"](KINDS * HEADS),
            up["chunk"](STATE, WIDTH), up["chunk"](8, WIDTH),
        ],
        [pltpu.VMEM((STATE, WIDTH), f32), pltpu.VMEM((8, WIDTH), f32)],
    )(first, sources, readers, in_hbm(sm), in_hbm(smt), in_hbm(own), in_hbm(dec))

    y, sums = flow(
        mix_kernel,
        [
            (struct((tokens, WIDTH)), up["token"](WIDTH)),
            (struct((chunks, 8, LANES)), up["chunk"](8, LANES)),
        ],
        unit, size * 16,
        [
            up["message"](PAIRS * rows), up["message"](rows), up["message"](second_rows),
            up["token"](WIDTH), up["token"](LANES), whole(STATE, WIDTH), up["chunk"](8, WIDTH),
            whole(1, WIDTH), whole(1, WIDTH),
        ],
    )(
        first, readers, in_hbm(second), in_hbm(within), in_hbm(sm), inbound, in_hbm(pre),
        own_gain, skip_row,
    )

    partner = lax.ppermute(sums, "sub", [(i, i ^ 1) for i in range(sub_count)])

    d_mixed, back, slab_back = flow(
        norm_kernel,
        [
            (struct((tokens, WIDTH), bf16), up["token"](WIDTH)),
            (struct((chunks, STATE, WIDTH)), up["chunk"](STATE, WIDTH)),
            (struct((STATE, WIDTH), bf16), whole(STATE, WIDTH)),
        ],
        2 * unit, size * 12,
        [
            up["message"](PAIRS * rows), up["message"](rows), up["message"](second_rows),
            up["token"](WIDTH), up["token"](LANES), up["chunk"](8, WIDTH), up["chunk"](8, LANES),
            up["chunk"](8, LANES), whole(1, WIDTH), whole(1, WIDTH),
        ],
        [pltpu.VMEM((STATE, WIDTH), f32)],
    )(first, readers, in_hbm(second), y, sm, in_hbm(pre), sums, partner, own_gain, skip_row)

    outer = carry_over(slab_back, decay, after, slab_count, -1)

    d_values, d_sources, d_readers, d_gates, e, starts, params = flow(
        local_kernel,
        [
            (struct((tokens, WIDTH)), up["token"](WIDTH)),
            (struct((tokens, STATE)), up["token"](STATE)),
            (struct((peers, rows, LANES), bf16), up["message"](rows)),
            (struct((peers, PAIRS * rows, LANES), bf16), up["message"](PAIRS * rows)),
            (struct((HEADS, tokens)), up["lane"](HEADS)),
            (struct((chunks, STATE, WIDTH)), up["chunk"](STATE, WIDTH)),
            (struct((8, LANES)), whole(8, LANES)),
        ],
        10 * unit, size * 16,
        [
            up["message"](PAIRS * rows), up["message"](rows), up["message"](rows),
            up["message"](second_rows), up["token"](WIDTH), up["token"](WIDTH), up["token"](LANES),
            up["lane"](KINDS * HEADS),
            up["chunk"](STATE, WIDTH), up["chunk"](8, WIDTH), whole(STATE, WIDTH),
            up["chunk"](8, LANES), up["chunk"](8, LANES), whole(1, WIDTH), whole(1, WIDTH),
        ],
        [pltpu.VMEM((8, WIDTH), f32), pltpu.VMEM((8, WIDTH), f32)],
    )(
        first, sources, readers, in_hbm(second), y, d_mixed, sm, smt, in_hbm(starts), in_hbm(pre), inbound,
        sums, partner, own_gain, skip_row,
    )

    (last,) = flow(
        last_kernel,
        [(hbm((peers, last_rows, LANES), bf16), pl.BlockSpec(memory_space=pl.ANY))],
        4 * unit, size * 16,
        [
            dn["message"](PAIRS * rows), dn["message"](rows), dn["token"](WIDTH), dn["token"](STATE),
            dn["message"](rows), dn["message"](PAIRS * rows),
            dn["token"](WIDTH), dn["lane"](HEADS), dn["token"](LANES), dn["lane"](KINDS * HEADS),
            whole(STATE, WIDTH), dn["chunk"](STATE, WIDTH), dn["chunk"](STATE, WIDTH),
            dn["chunk"](8, WIDTH), whole(1, WIDTH), whole(2 * HEADS, LANES), whole(8, LANES),
        ],
        [
            pltpu.VMEM((STATE, WIDTH), f32), pltpu.VMEM((2 * HEADS, LANES), f32),
            pltpu.VMEM((peers, last_rows, LANES), bf16),
            pltpu.SemaphoreType.DMA((grid[0] + 1,)),
        ],
    )(
        first, sources, d_values, d_sources, d_readers, d_gates, d_mixed, e, sm, smt, outer, back,
        starts, in_hbm(dec), skip_row, heads, params,
    )

    last_back = exchange(last)
    tile_at = LAST * rows // STEP_ROWS
    def tile(at):
        return pl.BlockSpec((peers, STEP_ROWS, LANES), lambda c: (0, at, 0))

    params = call(
        lambda *refs: unpack_params(sub_count, tensor_count, *refs),
        struct((8 + sub_count * PAIRS, LANES)),
        0, 4 * peers * STEP_ROWS * LANES, (1,),
        [tile(tile_at), tile(tile_at + 1), whole(tensor_count, LANES)],
        whole(8 + sub_count * PAIRS, LANES),
    )(last_back, last_back, mine)
    own_params, other_params = two_parts(params, "slab", slab_count)
    wide, narrow = struct((rows, CHANNELS), bf16), struct((rows, GROUPS * STATE), bf16)
    grad_x, grad_gates, grad_b, grad_c, grad_steps = call(
        lambda *refs: unpack(owners, *refs),
        (wide, wide, narrow, narrow, struct((rows, MIXER_HEADS), bf16)),
        0, 10 * rows * CHANNELS,
    )(last_back)
    row = struct((1, sub_count * HEADS))
    grad_logs, grad_skip, grad_bias, grad_gain = call(
        finish, (row, row, row, struct((sub_count * PAIRS, LANES))), 0, 1 << 16,
    )(own_params, other_params)
    return (
        grad_x,
        grad_gates,
        grad_b,
        grad_c,
        grad_steps,
        grad_logs.reshape(-1),
        grad_skip.reshape(-1),
        grad_bias.reshape(-1),
        grad_gain.reshape(-1),
    )


def solution(mesh):
    tensor_count = mesh.shape["tensor"]
    sub_count = OWNERS // tensor_count
    slab_count = mesh.shape["dp"] // sub_count
    devices = mesh.devices.reshape(slab_count, sub_count, tensor_count)
    split_mesh = Mesh(devices, ("slab", "sub", "tensor"))
    rows = P(("slab", "sub", "tensor"), None)
    param = P("tensor")

    def local(*arrays):
        return on_device(slab_count, sub_count, tensor_count, *arrays)

    return jax.shard_map(
        local,
        mesh=split_mesh,
        in_specs=(rows,) * 5 + (param,) * 4 + (rows,),
        out_specs=(rows,) * 5 + (param,) * 4,
        check_vma=False,
    )
```

```python
import jax
import jax.numpy as jnp
from jax import lax
from jax.experimental import pallas as pl
from jax.experimental.pallas import tpu as pltpu
from jax.sharding import Mesh
from jax.sharding import PartitionSpec as P

MIXER_HEADS = 128
HEAD_DIM = 64
STATE = 128
GROUPS = 8
CHANNELS = MIXER_HEADS * HEAD_DIM
HEADS = 8
WIDTH = HEADS * HEAD_DIM
GROUP_WIDTH = 2 * WIDTH
OWNERS = MIXER_HEADS // HEADS
LANES = 128
PAIRS = WIDTH // LANES
CHUNK = 128
STEP_ROWS = 16
epsilon = 1e-05
f32 = jnp.float32
bf16 = jnp.bfloat16

DT, CUM, WEIGHT, SHIFTED, ECUM, RATE, SIG = range(7)
KINDS = 8
CLAMP = 80.0


def mm(a, b):
    return jnp.dot(a, b, preferred_element_type=f32)


def mm_nt(a, b):
    return lax.dot_general(a, b, (((1,), (1,)), ((), ())), preferred_element_type=f32)


def mm_tn(a, b):
    return lax.dot_general(a, b, (((0,), (0,)), ((), ())), preferred_element_type=f32)


def mm_exact(a, b):
    return jnp.dot(a, b, precision=lax.Precision.HIGHEST, preferred_element_type=f32)


def two_terms(values):
    high = values.astype(bf16)
    return high, (values - high.astype(f32)).astype(bf16)


def two_terms_each(tiles):
    return zip(*(two_terms(tile) for tile in tiles))


def twice(a):
    return jnp.concatenate([a, a], axis=1)


def mm_two(a_twice, high, low):
    return mm(a_twice, jnp.concatenate([high, low], axis=0))


def sum_heads(ones_twice, highs, lows):
    return mm_nt(ones_twice, jnp.concatenate([*highs, *lows], axis=1))


def sigmoid(values):
    return 0.5 + 0.5 * jnp.tanh(0.5 * values)


def low_half(rows):
    return lax.broadcasted_iota(jnp.int32, (rows, LANES), 1) < HEAD_DIM


def spread_pair(values, kind, j):
    rows = values.shape[0]
    at = kind * HEADS + 2 * j
    return jnp.where(
        low_half(rows),
        jnp.broadcast_to(values[:, at : at + 1], (rows, LANES)),
        jnp.broadcast_to(values[:, at + 1 : at + 2], (rows, LANES)),
    )


def head_rows():
    row = lax.broadcasted_iota(jnp.int32, (16, WIDTH), 0)
    channel = lax.broadcasted_iota(jnp.int32, (16, WIDTH), 1) // HEAD_DIM
    return jnp.where(row == channel, 1.0, 0.0).astype(bf16)


def split_pair(block):
    low = low_half(block.shape[0])
    zero = jnp.zeros_like(block)
    return jnp.concatenate(
        [jnp.where(low, block, zero), jnp.where(low, zero, block)], axis=0
    )


def lanes(j):
    return slice(j * LANES, (j + 1) * LANES)


class Message:
    def __init__(self, rows):
        self.rows = rows
        self.per_chunk = CHUNK // rows

    def place(self, chunk, k):
        r = self.rows
        return (slice(chunk * self.per_chunk, (chunk + 1) * self.per_chunk), slice(k * r, (k + 1) * r))

    def get(self, ref, chunk, k):
        a, b = self.place(chunk, k)
        return ref[a, b, :].reshape(CHUNK, LANES)

    def put(self, ref, chunk, k, value):
        a, b = self.place(chunk, k)
        ref[a, b, :] = value.reshape(self.per_chunk, self.rows, LANES)


X, HALF = 0, PAIRS
FIRST = PAIRS + 1
Z, GRAD = 0, PAIRS
SECOND = 2 * PAIRS
LAST_X, LAST_Z, LAST_B, LAST_C = 0, PAIRS, 2 * PAIRS, 2 * PAIRS + 1
LAST = 2 * PAIRS + 2


def pack_first(x_ref, b_ref, c_ref, steps_ref, out_ref, by_head):
    r = x_ref.shape[0]
    step = pl.program_id(0) * pl.num_programs(1) + pl.program_id(1)
    subs = out_ref.shape[0]

    @pl.when(step == 0)
    def _():
        steps = steps_ref[...].astype(f32)
        by_head[...] = jnp.concatenate([steps, jnp.zeros((LANES - r, LANES), f32)], axis=0).T

    zero = jnp.zeros((STEP_ROWS - HEADS, LANES), f32)
    for s in range(subs):
        for j in range(PAIRS):
            out_ref[s, 0, j * r : (j + 1) * r, :] = x_ref[:, lanes(s * PAIRS + j)]
        half = b_ref if s % 2 == 0 else c_ref
        out_ref[s, 0, HALF * r : (HALF + 1) * r, :] = half[:, lanes(s // 2)]
        at = pl.multiple_of((step * subs + s) * HEADS, HEADS)
        mine = jnp.concatenate([by_head[pl.ds(at, HEADS), :], zero], axis=0)
        out_ref[s, 0, FIRST * r :, :] = mine.astype(bf16)


def pack_second(z_ref, grad_ref, out_ref):
    r = z_ref.shape[0]
    for s in range(out_ref.shape[0]):
        for j in range(PAIRS):
            at = lanes(s * PAIRS + j)
            out_ref[s, 0, (Z + j) * r : (Z + j + 1) * r, :] = z_ref[:, at]
            out_ref[s, 0, (GRAD + j) * r : (GRAD + j + 1) * r, :] = grad_ref[:, at]


def add_halves(owners, in_ref, block, out_ref):
    r = out_ref.shape[0]
    peer_of = {own: peer for peer, own in enumerate(owners)}
    for g in range(GROUPS):
        halves = [
            in_ref[peer_of[2 * g + k], block * r : (block + 1) * r, :].astype(f32) for k in range(2)
        ]
        out_ref[:, lanes(g)] = (halves[0] + halves[1]).astype(bf16)


def unpack(owners, in_ref, x_ref, z_ref, b_ref, c_ref, steps_ref):
    r = x_ref.shape[0]
    peer_of = {own: peer for peer, own in enumerate(owners)}
    for peer, own in enumerate(owners):
        for j in range(PAIRS):
            for block, ref in ((LAST_X, x_ref), (LAST_Z, z_ref)):
                at = slice((block + j) * r, (block + j + 1) * r)
                ref[:, lanes(own * PAIRS + j)] = in_ref[peer, at, :]
    add_halves(owners, in_ref, LAST_B, b_ref)
    add_halves(owners, in_ref, LAST_C, c_ref)
    by_head = jnp.concatenate(
        [
            in_ref[peer_of[own], LAST * r : LAST * r + STEP_ROWS, :].astype(f32)[:HEADS]
            for own in range(OWNERS)
        ],
        axis=0,
    )
    steps_ref[...] = by_head.T[:r, :].astype(bf16)


GAIN_ROW, SKIP_ROW, LOGS_ROW, BIAS_ROW = HEADS, HEADS + PAIRS, HEADS + PAIRS + 1, HEADS + PAIRS + 2


def unpack_params(sub_count, tensor_count, tile_ref, mine_ref, out_ref):
    lane = lax.broadcasted_iota(jnp.int32, (1, LANES), 1)
    totals = [jnp.zeros((1, LANES), f32) for _ in range(3)]
    for s in range(sub_count):
        rows = jnp.zeros((STEP_ROWS, LANES), f32)
        for t in range(tensor_count):
            mine = mine_ref[t : t + 1, :] > 0.0
            rows = jnp.where(mine, tile_ref[s * tensor_count + t].astype(f32), rows)
        for k, at in enumerate((LOGS_ROW, BIAS_ROW, SKIP_ROW)):
            part = jnp.where(lane < HEADS, rows[at : at + 1], 0.0)
            totals[k] = totals[k] + (part if s == 0 else pltpu.roll(part, s * HEADS, 1))
        out_ref[8 + s * PAIRS : 8 + (s + 1) * PAIRS, :] = rows[GAIN_ROW : GAIN_ROW + PAIRS]
    out_ref[:8, :] = jnp.concatenate(totals + [jnp.zeros((5, LANES), f32)], axis=0)


def state_kernel(
    message, per_step,
    first_ref, sources_ref, steps_ref, heads_ref, sm_ref, smt_ref, own_ref, dec_ref, state_ref, whole_ref,
    carry, rows_s,
):
    c = pl.program_id(0)

    @pl.when(c == 0)
    def _():
        carry[...] = jnp.zeros_like(carry)
        whole_ref[...] = jnp.ones_like(whole_ref)
        chunks = rows_s.shape[0]
        before = lax.broadcasted_iota(jnp.int32, (CHUNK, CHUNK), 0)
        after = lax.broadcasted_iota(jnp.int32, (CHUNK, CHUNK), 1)
        raws = []
        for k in range(chunks):
            raw = heads_ref[HEADS:, :]
            for p in range(message.per_chunk):
                part = steps_ref[k * message.per_chunk + p].astype(f32)[:HEADS]
                raw = raw + (part if p == 0 else pltpu.roll(part, p * message.rows, 1))
            raws.append(raw)
        raw = jnp.concatenate(raws, axis=0)
        small = jnp.exp(-jnp.abs(raw))
        series = small * (
            1.0 - small * (0.5 - small * (1.0 / 3 - small * (0.25 - small * 0.2)))
        )
        soft = jnp.maximum(raw, 0.0) + jnp.where(small < 0.015625, series, jnp.log(1.0 + small))
        sig = jnp.where(raw >= 0.0, 1.0, small) / (1.0 + small)
        decay_rate = jnp.concatenate([jnp.exp(heads_ref[:HEADS, :])] * chunks, axis=0)
        rate = -decay_rate * soft
        cum = mm_exact(rate, jnp.where(before <= after, 1.0, 0.0))
        rest = mm_exact(rate, jnp.where(before > after, 1.0, 0.0))
        kinds = [
            soft, cum, soft * jnp.exp(rest), cum - jnp.log(soft), jnp.exp(cum), rate, sig,
            jnp.zeros_like(soft),
        ]
        for k in range(chunks):
            at = slice(k * HEADS, (k + 1) * HEADS)
            rows_s[k] = jnp.concatenate([kind[at] for kind in kinds], axis=0)

    made = []
    state = [carry[:, lanes(j)] for j in range(PAIRS)]
    decays = [whole_ref[:, lanes(j)] for j in range(PAIRS)]
    for i in range(per_step):
        rows = rows_s[c * per_step + i]
        sm = jnp.concatenate([rows, jnp.zeros_like(rows)], axis=0).T
        last = jnp.broadcast_to(sm[CHUNK - 1 : CHUNK, :], (8, LANES))
        sources_t = twice(message.get(sources_ref, i, 0).T)
        decs, owns = [], []
        for j in range(PAIRS):
            dec = spread_pair(last, ECUM, j)
            scaled = message.get(first_ref, i, X + j).astype(f32) * spread_pair(sm, WEIGHT, j)
            own = mm_two(sources_t, *two_terms(scaled))
            state[j] = dec[0:1] * state[j] + own
            decays[j] = decays[j] * dec
            decs.append(dec)
            owns.append(own)
        made.append((rows, sm, decs, owns))
    for i, (rows, sm, decs, owns) in enumerate(made):
        smt_ref[:, lanes(i)] = rows
        sm_ref[i * CHUNK : (i + 1) * CHUNK, :] = sm
        for j in range(PAIRS):
            dec_ref[i, :, lanes(j)] = decs[j]
            own_ref[i, :, lanes(j)] = owns[j]
    for j in range(PAIRS):
        carry[:, lanes(j)] = state[j]
        whole_ref[:, lanes(j)] = decays[j]
        state_ref[:, lanes(j)] = state[j].astype(bf16)


def within_kernel(
    message, per_step,
    first_ref, sources_ref, readers_ref, sm_ref, smt_ref, own_ref, dec_ref, y_ref, start_ref, pre_ref, carry, pre,
):
    @pl.when(pl.program_id(0) == 0)
    def _():
        carry[...] = jnp.zeros_like(carry)
        pre[...] = jnp.ones_like(pre)

    t = lax.broadcasted_iota(jnp.int32, (CHUNK, CHUNK), 0)
    s = lax.broadcasted_iota(jnp.int32, (CHUNK, CHUNK), 1)
    made = []
    states = [carry[:, lanes(j)] for j in range(PAIRS)]
    before = pre[...]
    for i in range(per_step):
        rows = slice(i * CHUNK, (i + 1) * CHUNK)
        sm = sm_ref[rows, :]
        smt = smt_ref[:, lanes(i)]
        readers = message.get(readers_ref, i, 0)
        readers_twice = twice(readers)
        scores = jnp.where(t >= s, mm_nt(readers, message.get(sources_ref, i, 0)), 0.0)
        ys = []
        for j in range(PAIRS):
            weights = []
            for h in (2 * j, 2 * j + 1):
                here = sm[:, CUM * HEADS + h : CUM * HEADS + h + 1]
                there = smt[SHIFTED * HEADS + h : SHIFTED * HEADS + h + 1, :]
                weights.append(
                    (scores * jnp.exp(jnp.minimum(here - there, CLAMP))).astype(bf16)
                )
            values = split_pair(message.get(first_ref, i, X + j))
            within = mm(jnp.concatenate(weights, axis=1), values)
            carried = mm_two(readers_twice, *two_terms(states[j]))
            ys.append(within + spread_pair(sm, ECUM, j) * carried)
        made.append((ys, list(states), before))
        for j in range(PAIRS):
            states[j] = dec_ref[i, 0:1, lanes(j)] * states[j] + own_ref[i, :, lanes(j)]
        before = before * dec_ref[i]
    for i, (ys, starts, prefix) in enumerate(made):
        pre_ref[i] = prefix
        for j in range(PAIRS):
            y_ref[i * CHUNK : (i + 1) * CHUNK, lanes(j)] = ys[j]
            start_ref[i, :, lanes(j)] = starts[j]
    pre[...] = before
    for j in range(PAIRS):
        carry[:, lanes(j)] = states[j]


def mix_kernel(
    message, per_step,
    first_ref, readers_ref, second_ref, within_ref, sm_ref, inbound_ref, pre_ref, gain_ref, skip_ref,
    y_ref, sums_ref, second_out,
):
    second_out[...] = second_ref[...]
    made = []
    inbound = inbound_ref[...].astype(bf16)
    for i in range(per_step):
        rows = slice(i * CHUNK, (i + 1) * CHUNK)
        sm = sm_ref[rows, :]
        carried = mm(message.get(readers_ref, i, 0), inbound)
        power = jnp.zeros((CHUNK, LANES), f32)
        cross = jnp.zeros((CHUNK, LANES), f32)
        ys = []
        for j in range(PAIRS):
            at = lanes(j)
            decay = spread_pair(sm, ECUM, j) * pre_ref[i, 0:1, at]
            y = within_ref[rows, at] + decay * carried[:, at]
            ys.append(y)
            values = message.get(first_ref, i, X + j).astype(f32)
            gates = message.get(second_ref, i, Z + j).astype(f32)
            grad = message.get(second_ref, i, GRAD + j).astype(f32)
            gated = (y + skip_ref[0:1, at] * values) * (gates * sigmoid(gates))
            power = power + gated * gated
            cross = cross + grad * gain_ref[0:1, at] * gated
        made.append(
            (ys, jnp.sum(power.T, axis=0, keepdims=True), jnp.sum(cross.T, axis=0, keepdims=True))
        )
    for i, (ys, power, cross) in enumerate(made):
        for j in range(PAIRS):
            y_ref[i * CHUNK : (i + 1) * CHUNK, lanes(j)] = ys[j]
        sums_ref[i] = jnp.concatenate([power, cross, jnp.zeros((6, LANES), f32)], axis=0)


def norm_factors(sums):
    sums = sums * (1.0 / GROUP_WIDTH)
    inverse = lax.rsqrt(sums[0:1] + epsilon)
    pull = inverse * inverse * inverse * sums[1:2]
    return (
        jnp.broadcast_to(inverse, (CHUNK, LANES)).T,
        jnp.broadcast_to(pull, (CHUNK, LANES)).T,
    )


def norm_kernel(
    message, per_step,
    first_ref, readers_ref, second_ref, y_ref, sm_ref, pre_ref, sums_ref, other_ref, gain_ref, skip_ref,
    mixed_ref, back_ref, slab_ref,
    back_sum,
):
    @pl.when(pl.program_id(0) == 0)
    def _():
        back_sum[...] = jnp.zeros_like(back_sum)

    made = []
    sums = [back_sum[:, lanes(j)] for j in range(PAIRS)]
    for i in range(per_step):
        rows = slice(i * CHUNK, (i + 1) * CHUNK)
        sm = sm_ref[rows, :]
        readers_t = twice(message.get(readers_ref, i, 0).T)
        inverse, pull = norm_factors(sums_ref[i] + other_ref[i])
        for j in range(PAIRS):
            at = lanes(j)
            values = message.get(first_ref, i, X + j).astype(f32)
            gates = message.get(second_ref, i, Z + j).astype(f32)
            grad = message.get(second_ref, i, GRAD + j).astype(f32)
            silu = gates * sigmoid(gates)
            gated = (y_ref[rows, at] + skip_ref[0:1, at] * values) * silu
            d_mixed = (inverse * grad * gain_ref[0:1, at] - pull * gated) * silu
            back = mm_two(readers_t, *two_terms(d_mixed * spread_pair(sm, ECUM, j)))
            sums[j] = sums[j] + pre_ref[i, 0:1, at] * back
            made.append((i, j, d_mixed.astype(bf16), back))
    for i, j, d_mixed, back in made:
        mixed_ref[i * CHUNK : (i + 1) * CHUNK, lanes(j)] = d_mixed
        back_ref[i, :, lanes(j)] = back
    for j in range(PAIRS):
        back_sum[:, lanes(j)] = sums[j]
        slab_ref[:, lanes(j)] = sums[j].astype(bf16)


def local_kernel(
    message, per_step,
    first_ref, sources_ref, readers_ref, second_ref, y_ref, grad_ref, sm_ref, smt_ref, start_ref, pre_ref, inbound_ref,
    sums_ref, other_ref, gain_ref, skip_ref,
    values_out, sources_out, readers_out, gate_ref, e_ref, start_out, param_ref,
    gain_sum, skip_sum,
):
    c = pl.program_id(0)

    @pl.when(c == 0)
    def _():
        gain_sum[...] = jnp.zeros_like(gain_sum)
        skip_sum[...] = jnp.zeros_like(skip_sum)

    s = lax.broadcasted_iota(jnp.int32, (CHUNK, CHUNK), 0)
    t = lax.broadcasted_iota(jnp.int32, (CHUNK, CHUNK), 1)
    causal = t >= s
    ones = head_rows()
    ones_twice = twice(ones)
    made = []
    gains = [gain_sum[0:1, lanes(j)] for j in range(PAIRS)]
    skips = [skip_sum[0:1, lanes(j)] for j in range(PAIRS)]
    for i in range(per_step):
        rows = slice(i * CHUNK, (i + 1) * CHUNK)
        sm = sm_ref[rows, :]
        smt = smt_ref[:, lanes(i)]
        sources = message.get(sources_ref, i, 0)
        readers = message.get(readers_ref, i, 0)
        inverse, pull = norm_factors(sums_ref[i] + other_ref[i])
        scores = jnp.where(causal, mm_nt(sources, readers), 0.0)
        total = jnp.zeros((CHUNK, CHUNK), f32)
        d_values, d_gates, highs, lows, scaleds, starts = [], [], [], [], [], []
        for j in range(PAIRS):
            at = lanes(j)
            rounded = grad_ref[rows, at]
            grads = split_pair(rounded)
            x = message.get(first_ref, i, X + j)
            weight_grads = mm_nt(x, grads)
            weights = []
            for k, h in enumerate((2 * j, 2 * j + 1)):
                there = sm[:, SHIFTED * HEADS + h : SHIFTED * HEADS + h + 1]
                here = smt[CUM * HEADS + h : CUM * HEADS + h + 1, :]
                decay = jnp.exp(jnp.minimum(here - there, CLAMP))
                weights.append((scores * decay).astype(bf16))
                total = total + weight_grads[:, lanes(k)] * decay
            d_values.append(mm(jnp.concatenate(weights, axis=1), grads))

            values = x.astype(f32)
            gates = message.get(second_ref, i, Z + j).astype(f32)
            grad = message.get(second_ref, i, GRAD + j).astype(f32)
            y = y_ref[rows, at]
            mixed = y + skip_ref[0:1, at] * values
            sig = sigmoid(gates)
            silu = gates * sig
            gated = mixed * silu
            scaled = inverse * grad
            gains[j] = gains[j] + jnp.sum(scaled * gated, axis=0, keepdims=True)
            d_gated = scaled * gain_ref[0:1, at] - pull * gated
            d_gate = d_gated * mixed * (sig + silu * (1.0 - sig))
            d_gates.append(d_gate.astype(bf16))
            skips[j] = skips[j] + jnp.sum(values * (d_gated * silu), axis=0, keepdims=True)
            d_mixed = rounded.astype(f32)
            high, low = two_terms(d_mixed * y)
            highs.append(high)
            lows.append(low)
            scaleds.append((d_mixed * spread_pair(sm, ECUM, j)).astype(bf16))
            starts.append(
                start_ref[i, :, at] + pre_ref[i, 0:1, at] * inbound_ref[:, at].astype(f32)
            )
        e = sum_heads(ones_twice, highs, lows)
        total = jnp.where(causal, total, 0.0).astype(bf16)
        start = jnp.concatenate([part.astype(bf16) for part in starts], axis=1)
        d_readers = mm_tn(total, sources) + mm_nt(jnp.concatenate(scaleds, axis=1), start)
        made.append(
            (d_values, d_gates, starts, e[:HEADS], mm(total, readers), d_readers.astype(bf16))
        )
    for i, (d_values, d_gates, starts, e, d_sources, d_readers) in enumerate(made):
        rows = slice(i * CHUNK, (i + 1) * CHUNK)
        for j in range(PAIRS):
            values_out[rows, lanes(j)] = d_values[j]
            message.put(gate_ref, i, j, d_gates[j])
            start_out[i, :, lanes(j)] = starts[j]
        e_ref[:, lanes(i)] = e
        sources_out[rows, :] = d_sources
        message.put(readers_out, i, 0, d_readers)
    for j in range(PAIRS):
        gain_sum[0:1, lanes(j)] = gains[j]
        skip_sum[0:1, lanes(j)] = skips[j]

    @pl.when(c == pl.num_programs(0) - 1)
    def _():
        for j in range(PAIRS):
            param_ref[j : j + 1, :] = gain_sum[0:1, lanes(j)]
        high, low = two_terms(jnp.broadcast_to(skip_sum[0:1, :], (LANES, WIDTH)))
        skips = (mm_nt(high, ones) + mm_nt(low, ones))[0:1]
        param_ref[PAIRS : PAIRS + 1, :] = jnp.concatenate(
            [skips, jnp.zeros((1, LANES - 16), f32)], axis=1
        )
        param_ref[PAIRS + 1 :, :] = jnp.zeros((8 - PAIRS - 1, LANES), f32)


def last_kernel(
    message, per_step,
    first_ref, sources_ref, within_ref, d_sources_ref, d_readers_ref, gate_ref, grad_ref, e_ref, sm_ref, smt_ref, outer_ref,
    back_ref, start_ref, dec_ref, skip_ref, heads_ref, early_ref,
    out_ref,
    carry, sums, message_s, sent,
):
    c = pl.program_id(0)

    @pl.when(c == 0)
    def _():
        carry[...] = outer_ref[...].astype(f32)
        sums[...] = jnp.zeros_like(sums)

    r = message.rows
    ones = head_rows()
    ones_twice = twice(ones)
    before = lax.broadcasted_iota(jnp.int32, (CHUNK, CHUNK), 0)
    after = lax.broadcasted_iota(jnp.int32, (CHUNK, CHUNK), 1)
    earlier = jnp.where(before < after, 1.0, 0.0)
    decay_rate = jnp.exp(heads_ref[:HEADS, :])
    first_peer = (pl.num_programs(0) - 1 - c) * per_step * message.per_chunk
    span = per_step * message.per_chunk
    mine = message_s.at[pl.ds(first_peer, span)]

    def body_copy(step):
        peer = (pl.num_programs(0) - 1 - step) * span
        at = (pl.ds(peer, span), pl.ds(0, LAST * r))
        return pltpu.make_async_copy(message_s.at[at], out_ref.at[at], sent.at[step])

    made = []
    states = [carry[:, lanes(j)] for j in range(PAIRS)]
    logs_sum, steps_sum = sums[:HEADS, :], sums[HEADS:, :]
    for i in reversed(range(per_step)):
        rows = slice(i * CHUNK, (i + 1) * CHUNK)
        sm = sm_ref[rows, :]
        sources_twice = twice(message.get(sources_ref, i, 0))
        d_values, highs, lows, scaleds, rounded, fluxes = [], [], [], [], [], []
        for j in range(PAIRS):
            at = lanes(j)
            high, low = two_terms(states[j])
            rounded.append(high)
            values = message.get(first_ref, i, X + j).astype(f32)
            weight = spread_pair(sm, WEIGHT, j)
            grad = within_ref[rows, at] + weight * mm_two(sources_twice, high, low)
            skipped = skip_ref[0:1, at] * grad_ref[rows, at].astype(f32)
            d_values.append((grad + skipped).astype(bf16))
            high, low = two_terms(values * grad)
            highs.append(high)
            lows.append(low)
            scaleds.append((values * weight).astype(bf16))
            states[j] = dec_ref[i, 0:1, at] * states[j] + back_ref[i, :, at]
            fluxes.append(
                jnp.broadcast_to(
                    jnp.sum(start_ref[i, :, at] * states[j], axis=0, keepdims=True), (16, LANES)
                )
            )
        d_sources = d_sources_ref[rows, :] + mm_nt(
            jnp.concatenate(scaleds, axis=1), jnp.concatenate(rounded, axis=1)
        )
        g = sum_heads(ones_twice, highs, lows)[:HEADS]
        constant = sum_heads(ones_twice, *two_terms_each(fluxes))[:HEADS, 0:1]
        flux = constant + mm_exact(g - e_ref[:, lanes(i)], earlier)
        soft = smt_ref[DT * HEADS : (DT + 1) * HEADS, lanes(i)]
        rate = smt_ref[RATE * HEADS : (RATE + 1) * HEADS, lanes(i)]
        sig = smt_ref[SIG * HEADS : (SIG + 1) * HEADS, lanes(i)]
        steps = (g / soft - decay_rate * flux) * sig
        logs_sum = logs_sum + flux * rate
        steps_sum = steps_sum + steps
        steps = jnp.concatenate([steps, jnp.zeros_like(steps)], axis=0)
        made.append((i, d_values, d_sources.astype(bf16), steps))
    for i, d_values, d_sources, steps in made:
        for j in range(PAIRS):
            message.put(mine, i, LAST_X + j, d_values[j])
            message.put(mine, i, LAST_Z + j, message.get(gate_ref, i, j))
        message.put(mine, i, LAST_B, d_sources)
        message.put(mine, i, LAST_C, message.get(d_readers_ref, i, 0))
        for p in range(message.per_chunk):
            part = steps if p == 0 else pltpu.roll(steps, LANES - p * r, 1)
            mine[i * message.per_chunk + p, LAST * r : LAST * r + STEP_ROWS, :] = part.astype(bf16)
    for j in range(PAIRS):
        carry[:, lanes(j)] = states[j]
    sums[:HEADS, :] = logs_sum
    sums[HEADS:, :] = steps_sum
    body_copy(c).start()

    @pl.when(c == pl.num_programs(0) - 1)
    def _():
        late = []
        for k in range(2):
            column = jnp.sum(sums[k * HEADS : (k + 1) * HEADS, :], axis=1, keepdims=True)
            block = jnp.broadcast_to(column, (HEADS, LANES))
            block = jnp.concatenate([block, jnp.zeros((LANES - HEADS, LANES), f32)], axis=0)
            late.append(block.T[0:1, :])
        small = [
            jnp.zeros((HEADS, LANES), f32), early_ref[: PAIRS + 1, :], *late,
            jnp.zeros((STEP_ROWS - BIAS_ROW - 1, LANES), f32),
        ]
        small = jnp.concatenate(small, axis=0).astype(bf16)
        own_rows = lax.broadcasted_iota(jnp.int32, (STEP_ROWS, LANES), 0) < HEADS

        def fill(peer, unused):
            steps_at = slice(LAST * r, LAST * r + STEP_ROWS)
            message_s[peer, steps_at, :] = jnp.where(own_rows, message_s[peer, steps_at, :], small)
            return unused

        lax.fori_loop(0, message_s.shape[0], fill, 0)
        at = (slice(None), pl.ds(LAST * r, STEP_ROWS))
        steps = sent.shape[0] - 1
        tiles = pltpu.make_async_copy(message_s.at[at], out_ref.at[at], sent.at[steps])
        tiles.start()
        for step in range(steps):
            body_copy(step).wait()
        tiles.wait()


def finish(own_ref, other_ref, logs_ref, skip_ref, bias_ref, gain_ref):
    total = own_ref[...] + other_ref[...]
    count = logs_ref.shape[1]
    logs_ref[...] = total[0:1, :count]
    bias_ref[...] = total[1:2, :count]
    skip_ref[...] = total[2:3, :count]
    gain_ref[...] = total[8:]


def call(kernel, out_shape, flops, moved, grid=None, in_specs=None, out_specs=None, scratch=()):
    extra = {}
    if grid is not None:
        extra = dict(grid=grid, in_specs=in_specs, out_specs=out_specs)
    return pl.pallas_call(
        kernel,
        out_shape=out_shape,
        scratch_shapes=list(scratch),
        compiler_params=pltpu.CompilerParams(vmem_limit_bytes=16 * 1024 * 1024),
        cost_estimate=pl.CostEstimate(flops=flops, bytes_accessed=moved, transcendentals=0),
        **extra,
    )


def shifted(array, count, by):
    pairs = [(i, i + by) for i in range(count) if 0 <= i + by < count]
    return lax.ppermute(array, "slab", pairs)


def carry_over(state, decay, first_decay, count, sign):
    window, window_decay, step = state, decay, 1
    result = result_decay = None
    while step < count:
        arrived = shifted(window, count, sign * step)
        more = 2 * step < count
        if result is None:
            result = arrived
            if more:
                result_decay = first_decay
                window = (state.astype(f32) + decay[0:1] * arrived.astype(f32)).astype(bf16)
                window_decay = decay * first_decay
        else:
            if more:
                arrived_decay = shifted(window_decay, count, sign * step)
                window = (window.astype(f32) + window_decay[0:1] * arrived.astype(f32)).astype(bf16)
                window_decay = window_decay * arrived_decay
            result = result.astype(f32) + result_decay[0:1] * arrived.astype(f32)
            if more:
                result_decay = result_decay * arrived_decay
        step *= 2
    return jnp.zeros_like(state) if result is None else result


def two_parts(array, axis, count):
    step, other = 1, jnp.zeros_like(array)
    while step < count:
        array = array if step == 1 else array + other
        other = lax.ppermute(array, axis, [(i, i ^ step) for i in range(count)])
        step *= 2
    return array, other


def on_device(
    slab_count, sub_count, tensor_count,
    mixer_x, gate_z, b_matrix, c_matrix, raw_steps, decay_log, skip_gain, step_bias, norm_gain, out_grad,
):
    rows = mixer_x.shape[0]
    peers = sub_count * tensor_count
    tokens = rows * peers
    chunks = tokens // CHUNK
    per_step = min(2, chunks)
    grid = (chunks // per_step,)
    message = Message(rows)
    owners = [t * sub_count + s for s in range(sub_count) for t in range(tensor_count)]
    sub = lax.axis_index("sub")

    def struct(shape, kind=f32):
        return jax.ShapeDtypeStruct(shape, kind)

    def hbm(shape, kind=f32):
        return pltpu.HBM(shape, kind)

    def in_hbm(array):
        return pltpu.with_memory_space_constraint(array, pltpu.HBM)

    def exchange(array):
        return lax.all_to_all(array, ("sub", "tensor"), split_axis=0, concat_axis=0, tiled=True)

    own_logs = lax.dynamic_slice(decay_log, (sub * HEADS,), (HEADS,))
    own_bias = lax.dynamic_slice(step_bias, (sub * HEADS,), (HEADS,))
    own_skip = lax.dynamic_slice(skip_gain, (sub * HEADS,), (HEADS,))
    own_gain = lax.dynamic_slice(norm_gain, (sub * WIDTH,), (WIDTH,)).reshape(1, WIDTH)
    heads = jnp.broadcast_to(jnp.concatenate([own_logs, own_bias])[:, None], (2 * HEADS, LANES))
    skip_row = jnp.repeat(own_skip, HEAD_DIM).reshape(1, WIDTH)

    first_rows = FIRST * rows + STEP_ROWS
    second_rows = SECOND * rows
    last_rows = LAST * rows + STEP_ROWS

    def packed(kernel, height, arrays, whole_arrays=(), scratch=()):
        out = hbm((sub_count, tensor_count, height, LANES), bf16)
        moved = 4 * peers * height * LANES
        runs = 1
        parts = tensor_count * runs
        specs = [
            pl.BlockSpec((rows, a.shape[1] // parts), lambda t, k: (0, t * runs + k)) for a in arrays
        ] + [pl.BlockSpec(a.shape, lambda t, k: (0, 0)) for a in whole_arrays]
        out_spec = pl.BlockSpec((sub_count // runs, 1, height, LANES), lambda t, k: (k, t, 0, 0))
        made = call(kernel, out, 0, moved, (tensor_count, runs), specs, out_spec, scratch)(
            *(in_hbm(a) for a in (*arrays, *whole_arrays))
        )
        return made.reshape(peers, height, LANES)

    first = exchange(
        packed(
            pack_first, first_rows, (mixer_x, b_matrix, c_matrix), (raw_steps,),
            [pltpu.VMEM((LANES, LANES), f32)],
        )
    )
    tensor_rows = lax.broadcasted_iota(jnp.int32, (tensor_count, LANES), 0)
    mine = (tensor_rows == lax.axis_index("tensor")).astype(f32)
    half = first[:, HALF * rows : (HALF + 1) * rows, :]
    other_half = lax.ppermute(half, "sub", [(i, i ^ 1) for i in range(sub_count)])
    even = sub % 2 == 0
    sources, readers = jnp.where(even, half, other_half), jnp.where(even, other_half, half)
    gate_z, heads, skip_row, own_gain, mine = lax.optimization_barrier(
        (gate_z, heads, skip_row, own_gain, mine)
    )
    second = exchange(packed(pack_second, second_rows, (gate_z, out_grad)))

    def flow(kernel, shape_specs, flops, moved, in_specs, scratch=()):
        def body(*refs):
            return kernel(message, per_step, *refs)

        shapes = tuple(shape for shape, _ in shape_specs)
        specs = tuple(spec for _, spec in shape_specs)
        return call(body, shapes, flops, moved, grid, in_specs, specs, scratch)

    def spec(block, axis, down=False):
        def index(c):
            at = grid[0] - 1 - c if down else c
            return tuple(at if k == axis else 0 for k in range(len(block)))

        return pl.BlockSpec(block, index)

    span = per_step * CHUNK

    def specs_of(down):
        return dict(
            message=lambda height: spec((per_step * message.per_chunk, height, LANES), 0, down),
            token=lambda width: spec((span, width), 0, down),
            lane=lambda height: spec((height, span), 1, down),
            chunk=lambda *shape: spec((per_step,) + shape, 0, down),
        )

    up, dn = specs_of(False), specs_of(True)

    def whole(*shape):
        return pl.BlockSpec(shape, lambda c: (0,) * len(shape))

    unit = 2 * tokens * CHUNK * WIDTH
    size = tokens * WIDTH

    sm, smt, own, dec, state, decay = flow(
        state_kernel,
        [
            (hbm((tokens, LANES)), up["token"](LANES)),
            (hbm((KINDS * HEADS, tokens)), up["lane"](KINDS * HEADS)),
            (hbm((chunks, STATE, WIDTH)), up["chunk"](STATE, WIDTH)),
            (hbm((chunks, 8, WIDTH)), up["chunk"](8, WIDTH)),
            (struct((STATE, WIDTH), bf16), whole(STATE, WIDTH)),
            (struct((8, WIDTH)), whole(8, WIDTH)),
        ],
        2 * unit, size * 8,
        [
            up["message"](PAIRS * rows), up["message"](rows),
            pl.BlockSpec((peers, STEP_ROWS, LANES), lambda c: (0, FIRST * rows // STEP_ROWS, 0)),
            whole(2 * HEADS, LANES),
        ],
        [pltpu.VMEM((STATE, WIDTH), f32), pltpu.VMEM((chunks, KINDS * HEADS, LANES), f32)],
    )(first, sources, first, heads)

    before = after = None
    if slab_count > 2:
        before, after = shifted(decay, slab_count, 1), shifted(decay, slab_count, -1)
    inbound = carry_over(state, decay, before, slab_count, 1)

    within, starts, pre = flow(
        within_kernel,
        [
            (hbm((tokens, WIDTH)), up["token"](WIDTH)),
            (hbm((chunks, STATE, WIDTH)), up["chunk"](STATE, WIDTH)),
            (hbm((chunks, 8, WIDTH)), up["chunk"](8, WIDTH)),
        ],
        6 * unit, size * 16,
        [
            up["message"](PAIRS * rows), up["message"](rows), up["message"](rows),
            up["token"](LANES), up["lane"](KINDS * HEADS),
            up["chunk"](STATE, WIDTH), up["chunk"](8, WIDTH),
        ],
        [pltpu.VMEM((STATE, WIDTH), f32), pltpu.VMEM((8, WIDTH), f32)],
    )(first, sources, readers, in_hbm(sm), in_hbm(smt), in_hbm(own), in_hbm(dec))

    y, sums, second = flow(
        mix_kernel,
        [
            (struct((tokens, WIDTH)), up["token"](WIDTH)),
            (struct((chunks, 8, LANES)), up["chunk"](8, LANES)),
            (struct((peers, second_rows, LANES), bf16), up["message"](second_rows)),
        ],
        unit, size * 16,
        [
            up["message"](PAIRS * rows), up["message"](rows), up["message"](second_rows),
            up["token"](WIDTH), up["token"](LANES), whole(STATE, WIDTH), up["chunk"](8, WIDTH),
            whole(1, WIDTH), whole(1, WIDTH),
        ],
    )(
        first, readers, in_hbm(second), in_hbm(within), in_hbm(sm), inbound, in_hbm(pre),
        own_gain, skip_row,
    )

    partner = lax.ppermute(sums, "sub", [(i, i ^ 1) for i in range(sub_count)])

    d_mixed, back, slab_back = flow(
        norm_kernel,
        [
            (struct((tokens, WIDTH), bf16), up["token"](WIDTH)),
            (struct((chunks, STATE, WIDTH)), up["chunk"](STATE, WIDTH)),
            (struct((STATE, WIDTH), bf16), whole(STATE, WIDTH)),
        ],
        2 * unit, size * 12,
        [
            up["message"](PAIRS * rows), up["message"](rows), up["message"](second_rows),
            up["token"](WIDTH), up["token"](LANES), up["chunk"](8, WIDTH), up["chunk"](8, LANES),
            up["chunk"](8, LANES), whole(1, WIDTH), whole(1, WIDTH),
        ],
        [pltpu.VMEM((STATE, WIDTH), f32)],
    )(first, readers, second, y, sm, pre, sums, partner, own_gain, skip_row)

    outer = carry_over(slab_back, decay, after, slab_count, -1)

    d_values, d_sources, d_readers, d_gates, e, starts, params = flow(
        local_kernel,
        [
            (struct((tokens, WIDTH)), up["token"](WIDTH)),
            (struct((tokens, STATE)), up["token"](STATE)),
            (struct((peers, rows, LANES), bf16), up["message"](rows)),
            (struct((peers, PAIRS * rows, LANES), bf16), up["message"](PAIRS * rows)),
            (struct((HEADS, tokens)), up["lane"](HEADS)),
            (struct((chunks, STATE, WIDTH)), up["chunk"](STATE, WIDTH)),
            (struct((8, LANES)), whole(8, LANES)),
        ],
        10 * unit, size * 16,
        [
            up["message"](PAIRS * rows), up["message"](rows), up["message"](rows),
            up["message"](second_rows), up["token"](WIDTH), up["token"](WIDTH), up["token"](LANES),
            up["lane"](KINDS * HEADS),
            up["chunk"](STATE, WIDTH), up["chunk"](8, WIDTH), whole(STATE, WIDTH),
            up["chunk"](8, LANES), up["chunk"](8, LANES), whole(1, WIDTH), whole(1, WIDTH),
        ],
        [pltpu.VMEM((8, WIDTH), f32), pltpu.VMEM((8, WIDTH), f32)],
    )(
        first, sources, readers, second, y, d_mixed, sm, smt, starts, pre, inbound,
        sums, partner, own_gain, skip_row,
    )

    (last,) = flow(
        last_kernel,
        [(hbm((peers, last_rows, LANES), bf16), pl.BlockSpec(memory_space=pl.ANY))],
        4 * unit, size * 16,
        [
            dn["message"](PAIRS * rows), dn["message"](rows), dn["token"](WIDTH), dn["token"](STATE),
            dn["message"](rows), dn["message"](PAIRS * rows),
            dn["token"](WIDTH), dn["lane"](HEADS), dn["token"](LANES), dn["lane"](KINDS * HEADS),
            whole(STATE, WIDTH), dn["chunk"](STATE, WIDTH), dn["chunk"](STATE, WIDTH),
            dn["chunk"](8, WIDTH), whole(1, WIDTH), whole(2 * HEADS, LANES), whole(8, LANES),
        ],
        [
            pltpu.VMEM((STATE, WIDTH), f32), pltpu.VMEM((2 * HEADS, LANES), f32),
            pltpu.VMEM((peers, last_rows, LANES), bf16),
            pltpu.SemaphoreType.DMA((grid[0] + 1,)),
        ],
    )(
        first, sources, d_values, d_sources, d_readers, d_gates, d_mixed, e, sm, smt, outer, back,
        starts, dec, skip_row, heads, params,
    )

    last_back = exchange(last)
    tile_at = LAST * rows // STEP_ROWS
    def tile(at):
        return pl.BlockSpec((peers, STEP_ROWS, LANES), lambda c: (0, at, 0))

    params = call(
        lambda *refs: unpack_params(sub_count, tensor_count, *refs),
        struct((8 + sub_count * PAIRS, LANES)),
        0, 4 * peers * STEP_ROWS * LANES, (1,),
        [tile(tile_at), whole(tensor_count, LANES)],
        whole(8 + sub_count * PAIRS, LANES),
    )(last_back, mine)
    own_params, other_params = two_parts(params, "slab", slab_count)
    wide, narrow = struct((rows, CHANNELS), bf16), struct((rows, GROUPS * STATE), bf16)
    grad_x, grad_gates, grad_b, grad_c, grad_steps = call(
        lambda *refs: unpack(owners, *refs),
        (wide, wide, narrow, narrow, struct((rows, MIXER_HEADS), bf16)),
        0, 10 * rows * CHANNELS,
    )(last_back)
    row = struct((1, sub_count * HEADS))
    grad_logs, grad_skip, grad_bias, grad_gain = call(
        finish, (row, row, row, struct((sub_count * PAIRS, LANES))), 0, 1 << 16,
    )(own_params, other_params)
    return (
        grad_x,
        grad_gates,
        grad_b,
        grad_c,
        grad_steps,
        grad_logs.reshape(-1),
        grad_skip.reshape(-1),
        grad_bias.reshape(-1),
        grad_gain.reshape(-1),
    )


def solution(mesh):
    tensor_count = mesh.shape["tensor"]
    sub_count = OWNERS // tensor_count
    slab_count = mesh.shape["dp"] // sub_count
    devices = mesh.devices.reshape(slab_count, sub_count, tensor_count)
    split_mesh = Mesh(devices, ("slab", "sub", "tensor"))
    rows = P(("slab", "sub", "tensor"), None)
    param = P("tensor")

    def local(*arrays):
        return on_device(slab_count, sub_count, tensor_count, *arrays)

    return jax.shard_map(
        local,
        mesh=split_mesh,
        in_specs=(rows,) * 5 + (param,) * 4 + (rows,),
        out_specs=(rows,) * 5 + (param,) * 4,
        check_vma=False,
    )
```

```python
import jax
import jax.numpy as jnp
from jax import lax
from jax.experimental import pallas as pl
from jax.experimental.pallas import tpu as pltpu
from jax.sharding import Mesh
from jax.sharding import PartitionSpec as P

MIXER_HEADS = 128
HEAD_DIM = 64
STATE = 128
GROUPS = 8
CHANNELS = MIXER_HEADS * HEAD_DIM
HEADS = 8
WIDTH = HEADS * HEAD_DIM
GROUP_WIDTH = 2 * WIDTH
OWNERS = MIXER_HEADS // HEADS
LANES = 128
PAIRS = WIDTH // LANES
CHUNK = 128
STEP_ROWS = 16
epsilon = 1e-05
f32 = jnp.float32
bf16 = jnp.bfloat16

DT, CUM, WEIGHT, SHIFTED, ECUM, RATE, SIG = range(7)
KINDS = 8
CLAMP = 80.0


def mm(a, b):
    return jnp.dot(a, b, preferred_element_type=f32)


def mm_nt(a, b):
    return lax.dot_general(a, b, (((1,), (1,)), ((), ())), preferred_element_type=f32)


def mm_tn(a, b):
    return lax.dot_general(a, b, (((0,), (0,)), ((), ())), preferred_element_type=f32)


def mm_exact(a, b):
    return jnp.dot(a, b, precision=lax.Precision.HIGHEST, preferred_element_type=f32)


def two_terms(values):
    high = values.astype(bf16)
    return high, (values - high.astype(f32)).astype(bf16)


def two_terms_each(tiles):
    return zip(*(two_terms(tile) for tile in tiles))


def twice(a):
    return jnp.concatenate([a, a], axis=1)


def mm_two(a_twice, high, low):
    return mm(a_twice, jnp.concatenate([high, low], axis=0))


def sum_heads(ones_twice, highs, lows):
    return mm_nt(ones_twice, jnp.concatenate([*highs, *lows], axis=1))


def sigmoid(values):
    return 0.5 + 0.5 * jnp.tanh(0.5 * values)


def low_half(rows):
    return lax.broadcasted_iota(jnp.int32, (rows, LANES), 1) < HEAD_DIM


def spread_pair(values, kind, j):
    rows = values.shape[0]
    at = kind * HEADS + 2 * j
    return jnp.where(
        low_half(rows),
        jnp.broadcast_to(values[:, at : at + 1], (rows, LANES)),
        jnp.broadcast_to(values[:, at + 1 : at + 2], (rows, LANES)),
    )


def head_rows():
    row = lax.broadcasted_iota(jnp.int32, (16, WIDTH), 0)
    channel = lax.broadcasted_iota(jnp.int32, (16, WIDTH), 1) // HEAD_DIM
    return jnp.where(row == channel, 1.0, 0.0).astype(bf16)


def split_pair(block):
    low = low_half(block.shape[0])
    zero = jnp.zeros_like(block)
    return jnp.concatenate(
        [jnp.where(low, block, zero), jnp.where(low, zero, block)], axis=0
    )


def lanes(j):
    return slice(j * LANES, (j + 1) * LANES)


class Message:
    def __init__(self, rows):
        self.rows = rows
        self.per_chunk = CHUNK // rows

    def place(self, chunk, k):
        r = self.rows
        return (slice(chunk * self.per_chunk, (chunk + 1) * self.per_chunk), slice(k * r, (k + 1) * r))

    def get(self, ref, chunk, k):
        a, b = self.place(chunk, k)
        return ref[a, b, :].reshape(CHUNK, LANES)

    def put(self, ref, chunk, k, value):
        a, b = self.place(chunk, k)
        ref[a, b, :] = value.reshape(self.per_chunk, self.rows, LANES)


X, HALF = 0, PAIRS
FIRST = PAIRS + 1
Z, GRAD = 0, PAIRS
SECOND = 2 * PAIRS
LAST_X, LAST_B, LAST_Z, LAST_C = 0, PAIRS, PAIRS + 1, 2 * PAIRS + 1
LAST = 2 * PAIRS + 2


def pack_first(x_ref, b_ref, c_ref, steps_ref, out_ref, by_head):
    r = x_ref.shape[0]
    step = pl.program_id(0) * pl.num_programs(1) + pl.program_id(1)
    subs = out_ref.shape[0]

    @pl.when(step == 0)
    def _():
        steps = steps_ref[...].astype(f32)
        by_head[...] = jnp.concatenate([steps, jnp.zeros((LANES - r, LANES), f32)], axis=0).T

    zero = jnp.zeros((STEP_ROWS - HEADS, LANES), f32)
    for s in range(subs):
        for j in range(PAIRS):
            out_ref[s, 0, j * r : (j + 1) * r, :] = x_ref[:, lanes(s * PAIRS + j)]
        half = b_ref if s % 2 == 0 else c_ref
        out_ref[s, 0, HALF * r : (HALF + 1) * r, :] = half[:, lanes(s // 2)]
        at = pl.multiple_of((step * subs + s) * HEADS, HEADS)
        mine = jnp.concatenate([by_head[pl.ds(at, HEADS), :], zero], axis=0)
        out_ref[s, 0, FIRST * r :, :] = mine.astype(bf16)


def pack_second(z_ref, grad_ref, out_ref):
    r = z_ref.shape[0]
    for s in range(out_ref.shape[0]):
        for j in range(PAIRS):
            at = lanes(s * PAIRS + j)
            out_ref[s, 0, (Z + j) * r : (Z + j + 1) * r, :] = z_ref[:, at]
            out_ref[s, 0, (GRAD + j) * r : (GRAD + j + 1) * r, :] = grad_ref[:, at]


def add_halves(owners, in_ref, block, out_ref):
    r = out_ref.shape[0]
    peer_of = {own: peer for peer, own in enumerate(owners)}
    for g in range(GROUPS):
        halves = [
            in_ref[peer_of[2 * g + k], block * r : (block + 1) * r, :].astype(f32) for k in range(2)
        ]
        out_ref[:, lanes(g)] = (halves[0] + halves[1]).astype(bf16)


def unpack(owners, in_ref, x_ref, z_ref, b_ref, c_ref, steps_ref):
    r = x_ref.shape[0]
    peer_of = {own: peer for peer, own in enumerate(owners)}
    for peer, own in enumerate(owners):
        for j in range(PAIRS):
            for block, ref in ((LAST_X, x_ref), (LAST_Z, z_ref)):
                at = slice((block + j) * r, (block + j + 1) * r)
                ref[:, lanes(own * PAIRS + j)] = in_ref[peer, at, :]
    add_halves(owners, in_ref, LAST_B, b_ref)
    add_halves(owners, in_ref, LAST_C, c_ref)
    by_head = jnp.concatenate(
        [
            in_ref[peer_of[own], LAST * r : LAST * r + STEP_ROWS, :].astype(f32)[:HEADS]
            for own in range(OWNERS)
        ],
        axis=0,
    )
    steps_ref[...] = by_head.T[:r, :].astype(bf16)


GAIN_ROW, SKIP_ROW, LOGS_ROW, BIAS_ROW = HEADS, HEADS + PAIRS, HEADS + PAIRS + 1, HEADS + PAIRS + 2


def unpack_params(sub_count, tensor_count, tile_ref, mine_ref, out_ref):
    lane = lax.broadcasted_iota(jnp.int32, (1, LANES), 1)
    totals = [jnp.zeros((1, LANES), f32) for _ in range(3)]
    for s in range(sub_count):
        rows = jnp.zeros((STEP_ROWS, LANES), f32)
        for t in range(tensor_count):
            mine = mine_ref[t : t + 1, :] > 0.0
            rows = jnp.where(mine, tile_ref[s * tensor_count + t].astype(f32), rows)
        for k, at in enumerate((LOGS_ROW, BIAS_ROW, SKIP_ROW)):
            part = jnp.where(lane < HEADS, rows[at : at + 1], 0.0)
            totals[k] = totals[k] + (part if s == 0 else pltpu.roll(part, s * HEADS, 1))
        out_ref[8 + s * PAIRS : 8 + (s + 1) * PAIRS, :] = rows[GAIN_ROW : GAIN_ROW + PAIRS]
    out_ref[:8, :] = jnp.concatenate(totals + [jnp.zeros((5, LANES), f32)], axis=0)


def state_kernel(
    message, per_step,
    first_ref, sources_ref, steps_ref, heads_ref, sm_ref, smt_ref, own_ref, dec_ref, state_ref, whole_ref,
    carry, rows_s,
):
    c = pl.program_id(0)

    @pl.when(c == 0)
    def _():
        carry[...] = jnp.zeros_like(carry)
        whole_ref[...] = jnp.ones_like(whole_ref)
        chunks = rows_s.shape[0]
        before = lax.broadcasted_iota(jnp.int32, (CHUNK, CHUNK), 0)
        after = lax.broadcasted_iota(jnp.int32, (CHUNK, CHUNK), 1)
        raws = []
        for k in range(chunks):
            raw = heads_ref[HEADS:, :]
            for p in range(message.per_chunk):
                part = steps_ref[k * message.per_chunk + p].astype(f32)[:HEADS]
                raw = raw + (part if p == 0 else pltpu.roll(part, p * message.rows, 1))
            raws.append(raw)
        raw = jnp.concatenate(raws, axis=0)
        small = jnp.exp(-jnp.abs(raw))
        series = small * (
            1.0 - small * (0.5 - small * (1.0 / 3 - small * (0.25 - small * 0.2)))
        )
        soft = jnp.maximum(raw, 0.0) + jnp.where(small < 0.015625, series, jnp.log(1.0 + small))
        sig = jnp.where(raw >= 0.0, 1.0, small) / (1.0 + small)
        decay_rate = jnp.concatenate([jnp.exp(heads_ref[:HEADS, :])] * chunks, axis=0)
        rate = -decay_rate * soft
        cum = mm_exact(rate, jnp.where(before <= after, 1.0, 0.0))
        rest = mm_exact(rate, jnp.where(before > after, 1.0, 0.0))
        kinds = [
            soft, cum, soft * jnp.exp(rest), cum - jnp.log(soft), jnp.exp(cum), rate, sig,
            jnp.zeros_like(soft),
        ]
        for k in range(chunks):
            at = slice(k * HEADS, (k + 1) * HEADS)
            rows_s[k] = jnp.concatenate([kind[at] for kind in kinds], axis=0)

    made = []
    state = [carry[:, lanes(j)] for j in range(PAIRS)]
    decays = [whole_ref[:, lanes(j)] for j in range(PAIRS)]
    for i in range(per_step):
        rows = rows_s[c * per_step + i]
        sm = jnp.concatenate([rows, jnp.zeros_like(rows)], axis=0).T
        last = jnp.broadcast_to(sm[CHUNK - 1 : CHUNK, :], (8, LANES))
        sources_t = twice(message.get(sources_ref, i, 0).T)
        decs, owns = [], []
        for j in range(PAIRS):
            dec = spread_pair(last, ECUM, j)
            scaled = message.get(first_ref, i, X + j).astype(f32) * spread_pair(sm, WEIGHT, j)
            own = mm_two(sources_t, *two_terms(scaled))
            state[j] = dec[0:1] * state[j] + own
            decays[j] = decays[j] * dec
            decs.append(dec)
            owns.append(own)
        made.append((rows, sm, decs, owns))
    for i, (rows, sm, decs, owns) in enumerate(made):
        smt_ref[:, lanes(i)] = rows
        sm_ref[i * CHUNK : (i + 1) * CHUNK, :] = sm
        for j in range(PAIRS):
            dec_ref[i, :, lanes(j)] = decs[j]
            own_ref[i, :, lanes(j)] = owns[j]
    for j in range(PAIRS):
        carry[:, lanes(j)] = state[j]
        whole_ref[:, lanes(j)] = decays[j]
        state_ref[:, lanes(j)] = state[j].astype(bf16)


def within_kernel(
    message, per_step,
    first_ref, sources_ref, readers_ref, sm_ref, smt_ref, own_ref, dec_ref, y_ref, start_ref, pre_ref, carry, pre,
):
    @pl.when(pl.program_id(0) == 0)
    def _():
        carry[...] = jnp.zeros_like(carry)
        pre[...] = jnp.ones_like(pre)

    t = lax.broadcasted_iota(jnp.int32, (CHUNK, CHUNK), 0)
    s = lax.broadcasted_iota(jnp.int32, (CHUNK, CHUNK), 1)
    made = []
    states = [carry[:, lanes(j)] for j in range(PAIRS)]
    before = pre[...]
    for i in range(per_step):
        rows = slice(i * CHUNK, (i + 1) * CHUNK)
        sm = sm_ref[rows, :]
        smt = smt_ref[:, lanes(i)]
        readers = message.get(readers_ref, i, 0)
        readers_twice = twice(readers)
        scores = jnp.where(t >= s, mm_nt(readers, message.get(sources_ref, i, 0)), 0.0)
        ys = []
        for j in range(PAIRS):
            weights = []
            for h in (2 * j, 2 * j + 1):
                here = sm[:, CUM * HEADS + h : CUM * HEADS + h + 1]
                there = smt[SHIFTED * HEADS + h : SHIFTED * HEADS + h + 1, :]
                weights.append(
                    (scores * jnp.exp(jnp.minimum(here - there, CLAMP))).astype(bf16)
                )
            values = split_pair(message.get(first_ref, i, X + j))
            within = mm(jnp.concatenate(weights, axis=1), values)
            carried = mm_two(readers_twice, *two_terms(states[j]))
            ys.append(within + spread_pair(sm, ECUM, j) * carried)
        made.append((ys, list(states), before))
        for j in range(PAIRS):
            states[j] = dec_ref[i, 0:1, lanes(j)] * states[j] + own_ref[i, :, lanes(j)]
        before = before * dec_ref[i]
    for i, (ys, starts, prefix) in enumerate(made):
        pre_ref[i] = prefix
        for j in range(PAIRS):
            y_ref[i * CHUNK : (i + 1) * CHUNK, lanes(j)] = ys[j]
            start_ref[i, :, lanes(j)] = starts[j]
    pre[...] = before
    for j in range(PAIRS):
        carry[:, lanes(j)] = states[j]


def mix_kernel(
    message, per_step,
    first_ref, readers_ref, second_hbm, within_hbm, sm_ref, inbound_ref, pre_ref, gain_ref, skip_ref,
    y_ref, sums_ref, second_ref, arrived,
):
    c = pl.program_id(0)
    peers, tokens = per_step * message.per_chunk, per_step * CHUNK

    def copies(step):
        at = pl.ds(step * peers, peers)
        rows = pl.ds(step * tokens, tokens)
        return (
            pltpu.make_async_copy(within_hbm.at[rows], y_ref.at[rows], arrived.at[0, step]),
            pltpu.make_async_copy(second_hbm.at[at], second_ref.at[at], arrived.at[1, step]),
        )

    @pl.when(c == 0)
    def _():
        for step in range(arrived.shape[1]):
            for copy in copies(step):
                copy.start()

    for copy in copies(c):
        copy.wait()
    mine = second_ref.at[pl.ds(c * peers, peers)]
    inbound = inbound_ref[...].astype(bf16)
    for i in range(per_step):
        rows = slice(i * CHUNK, (i + 1) * CHUNK)
        y_rows = pl.ds(pl.multiple_of(c * tokens + i * CHUNK, CHUNK), CHUNK)
        sm = sm_ref[rows, :]
        carried = mm(message.get(readers_ref, i, 0), inbound)
        power = jnp.zeros((CHUNK, LANES), f32)
        cross = jnp.zeros((CHUNK, LANES), f32)
        for j in range(PAIRS):
            at = lanes(j)
            decay = spread_pair(sm, ECUM, j) * pre_ref[i, 0:1, at]
            y = y_ref[y_rows, at] + decay * carried[:, at]
            y_ref[y_rows, at] = y
            values = message.get(first_ref, i, X + j).astype(f32)
            gates = message.get(mine, i, Z + j).astype(f32)
            grad = message.get(mine, i, GRAD + j).astype(f32)
            gated = (y + skip_ref[0:1, at] * values) * (gates * sigmoid(gates))
            power = power + gated * gated
            cross = cross + grad * gain_ref[0:1, at] * gated
        sums_ref[i, 0:1, :] = jnp.sum(power.T, axis=0, keepdims=True)
        sums_ref[i, 1:2, :] = jnp.sum(cross.T, axis=0, keepdims=True)
        sums_ref[i, 2:, :] = jnp.zeros((6, LANES), f32)


def norm_factors(sums):
    sums = sums * (1.0 / GROUP_WIDTH)
    inverse = lax.rsqrt(sums[0:1] + epsilon)
    pull = inverse * inverse * inverse * sums[1:2]
    return (
        jnp.broadcast_to(inverse, (CHUNK, LANES)).T,
        jnp.broadcast_to(pull, (CHUNK, LANES)).T,
    )


def norm_kernel(
    message, per_step,
    first_ref, readers_ref, second_ref, y_ref, sm_ref, pre_ref, sums_ref, other_ref, gain_ref, skip_ref,
    mixed_ref, back_ref, slab_ref,
    back_sum,
):
    @pl.when(pl.program_id(0) == 0)
    def _():
        back_sum[...] = jnp.zeros_like(back_sum)

    sums = [back_sum[:, lanes(j)] for j in range(PAIRS)]
    for i in range(per_step):
        rows = slice(i * CHUNK, (i + 1) * CHUNK)
        sm = sm_ref[rows, :]
        readers_t = twice(message.get(readers_ref, i, 0).T)
        inverse, pull = norm_factors(sums_ref[i] + other_ref[i])
        for j in range(PAIRS):
            at = lanes(j)
            values = message.get(first_ref, i, X + j).astype(f32)
            gates = message.get(second_ref, i, Z + j).astype(f32)
            grad = message.get(second_ref, i, GRAD + j).astype(f32)
            silu = gates * sigmoid(gates)
            gated = (y_ref[rows, at] + skip_ref[0:1, at] * values) * silu
            d_mixed = (inverse * grad * gain_ref[0:1, at] - pull * gated) * silu
            back = mm_two(readers_t, *two_terms(d_mixed * spread_pair(sm, ECUM, j)))
            sums[j] = sums[j] + pre_ref[i, 0:1, at] * back
            mixed_ref[rows, at] = d_mixed.astype(bf16)
            back_ref[i, :, at] = back
    for j in range(PAIRS):
        back_sum[:, lanes(j)] = sums[j]
        slab_ref[:, lanes(j)] = sums[j].astype(bf16)


def local_kernel(
    message, per_step,
    first_ref, sources_ref, readers_ref, second_ref, y_ref, grad_ref, sm_ref, smt_ref, start_ref, pre_ref, inbound_ref,
    sums_ref, other_ref, gain_ref, skip_ref,
    values_out, sources_out, readers_out, gate_ref, e_ref, start_out, param_ref,
    gain_sum, skip_sum,
):
    c = pl.program_id(0)

    @pl.when(c == 0)
    def _():
        gain_sum[...] = jnp.zeros_like(gain_sum)
        skip_sum[...] = jnp.zeros_like(skip_sum)

    s = lax.broadcasted_iota(jnp.int32, (CHUNK, CHUNK), 0)
    t = lax.broadcasted_iota(jnp.int32, (CHUNK, CHUNK), 1)
    causal = t >= s
    ones = head_rows()
    ones_twice = twice(ones)
    gains = [gain_sum[0:1, lanes(j)] for j in range(PAIRS)]
    skips = [skip_sum[0:1, lanes(j)] for j in range(PAIRS)]
    for i in range(per_step):
        rows = slice(i * CHUNK, (i + 1) * CHUNK)
        sm = sm_ref[rows, :]
        smt = smt_ref[:, lanes(i)]
        sources = message.get(sources_ref, i, 0)
        readers = message.get(readers_ref, i, 0)
        inverse, pull = norm_factors(sums_ref[i] + other_ref[i])
        scores = jnp.where(causal, mm_nt(sources, readers), 0.0)
        total = jnp.zeros((CHUNK, CHUNK), f32)
        d_values, d_gates, highs, lows, scaleds, starts = [], [], [], [], [], []
        for j in range(PAIRS):
            at = lanes(j)
            rounded = grad_ref[rows, at]
            grads = split_pair(rounded)
            x = message.get(first_ref, i, X + j)
            weight_grads = mm_nt(x, grads)
            weights = []
            for k, h in enumerate((2 * j, 2 * j + 1)):
                there = sm[:, SHIFTED * HEADS + h : SHIFTED * HEADS + h + 1]
                here = smt[CUM * HEADS + h : CUM * HEADS + h + 1, :]
                decay = jnp.exp(jnp.minimum(here - there, CLAMP))
                weights.append((scores * decay).astype(bf16))
                total = total + weight_grads[:, lanes(k)] * decay
            d_values.append(mm(jnp.concatenate(weights, axis=1), grads))

            values = x.astype(f32)
            gates = message.get(second_ref, i, Z + j).astype(f32)
            grad = message.get(second_ref, i, GRAD + j).astype(f32)
            y = y_ref[rows, at]
            mixed = y + skip_ref[0:1, at] * values
            sig = sigmoid(gates)
            silu = gates * sig
            gated = mixed * silu
            scaled = inverse * grad
            gains[j] = gains[j] + jnp.sum(scaled * gated, axis=0, keepdims=True)
            d_gated = scaled * gain_ref[0:1, at] - pull * gated
            d_gate = d_gated * mixed * (sig + silu * (1.0 - sig))
            d_gates.append(d_gate.astype(bf16))
            skips[j] = skips[j] + jnp.sum(values * (d_gated * silu), axis=0, keepdims=True)
            d_mixed = rounded.astype(f32)
            high, low = two_terms(d_mixed * y)
            highs.append(high)
            lows.append(low)
            scaleds.append((d_mixed * spread_pair(sm, ECUM, j)).astype(bf16))
            starts.append(
                start_ref[i, :, at] + pre_ref[i, 0:1, at] * inbound_ref[:, at].astype(f32)
            )
        e = sum_heads(ones_twice, highs, lows)
        total = jnp.where(causal, total, 0.0).astype(bf16)
        start = jnp.concatenate([part.astype(bf16) for part in starts], axis=1)
        d_readers = mm_tn(total, sources) + mm_nt(jnp.concatenate(scaleds, axis=1), start)
        for j in range(PAIRS):
            values_out[rows, lanes(j)] = d_values[j]
            message.put(gate_ref, i, j, d_gates[j])
            start_out[i, :, lanes(j)] = starts[j]
        e_ref[:, lanes(i)] = e[:HEADS]
        sources_out[rows, :] = mm(total, readers)
        message.put(readers_out, i, 0, d_readers.astype(bf16))
    for j in range(PAIRS):
        gain_sum[0:1, lanes(j)] = gains[j]
        skip_sum[0:1, lanes(j)] = skips[j]

    @pl.when(c == pl.num_programs(0) - 1)
    def _():
        for j in range(PAIRS):
            param_ref[j : j + 1, :] = gain_sum[0:1, lanes(j)]
        high, low = two_terms(jnp.broadcast_to(skip_sum[0:1, :], (LANES, WIDTH)))
        skips = (mm_nt(high, ones) + mm_nt(low, ones))[0:1]
        param_ref[PAIRS : PAIRS + 1, :] = jnp.concatenate(
            [skips, jnp.zeros((1, LANES - 16), f32)], axis=1
        )
        param_ref[PAIRS + 1 :, :] = jnp.zeros((8 - PAIRS - 1, LANES), f32)


def last_kernel(
    message, per_step,
    first_ref, sources_ref, within_ref, d_sources_ref, d_readers_ref, gate_ref, grad_ref, e_ref, sm_ref, smt_ref, outer_ref,
    back_ref, start_ref, dec_ref, skip_ref, heads_ref, early_ref,
    out_ref,
    carry, sums, message_s, sent,
):
    c = pl.program_id(0)

    @pl.when(c == 0)
    def _():
        carry[...] = outer_ref[...].astype(f32)
        sums[...] = jnp.zeros_like(sums)

    r = message.rows
    ones = head_rows()
    ones_twice = twice(ones)
    before = lax.broadcasted_iota(jnp.int32, (CHUNK, CHUNK), 0)
    after = lax.broadcasted_iota(jnp.int32, (CHUNK, CHUNK), 1)
    earlier = jnp.where(before < after, 1.0, 0.0)
    decay_rate = jnp.exp(heads_ref[:HEADS, :])
    first_peer = (pl.num_programs(0) - 1 - c) * per_step * message.per_chunk
    mine = message_s.at[pl.ds(first_peer, per_step * message.per_chunk)]
    chunks = sent.shape[0] - 3

    def body_copy(chunk):
        at = (pl.ds(chunk * message.per_chunk, message.per_chunk), pl.ds(0, LAST_Z * r))
        return pltpu.make_async_copy(message_s.at[at], out_ref.at[at], sent.at[chunk])

    gates_copy = pltpu.make_async_copy(
        gate_ref, out_ref.at[:, pl.ds(LAST_Z * r, PAIRS * r)], sent.at[chunks]
    )
    readers_copy = pltpu.make_async_copy(
        d_readers_ref, out_ref.at[:, pl.ds(LAST_C * r, r)], sent.at[chunks + 1]
    )

    @pl.when(c == 0)
    def _():
        gates_copy.start()
        readers_copy.start()

    states = [carry[:, lanes(j)] for j in range(PAIRS)]
    logs_sum, steps_sum = sums[:HEADS, :], sums[HEADS:, :]
    for i in reversed(range(per_step)):
        rows = slice(i * CHUNK, (i + 1) * CHUNK)
        sm = sm_ref[rows, :]
        sources_twice = twice(message.get(sources_ref, i, 0))
        d_values, highs, lows, scaleds, rounded, fluxes = [], [], [], [], [], []
        for j in range(PAIRS):
            at = lanes(j)
            high, low = two_terms(states[j])
            rounded.append(high)
            values = message.get(first_ref, i, X + j).astype(f32)
            weight = spread_pair(sm, WEIGHT, j)
            grad = within_ref[rows, at] + weight * mm_two(sources_twice, high, low)
            skipped = skip_ref[0:1, at] * grad_ref[rows, at].astype(f32)
            d_values.append((grad + skipped).astype(bf16))
            high, low = two_terms(values * grad)
            highs.append(high)
            lows.append(low)
            scaleds.append((values * weight).astype(bf16))
            states[j] = dec_ref[i, 0:1, at] * states[j] + back_ref[i, :, at]
            fluxes.append(
                jnp.broadcast_to(
                    jnp.sum(start_ref[i, :, at] * states[j], axis=0, keepdims=True), (16, LANES)
                )
            )
        d_sources = d_sources_ref[rows, :] + mm_nt(
            jnp.concatenate(scaleds, axis=1), jnp.concatenate(rounded, axis=1)
        )
        g = sum_heads(ones_twice, highs, lows)[:HEADS]
        constant = sum_heads(ones_twice, *two_terms_each(fluxes))[:HEADS, 0:1]
        flux = constant + mm_exact(g - e_ref[:, lanes(i)], earlier)
        soft = smt_ref[DT * HEADS : (DT + 1) * HEADS, lanes(i)]
        rate = smt_ref[RATE * HEADS : (RATE + 1) * HEADS, lanes(i)]
        sig = smt_ref[SIG * HEADS : (SIG + 1) * HEADS, lanes(i)]
        steps = (g / soft - decay_rate * flux) * sig
        logs_sum = logs_sum + flux * rate
        steps_sum = steps_sum + steps
        steps = jnp.concatenate([steps, jnp.zeros_like(steps)], axis=0)
        for j in range(PAIRS):
            message.put(mine, i, LAST_X + j, d_values[j])
        message.put(mine, i, LAST_B, d_sources.astype(bf16))
        for p in range(message.per_chunk):
            part = steps if p == 0 else pltpu.roll(steps, LANES - p * r, 1)
            mine[i * message.per_chunk + p, LAST * r : LAST * r + STEP_ROWS, :] = part.astype(bf16)
        body_copy((pl.num_programs(0) - 1 - c) * per_step + i).start()
    for j in range(PAIRS):
        carry[:, lanes(j)] = states[j]
    sums[:HEADS, :] = logs_sum
    sums[HEADS:, :] = steps_sum

    @pl.when(c == pl.num_programs(0) - 1)
    def _():
        late = []
        for k in range(2):
            column = jnp.sum(sums[k * HEADS : (k + 1) * HEADS, :], axis=1, keepdims=True)
            block = jnp.broadcast_to(column, (HEADS, LANES))
            block = jnp.concatenate([block, jnp.zeros((LANES - HEADS, LANES), f32)], axis=0)
            late.append(block.T[0:1, :])
        small = [
            jnp.zeros((HEADS, LANES), f32), early_ref[: PAIRS + 1, :], *late,
            jnp.zeros((STEP_ROWS - BIAS_ROW - 1, LANES), f32),
        ]
        small = jnp.concatenate(small, axis=0).astype(bf16)
        own_rows = lax.broadcasted_iota(jnp.int32, (STEP_ROWS, LANES), 0) < HEADS

        def fill(peer, unused):
            steps_at = slice(LAST * r, LAST * r + STEP_ROWS)
            message_s[peer, steps_at, :] = jnp.where(own_rows, message_s[peer, steps_at, :], small)
            return unused

        lax.fori_loop(0, message_s.shape[0], fill, 0)
        at = (slice(None), pl.ds(LAST * r, STEP_ROWS))
        tiles = pltpu.make_async_copy(message_s.at[at], out_ref.at[at], sent.at[chunks + 2])
        tiles.start()
        for chunk in range(chunks):
            body_copy(chunk).wait()
        gates_copy.wait()
        readers_copy.wait()
        tiles.wait()


def finish(own_ref, other_ref, logs_ref, skip_ref, bias_ref, gain_ref):
    total = own_ref[...] + other_ref[...]
    count = logs_ref.shape[1]
    logs_ref[...] = total[0:1, :count]
    bias_ref[...] = total[1:2, :count]
    skip_ref[...] = total[2:3, :count]
    gain_ref[...] = total[8:]


def call(kernel, out_shape, flops, moved, grid=None, in_specs=None, out_specs=None, scratch=()):
    extra = {}
    if grid is not None:
        extra = dict(grid=grid, in_specs=in_specs, out_specs=out_specs)
    return pl.pallas_call(
        kernel,
        out_shape=out_shape,
        scratch_shapes=list(scratch),
        compiler_params=pltpu.CompilerParams(vmem_limit_bytes=28 * 1024 * 1024),
        cost_estimate=pl.CostEstimate(flops=flops, bytes_accessed=moved, transcendentals=0),
        **extra,
    )


def shifted(array, count, by):
    pairs = [(i, i + by) for i in range(count) if 0 <= i + by < count]
    return lax.ppermute(array, "slab", pairs)


def carry_over(state, decay, first_decay, count, sign):
    window, window_decay, step = state, decay, 1
    result = result_decay = None
    while step < count:
        arrived = shifted(window, count, sign * step)
        more = 2 * step < count
        if result is None:
            result = arrived
            if more:
                result_decay = first_decay
                window = (state.astype(f32) + decay[0:1] * arrived.astype(f32)).astype(bf16)
                window_decay = decay * first_decay
        else:
            if more:
                arrived_decay = shifted(window_decay, count, sign * step)
                window = (window.astype(f32) + window_decay[0:1] * arrived.astype(f32)).astype(bf16)
                window_decay = window_decay * arrived_decay
            result = result.astype(f32) + result_decay[0:1] * arrived.astype(f32)
            if more:
                result_decay = result_decay * arrived_decay
        step *= 2
    return jnp.zeros_like(state) if result is None else result


def two_parts(array, axis, count):
    step, other = 1, jnp.zeros_like(array)
    while step < count:
        array = array if step == 1 else array + other
        other = lax.ppermute(array, axis, [(i, i ^ step) for i in range(count)])
        step *= 2
    return array, other


def on_device(
    slab_count, sub_count, tensor_count,
    mixer_x, gate_z, b_matrix, c_matrix, raw_steps, decay_log, skip_gain, step_bias, norm_gain, out_grad,
):
    rows = mixer_x.shape[0]
    peers = sub_count * tensor_count
    tokens = rows * peers
    chunks = tokens // CHUNK
    message = Message(rows)
    owners = [t * sub_count + s for s in range(sub_count) for t in range(tensor_count)]
    sub = lax.axis_index("sub")

    def struct(shape, kind=f32):
        return jax.ShapeDtypeStruct(shape, kind)

    def hbm(shape, kind=f32):
        return pltpu.HBM(shape, kind)

    def in_hbm(array):
        return pltpu.with_memory_space_constraint(array, pltpu.HBM)

    def exchange(array):
        return lax.all_to_all(array, ("sub", "tensor"), split_axis=0, concat_axis=0, tiled=True)

    own_logs = lax.dynamic_slice(decay_log, (sub * HEADS,), (HEADS,))
    own_bias = lax.dynamic_slice(step_bias, (sub * HEADS,), (HEADS,))
    own_skip = lax.dynamic_slice(skip_gain, (sub * HEADS,), (HEADS,))
    own_gain = lax.dynamic_slice(norm_gain, (sub * WIDTH,), (WIDTH,)).reshape(1, WIDTH)
    heads = jnp.broadcast_to(jnp.concatenate([own_logs, own_bias])[:, None], (2 * HEADS, LANES))
    skip_row = jnp.repeat(own_skip, HEAD_DIM).reshape(1, WIDTH)

    first_rows = FIRST * rows + STEP_ROWS
    second_rows = SECOND * rows
    last_rows = LAST * rows + STEP_ROWS

    def packed(kernel, height, arrays, whole_arrays=(), scratch=()):
        out = hbm((sub_count, tensor_count, height, LANES), bf16)
        moved = 4 * peers * height * LANES
        runs = 1
        parts = tensor_count * runs
        specs = [
            pl.BlockSpec((rows, a.shape[1] // parts), lambda t, k: (0, t * runs + k)) for a in arrays
        ] + [pl.BlockSpec(a.shape, lambda t, k: (0, 0)) for a in whole_arrays]
        out_spec = pl.BlockSpec((sub_count // runs, 1, height, LANES), lambda t, k: (k, t, 0, 0))
        made = call(kernel, out, 0, moved, (tensor_count, runs), specs, out_spec, scratch)(
            *(in_hbm(a) for a in (*arrays, *whole_arrays))
        )
        return made.reshape(peers, height, LANES)

    first = exchange(
        packed(
            pack_first, first_rows, (mixer_x, b_matrix, c_matrix), (raw_steps,),
            [pltpu.VMEM((LANES, LANES), f32)],
        )
    )
    tensor_rows = lax.broadcasted_iota(jnp.int32, (tensor_count, LANES), 0)
    mine = (tensor_rows == lax.axis_index("tensor")).astype(f32)
    half = first[:, HALF * rows : (HALF + 1) * rows, :]
    other_half = lax.ppermute(half, "sub", [(i, i ^ 1) for i in range(sub_count)])
    even = sub % 2 == 0
    sources, readers = jnp.where(even, half, other_half), jnp.where(even, other_half, half)
    gate_z, heads, skip_row, own_gain, mine = lax.optimization_barrier(
        (gate_z, heads, skip_row, own_gain, mine)
    )
    second = exchange(packed(pack_second, second_rows, (gate_z, out_grad)))

    def flow(kernel, shape_specs, flops, moved, in_specs, scratch=(), per=2):
        per = min(per, chunks)

        def body(*refs):
            return kernel(message, per, *refs)

        shapes = tuple(shape for shape, _ in shape_specs)
        specs = tuple(spec for _, spec in shape_specs)
        return call(body, shapes, flops, moved, (chunks // per,), in_specs, specs, scratch)

    def specs_of(per, down=False):
        per = min(per, chunks)
        steps = chunks // per

        def spec(block, axis):
            def index(c):
                at = steps - 1 - c if down else c
                return tuple(at if k == axis else 0 for k in range(len(block)))

            return pl.BlockSpec(block, index)

        return dict(
            message=lambda height: spec((per * message.per_chunk, height, LANES), 0),
            token=lambda width: spec((per * CHUNK, width), 0),
            lane=lambda height: spec((height, per * CHUNK), 1),
            chunk=lambda *shape: spec((per,) + shape, 0),
        )

    up = specs_of(2)
    many = specs_of(4)
    dn = specs_of(8, down=True)

    def whole(*shape):
        return pl.BlockSpec(shape, lambda c: (0,) * len(shape))

    unit = 2 * tokens * CHUNK * WIDTH
    size = tokens * WIDTH

    sm, smt, own, dec, state, decay = flow(
        state_kernel,
        [
            (hbm((tokens, LANES)), up["token"](LANES)),
            (hbm((KINDS * HEADS, tokens)), up["lane"](KINDS * HEADS)),
            (hbm((chunks, STATE, WIDTH)), up["chunk"](STATE, WIDTH)),
            (hbm((chunks, 8, WIDTH)), up["chunk"](8, WIDTH)),
            (struct((STATE, WIDTH), bf16), whole(STATE, WIDTH)),
            (struct((8, WIDTH)), whole(8, WIDTH)),
        ],
        2 * unit, size * 8,
        [
            up["message"](PAIRS * rows), up["message"](rows),
            pl.BlockSpec((peers, STEP_ROWS, LANES), lambda c: (0, FIRST * rows // STEP_ROWS, 0)),
            whole(2 * HEADS, LANES),
        ],
        [pltpu.VMEM((STATE, WIDTH), f32), pltpu.VMEM((chunks, KINDS * HEADS, LANES), f32)],
    )(first, sources, first, heads)

    before = after = None
    if slab_count > 2:
        before, after = shifted(decay, slab_count, 1), shifted(decay, slab_count, -1)
    inbound = carry_over(state, decay, before, slab_count, 1)

    within, starts, pre = flow(
        within_kernel,
        [
            (hbm((tokens, WIDTH)), up["token"](WIDTH)),
            (hbm((chunks, STATE, WIDTH)), up["chunk"](STATE, WIDTH)),
            (hbm((chunks, 8, WIDTH)), up["chunk"](8, WIDTH)),
        ],
        6 * unit, size * 16,
        [
            up["message"](PAIRS * rows), up["message"](rows), up["message"](rows),
            up["token"](LANES), up["lane"](KINDS * HEADS),
            up["chunk"](STATE, WIDTH), up["chunk"](8, WIDTH),
        ],
        [pltpu.VMEM((STATE, WIDTH), f32), pltpu.VMEM((8, WIDTH), f32)],
    )(first, sources, readers, in_hbm(sm), in_hbm(smt), in_hbm(own), in_hbm(dec))

    anywhere = pl.BlockSpec(memory_space=pl.ANY)
    y, sums, second = flow(
        mix_kernel,
        [
            (struct((tokens, WIDTH)), whole(tokens, WIDTH)),
            (struct((chunks, 8, LANES)), up["chunk"](8, LANES)),
            (struct((peers, second_rows, LANES), bf16), whole(peers, second_rows, LANES)),
        ],
        unit, size * 16,
        [
            up["message"](PAIRS * rows), up["message"](rows), anywhere, anywhere,
            up["token"](LANES), whole(STATE, WIDTH), up["chunk"](8, WIDTH),
            whole(1, WIDTH), whole(1, WIDTH),
        ],
        [pltpu.SemaphoreType.DMA((2, chunks // min(2, chunks)))],
    )(
        first, readers, in_hbm(second), in_hbm(within), in_hbm(sm), inbound, in_hbm(pre),
        own_gain, skip_row,
    )

    partner = lax.ppermute(sums, "sub", [(i, i ^ 1) for i in range(sub_count)])

    d_mixed, back, slab_back = flow(
        norm_kernel,
        [
            (struct((tokens, WIDTH), bf16), many["token"](WIDTH)),
            (struct((chunks, STATE, WIDTH)), many["chunk"](STATE, WIDTH)),
            (struct((STATE, WIDTH), bf16), whole(STATE, WIDTH)),
        ],
        2 * unit, size * 12,
        [
            many["message"](PAIRS * rows), many["message"](rows), many["message"](second_rows),
            many["token"](WIDTH), many["token"](LANES), many["chunk"](8, WIDTH), many["chunk"](8, LANES),
            many["chunk"](8, LANES), whole(1, WIDTH), whole(1, WIDTH),
        ],
        [pltpu.VMEM((STATE, WIDTH), f32)],
        per=4,
    )(first, readers, second, y, sm, pre, sums, partner, own_gain, skip_row)

    outer = carry_over(slab_back, decay, after, slab_count, -1)

    d_values, d_sources, d_readers, d_gates, e, starts, params = flow(
        local_kernel,
        [
            (struct((tokens, WIDTH)), many["token"](WIDTH)),
            (struct((tokens, STATE)), many["token"](STATE)),
            (struct((peers, rows, LANES), bf16), many["message"](rows)),
            (struct((peers, PAIRS * rows, LANES), bf16), many["message"](PAIRS * rows)),
            (struct((HEADS, tokens)), many["lane"](HEADS)),
            (struct((chunks, STATE, WIDTH)), many["chunk"](STATE, WIDTH)),
            (struct((8, LANES)), whole(8, LANES)),
        ],
        10 * unit, size * 16,
        [
            many["message"](PAIRS * rows), many["message"](rows), many["message"](rows),
            many["message"](second_rows), many["token"](WIDTH), many["token"](WIDTH), many["token"](LANES),
            many["lane"](KINDS * HEADS),
            many["chunk"](STATE, WIDTH), many["chunk"](8, WIDTH), whole(STATE, WIDTH),
            many["chunk"](8, LANES), many["chunk"](8, LANES), whole(1, WIDTH), whole(1, WIDTH),
        ],
        [pltpu.VMEM((8, WIDTH), f32), pltpu.VMEM((8, WIDTH), f32)],
        per=4,
    )(
        first, sources, readers, second, y, d_mixed, sm, smt, starts, pre, inbound,
        sums, partner, own_gain, skip_row,
    )

    (last,) = flow(
        last_kernel,
        [(hbm((peers, last_rows, LANES), bf16), anywhere)],
        4 * unit, size * 16,
        [
            dn["message"](PAIRS * rows), dn["message"](rows), dn["token"](WIDTH), dn["token"](STATE),
            anywhere, anywhere,
            dn["token"](WIDTH), dn["lane"](HEADS), dn["token"](LANES), dn["lane"](KINDS * HEADS),
            whole(STATE, WIDTH), dn["chunk"](STATE, WIDTH), dn["chunk"](STATE, WIDTH),
            dn["chunk"](8, WIDTH), whole(1, WIDTH), whole(2 * HEADS, LANES), whole(8, LANES),
        ],
        [
            pltpu.VMEM((STATE, WIDTH), f32), pltpu.VMEM((2 * HEADS, LANES), f32),
            pltpu.VMEM((peers, last_rows, LANES), bf16),
            pltpu.SemaphoreType.DMA((chunks + 3,)),
        ],
        per=8,
    )(
        first, sources, d_values, d_sources, d_readers, d_gates, d_mixed, e, sm, smt, outer, back,
        starts, dec, skip_row, heads, params,
    )

    last_back = exchange(last)
    tile_at = LAST * rows // STEP_ROWS
    def tile(at):
        return pl.BlockSpec((peers, STEP_ROWS, LANES), lambda c: (0, at, 0))

    params = call(
        lambda *refs: unpack_params(sub_count, tensor_count, *refs),
        struct((8 + sub_count * PAIRS, LANES)),
        0, 4 * peers * STEP_ROWS * LANES, (1,),
        [tile(tile_at), whole(tensor_count, LANES)],
        whole(8 + sub_count * PAIRS, LANES),
    )(last_back, mine)
    own_params, other_params = two_parts(params, "slab", slab_count)
    wide, narrow = struct((rows, CHANNELS), bf16), struct((rows, GROUPS * STATE), bf16)
    grad_x, grad_gates, grad_b, grad_c, grad_steps = call(
        lambda *refs: unpack(owners, *refs),
        (wide, wide, narrow, narrow, struct((rows, MIXER_HEADS), bf16)),
        0, 10 * rows * CHANNELS,
    )(last_back)
    row = struct((1, sub_count * HEADS))
    grad_logs, grad_skip, grad_bias, grad_gain = call(
        finish, (row, row, row, struct((sub_count * PAIRS, LANES))), 0, 1 << 16,
    )(own_params, other_params)
    return (
        grad_x,
        grad_gates,
        grad_b,
        grad_c,
        grad_steps,
        grad_logs.reshape(-1),
        grad_skip.reshape(-1),
        grad_bias.reshape(-1),
        grad_gain.reshape(-1),
    )


def solution(mesh):
    tensor_count = mesh.shape["tensor"]
    sub_count = OWNERS // tensor_count
    slab_count = mesh.shape["dp"] // sub_count
    devices = mesh.devices.reshape(slab_count, sub_count, tensor_count)
    split_mesh = Mesh(devices, ("slab", "sub", "tensor"))
    rows = P(("slab", "sub", "tensor"), None)
    param = P("tensor")

    def local(*arrays):
        return on_device(slab_count, sub_count, tensor_count, *arrays)

    return jax.shard_map(
        local,
        mesh=split_mesh,
        in_specs=(rows,) * 5 + (param,) * 4 + (rows,),
        out_specs=(rows,) * 5 + (param,) * 4,
        check_vma=False,
    )
```

```python
import jax
import jax.numpy as jnp
from jax import lax
from jax.experimental import pallas as pl
from jax.experimental.pallas import tpu as pltpu
from jax.sharding import Mesh
from jax.sharding import PartitionSpec as P

MIXER_HEADS = 128
HEAD_DIM = 64
STATE = 128
GROUPS = 8
CHANNELS = MIXER_HEADS * HEAD_DIM
HEADS = 8
WIDTH = HEADS * HEAD_DIM
GROUP_WIDTH = 2 * WIDTH
OWNERS = MIXER_HEADS // HEADS
LANES = 128
PAIRS = WIDTH // LANES
CHUNK = 128
STEP_ROWS = 16
epsilon = 1e-05
f32 = jnp.float32
bf16 = jnp.bfloat16

DT, CUM, WEIGHT, SHIFTED, ECUM, RATE, SIG = range(7)
KINDS = 8
CLAMP = 80.0


def mm(a, b):
    return jnp.dot(a, b, preferred_element_type=f32)


def mm_nt(a, b):
    return lax.dot_general(a, b, (((1,), (1,)), ((), ())), preferred_element_type=f32)


def mm_tn(a, b):
    return lax.dot_general(a, b, (((0,), (0,)), ((), ())), preferred_element_type=f32)


def mm_exact(a, b):
    return jnp.dot(a, b, precision=lax.Precision.HIGHEST, preferred_element_type=f32)


def two_terms(values):
    high = values.astype(bf16)
    return high, (values - high.astype(f32)).astype(bf16)


def two_terms_each(tiles):
    return zip(*(two_terms(tile) for tile in tiles))


def twice(a):
    return jnp.concatenate([a, a], axis=1)


def mm_two(a_twice, high, low):
    return mm(a_twice, jnp.concatenate([high, low], axis=0))


def sum_heads(ones_twice, highs, lows):
    return mm_nt(ones_twice, jnp.concatenate([*highs, *lows], axis=1))


def sigmoid(values):
    return 0.5 + 0.5 * jnp.tanh(0.5 * values)


def low_half(rows):
    return lax.broadcasted_iota(jnp.int32, (rows, LANES), 1) < HEAD_DIM


def spread_pair(values, kind, j):
    rows = values.shape[0]
    at = kind * HEADS + 2 * j
    return jnp.where(
        low_half(rows),
        jnp.broadcast_to(values[:, at : at + 1], (rows, LANES)),
        jnp.broadcast_to(values[:, at + 1 : at + 2], (rows, LANES)),
    )


def head_rows():
    row = lax.broadcasted_iota(jnp.int32, (16, WIDTH), 0)
    channel = lax.broadcasted_iota(jnp.int32, (16, WIDTH), 1) // HEAD_DIM
    return jnp.where(row == channel, 1.0, 0.0).astype(bf16)


def split_pair(block):
    low = low_half(block.shape[0])
    zero = jnp.zeros_like(block)
    return jnp.concatenate(
        [jnp.where(low, block, zero), jnp.where(low, zero, block)], axis=0
    )


def lanes(j):
    return slice(j * LANES, (j + 1) * LANES)


class Message:
    def __init__(self, rows):
        self.rows = rows
        self.per_chunk = CHUNK // rows

    def place(self, chunk, k):
        r = self.rows
        return (slice(chunk * self.per_chunk, (chunk + 1) * self.per_chunk), slice(k * r, (k + 1) * r))

    def get(self, ref, chunk, k):
        a, b = self.place(chunk, k)
        return ref[a, b, :].reshape(CHUNK, LANES)

    def put(self, ref, chunk, k, value):
        a, b = self.place(chunk, k)
        ref[a, b, :] = value.reshape(self.per_chunk, self.rows, LANES)


X, HALF = 0, PAIRS
FIRST = PAIRS + 1
Z, GRAD = 0, PAIRS
SECOND = 2 * PAIRS
LAST_X, LAST_B, LAST_Z, LAST_C = 0, PAIRS, PAIRS + 1, 2 * PAIRS + 1
LAST = 2 * PAIRS + 2


def pack_first(x_ref, b_ref, c_ref, steps_ref, out_ref, by_head):
    r = x_ref.shape[0]
    step = pl.program_id(0) * pl.num_programs(1) + pl.program_id(1)
    subs = out_ref.shape[0]

    @pl.when(step == 0)
    def _():
        steps = steps_ref[...].astype(f32)
        by_head[...] = jnp.concatenate([steps, jnp.zeros((LANES - r, LANES), f32)], axis=0).T

    zero = jnp.zeros((STEP_ROWS - HEADS, LANES), f32)
    for s in range(subs):
        for j in range(PAIRS):
            out_ref[s, 0, j * r : (j + 1) * r, :] = x_ref[:, lanes(s * PAIRS + j)]
        half = b_ref if s % 2 == 0 else c_ref
        out_ref[s, 0, HALF * r : (HALF + 1) * r, :] = half[:, lanes(s // 2)]
        at = pl.multiple_of((step * subs + s) * HEADS, HEADS)
        mine = jnp.concatenate([by_head[pl.ds(at, HEADS), :], zero], axis=0)
        out_ref[s, 0, FIRST * r :, :] = mine.astype(bf16)


def pack_second(z_ref, grad_ref, out_ref):
    r = z_ref.shape[0]
    for s in range(out_ref.shape[0]):
        for j in range(PAIRS):
            at = lanes(s * PAIRS + j)
            out_ref[s, 0, (Z + j) * r : (Z + j + 1) * r, :] = z_ref[:, at]
            out_ref[s, 0, (GRAD + j) * r : (GRAD + j + 1) * r, :] = grad_ref[:, at]


def add_halves(owners, in_ref, block, out_ref):
    r = out_ref.shape[0]
    peer_of = {own: peer for peer, own in enumerate(owners)}
    for g in range(GROUPS):
        halves = [
            in_ref[peer_of[2 * g + k], block * r : (block + 1) * r, :].astype(f32) for k in range(2)
        ]
        out_ref[:, lanes(g)] = (halves[0] + halves[1]).astype(bf16)


def unpack(owners, in_ref, x_ref, z_ref, b_ref, c_ref, steps_ref):
    r = x_ref.shape[0]
    peer_of = {own: peer for peer, own in enumerate(owners)}
    for peer, own in enumerate(owners):
        for j in range(PAIRS):
            for block, ref in ((LAST_X, x_ref), (LAST_Z, z_ref)):
                at = slice((block + j) * r, (block + j + 1) * r)
                ref[:, lanes(own * PAIRS + j)] = in_ref[peer, at, :]
    add_halves(owners, in_ref, LAST_B, b_ref)
    add_halves(owners, in_ref, LAST_C, c_ref)
    by_head = jnp.concatenate(
        [
            in_ref[peer_of[own], LAST * r : LAST * r + STEP_ROWS, :].astype(f32)[:HEADS]
            for own in range(OWNERS)
        ],
        axis=0,
    )
    steps_ref[...] = by_head.T[:r, :].astype(bf16)


GAIN_ROW, SKIP_ROW, LOGS_ROW, BIAS_ROW = HEADS, HEADS + PAIRS, HEADS + PAIRS + 1, HEADS + PAIRS + 2


def unpack_params(sub_count, tensor_count, tile_ref, mine_ref, out_ref):
    lane = lax.broadcasted_iota(jnp.int32, (1, LANES), 1)
    totals = [jnp.zeros((1, LANES), f32) for _ in range(3)]
    for s in range(sub_count):
        rows = jnp.zeros((STEP_ROWS, LANES), f32)
        for t in range(tensor_count):
            mine = mine_ref[t : t + 1, :] > 0.0
            rows = jnp.where(mine, tile_ref[s * tensor_count + t].astype(f32), rows)
        for k, at in enumerate((LOGS_ROW, BIAS_ROW, SKIP_ROW)):
            part = jnp.where(lane < HEADS, rows[at : at + 1], 0.0)
            totals[k] = totals[k] + (part if s == 0 else pltpu.roll(part, s * HEADS, 1))
        out_ref[8 + s * PAIRS : 8 + (s + 1) * PAIRS, :] = rows[GAIN_ROW : GAIN_ROW + PAIRS]
    out_ref[:8, :] = jnp.concatenate(totals + [jnp.zeros((5, LANES), f32)], axis=0)


def state_kernel(
    message, per_step,
    first_ref, sources_ref, steps_ref, heads_ref, sm_ref, smt_ref, own_ref, dec_ref, state_ref, whole_ref,
    carry, rows_s,
):
    c = pl.program_id(0)

    @pl.when(c == 0)
    def _():
        carry[...] = jnp.zeros_like(carry)
        whole_ref[...] = jnp.ones_like(whole_ref)
        chunks = rows_s.shape[0]
        before = lax.broadcasted_iota(jnp.int32, (CHUNK, CHUNK), 0)
        after = lax.broadcasted_iota(jnp.int32, (CHUNK, CHUNK), 1)
        raws = []
        for k in range(chunks):
            raw = heads_ref[HEADS:, :]
            for p in range(message.per_chunk):
                part = steps_ref[k * message.per_chunk + p].astype(f32)[:HEADS]
                raw = raw + (part if p == 0 else pltpu.roll(part, p * message.rows, 1))
            raws.append(raw)
        raw = jnp.concatenate(raws, axis=0)
        small = jnp.exp(-jnp.abs(raw))
        series = small * (
            1.0 - small * (0.5 - small * (1.0 / 3 - small * (0.25 - small * 0.2)))
        )
        soft = jnp.maximum(raw, 0.0) + jnp.where(small < 0.015625, series, jnp.log(1.0 + small))
        sig = jnp.where(raw >= 0.0, 1.0, small) / (1.0 + small)
        decay_rate = jnp.concatenate([jnp.exp(heads_ref[:HEADS, :])] * chunks, axis=0)
        rate = -decay_rate * soft
        cum = mm_exact(rate, jnp.where(before <= after, 1.0, 0.0))
        rest = mm_exact(rate, jnp.where(before > after, 1.0, 0.0))
        kinds = [
            soft, cum, soft * jnp.exp(rest), cum - jnp.log(soft), jnp.exp(cum), rate, sig,
            jnp.zeros_like(soft),
        ]
        for k in range(chunks):
            at = slice(k * HEADS, (k + 1) * HEADS)
            rows_s[k] = jnp.concatenate([kind[at] for kind in kinds], axis=0)

    made = []
    state = [carry[:, lanes(j)] for j in range(PAIRS)]
    decays = [whole_ref[:, lanes(j)] for j in range(PAIRS)]
    for i in range(per_step):
        rows = rows_s[c * per_step + i]
        sm = jnp.concatenate([rows, jnp.zeros_like(rows)], axis=0).T
        last = jnp.broadcast_to(sm[CHUNK - 1 : CHUNK, :], (8, LANES))
        sources_t = twice(message.get(sources_ref, i, 0).T)
        decs, owns = [], []
        for j in range(PAIRS):
            dec = spread_pair(last, ECUM, j)
            scaled = message.get(first_ref, i, X + j).astype(f32) * spread_pair(sm, WEIGHT, j)
            own = mm_two(sources_t, *two_terms(scaled))
            state[j] = dec[0:1] * state[j] + own
            decays[j] = decays[j] * dec
            decs.append(dec)
            owns.append(own)
        made.append((rows, sm, decs, owns))
    for i, (rows, sm, decs, owns) in enumerate(made):
        smt_ref[:, lanes(i)] = rows
        sm_ref[i * CHUNK : (i + 1) * CHUNK, :] = sm
        for j in range(PAIRS):
            dec_ref[i, :, lanes(j)] = decs[j]
            own_ref[i, :, lanes(j)] = owns[j]
    for j in range(PAIRS):
        carry[:, lanes(j)] = state[j]
        whole_ref[:, lanes(j)] = decays[j]
        state_ref[:, lanes(j)] = state[j].astype(bf16)


def within_kernel(
    message, per_step,
    first_ref, sources_ref, readers_ref, sm_ref, smt_ref, own_ref, dec_ref, y_ref, start_ref, pre_ref, carry, pre,
):
    @pl.when(pl.program_id(0) == 0)
    def _():
        carry[...] = jnp.zeros_like(carry)
        pre[...] = jnp.ones_like(pre)

    t = lax.broadcasted_iota(jnp.int32, (CHUNK, CHUNK), 0)
    s = lax.broadcasted_iota(jnp.int32, (CHUNK, CHUNK), 1)
    made = []
    states = [carry[:, lanes(j)] for j in range(PAIRS)]
    before = pre[...]
    for i in range(per_step):
        rows = slice(i * CHUNK, (i + 1) * CHUNK)
        sm = sm_ref[rows, :]
        smt = smt_ref[:, lanes(i)]
        readers = message.get(readers_ref, i, 0)
        readers_twice = twice(readers)
        scores = jnp.where(t >= s, mm_nt(readers, message.get(sources_ref, i, 0)), 0.0)
        ys = []
        for j in range(PAIRS):
            weights = []
            for h in (2 * j, 2 * j + 1):
                here = sm[:, CUM * HEADS + h : CUM * HEADS + h + 1]
                there = smt[SHIFTED * HEADS + h : SHIFTED * HEADS + h + 1, :]
                weights.append(
                    (scores * jnp.exp(jnp.minimum(here - there, CLAMP))).astype(bf16)
                )
            values = split_pair(message.get(first_ref, i, X + j))
            within = mm(jnp.concatenate(weights, axis=1), values)
            carried = mm_two(readers_twice, *two_terms(states[j]))
            ys.append(within + spread_pair(sm, ECUM, j) * carried)
        made.append((ys, list(states), before))
        for j in range(PAIRS):
            states[j] = dec_ref[i, 0:1, lanes(j)] * states[j] + own_ref[i, :, lanes(j)]
        before = before * dec_ref[i]
    for i, (ys, starts, prefix) in enumerate(made):
        pre_ref[i] = prefix
        for j in range(PAIRS):
            y_ref[i * CHUNK : (i + 1) * CHUNK, lanes(j)] = ys[j]
            start_ref[i, :, lanes(j)] = starts[j]
    pre[...] = before
    for j in range(PAIRS):
        carry[:, lanes(j)] = states[j]


def mix_kernel(
    message, per_step,
    first_ref, readers_ref, second_ref, within_ref, ecum_ref, inbound_ref, pre_ref, gain_ref, skip_ref,
    y_ref, sums_ref,
):
    inbound = inbound_ref[...].astype(bf16)
    fill = jnp.zeros((LANES - HEADS, CHUNK), f32)
    for i in range(per_step):
        rows = slice(i * CHUNK, (i + 1) * CHUNK)
        ecum = jnp.concatenate([ecum_ref[:, lanes(i)], fill], axis=0).T
        carried = mm(message.get(readers_ref, i, 0), inbound)
        power = jnp.zeros((CHUNK, LANES), f32)
        cross = jnp.zeros((CHUNK, LANES), f32)
        for j in range(PAIRS):
            at = lanes(j)
            decay = spread_pair(ecum, 0, j) * pre_ref[i, 0:1, at]
            y = within_ref[rows, at] + decay * carried[:, at]
            y_ref[rows, at] = y
            values = message.get(first_ref, i, X + j).astype(f32)
            gates = message.get(second_ref, i, Z + j).astype(f32)
            grad = message.get(second_ref, i, GRAD + j).astype(f32)
            gated = (y + skip_ref[0:1, at] * values) * (gates * sigmoid(gates))
            power = power + gated * gated
            cross = cross + grad * gain_ref[0:1, at] * gated
        sums_ref[i, 0:1, :] = jnp.sum(power.T, axis=0, keepdims=True)
        sums_ref[i, 1:2, :] = jnp.sum(cross.T, axis=0, keepdims=True)
        sums_ref[i, 2:, :] = jnp.zeros((6, LANES), f32)


def norm_factors(sums):
    sums = sums * (1.0 / GROUP_WIDTH)
    inverse = lax.rsqrt(sums[0:1] + epsilon)
    pull = inverse * inverse * inverse * sums[1:2]
    return (
        jnp.broadcast_to(inverse, (CHUNK, LANES)).T,
        jnp.broadcast_to(pull, (CHUNK, LANES)).T,
    )


def norm_kernel(
    message, per_step,
    first_ref, readers_ref, second_ref, y_ref, sm_ref, pre_ref, sums_ref, other_ref, gain_ref, skip_ref,
    mixed_ref, back_ref, slab_ref,
    back_sum,
):
    @pl.when(pl.program_id(0) == 0)
    def _():
        back_sum[...] = jnp.zeros_like(back_sum)

    sums = [back_sum[:, lanes(j)] for j in range(PAIRS)]
    for i in range(per_step):
        rows = slice(i * CHUNK, (i + 1) * CHUNK)
        sm = sm_ref[rows, :]
        readers_t = twice(message.get(readers_ref, i, 0).T)
        inverse, pull = norm_factors(sums_ref[i] + other_ref[i])
        for j in range(PAIRS):
            at = lanes(j)
            values = message.get(first_ref, i, X + j).astype(f32)
            gates = message.get(second_ref, i, Z + j).astype(f32)
            grad = message.get(second_ref, i, GRAD + j).astype(f32)
            silu = gates * sigmoid(gates)
            gated = (y_ref[rows, at] + skip_ref[0:1, at] * values) * silu
            d_mixed = (inverse * grad * gain_ref[0:1, at] - pull * gated) * silu
            back = mm_two(readers_t, *two_terms(d_mixed * spread_pair(sm, ECUM, j)))
            sums[j] = sums[j] + pre_ref[i, 0:1, at] * back
            mixed_ref[rows, at] = d_mixed.astype(bf16)
            back_ref[i, :, at] = back
    for j in range(PAIRS):
        back_sum[:, lanes(j)] = sums[j]
        slab_ref[:, lanes(j)] = sums[j].astype(bf16)


def local_kernel(
    message, per_step,
    first_ref, sources_ref, readers_ref, second_ref, y_ref, grad_ref, sm_ref, smt_ref, start_ref, pre_ref, inbound_ref,
    sums_ref, other_ref, gain_ref, skip_ref,
    values_out, sources_out, readers_out, gate_ref, e_ref, start_out, param_ref,
    gain_sum, skip_sum,
):
    c = pl.program_id(0)

    @pl.when(c == 0)
    def _():
        gain_sum[...] = jnp.zeros_like(gain_sum)
        skip_sum[...] = jnp.zeros_like(skip_sum)

    s = lax.broadcasted_iota(jnp.int32, (CHUNK, CHUNK), 0)
    t = lax.broadcasted_iota(jnp.int32, (CHUNK, CHUNK), 1)
    causal = t >= s
    ones = head_rows()
    ones_twice = twice(ones)
    gains = [gain_sum[0:1, lanes(j)] for j in range(PAIRS)]
    skips = [skip_sum[0:1, lanes(j)] for j in range(PAIRS)]
    for i in range(per_step):
        rows = slice(i * CHUNK, (i + 1) * CHUNK)
        sm = sm_ref[rows, :]
        smt = smt_ref[:, lanes(i)]
        sources = message.get(sources_ref, i, 0)
        readers = message.get(readers_ref, i, 0)
        inverse, pull = norm_factors(sums_ref[i] + other_ref[i])
        scores = jnp.where(causal, mm_nt(sources, readers), 0.0)
        total = jnp.zeros((CHUNK, CHUNK), f32)
        d_values, d_gates, highs, lows, scaleds, starts = [], [], [], [], [], []
        for j in range(PAIRS):
            at = lanes(j)
            rounded = grad_ref[rows, at]
            grads = split_pair(rounded)
            x = message.get(first_ref, i, X + j)
            weight_grads = mm_nt(x, grads)
            weights = []
            for k, h in enumerate((2 * j, 2 * j + 1)):
                there = sm[:, SHIFTED * HEADS + h : SHIFTED * HEADS + h + 1]
                here = smt[CUM * HEADS + h : CUM * HEADS + h + 1, :]
                decay = jnp.exp(jnp.minimum(here - there, CLAMP))
                weights.append((scores * decay).astype(bf16))
                total = total + weight_grads[:, lanes(k)] * decay
            d_values.append(mm(jnp.concatenate(weights, axis=1), grads))

            values = x.astype(f32)
            gates = message.get(second_ref, i, Z + j).astype(f32)
            grad = message.get(second_ref, i, GRAD + j).astype(f32)
            y = y_ref[rows, at]
            mixed = y + skip_ref[0:1, at] * values
            sig = sigmoid(gates)
            silu = gates * sig
            gated = mixed * silu
            scaled = inverse * grad
            gains[j] = gains[j] + jnp.sum(scaled * gated, axis=0, keepdims=True)
            d_gated = scaled * gain_ref[0:1, at] - pull * gated
            d_gate = d_gated * mixed * (sig + silu * (1.0 - sig))
            d_gates.append(d_gate.astype(bf16))
            skips[j] = skips[j] + jnp.sum(values * (d_gated * silu), axis=0, keepdims=True)
            d_mixed = rounded.astype(f32)
            high, low = two_terms(d_mixed * y)
            highs.append(high)
            lows.append(low)
            scaleds.append((d_mixed * spread_pair(sm, ECUM, j)).astype(bf16))
            starts.append(
                start_ref[i, :, at] + pre_ref[i, 0:1, at] * inbound_ref[:, at].astype(f32)
            )
        e = sum_heads(ones_twice, highs, lows)
        total = jnp.where(causal, total, 0.0).astype(bf16)
        start = jnp.concatenate([part.astype(bf16) for part in starts], axis=1)
        d_readers = mm_tn(total, sources) + mm_nt(jnp.concatenate(scaleds, axis=1), start)
        for j in range(PAIRS):
            values_out[rows, lanes(j)] = d_values[j]
            message.put(gate_ref, i, j, d_gates[j])
            start_out[i, :, lanes(j)] = starts[j]
        e_ref[:, lanes(i)] = e[:HEADS]
        sources_out[rows, :] = mm(total, readers)
        message.put(readers_out, i, 0, d_readers.astype(bf16))
    for j in range(PAIRS):
        gain_sum[0:1, lanes(j)] = gains[j]
        skip_sum[0:1, lanes(j)] = skips[j]

    @pl.when(c == pl.num_programs(0) - 1)
    def _():
        for j in range(PAIRS):
            param_ref[j : j + 1, :] = gain_sum[0:1, lanes(j)]
        high, low = two_terms(jnp.broadcast_to(skip_sum[0:1, :], (LANES, WIDTH)))
        skips = (mm_nt(high, ones) + mm_nt(low, ones))[0:1]
        param_ref[PAIRS : PAIRS + 1, :] = jnp.concatenate(
            [skips, jnp.zeros((1, LANES - 16), f32)], axis=1
        )
        param_ref[PAIRS + 1 :, :] = jnp.zeros((8 - PAIRS - 1, LANES), f32)


def last_kernel(
    message, per_step,
    first_ref, sources_ref, within_ref, d_sources_ref, d_readers_ref, gate_ref, grad_ref, e_ref, sm_ref, smt_ref, outer_ref,
    back_ref, start_ref, dec_ref, skip_ref, heads_ref, early_ref,
    out_ref,
    carry, sums, message_s, sent,
):
    c = pl.program_id(0)

    @pl.when(c == 0)
    def _():
        carry[...] = outer_ref[...].astype(f32)
        sums[...] = jnp.zeros_like(sums)

    r = message.rows
    ones = head_rows()
    ones_twice = twice(ones)
    before = lax.broadcasted_iota(jnp.int32, (CHUNK, CHUNK), 0)
    after = lax.broadcasted_iota(jnp.int32, (CHUNK, CHUNK), 1)
    earlier = jnp.where(before < after, 1.0, 0.0)
    decay_rate = jnp.exp(heads_ref[:HEADS, :])
    first_peer = (pl.num_programs(0) - 1 - c) * per_step * message.per_chunk
    mine = message_s.at[pl.ds(first_peer, per_step * message.per_chunk)]
    chunks = sent.shape[0] - 3

    def body_copy(chunk):
        at = (pl.ds(chunk * message.per_chunk, message.per_chunk), pl.ds(0, LAST_Z * r))
        return pltpu.make_async_copy(message_s.at[at], out_ref.at[at], sent.at[chunk])

    gates_copy = pltpu.make_async_copy(
        gate_ref, out_ref.at[:, pl.ds(LAST_Z * r, PAIRS * r)], sent.at[chunks]
    )
    readers_copy = pltpu.make_async_copy(
        d_readers_ref, out_ref.at[:, pl.ds(LAST_C * r, r)], sent.at[chunks + 1]
    )

    @pl.when(c == 0)
    def _():
        gates_copy.start()
        readers_copy.start()

    states = [carry[:, lanes(j)] for j in range(PAIRS)]
    logs_sum, steps_sum = sums[:HEADS, :], sums[HEADS:, :]
    for i in reversed(range(per_step)):
        rows = slice(i * CHUNK, (i + 1) * CHUNK)
        sm = sm_ref[rows, :]
        sources_twice = twice(message.get(sources_ref, i, 0))
        d_values, highs, lows, scaleds, rounded, fluxes = [], [], [], [], [], []
        for j in range(PAIRS):
            at = lanes(j)
            high, low = two_terms(states[j])
            rounded.append(high)
            values = message.get(first_ref, i, X + j).astype(f32)
            weight = spread_pair(sm, WEIGHT, j)
            grad = within_ref[rows, at] + weight * mm_two(sources_twice, high, low)
            skipped = skip_ref[0:1, at] * grad_ref[rows, at].astype(f32)
            d_values.append((grad + skipped).astype(bf16))
            high, low = two_terms(values * grad)
            highs.append(high)
            lows.append(low)
            scaleds.append((values * weight).astype(bf16))
            states[j] = dec_ref[i, 0:1, at] * states[j] + back_ref[i, :, at]
            fluxes.append(
                jnp.broadcast_to(
                    jnp.sum(start_ref[i, :, at] * states[j], axis=0, keepdims=True), (16, LANES)
                )
            )
        d_sources = d_sources_ref[rows, :] + mm_nt(
            jnp.concatenate(scaleds, axis=1), jnp.concatenate(rounded, axis=1)
        )
        g = sum_heads(ones_twice, highs, lows)[:HEADS]
        constant = sum_heads(ones_twice, *two_terms_each(fluxes))[:HEADS, 0:1]
        flux = constant + mm_exact(g - e_ref[:, lanes(i)], earlier)
        soft = smt_ref[DT * HEADS : (DT + 1) * HEADS, lanes(i)]
        rate = smt_ref[RATE * HEADS : (RATE + 1) * HEADS, lanes(i)]
        sig = smt_ref[SIG * HEADS : (SIG + 1) * HEADS, lanes(i)]
        steps = (g / soft - decay_rate * flux) * sig
        logs_sum = logs_sum + flux * rate
        steps_sum = steps_sum + steps
        steps = jnp.concatenate([steps, jnp.zeros_like(steps)], axis=0)
        for j in range(PAIRS):
            message.put(mine, i, LAST_X + j, d_values[j])
        message.put(mine, i, LAST_B, d_sources.astype(bf16))
        for p in range(message.per_chunk):
            part = steps if p == 0 else pltpu.roll(steps, LANES - p * r, 1)
            mine[i * message.per_chunk + p, LAST * r : LAST * r + STEP_ROWS, :] = part.astype(bf16)
        body_copy((pl.num_programs(0) - 1 - c) * per_step + i).start()
    for j in range(PAIRS):
        carry[:, lanes(j)] = states[j]
    sums[:HEADS, :] = logs_sum
    sums[HEADS:, :] = steps_sum

    @pl.when(c == pl.num_programs(0) - 1)
    def _():
        late = []
        for k in range(2):
            column = jnp.sum(sums[k * HEADS : (k + 1) * HEADS, :], axis=1, keepdims=True)
            block = jnp.broadcast_to(column, (HEADS, LANES))
            block = jnp.concatenate([block, jnp.zeros((LANES - HEADS, LANES), f32)], axis=0)
            late.append(block.T[0:1, :])
        small = [
            jnp.zeros((HEADS, LANES), f32), early_ref[: PAIRS + 1, :], *late,
            jnp.zeros((STEP_ROWS - BIAS_ROW - 1, LANES), f32),
        ]
        small = jnp.concatenate(small, axis=0).astype(bf16)
        own_rows = lax.broadcasted_iota(jnp.int32, (STEP_ROWS, LANES), 0) < HEADS

        def fill(peer, unused):
            steps_at = slice(LAST * r, LAST * r + STEP_ROWS)
            message_s[peer, steps_at, :] = jnp.where(own_rows, message_s[peer, steps_at, :], small)
            return unused

        lax.fori_loop(0, message_s.shape[0], fill, 0)
        at = (slice(None), pl.ds(LAST * r, STEP_ROWS))
        tiles = pltpu.make_async_copy(message_s.at[at], out_ref.at[at], sent.at[chunks + 2])
        tiles.start()
        for chunk in range(chunks):
            body_copy(chunk).wait()
        gates_copy.wait()
        readers_copy.wait()
        tiles.wait()


def finish(own_ref, other_ref, logs_ref, skip_ref, bias_ref, gain_ref):
    total = own_ref[...] + other_ref[...]
    count = logs_ref.shape[1]
    logs_ref[...] = total[0:1, :count]
    bias_ref[...] = total[1:2, :count]
    skip_ref[...] = total[2:3, :count]
    gain_ref[...] = total[8:]


def call(kernel, out_shape, flops, moved, grid=None, in_specs=None, out_specs=None, scratch=()):
    extra = {}
    if grid is not None:
        extra = dict(grid=grid, in_specs=in_specs, out_specs=out_specs)
    return pl.pallas_call(
        kernel,
        out_shape=out_shape,
        scratch_shapes=list(scratch),
        compiler_params=pltpu.CompilerParams(vmem_limit_bytes=28 * 1024 * 1024),
        cost_estimate=pl.CostEstimate(flops=flops, bytes_accessed=moved, transcendentals=0),
        **extra,
    )


def shifted(array, count, by):
    pairs = [(i, i + by) for i in range(count) if 0 <= i + by < count]
    return lax.ppermute(array, "slab", pairs)


def carry_over(state, decay, first_decay, count, sign):
    window, window_decay, step = state, decay, 1
    result = result_decay = None
    while step < count:
        arrived = shifted(window, count, sign * step)
        more = 2 * step < count
        if result is None:
            result = arrived
            if more:
                result_decay = first_decay
                window = (state.astype(f32) + decay[0:1] * arrived.astype(f32)).astype(bf16)
                window_decay = decay * first_decay
        else:
            if more:
                arrived_decay = shifted(window_decay, count, sign * step)
                window = (window.astype(f32) + window_decay[0:1] * arrived.astype(f32)).astype(bf16)
                window_decay = window_decay * arrived_decay
            result = result.astype(f32) + result_decay[0:1] * arrived.astype(f32)
            if more:
                result_decay = result_decay * arrived_decay
        step *= 2
    return jnp.zeros_like(state) if result is None else result


def two_parts(array, axis, count):
    step, other = 1, jnp.zeros_like(array)
    while step < count:
        array = array if step == 1 else array + other
        other = lax.ppermute(array, axis, [(i, i ^ step) for i in range(count)])
        step *= 2
    return array, other


def on_device(
    slab_count, sub_count, tensor_count,
    mixer_x, gate_z, b_matrix, c_matrix, raw_steps, decay_log, skip_gain, step_bias, norm_gain, out_grad,
):
    rows = mixer_x.shape[0]
    peers = sub_count * tensor_count
    tokens = rows * peers
    chunks = tokens // CHUNK
    message = Message(rows)
    owners = [t * sub_count + s for s in range(sub_count) for t in range(tensor_count)]
    sub = lax.axis_index("sub")

    def struct(shape, kind=f32):
        return jax.ShapeDtypeStruct(shape, kind)

    def hbm(shape, kind=f32):
        return pltpu.HBM(shape, kind)

    def in_hbm(array):
        return pltpu.with_memory_space_constraint(array, pltpu.HBM)

    def exchange(array):
        return lax.all_to_all(array, ("sub", "tensor"), split_axis=0, concat_axis=0, tiled=True)

    own_logs = lax.dynamic_slice(decay_log, (sub * HEADS,), (HEADS,))
    own_bias = lax.dynamic_slice(step_bias, (sub * HEADS,), (HEADS,))
    own_skip = lax.dynamic_slice(skip_gain, (sub * HEADS,), (HEADS,))
    own_gain = lax.dynamic_slice(norm_gain, (sub * WIDTH,), (WIDTH,)).reshape(1, WIDTH)
    heads = jnp.broadcast_to(jnp.concatenate([own_logs, own_bias])[:, None], (2 * HEADS, LANES))
    skip_row = jnp.repeat(own_skip, HEAD_DIM).reshape(1, WIDTH)

    first_rows = FIRST * rows + STEP_ROWS
    second_rows = SECOND * rows
    last_rows = LAST * rows + STEP_ROWS

    def packed(kernel, height, arrays, whole_arrays=(), scratch=()):
        out = hbm((sub_count, tensor_count, height, LANES), bf16)
        moved = 4 * peers * height * LANES
        runs = 1
        parts = tensor_count * runs
        specs = [
            pl.BlockSpec((rows, a.shape[1] // parts), lambda t, k: (0, t * runs + k)) for a in arrays
        ] + [pl.BlockSpec(a.shape, lambda t, k: (0, 0)) for a in whole_arrays]
        out_spec = pl.BlockSpec((sub_count // runs, 1, height, LANES), lambda t, k: (k, t, 0, 0))
        made = call(kernel, out, 0, moved, (tensor_count, runs), specs, out_spec, scratch)(
            *(in_hbm(a) for a in (*arrays, *whole_arrays))
        )
        return made.reshape(peers, height, LANES)

    first = exchange(
        packed(
            pack_first, first_rows, (mixer_x, b_matrix, c_matrix), (raw_steps,),
            [pltpu.VMEM((LANES, LANES), f32)],
        )
    )
    tensor_rows = lax.broadcasted_iota(jnp.int32, (tensor_count, LANES), 0)
    mine = (tensor_rows == lax.axis_index("tensor")).astype(f32)
    half = first[:, HALF * rows : (HALF + 1) * rows, :]
    other_half = lax.ppermute(half, "sub", [(i, i ^ 1) for i in range(sub_count)])
    even = sub % 2 == 0
    sources, readers = jnp.where(even, half, other_half), jnp.where(even, other_half, half)
    gate_z, heads, skip_row, own_gain, mine = lax.optimization_barrier(
        (gate_z, heads, skip_row, own_gain, mine)
    )
    second = exchange(packed(pack_second, second_rows, (gate_z, out_grad)))

    def flow(kernel, shape_specs, flops, moved, in_specs, scratch=(), per=2):
        per = min(per, chunks)

        def body(*refs):
            return kernel(message, per, *refs)

        shapes = tuple(shape for shape, _ in shape_specs)
        specs = tuple(spec for _, spec in shape_specs)
        return call(body, shapes, flops, moved, (chunks // per,), in_specs, specs, scratch)

    def specs_of(per, down=False):
        per = min(per, chunks)
        steps = chunks // per

        def spec(block, axis):
            def index(c):
                at = steps - 1 - c if down else c
                return tuple(at if k == axis else 0 for k in range(len(block)))

            return pl.BlockSpec(block, index)

        return dict(
            message=lambda height: spec((per * message.per_chunk, height, LANES), 0),
            token=lambda width: spec((per * CHUNK, width), 0),
            lane=lambda height: spec((height, per * CHUNK), 1),
            chunk=lambda *shape: spec((per,) + shape, 0),
        )

    up = specs_of(2)
    many = specs_of(4)
    dn = specs_of(8, down=True)

    def whole(*shape):
        return pl.BlockSpec(shape, lambda c: (0,) * len(shape))

    unit = 2 * tokens * CHUNK * WIDTH
    size = tokens * WIDTH

    sm, smt, own, dec, state, decay = flow(
        state_kernel,
        [
            (hbm((tokens, LANES)), up["token"](LANES)),
            (hbm((KINDS * HEADS, tokens)), up["lane"](KINDS * HEADS)),
            (hbm((chunks, STATE, WIDTH)), up["chunk"](STATE, WIDTH)),
            (hbm((chunks, 8, WIDTH)), up["chunk"](8, WIDTH)),
            (struct((STATE, WIDTH), bf16), whole(STATE, WIDTH)),
            (struct((8, WIDTH)), whole(8, WIDTH)),
        ],
        2 * unit, size * 8,
        [
            up["message"](PAIRS * rows), up["message"](rows),
            pl.BlockSpec((peers, STEP_ROWS, LANES), lambda c: (0, FIRST * rows // STEP_ROWS, 0)),
            whole(2 * HEADS, LANES),
        ],
        [pltpu.VMEM((STATE, WIDTH), f32), pltpu.VMEM((chunks, KINDS * HEADS, LANES), f32)],
    )(first, in_hbm(sources), first, heads)

    before = after = None
    if slab_count > 2:
        before, after = shifted(decay, slab_count, 1), shifted(decay, slab_count, -1)
    inbound = carry_over(state, decay, before, slab_count, 1)

    within, starts, pre = flow(
        within_kernel,
        [
            (hbm((tokens, WIDTH)), up["token"](WIDTH)),
            (hbm((chunks, STATE, WIDTH)), up["chunk"](STATE, WIDTH)),
            (hbm((chunks, 8, WIDTH)), up["chunk"](8, WIDTH)),
        ],
        6 * unit, size * 16,
        [
            up["message"](PAIRS * rows), up["message"](rows), up["message"](rows),
            up["token"](LANES), up["lane"](KINDS * HEADS),
            up["chunk"](STATE, WIDTH), up["chunk"](8, WIDTH),
        ],
        [pltpu.VMEM((STATE, WIDTH), f32), pltpu.VMEM((8, WIDTH), f32)],
    )(first, in_hbm(sources), in_hbm(readers), in_hbm(sm), in_hbm(smt), in_hbm(own), in_hbm(dec))

    anywhere = pl.BlockSpec(memory_space=pl.ANY)
    per_mix = min(2, chunks)
    ecum_block = pl.BlockSpec((HEADS, per_mix * CHUNK), lambda c: (ECUM, c))
    y, sums = flow(
        mix_kernel,
        [
            (struct((tokens, WIDTH)), up["token"](WIDTH)),
            (struct((chunks, 8, LANES)), up["chunk"](8, LANES)),
        ],
        unit, size * 16,
        [
            up["message"](PAIRS * rows), up["message"](rows), up["message"](second_rows),
            up["token"](WIDTH), ecum_block, whole(STATE, WIDTH), up["chunk"](8, WIDTH),
            whole(1, WIDTH), whole(1, WIDTH),
        ],
        per=per_mix,
    )(
        first, in_hbm(readers), second, in_hbm(within), in_hbm(smt), inbound, in_hbm(pre),
        own_gain, skip_row,
    )

    partner = lax.ppermute(sums, "sub", [(i, i ^ 1) for i in range(sub_count)])

    d_mixed, back, slab_back = flow(
        norm_kernel,
        [
            (struct((tokens, WIDTH), bf16), many["token"](WIDTH)),
            (struct((chunks, STATE, WIDTH)), many["chunk"](STATE, WIDTH)),
            (struct((STATE, WIDTH), bf16), whole(STATE, WIDTH)),
        ],
        2 * unit, size * 12,
        [
            many["message"](PAIRS * rows), many["message"](rows), many["message"](second_rows),
            many["token"](WIDTH), many["token"](LANES), many["chunk"](8, WIDTH), many["chunk"](8, LANES),
            many["chunk"](8, LANES), whole(1, WIDTH), whole(1, WIDTH),
        ],
        [pltpu.VMEM((STATE, WIDTH), f32)],
        per=4,
    )(first, readers, second, y, sm, pre, sums, partner, own_gain, skip_row)

    outer = carry_over(slab_back, decay, after, slab_count, -1)

    d_values, d_sources, d_readers, d_gates, e, starts, params = flow(
        local_kernel,
        [
            (struct((tokens, WIDTH)), many["token"](WIDTH)),
            (struct((tokens, STATE)), many["token"](STATE)),
            (struct((peers, rows, LANES), bf16), many["message"](rows)),
            (struct((peers, PAIRS * rows, LANES), bf16), many["message"](PAIRS * rows)),
            (struct((HEADS, tokens)), many["lane"](HEADS)),
            (struct((chunks, STATE, WIDTH)), many["chunk"](STATE, WIDTH)),
            (struct((8, LANES)), whole(8, LANES)),
        ],
        10 * unit, size * 16,
        [
            many["message"](PAIRS * rows), many["message"](rows), many["message"](rows),
            many["message"](second_rows), many["token"](WIDTH), many["token"](WIDTH), many["token"](LANES),
            many["lane"](KINDS * HEADS),
            many["chunk"](STATE, WIDTH), many["chunk"](8, WIDTH), whole(STATE, WIDTH),
            many["chunk"](8, LANES), many["chunk"](8, LANES), whole(1, WIDTH), whole(1, WIDTH),
        ],
        [pltpu.VMEM((8, WIDTH), f32), pltpu.VMEM((8, WIDTH), f32)],
        per=4,
    )(
        first, sources, readers, second, y, d_mixed, sm, smt, starts, pre, inbound,
        sums, partner, own_gain, skip_row,
    )

    (last,) = flow(
        last_kernel,
        [(hbm((peers, last_rows, LANES), bf16), anywhere)],
        4 * unit, size * 16,
        [
            dn["message"](PAIRS * rows), dn["message"](rows), dn["token"](WIDTH), dn["token"](STATE),
            anywhere, anywhere,
            dn["token"](WIDTH), dn["lane"](HEADS), dn["token"](LANES), dn["lane"](KINDS * HEADS),
            whole(STATE, WIDTH), dn["chunk"](STATE, WIDTH), dn["chunk"](STATE, WIDTH),
            dn["chunk"](8, WIDTH), whole(1, WIDTH), whole(2 * HEADS, LANES), whole(8, LANES),
        ],
        [
            pltpu.VMEM((STATE, WIDTH), f32), pltpu.VMEM((2 * HEADS, LANES), f32),
            pltpu.VMEM((peers, last_rows, LANES), bf16),
            pltpu.SemaphoreType.DMA((chunks + 3,)),
        ],
        per=8,
    )(
        first, sources, d_values, d_sources, d_readers, d_gates, d_mixed, e, sm, smt, outer, back,
        starts, dec, skip_row, heads, params,
    )

    last_back = exchange(last)
    tile_at = LAST * rows // STEP_ROWS
    def tile(at):
        return pl.BlockSpec((peers, STEP_ROWS, LANES), lambda c: (0, at, 0))

    params = call(
        lambda *refs: unpack_params(sub_count, tensor_count, *refs),
        struct((8 + sub_count * PAIRS, LANES)),
        0, 4 * peers * STEP_ROWS * LANES, (1,),
        [tile(tile_at), whole(tensor_count, LANES)],
        whole(8 + sub_count * PAIRS, LANES),
    )(last_back, mine)
    own_params, other_params = two_parts(params, "slab", slab_count)
    wide, narrow = struct((rows, CHANNELS), bf16), struct((rows, GROUPS * STATE), bf16)
    grad_x, grad_gates, grad_b, grad_c, grad_steps = call(
        lambda *refs: unpack(owners, *refs),
        (wide, wide, narrow, narrow, struct((rows, MIXER_HEADS), bf16)),
        0, 10 * rows * CHANNELS,
    )(last_back)
    row = struct((1, sub_count * HEADS))
    grad_logs, grad_skip, grad_bias, grad_gain = call(
        finish, (row, row, row, struct((sub_count * PAIRS, LANES))), 0, 1 << 16,
    )(own_params, other_params)
    return (
        grad_x,
        grad_gates,
        grad_b,
        grad_c,
        grad_steps,
        grad_logs.reshape(-1),
        grad_skip.reshape(-1),
        grad_bias.reshape(-1),
        grad_gain.reshape(-1),
    )


def solution(mesh):
    tensor_count = mesh.shape["tensor"]
    sub_count = OWNERS // tensor_count
    slab_count = mesh.shape["dp"] // sub_count
    devices = mesh.devices.reshape(slab_count, sub_count, tensor_count)
    split_mesh = Mesh(devices, ("slab", "sub", "tensor"))
    rows = P(("slab", "sub", "tensor"), None)
    param = P("tensor")

    def local(*arrays):
        return on_device(slab_count, sub_count, tensor_count, *arrays)

    return jax.shard_map(
        local,
        mesh=split_mesh,
        in_specs=(rows,) * 5 + (param,) * 4 + (rows,),
        out_specs=(rows,) * 5 + (param,) * 4,
        check_vma=False,
    )
```

```python
import jax
import jax.numpy as jnp
from jax import lax
from jax.experimental import pallas as pl
from jax.experimental.pallas import tpu as pltpu
from jax.sharding import Mesh
from jax.sharding import PartitionSpec as P

MIXER_HEADS = 128
HEAD_DIM = 64
STATE = 128
GROUPS = 8
CHANNELS = MIXER_HEADS * HEAD_DIM
HEADS = 8
WIDTH = HEADS * HEAD_DIM
GROUP_WIDTH = 2 * WIDTH
OWNERS = MIXER_HEADS // HEADS
LANES = 128
PAIRS = WIDTH // LANES
CHUNK = 128
STEP_ROWS = 16
epsilon = 1e-05
f32 = jnp.float32
bf16 = jnp.bfloat16

DT, CUM, WEIGHT, SHIFTED, ECUM, RATE, SIG = range(7)
KINDS = 8
CLAMP = 80.0


def mm(a, b):
    return jnp.dot(a, b, preferred_element_type=f32)


def mm_nt(a, b):
    return lax.dot_general(a, b, (((1,), (1,)), ((), ())), preferred_element_type=f32)


def mm_tn(a, b):
    return lax.dot_general(a, b, (((0,), (0,)), ((), ())), preferred_element_type=f32)


def mm_exact(a, b):
    return jnp.dot(a, b, precision=lax.Precision.HIGHEST, preferred_element_type=f32)


def two_terms(values):
    high = values.astype(bf16)
    return high, (values - high.astype(f32)).astype(bf16)


def two_terms_each(tiles):
    return zip(*(two_terms(tile) for tile in tiles))


def twice(a):
    return jnp.concatenate([a, a], axis=1)


def mm_two(a_twice, high, low):
    return mm(a_twice, jnp.concatenate([high, low], axis=0))


def sum_heads(ones_twice, highs, lows):
    return mm_nt(ones_twice, jnp.concatenate([*highs, *lows], axis=1))


def sigmoid(values):
    return 0.5 + 0.5 * jnp.tanh(0.5 * values)


def low_half(rows):
    return lax.broadcasted_iota(jnp.int32, (rows, LANES), 1) < HEAD_DIM


def spread_pair(values, kind, j):
    rows = values.shape[0]
    at = kind * HEADS + 2 * j
    return jnp.where(
        low_half(rows),
        jnp.broadcast_to(values[:, at : at + 1], (rows, LANES)),
        jnp.broadcast_to(values[:, at + 1 : at + 2], (rows, LANES)),
    )


def head_rows():
    row = lax.broadcasted_iota(jnp.int32, (16, WIDTH), 0)
    channel = lax.broadcasted_iota(jnp.int32, (16, WIDTH), 1) // HEAD_DIM
    return jnp.where(row == channel, 1.0, 0.0).astype(bf16)


def split_pair(block):
    low = low_half(block.shape[0])
    zero = jnp.zeros_like(block)
    return jnp.concatenate(
        [jnp.where(low, block, zero), jnp.where(low, zero, block)], axis=0
    )


def lanes(j):
    return slice(j * LANES, (j + 1) * LANES)


class Message:
    def __init__(self, rows):
        self.rows = rows
        self.per_chunk = CHUNK // rows

    def place(self, chunk, k):
        r = self.rows
        return (slice(chunk * self.per_chunk, (chunk + 1) * self.per_chunk), slice(k * r, (k + 1) * r))

    def get(self, ref, chunk, k):
        a, b = self.place(chunk, k)
        return ref[a, b, :].reshape(CHUNK, LANES)

    def put(self, ref, chunk, k, value):
        a, b = self.place(chunk, k)
        ref[a, b, :] = value.reshape(self.per_chunk, self.rows, LANES)


X, HALF = 0, PAIRS
FIRST = PAIRS + 1
Z, GRAD = 0, PAIRS
SECOND = 2 * PAIRS
LAST_X, LAST_B, LAST_Z, LAST_C = 0, PAIRS, PAIRS + 1, 2 * PAIRS + 1
LAST = 2 * PAIRS + 2


def pack_first(x_ref, b_ref, c_ref, steps_ref, out_ref, by_head):
    r = x_ref.shape[0]
    step = pl.program_id(0) * pl.num_programs(1) + pl.program_id(1)
    subs = out_ref.shape[0]

    @pl.when(step == 0)
    def _():
        steps = steps_ref[...].astype(f32)
        by_head[...] = jnp.concatenate([steps, jnp.zeros((LANES - r, LANES), f32)], axis=0).T

    zero = jnp.zeros((STEP_ROWS - HEADS, LANES), f32)
    for s in range(subs):
        for j in range(PAIRS):
            out_ref[s, 0, j * r : (j + 1) * r, :] = x_ref[:, lanes(s * PAIRS + j)]
        half = b_ref if s % 2 == 0 else c_ref
        out_ref[s, 0, HALF * r : (HALF + 1) * r, :] = half[:, lanes(s // 2)]
        at = pl.multiple_of((step * subs + s) * HEADS, HEADS)
        mine = jnp.concatenate([by_head[pl.ds(at, HEADS), :], zero], axis=0)
        out_ref[s, 0, FIRST * r :, :] = mine.astype(bf16)


def pack_second(z_ref, grad_ref, out_ref):
    r = z_ref.shape[0]
    for s in range(out_ref.shape[0]):
        for j in range(PAIRS):
            at = lanes(s * PAIRS + j)
            out_ref[s, 0, (Z + j) * r : (Z + j + 1) * r, :] = z_ref[:, at]
            out_ref[s, 0, (GRAD + j) * r : (GRAD + j + 1) * r, :] = grad_ref[:, at]


def add_halves(owners, in_ref, block, out_ref):
    r = out_ref.shape[0]
    peer_of = {own: peer for peer, own in enumerate(owners)}
    for g in range(GROUPS):
        halves = [
            in_ref[peer_of[2 * g + k], block * r : (block + 1) * r, :].astype(f32) for k in range(2)
        ]
        out_ref[:, lanes(g)] = (halves[0] + halves[1]).astype(bf16)


def unpack(owners, in_ref, x_ref, z_ref, b_ref, c_ref, steps_ref):
    r = x_ref.shape[0]
    peer_of = {own: peer for peer, own in enumerate(owners)}
    for peer, own in enumerate(owners):
        for j in range(PAIRS):
            for block, ref in ((LAST_X, x_ref), (LAST_Z, z_ref)):
                at = slice((block + j) * r, (block + j + 1) * r)
                ref[:, lanes(own * PAIRS + j)] = in_ref[peer, at, :]
    add_halves(owners, in_ref, LAST_B, b_ref)
    add_halves(owners, in_ref, LAST_C, c_ref)
    by_head = jnp.concatenate(
        [
            in_ref[peer_of[own], LAST * r : LAST * r + STEP_ROWS, :].astype(f32)[:HEADS]
            for own in range(OWNERS)
        ],
        axis=0,
    )
    steps_ref[...] = by_head.T[:r, :].astype(bf16)


GAIN_ROW, SKIP_ROW, LOGS_ROW, BIAS_ROW = HEADS, HEADS + PAIRS, HEADS + PAIRS + 1, HEADS + PAIRS + 2


def unpack_params(sub_count, tensor_count, tile_ref, mine_ref, out_ref):
    lane = lax.broadcasted_iota(jnp.int32, (1, LANES), 1)
    totals = [jnp.zeros((1, LANES), f32) for _ in range(3)]
    for s in range(sub_count):
        rows = jnp.zeros((STEP_ROWS, LANES), f32)
        for t in range(tensor_count):
            mine = mine_ref[t : t + 1, :] > 0.0
            rows = jnp.where(mine, tile_ref[s * tensor_count + t].astype(f32), rows)
        for k, at in enumerate((LOGS_ROW, BIAS_ROW, SKIP_ROW)):
            part = jnp.where(lane < HEADS, rows[at : at + 1], 0.0)
            totals[k] = totals[k] + (part if s == 0 else pltpu.roll(part, s * HEADS, 1))
        out_ref[8 + s * PAIRS : 8 + (s + 1) * PAIRS, :] = rows[GAIN_ROW : GAIN_ROW + PAIRS]
    out_ref[:8, :] = jnp.concatenate(totals + [jnp.zeros((5, LANES), f32)], axis=0)


def state_kernel(
    message, per_step,
    first_ref, sources_ref, steps_ref, heads_ref, sm_ref, smt_ref, own_ref, dec_ref, state_ref, whole_ref,
    carry, rows_s,
):
    c = pl.program_id(0)

    @pl.when(c == 0)
    def _():
        carry[...] = jnp.zeros_like(carry)
        whole_ref[...] = jnp.ones_like(whole_ref)
        chunks = rows_s.shape[0]
        before = lax.broadcasted_iota(jnp.int32, (CHUNK, CHUNK), 0)
        after = lax.broadcasted_iota(jnp.int32, (CHUNK, CHUNK), 1)
        raws = []
        for k in range(chunks):
            raw = heads_ref[HEADS:, :]
            for p in range(message.per_chunk):
                part = steps_ref[k * message.per_chunk + p].astype(f32)[:HEADS]
                raw = raw + (part if p == 0 else pltpu.roll(part, p * message.rows, 1))
            raws.append(raw)
        raw = jnp.concatenate(raws, axis=0)
        small = jnp.exp(-jnp.abs(raw))
        series = small * (
            1.0 - small * (0.5 - small * (1.0 / 3 - small * (0.25 - small * 0.2)))
        )
        soft = jnp.maximum(raw, 0.0) + jnp.where(small < 0.015625, series, jnp.log(1.0 + small))
        sig = jnp.where(raw >= 0.0, 1.0, small) / (1.0 + small)
        decay_rate = jnp.concatenate([jnp.exp(heads_ref[:HEADS, :])] * chunks, axis=0)
        rate = -decay_rate * soft
        cum = mm_exact(rate, jnp.where(before <= after, 1.0, 0.0))
        rest = mm_exact(rate, jnp.where(before > after, 1.0, 0.0))
        kinds = [
            soft, cum, soft * jnp.exp(rest), cum - jnp.log(soft), jnp.exp(cum), rate, sig,
            jnp.zeros_like(soft),
        ]
        for k in range(chunks):
            at = slice(k * HEADS, (k + 1) * HEADS)
            rows_s[k] = jnp.concatenate([kind[at] for kind in kinds], axis=0)

    made = []
    state = [carry[:, lanes(j)] for j in range(PAIRS)]
    decays = [whole_ref[:, lanes(j)] for j in range(PAIRS)]
    for i in range(per_step):
        rows = rows_s[c * per_step + i]
        sm = jnp.concatenate([rows, jnp.zeros_like(rows)], axis=0).T
        last = jnp.broadcast_to(sm[CHUNK - 1 : CHUNK, :], (8, LANES))
        sources_t = twice(message.get(sources_ref, i, 0).T)
        decs, owns = [], []
        for j in range(PAIRS):
            dec = spread_pair(last, ECUM, j)
            scaled = message.get(first_ref, i, X + j).astype(f32) * spread_pair(sm, WEIGHT, j)
            own = mm_two(sources_t, *two_terms(scaled))
            state[j] = dec[0:1] * state[j] + own
            decays[j] = decays[j] * dec
            decs.append(dec)
            owns.append(own)
        made.append((rows, sm, decs, owns))
    for i, (rows, sm, decs, owns) in enumerate(made):
        smt_ref[:, lanes(i)] = rows
        sm_ref[i * CHUNK : (i + 1) * CHUNK, :] = sm
        for j in range(PAIRS):
            dec_ref[i, :, lanes(j)] = decs[j]
            own_ref[i, :, lanes(j)] = owns[j]
    for j in range(PAIRS):
        carry[:, lanes(j)] = state[j]
        whole_ref[:, lanes(j)] = decays[j]
        state_ref[:, lanes(j)] = state[j].astype(bf16)


def within_kernel(
    message, per_step,
    first_ref, sources_ref, readers_ref, sm_ref, smt_ref, own_ref, dec_ref, y_ref, start_ref, pre_ref, carry, pre,
):
    @pl.when(pl.program_id(0) == 0)
    def _():
        carry[...] = jnp.zeros_like(carry)
        pre[...] = jnp.ones_like(pre)

    t = lax.broadcasted_iota(jnp.int32, (CHUNK, CHUNK), 0)
    s = lax.broadcasted_iota(jnp.int32, (CHUNK, CHUNK), 1)
    made = []
    states = [carry[:, lanes(j)] for j in range(PAIRS)]
    before = pre[...]
    for i in range(per_step):
        rows = slice(i * CHUNK, (i + 1) * CHUNK)
        sm = sm_ref[rows, :]
        smt = smt_ref[:, lanes(i)]
        readers = message.get(readers_ref, i, 0)
        readers_twice = twice(readers)
        scores = jnp.where(t >= s, mm_nt(readers, message.get(sources_ref, i, 0)), 0.0)
        ys = []
        for j in range(PAIRS):
            weights = []
            for h in (2 * j, 2 * j + 1):
                here = sm[:, CUM * HEADS + h : CUM * HEADS + h + 1]
                there = smt[SHIFTED * HEADS + h : SHIFTED * HEADS + h + 1, :]
                weights.append(
                    (scores * jnp.exp(jnp.minimum(here - there, CLAMP))).astype(bf16)
                )
            values = split_pair(message.get(first_ref, i, X + j))
            within = mm(jnp.concatenate(weights, axis=1), values)
            carried = mm_two(readers_twice, *two_terms(states[j]))
            ys.append(within + spread_pair(sm, ECUM, j) * carried)
        made.append((ys, list(states), before))
        for j in range(PAIRS):
            states[j] = dec_ref[i, 0:1, lanes(j)] * states[j] + own_ref[i, :, lanes(j)]
        before = before * dec_ref[i]
    for i, (ys, starts, prefix) in enumerate(made):
        pre_ref[i] = prefix
        for j in range(PAIRS):
            y_ref[i * CHUNK : (i + 1) * CHUNK, lanes(j)] = ys[j]
            start_ref[i, :, lanes(j)] = starts[j]
    pre[...] = before
    for j in range(PAIRS):
        carry[:, lanes(j)] = states[j]


def mix_kernel(
    message, per_step,
    first_ref, readers_ref, second_ref, within_ref, ecum_ref, inbound_ref, pre_ref, gain_ref, skip_ref,
    y_ref, sums_ref,
):
    inbound = inbound_ref[...].astype(bf16)
    fill = jnp.zeros((LANES - HEADS, CHUNK), f32)
    for i in range(per_step):
        rows = slice(i * CHUNK, (i + 1) * CHUNK)
        ecum = jnp.concatenate([ecum_ref[:, lanes(i)], fill], axis=0).T
        carried = mm(message.get(readers_ref, i, 0), inbound)
        power = jnp.zeros((CHUNK, LANES), f32)
        cross = jnp.zeros((CHUNK, LANES), f32)
        for j in range(PAIRS):
            at = lanes(j)
            decay = spread_pair(ecum, 0, j) * pre_ref[i, 0:1, at]
            y = within_ref[rows, at] + decay * carried[:, at]
            y_ref[rows, at] = y
            values = message.get(first_ref, i, X + j).astype(f32)
            gates = message.get(second_ref, i, Z + j).astype(f32)
            grad = message.get(second_ref, i, GRAD + j).astype(f32)
            gated = (y + skip_ref[0:1, at] * values) * (gates * sigmoid(gates))
            power = power + gated * gated
            cross = cross + grad * gain_ref[0:1, at] * gated
        sums_ref[i, 0:1, :] = jnp.sum(power.T, axis=0, keepdims=True)
        sums_ref[i, 1:2, :] = jnp.sum(cross.T, axis=0, keepdims=True)
        sums_ref[i, 2:, :] = jnp.zeros((6, LANES), f32)


def norm_factors(sums):
    sums = sums * (1.0 / GROUP_WIDTH)
    inverse = lax.rsqrt(sums[0:1] + epsilon)
    pull = inverse * inverse * inverse * sums[1:2]
    return (
        jnp.broadcast_to(inverse, (CHUNK, LANES)).T,
        jnp.broadcast_to(pull, (CHUNK, LANES)).T,
    )


def norm_kernel(
    message, per_step,
    first_ref, readers_ref, second_ref, y_ref, sm_ref, pre_ref, sums_ref, other_ref, gain_ref, skip_ref,
    mixed_ref, back_ref, slab_ref,
    back_sum,
):
    @pl.when(pl.program_id(0) == 0)
    def _():
        back_sum[...] = jnp.zeros_like(back_sum)

    sums = [back_sum[:, lanes(j)] for j in range(PAIRS)]
    for i in range(per_step):
        rows = slice(i * CHUNK, (i + 1) * CHUNK)
        sm = sm_ref[rows, :]
        readers_t = twice(message.get(readers_ref, i, 0).T)
        inverse, pull = norm_factors(sums_ref[i] + other_ref[i])
        for j in range(PAIRS):
            at = lanes(j)
            values = message.get(first_ref, i, X + j).astype(f32)
            gates = message.get(second_ref, i, Z + j).astype(f32)
            grad = message.get(second_ref, i, GRAD + j).astype(f32)
            silu = gates * sigmoid(gates)
            gated = (y_ref[rows, at] + skip_ref[0:1, at] * values) * silu
            d_mixed = (inverse * grad * gain_ref[0:1, at] - pull * gated) * silu
            back = mm_two(readers_t, *two_terms(d_mixed * spread_pair(sm, ECUM, j)))
            sums[j] = sums[j] + pre_ref[i, 0:1, at] * back
            mixed_ref[rows, at] = d_mixed.astype(bf16)
            back_ref[i, :, at] = back
    for j in range(PAIRS):
        back_sum[:, lanes(j)] = sums[j]
        slab_ref[:, lanes(j)] = sums[j].astype(bf16)


def local_kernel(
    message, per_step,
    first_ref, sources_ref, readers_ref, second_ref, y_ref, grad_ref, sm_ref, smt_ref, start_ref, pre_ref, inbound_ref,
    sums_ref, other_ref, gain_ref, skip_ref,
    values_out, sources_out, readers_out, gate_ref, e_ref, start_out, param_ref,
    gain_sum, skip_sum,
):
    c = pl.program_id(0)

    @pl.when(c == 0)
    def _():
        gain_sum[...] = jnp.zeros_like(gain_sum)
        skip_sum[...] = jnp.zeros_like(skip_sum)

    s = lax.broadcasted_iota(jnp.int32, (CHUNK, CHUNK), 0)
    t = lax.broadcasted_iota(jnp.int32, (CHUNK, CHUNK), 1)
    causal = t >= s
    ones = head_rows()
    ones_twice = twice(ones)
    gains = [gain_sum[0:1, lanes(j)] for j in range(PAIRS)]
    skips = [skip_sum[0:1, lanes(j)] for j in range(PAIRS)]
    for i in range(per_step):
        rows = slice(i * CHUNK, (i + 1) * CHUNK)
        sm = sm_ref[rows, :]
        smt = smt_ref[:, lanes(i)]
        sources = message.get(sources_ref, i, 0)
        readers = message.get(readers_ref, i, 0)
        inverse, pull = norm_factors(sums_ref[i] + other_ref[i])
        scores = jnp.where(causal, mm_nt(sources, readers), 0.0)
        total = jnp.zeros((CHUNK, CHUNK), f32)
        d_values, d_gates, highs, lows, scaleds, starts = [], [], [], [], [], []
        for j in range(PAIRS):
            at = lanes(j)
            rounded = grad_ref[rows, at]
            grads = split_pair(rounded)
            x = message.get(first_ref, i, X + j)
            weight_grads = mm_nt(x, grads)
            weights = []
            for k, h in enumerate((2 * j, 2 * j + 1)):
                there = sm[:, SHIFTED * HEADS + h : SHIFTED * HEADS + h + 1]
                here = smt[CUM * HEADS + h : CUM * HEADS + h + 1, :]
                decay = jnp.exp(jnp.minimum(here - there, CLAMP))
                weights.append((scores * decay).astype(bf16))
                total = total + weight_grads[:, lanes(k)] * decay
            d_values.append(mm(jnp.concatenate(weights, axis=1), grads))

            values = x.astype(f32)
            gates = message.get(second_ref, i, Z + j).astype(f32)
            grad = message.get(second_ref, i, GRAD + j).astype(f32)
            y = y_ref[rows, at]
            mixed = y + skip_ref[0:1, at] * values
            sig = sigmoid(gates)
            silu = gates * sig
            gated = mixed * silu
            scaled = inverse * grad
            gains[j] = gains[j] + jnp.sum(scaled * gated, axis=0, keepdims=True)
            d_gated = scaled * gain_ref[0:1, at] - pull * gated
            d_gate = d_gated * mixed * (sig + silu * (1.0 - sig))
            d_gates.append(d_gate.astype(bf16))
            skips[j] = skips[j] + jnp.sum(values * (d_gated * silu), axis=0, keepdims=True)
            d_mixed = rounded.astype(f32)
            high, low = two_terms(d_mixed * y)
            highs.append(high)
            lows.append(low)
            scaleds.append((d_mixed * spread_pair(sm, ECUM, j)).astype(bf16))
            starts.append(
                start_ref[i, :, at] + pre_ref[i, 0:1, at] * inbound_ref[:, at].astype(f32)
            )
        e = sum_heads(ones_twice, highs, lows)
        total = jnp.where(causal, total, 0.0).astype(bf16)
        start = jnp.concatenate([part.astype(bf16) for part in starts], axis=1)
        d_readers = mm_tn(total, sources) + mm_nt(jnp.concatenate(scaleds, axis=1), start)
        for j in range(PAIRS):
            values_out[rows, lanes(j)] = d_values[j]
            message.put(gate_ref, i, j, d_gates[j])
            start_out[i, :, lanes(j)] = starts[j]
        e_ref[:, lanes(i)] = e[:HEADS]
        sources_out[rows, :] = mm(total, readers)
        message.put(readers_out, i, 0, d_readers.astype(bf16))
    for j in range(PAIRS):
        gain_sum[0:1, lanes(j)] = gains[j]
        skip_sum[0:1, lanes(j)] = skips[j]

    @pl.when(c == pl.num_programs(0) - 1)
    def _():
        for j in range(PAIRS):
            param_ref[j : j + 1, :] = gain_sum[0:1, lanes(j)]
        high, low = two_terms(jnp.broadcast_to(skip_sum[0:1, :], (LANES, WIDTH)))
        skips = (mm_nt(high, ones) + mm_nt(low, ones))[0:1]
        param_ref[PAIRS : PAIRS + 1, :] = jnp.concatenate(
            [skips, jnp.zeros((1, LANES - 16), f32)], axis=1
        )
        param_ref[PAIRS + 1 :, :] = jnp.zeros((8 - PAIRS - 1, LANES), f32)


def last_kernel(
    message, per_step,
    first_ref, sources_ref, within_ref, d_sources_ref, d_readers_ref, gate_ref, grad_ref, e_ref, sm_ref, smt_ref, outer_ref,
    back_ref, start_ref, dec_ref, skip_ref, heads_ref, early_ref,
    out_ref,
    carry, sums, message_s, sent,
):
    c = pl.program_id(0)

    @pl.when(c == 0)
    def _():
        carry[...] = outer_ref[...].astype(f32)
        sums[...] = jnp.zeros_like(sums)

    r = message.rows
    ones = head_rows()
    ones_twice = twice(ones)
    before = lax.broadcasted_iota(jnp.int32, (CHUNK, CHUNK), 0)
    after = lax.broadcasted_iota(jnp.int32, (CHUNK, CHUNK), 1)
    earlier = jnp.where(before < after, 1.0, 0.0)
    decay_rate = jnp.exp(heads_ref[:HEADS, :])
    first_peer = (pl.num_programs(0) - 1 - c) * per_step * message.per_chunk
    mine = message_s.at[pl.ds(first_peer, per_step * message.per_chunk)]
    chunks = sent.shape[0] - 3

    def body_copy(chunk):
        at = (pl.ds(chunk * message.per_chunk, message.per_chunk), pl.ds(0, LAST_Z * r))
        return pltpu.make_async_copy(message_s.at[at], out_ref.at[at], sent.at[chunk])

    gates_copy = pltpu.make_async_copy(
        gate_ref, out_ref.at[:, pl.ds(LAST_Z * r, PAIRS * r)], sent.at[chunks]
    )
    readers_copy = pltpu.make_async_copy(
        d_readers_ref, out_ref.at[:, pl.ds(LAST_C * r, r)], sent.at[chunks + 1]
    )

    @pl.when(c == 0)
    def _():
        gates_copy.start()
        readers_copy.start()

    states = [carry[:, lanes(j)] for j in range(PAIRS)]
    logs_sum, steps_sum = sums[:HEADS, :], sums[HEADS:, :]
    for i in reversed(range(per_step)):
        rows = slice(i * CHUNK, (i + 1) * CHUNK)
        sm = sm_ref[rows, :]
        sources_twice = twice(message.get(sources_ref, i, 0))
        d_values, highs, lows, scaleds, rounded, fluxes = [], [], [], [], [], []
        for j in range(PAIRS):
            at = lanes(j)
            high, low = two_terms(states[j])
            rounded.append(high)
            values = message.get(first_ref, i, X + j).astype(f32)
            weight = spread_pair(sm, WEIGHT, j)
            grad = within_ref[rows, at] + weight * mm_two(sources_twice, high, low)
            skipped = skip_ref[0:1, at] * grad_ref[rows, at].astype(f32)
            d_values.append((grad + skipped).astype(bf16))
            high, low = two_terms(values * grad)
            highs.append(high)
            lows.append(low)
            scaleds.append((values * weight).astype(bf16))
            states[j] = dec_ref[i, 0:1, at] * states[j] + back_ref[i, :, at]
            fluxes.append(
                jnp.broadcast_to(
                    jnp.sum(start_ref[i, :, at] * states[j], axis=0, keepdims=True), (16, LANES)
                )
            )
        d_sources = d_sources_ref[rows, :] + mm_nt(
            jnp.concatenate(scaleds, axis=1), jnp.concatenate(rounded, axis=1)
        )
        g = sum_heads(ones_twice, highs, lows)[:HEADS]
        constant = sum_heads(ones_twice, *two_terms_each(fluxes))[:HEADS, 0:1]
        flux = constant + mm_exact(g - e_ref[:, lanes(i)], earlier)
        soft = smt_ref[DT * HEADS : (DT + 1) * HEADS, lanes(i)]
        rate = smt_ref[RATE * HEADS : (RATE + 1) * HEADS, lanes(i)]
        sig = smt_ref[SIG * HEADS : (SIG + 1) * HEADS, lanes(i)]
        steps = (g / soft - decay_rate * flux) * sig
        logs_sum = logs_sum + flux * rate
        steps_sum = steps_sum + steps
        steps = jnp.concatenate([steps, jnp.zeros_like(steps)], axis=0)
        for j in range(PAIRS):
            message.put(mine, i, LAST_X + j, d_values[j])
        message.put(mine, i, LAST_B, d_sources.astype(bf16))
        for p in range(message.per_chunk):
            part = steps if p == 0 else pltpu.roll(steps, LANES - p * r, 1)
            mine[i * message.per_chunk + p, LAST * r : LAST * r + STEP_ROWS, :] = part.astype(bf16)
        body_copy((pl.num_programs(0) - 1 - c) * per_step + i).start()
    for j in range(PAIRS):
        carry[:, lanes(j)] = states[j]
    sums[:HEADS, :] = logs_sum
    sums[HEADS:, :] = steps_sum

    @pl.when(c == pl.num_programs(0) - 1)
    def _():
        late = []
        for k in range(2):
            column = jnp.sum(sums[k * HEADS : (k + 1) * HEADS, :], axis=1, keepdims=True)
            block = jnp.broadcast_to(column, (HEADS, LANES))
            block = jnp.concatenate([block, jnp.zeros((LANES - HEADS, LANES), f32)], axis=0)
            late.append(block.T[0:1, :])
        small = [
            jnp.zeros((HEADS, LANES), f32), early_ref[: PAIRS + 1, :], *late,
            jnp.zeros((STEP_ROWS - BIAS_ROW - 1, LANES), f32),
        ]
        small = jnp.concatenate(small, axis=0).astype(bf16)
        own_rows = lax.broadcasted_iota(jnp.int32, (STEP_ROWS, LANES), 0) < HEADS

        def fill(peer, unused):
            steps_at = slice(LAST * r, LAST * r + STEP_ROWS)
            message_s[peer, steps_at, :] = jnp.where(own_rows, message_s[peer, steps_at, :], small)
            return unused

        lax.fori_loop(0, message_s.shape[0], fill, 0)
        at = (slice(None), pl.ds(LAST * r, STEP_ROWS))
        tiles = pltpu.make_async_copy(message_s.at[at], out_ref.at[at], sent.at[chunks + 2])
        tiles.start()
        for chunk in range(chunks):
            body_copy(chunk).wait()
        gates_copy.wait()
        readers_copy.wait()
        tiles.wait()


def finish(own_ref, other_ref, logs_ref, skip_ref, bias_ref, gain_ref):
    total = own_ref[...] + other_ref[...]
    count = logs_ref.shape[1]
    logs_ref[...] = total[0:1, :count]
    bias_ref[...] = total[1:2, :count]
    skip_ref[...] = total[2:3, :count]
    gain_ref[...] = total[8:]


def call(kernel, out_shape, flops, moved, grid=None, in_specs=None, out_specs=None, scratch=()):
    extra = {}
    if grid is not None:
        extra = dict(grid=grid, in_specs=in_specs, out_specs=out_specs)
    return pl.pallas_call(
        kernel,
        out_shape=out_shape,
        scratch_shapes=list(scratch),
        compiler_params=pltpu.CompilerParams(vmem_limit_bytes=28 * 1024 * 1024),
        cost_estimate=pl.CostEstimate(flops=flops, bytes_accessed=moved, transcendentals=0),
        **extra,
    )


def shifted(array, count, by):
    pairs = [(i, i + by) for i in range(count) if 0 <= i + by < count]
    return lax.ppermute(array, "slab", pairs)


def carry_over(state, decay, first_decay, count, sign):
    window, window_decay, step = state, decay, 1
    result = result_decay = None
    while step < count:
        arrived = shifted(window, count, sign * step)
        more = 2 * step < count
        if result is None:
            result = arrived
            if more:
                result_decay = first_decay
                window = (state.astype(f32) + decay[0:1] * arrived.astype(f32)).astype(bf16)
                window_decay = decay * first_decay
        else:
            if more:
                arrived_decay = shifted(window_decay, count, sign * step)
                window = (window.astype(f32) + window_decay[0:1] * arrived.astype(f32)).astype(bf16)
                window_decay = window_decay * arrived_decay
            result = result.astype(f32) + result_decay[0:1] * arrived.astype(f32)
            if more:
                result_decay = result_decay * arrived_decay
        step *= 2
    return jnp.zeros_like(state) if result is None else result


def two_parts(array, axis, count):
    step, other = 1, jnp.zeros_like(array)
    while step < count:
        array = array if step == 1 else array + other
        other = lax.ppermute(array, axis, [(i, i ^ step) for i in range(count)])
        step *= 2
    return array, other


def on_device(
    slab_count, sub_count, tensor_count,
    mixer_x, gate_z, b_matrix, c_matrix, raw_steps, decay_log, skip_gain, step_bias, norm_gain, out_grad,
):
    rows = mixer_x.shape[0]
    peers = sub_count * tensor_count
    tokens = rows * peers
    chunks = tokens // CHUNK
    message = Message(rows)
    owners = [t * sub_count + s for s in range(sub_count) for t in range(tensor_count)]
    sub = lax.axis_index("sub")

    def struct(shape, kind=f32):
        return jax.ShapeDtypeStruct(shape, kind)

    def hbm(shape, kind=f32):
        return pltpu.HBM(shape, kind)

    def in_hbm(array):
        return pltpu.with_memory_space_constraint(array, pltpu.HBM)

    def exchange(array):
        return lax.all_to_all(array, ("sub", "tensor"), split_axis=0, concat_axis=0, tiled=True)

    own_logs = lax.dynamic_slice(decay_log, (sub * HEADS,), (HEADS,))
    own_bias = lax.dynamic_slice(step_bias, (sub * HEADS,), (HEADS,))
    own_skip = lax.dynamic_slice(skip_gain, (sub * HEADS,), (HEADS,))
    own_gain = lax.dynamic_slice(norm_gain, (sub * WIDTH,), (WIDTH,)).reshape(1, WIDTH)
    heads = jnp.broadcast_to(jnp.concatenate([own_logs, own_bias])[:, None], (2 * HEADS, LANES))
    skip_row = jnp.repeat(own_skip, HEAD_DIM).reshape(1, WIDTH)

    first_rows = FIRST * rows + STEP_ROWS
    second_rows = SECOND * rows
    last_rows = LAST * rows + STEP_ROWS

    def packed(kernel, height, arrays, whole_arrays=(), scratch=()):
        out = hbm((sub_count, tensor_count, height, LANES), bf16)
        moved = 4 * peers * height * LANES
        runs = 1
        parts = tensor_count * runs
        specs = [
            pl.BlockSpec((rows, a.shape[1] // parts), lambda t, k: (0, t * runs + k)) for a in arrays
        ] + [pl.BlockSpec(a.shape, lambda t, k: (0, 0)) for a in whole_arrays]
        out_spec = pl.BlockSpec((sub_count // runs, 1, height, LANES), lambda t, k: (k, t, 0, 0))
        made = call(kernel, out, 0, moved, (tensor_count, runs), specs, out_spec, scratch)(
            *(in_hbm(a) for a in (*arrays, *whole_arrays))
        )
        return made.reshape(peers, height, LANES)

    first = exchange(
        packed(
            pack_first, first_rows, (mixer_x, b_matrix, c_matrix), (raw_steps,),
            [pltpu.VMEM((LANES, LANES), f32)],
        )
    )
    tensor_rows = lax.broadcasted_iota(jnp.int32, (tensor_count, LANES), 0)
    mine = (tensor_rows == lax.axis_index("tensor")).astype(f32)
    half = first[:, HALF * rows : (HALF + 1) * rows, :]
    other_half = lax.ppermute(half, "sub", [(i, i ^ 1) for i in range(sub_count)])
    even = sub % 2 == 0
    sources, readers = jnp.where(even, half, other_half), jnp.where(even, other_half, half)
    gate_z, heads, skip_row, own_gain, mine = lax.optimization_barrier(
        (gate_z, heads, skip_row, own_gain, mine)
    )
    second = exchange(packed(pack_second, second_rows, (gate_z, out_grad)))

    def flow(kernel, shape_specs, flops, moved, in_specs, scratch=(), per=2):
        per = min(per, chunks)

        def body(*refs):
            return kernel(message, per, *refs)

        shapes = tuple(shape for shape, _ in shape_specs)
        specs = tuple(spec for _, spec in shape_specs)
        return call(body, shapes, flops, moved, (chunks // per,), in_specs, specs, scratch)

    def specs_of(per, down=False):
        per = min(per, chunks)
        steps = chunks // per

        def spec(block, axis):
            def index(c):
                at = steps - 1 - c if down else c
                return tuple(at if k == axis else 0 for k in range(len(block)))

            return pl.BlockSpec(block, index)

        return dict(
            message=lambda height: spec((per * message.per_chunk, height, LANES), 0),
            token=lambda width: spec((per * CHUNK, width), 0),
            lane=lambda height: spec((height, per * CHUNK), 1),
            chunk=lambda *shape: spec((per,) + shape, 0),
        )

    up = specs_of(2)
    many = specs_of(4)
    dn = specs_of(8, down=True)

    def whole(*shape):
        return pl.BlockSpec(shape, lambda c: (0,) * len(shape))

    unit = 2 * tokens * CHUNK * WIDTH
    size = tokens * WIDTH

    sm, smt, own, dec, state, decay = flow(
        state_kernel,
        [
            (hbm((tokens, LANES)), up["token"](LANES)),
            (hbm((KINDS * HEADS, tokens)), up["lane"](KINDS * HEADS)),
            (hbm((chunks, STATE, WIDTH)), up["chunk"](STATE, WIDTH)),
            (hbm((chunks, 8, WIDTH)), up["chunk"](8, WIDTH)),
            (struct((STATE, WIDTH), bf16), whole(STATE, WIDTH)),
            (struct((8, WIDTH)), whole(8, WIDTH)),
        ],
        2 * unit, size * 8,
        [
            up["message"](PAIRS * rows), up["message"](rows),
            pl.BlockSpec((peers, STEP_ROWS, LANES), lambda c: (0, FIRST * rows // STEP_ROWS, 0)),
            whole(2 * HEADS, LANES),
        ],
        [pltpu.VMEM((STATE, WIDTH), f32), pltpu.VMEM((chunks, KINDS * HEADS, LANES), f32)],
    )(first, in_hbm(sources), first, heads)

    before = after = None
    if slab_count > 2:
        before, after = shifted(decay, slab_count, 1), shifted(decay, slab_count, -1)
    inbound = carry_over(state, decay, before, slab_count, 1)

    within, starts, pre = flow(
        within_kernel,
        [
            (hbm((tokens, WIDTH)), up["token"](WIDTH)),
            (hbm((chunks, STATE, WIDTH)), up["chunk"](STATE, WIDTH)),
            (hbm((chunks, 8, WIDTH)), up["chunk"](8, WIDTH)),
        ],
        6 * unit, size * 16,
        [
            up["message"](PAIRS * rows), up["message"](rows), up["message"](rows),
            up["token"](LANES), up["lane"](KINDS * HEADS),
            up["chunk"](STATE, WIDTH), up["chunk"](8, WIDTH),
        ],
        [pltpu.VMEM((STATE, WIDTH), f32), pltpu.VMEM((8, WIDTH), f32)],
    )(first, in_hbm(sources), in_hbm(readers), in_hbm(sm), in_hbm(smt), in_hbm(own), in_hbm(dec))

    anywhere = pl.BlockSpec(memory_space=pl.ANY)
    per_mix = min(4, chunks)
    ecum_block = pl.BlockSpec((HEADS, per_mix * CHUNK), lambda c: (ECUM, c))
    y, sums = flow(
        mix_kernel,
        [
            (struct((tokens, WIDTH)), many["token"](WIDTH)),
            (struct((chunks, 8, LANES)), many["chunk"](8, LANES)),
        ],
        unit, size * 16,
        [
            many["message"](PAIRS * rows), many["message"](rows), many["message"](second_rows),
            many["token"](WIDTH), ecum_block, whole(STATE, WIDTH), many["chunk"](8, WIDTH),
            whole(1, WIDTH), whole(1, WIDTH),
        ],
        per=per_mix,
    )(
        first, in_hbm(readers), second, in_hbm(within), in_hbm(smt), in_hbm(inbound), in_hbm(pre),
        own_gain, skip_row,
    )

    partner = lax.ppermute(sums, "sub", [(i, i ^ 1) for i in range(sub_count)])

    d_mixed, back, slab_back = flow(
        norm_kernel,
        [
            (struct((tokens, WIDTH), bf16), many["token"](WIDTH)),
            (struct((chunks, STATE, WIDTH)), many["chunk"](STATE, WIDTH)),
            (struct((STATE, WIDTH), bf16), whole(STATE, WIDTH)),
        ],
        2 * unit, size * 12,
        [
            many["message"](PAIRS * rows), many["message"](rows), many["message"](second_rows),
            many["token"](WIDTH), many["token"](LANES), many["chunk"](8, WIDTH), many["chunk"](8, LANES),
            many["chunk"](8, LANES), whole(1, WIDTH), whole(1, WIDTH),
        ],
        [pltpu.VMEM((STATE, WIDTH), f32)],
        per=4,
    )(first, readers, second, y, sm, pre, sums, partner, own_gain, skip_row)

    outer = carry_over(slab_back, decay, after, slab_count, -1)

    d_values, d_sources, d_readers, d_gates, e, starts, params = flow(
        local_kernel,
        [
            (struct((tokens, WIDTH)), many["token"](WIDTH)),
            (struct((tokens, STATE)), many["token"](STATE)),
            (struct((peers, rows, LANES), bf16), many["message"](rows)),
            (struct((peers, PAIRS * rows, LANES), bf16), many["message"](PAIRS * rows)),
            (struct((HEADS, tokens)), many["lane"](HEADS)),
            (struct((chunks, STATE, WIDTH)), many["chunk"](STATE, WIDTH)),
            (struct((8, LANES)), whole(8, LANES)),
        ],
        10 * unit, size * 16,
        [
            many["message"](PAIRS * rows), many["message"](rows), many["message"](rows),
            many["message"](second_rows), many["token"](WIDTH), many["token"](WIDTH), many["token"](LANES),
            many["lane"](KINDS * HEADS),
            many["chunk"](STATE, WIDTH), many["chunk"](8, WIDTH), whole(STATE, WIDTH),
            many["chunk"](8, LANES), many["chunk"](8, LANES), whole(1, WIDTH), whole(1, WIDTH),
        ],
        [pltpu.VMEM((8, WIDTH), f32), pltpu.VMEM((8, WIDTH), f32)],
        per=4,
    )(
        first, sources, readers, second, y, d_mixed, sm, smt, in_hbm(starts), pre, in_hbm(inbound),
        sums, partner, own_gain, skip_row,
    )

    (last,) = flow(
        last_kernel,
        [(hbm((peers, last_rows, LANES), bf16), anywhere)],
        4 * unit, size * 16,
        [
            dn["message"](PAIRS * rows), dn["message"](rows), dn["token"](WIDTH), dn["token"](STATE),
            anywhere, anywhere,
            dn["token"](WIDTH), dn["lane"](HEADS), dn["token"](LANES), dn["lane"](KINDS * HEADS),
            whole(STATE, WIDTH), dn["chunk"](STATE, WIDTH), dn["chunk"](STATE, WIDTH),
            dn["chunk"](8, WIDTH), whole(1, WIDTH), whole(2 * HEADS, LANES), whole(8, LANES),
        ],
        [
            pltpu.VMEM((STATE, WIDTH), f32), pltpu.VMEM((2 * HEADS, LANES), f32),
            pltpu.VMEM((peers, last_rows, LANES), bf16),
            pltpu.SemaphoreType.DMA((chunks + 3,)),
        ],
        per=8,
    )(
        first, sources, d_values, d_sources, d_readers, d_gates, d_mixed, e, sm, smt, outer, back,
        starts, dec, skip_row, heads, params,
    )

    last_back = exchange(last)
    tile_at = LAST * rows // STEP_ROWS
    def tile(at):
        return pl.BlockSpec((peers, STEP_ROWS, LANES), lambda c: (0, at, 0))

    params = call(
        lambda *refs: unpack_params(sub_count, tensor_count, *refs),
        struct((8 + sub_count * PAIRS, LANES)),
        0, 4 * peers * STEP_ROWS * LANES, (1,),
        [tile(tile_at), whole(tensor_count, LANES)],
        whole(8 + sub_count * PAIRS, LANES),
    )(last_back, mine)
    own_params, other_params = two_parts(params, "slab", slab_count)
    wide, narrow = struct((rows, CHANNELS), bf16), struct((rows, GROUPS * STATE), bf16)
    grad_x, grad_gates, grad_b, grad_c, grad_steps = call(
        lambda *refs: unpack(owners, *refs),
        (wide, wide, narrow, narrow, struct((rows, MIXER_HEADS), bf16)),
        0, 10 * rows * CHANNELS,
    )(last_back)
    row = struct((1, sub_count * HEADS))
    grad_logs, grad_skip, grad_bias, grad_gain = call(
        finish, (row, row, row, struct((sub_count * PAIRS, LANES))), 0, 1 << 16,
    )(own_params, other_params)
    return (
        grad_x,
        grad_gates,
        grad_b,
        grad_c,
        grad_steps,
        grad_logs.reshape(-1),
        grad_skip.reshape(-1),
        grad_bias.reshape(-1),
        grad_gain.reshape(-1),
    )


def solution(mesh):
    tensor_count = mesh.shape["tensor"]
    sub_count = OWNERS // tensor_count
    slab_count = mesh.shape["dp"] // sub_count
    devices = mesh.devices.reshape(slab_count, sub_count, tensor_count)
    split_mesh = Mesh(devices, ("slab", "sub", "tensor"))
    rows = P(("slab", "sub", "tensor"), None)
    param = P("tensor")

    def local(*arrays):
        return on_device(slab_count, sub_count, tensor_count, *arrays)

    return jax.shard_map(
        local,
        mesh=split_mesh,
        in_specs=(rows,) * 5 + (param,) * 4 + (rows,),
        out_specs=(rows,) * 5 + (param,) * 4,
        check_vma=False,
    )
```

```python
import jax
import jax.numpy as jnp
from jax import lax
from jax.experimental import pallas as pl
from jax.experimental.pallas import tpu as pltpu
from jax.sharding import Mesh
from jax.sharding import PartitionSpec as P

MIXER_HEADS = 128
HEAD_DIM = 64
STATE = 128
GROUPS = 8
CHANNELS = MIXER_HEADS * HEAD_DIM
HEADS = 8
WIDTH = HEADS * HEAD_DIM
GROUP_WIDTH = 2 * WIDTH
OWNERS = MIXER_HEADS // HEADS
LANES = 128
PAIRS = WIDTH // LANES
CHUNK = 128
STEP_ROWS = 16
epsilon = 1e-05
f32 = jnp.float32
bf16 = jnp.bfloat16

DT, CUM, WEIGHT, SHIFTED, ECUM, RATE, SIG = range(7)
KINDS = 8
CLAMP = 80.0


def mm(a, b):
    return jnp.dot(a, b, preferred_element_type=f32)


def mm_nt(a, b):
    return lax.dot_general(a, b, (((1,), (1,)), ((), ())), preferred_element_type=f32)


def mm_tn(a, b):
    return lax.dot_general(a, b, (((0,), (0,)), ((), ())), preferred_element_type=f32)


def mm_exact(a, b):
    return jnp.dot(a, b, precision=lax.Precision.HIGHEST, preferred_element_type=f32)


def two_terms(values):
    high = values.astype(bf16)
    return high, (values - high.astype(f32)).astype(bf16)


def two_terms_each(tiles):
    return zip(*(two_terms(tile) for tile in tiles))


def twice(a):
    return jnp.concatenate([a, a], axis=1)


def mm_two(a_twice, high, low):
    return mm(a_twice, jnp.concatenate([high, low], axis=0))


def sum_heads(ones_twice, highs, lows):
    return mm_nt(ones_twice, jnp.concatenate([*highs, *lows], axis=1))


def sigmoid(values):
    return 0.5 + 0.5 * jnp.tanh(0.5 * values)


def low_half(rows):
    return lax.broadcasted_iota(jnp.int32, (rows, LANES), 1) < HEAD_DIM


def spread_pair(values, kind, j):
    rows = values.shape[0]
    at = kind * HEADS + 2 * j
    return jnp.where(
        low_half(rows),
        jnp.broadcast_to(values[:, at : at + 1], (rows, LANES)),
        jnp.broadcast_to(values[:, at + 1 : at + 2], (rows, LANES)),
    )


def head_rows():
    row = lax.broadcasted_iota(jnp.int32, (16, WIDTH), 0)
    channel = lax.broadcasted_iota(jnp.int32, (16, WIDTH), 1) // HEAD_DIM
    return jnp.where(row == channel, 1.0, 0.0).astype(bf16)


def split_pair(block):
    low = low_half(block.shape[0])
    zero = jnp.zeros_like(block)
    return jnp.concatenate(
        [jnp.where(low, block, zero), jnp.where(low, zero, block)], axis=0
    )


def lanes(j):
    return slice(j * LANES, (j + 1) * LANES)


class Message:
    def __init__(self, rows):
        self.rows = rows
        self.per_chunk = CHUNK // rows

    def place(self, chunk, k):
        r = self.rows
        return (slice(chunk * self.per_chunk, (chunk + 1) * self.per_chunk), slice(k * r, (k + 1) * r))

    def get(self, ref, chunk, k):
        a, b = self.place(chunk, k)
        return ref[a, b, :].reshape(CHUNK, LANES)

    def put(self, ref, chunk, k, value):
        a, b = self.place(chunk, k)
        ref[a, b, :] = value.reshape(self.per_chunk, self.rows, LANES)


X, HALF = 0, PAIRS
FIRST = PAIRS + 1
Z, GRAD = 0, PAIRS
SECOND = 2 * PAIRS
LAST_X, LAST_B, LAST_Z, LAST_C = 0, PAIRS, PAIRS + 1, 2 * PAIRS + 1
LAST = 2 * PAIRS + 2


def pack_first(x_ref, b_ref, c_ref, steps_ref, out_ref, by_head):
    r = x_ref.shape[0]
    step = pl.program_id(0) * pl.num_programs(1) + pl.program_id(1)
    subs = out_ref.shape[0]

    @pl.when(step == 0)
    def _():
        steps = steps_ref[...].astype(f32)
        by_head[...] = jnp.concatenate([steps, jnp.zeros((LANES - r, LANES), f32)], axis=0).T

    zero = jnp.zeros((STEP_ROWS - HEADS, LANES), f32)
    for s in range(subs):
        for j in range(PAIRS):
            out_ref[s, 0, j * r : (j + 1) * r, :] = x_ref[:, lanes(s * PAIRS + j)]
        half = b_ref if s % 2 == 0 else c_ref
        out_ref[s, 0, HALF * r : (HALF + 1) * r, :] = half[:, lanes(s // 2)]
        at = pl.multiple_of((step * subs + s) * HEADS, HEADS)
        mine = jnp.concatenate([by_head[pl.ds(at, HEADS), :], zero], axis=0)
        out_ref[s, 0, FIRST * r :, :] = mine.astype(bf16)


def pack_second(z_ref, grad_ref, out_ref):
    r = z_ref.shape[0]
    for s in range(out_ref.shape[0]):
        for j in range(PAIRS):
            at = lanes(s * PAIRS + j)
            out_ref[s, 0, (Z + j) * r : (Z + j + 1) * r, :] = z_ref[:, at]
            out_ref[s, 0, (GRAD + j) * r : (GRAD + j + 1) * r, :] = grad_ref[:, at]


def add_halves(owners, in_ref, block, out_ref):
    r = out_ref.shape[0]
    peer_of = {own: peer for peer, own in enumerate(owners)}
    for g in range(GROUPS):
        halves = [
            in_ref[peer_of[2 * g + k], block * r : (block + 1) * r, :].astype(f32) for k in range(2)
        ]
        out_ref[:, lanes(g)] = (halves[0] + halves[1]).astype(bf16)


def unpack(owners, in_ref, x_ref, z_ref, b_ref, c_ref, steps_ref):
    r = x_ref.shape[0]
    peer_of = {own: peer for peer, own in enumerate(owners)}
    for peer, own in enumerate(owners):
        for j in range(PAIRS):
            for block, ref in ((LAST_X, x_ref), (LAST_Z, z_ref)):
                at = slice((block + j) * r, (block + j + 1) * r)
                ref[:, lanes(own * PAIRS + j)] = in_ref[peer, at, :]
    add_halves(owners, in_ref, LAST_B, b_ref)
    add_halves(owners, in_ref, LAST_C, c_ref)
    by_head = jnp.concatenate(
        [
            in_ref[peer_of[own], LAST * r : LAST * r + STEP_ROWS, :].astype(f32)[:HEADS]
            for own in range(OWNERS)
        ],
        axis=0,
    )
    steps_ref[...] = by_head.T[:r, :].astype(bf16)


GAIN_ROW, SKIP_ROW, LOGS_ROW, BIAS_ROW = HEADS, HEADS + PAIRS, HEADS + PAIRS + 1, HEADS + PAIRS + 2


def unpack_params(sub_count, tensor_count, tile_ref, mine_ref, out_ref):
    lane = lax.broadcasted_iota(jnp.int32, (1, LANES), 1)
    totals = [jnp.zeros((1, LANES), f32) for _ in range(3)]
    for s in range(sub_count):
        rows = jnp.zeros((STEP_ROWS, LANES), f32)
        for t in range(tensor_count):
            mine = mine_ref[t : t + 1, :] > 0.0
            rows = jnp.where(mine, tile_ref[s * tensor_count + t].astype(f32), rows)
        for k, at in enumerate((LOGS_ROW, BIAS_ROW, SKIP_ROW)):
            part = jnp.where(lane < HEADS, rows[at : at + 1], 0.0)
            totals[k] = totals[k] + (part if s == 0 else pltpu.roll(part, s * HEADS, 1))
        out_ref[8 + s * PAIRS : 8 + (s + 1) * PAIRS, :] = rows[GAIN_ROW : GAIN_ROW + PAIRS]
    out_ref[:8, :] = jnp.concatenate(totals + [jnp.zeros((5, LANES), f32)], axis=0)


def state_kernel(
    message, per_step,
    first_ref, sources_ref, steps_ref, heads_ref, sm_ref, smt_ref, own_ref, dec_ref, state_ref, whole_ref,
    carry, rows_s,
):
    c = pl.program_id(0)

    @pl.when(c == 0)
    def _():
        carry[...] = jnp.zeros_like(carry)
        whole_ref[...] = jnp.ones_like(whole_ref)
        chunks = rows_s.shape[0]
        before = lax.broadcasted_iota(jnp.int32, (CHUNK, CHUNK), 0)
        after = lax.broadcasted_iota(jnp.int32, (CHUNK, CHUNK), 1)
        raws = []
        for k in range(chunks):
            raw = heads_ref[HEADS:, :]
            for p in range(message.per_chunk):
                part = steps_ref[k * message.per_chunk + p].astype(f32)[:HEADS]
                raw = raw + (part if p == 0 else pltpu.roll(part, p * message.rows, 1))
            raws.append(raw)
        raw = jnp.concatenate(raws, axis=0)
        small = jnp.exp(-jnp.abs(raw))
        series = small * (
            1.0 - small * (0.5 - small * (1.0 / 3 - small * (0.25 - small * 0.2)))
        )
        soft = jnp.maximum(raw, 0.0) + jnp.where(small < 0.015625, series, jnp.log(1.0 + small))
        sig = jnp.where(raw >= 0.0, 1.0, small) / (1.0 + small)
        decay_rate = jnp.concatenate([jnp.exp(heads_ref[:HEADS, :])] * chunks, axis=0)
        rate = -decay_rate * soft
        cum = mm_exact(rate, jnp.where(before <= after, 1.0, 0.0))
        rest = mm_exact(rate, jnp.where(before > after, 1.0, 0.0))
        kinds = [
            soft, cum, soft * jnp.exp(rest), cum - jnp.log(soft), jnp.exp(cum), rate, sig,
            jnp.zeros_like(soft),
        ]
        for k in range(chunks):
            at = slice(k * HEADS, (k + 1) * HEADS)
            rows_s[k] = jnp.concatenate([kind[at] for kind in kinds], axis=0)

    made = []
    state = [carry[:, lanes(j)] for j in range(PAIRS)]
    decays = [whole_ref[:, lanes(j)] for j in range(PAIRS)]
    for i in range(per_step):
        rows = rows_s[c * per_step + i]
        sm = jnp.concatenate([rows, jnp.zeros_like(rows)], axis=0).T
        last = jnp.broadcast_to(sm[CHUNK - 1 : CHUNK, :], (8, LANES))
        sources_t = twice(message.get(sources_ref, i, 0).T)
        decs, owns = [], []
        for j in range(PAIRS):
            dec = spread_pair(last, ECUM, j)
            scaled = message.get(first_ref, i, X + j).astype(f32) * spread_pair(sm, WEIGHT, j)
            own = mm_two(sources_t, *two_terms(scaled))
            state[j] = dec[0:1] * state[j] + own
            decays[j] = decays[j] * dec
            decs.append(dec)
            owns.append(own)
        made.append((rows, sm, decs, owns))
    for i, (rows, sm, decs, owns) in enumerate(made):
        smt_ref[:, lanes(i)] = rows
        sm_ref[i * CHUNK : (i + 1) * CHUNK, :] = sm
        for j in range(PAIRS):
            dec_ref[i, :, lanes(j)] = decs[j]
            own_ref[i, :, lanes(j)] = owns[j]
    for j in range(PAIRS):
        carry[:, lanes(j)] = state[j]
        whole_ref[:, lanes(j)] = decays[j]
        state_ref[:, lanes(j)] = state[j].astype(bf16)


def within_kernel(
    message, per_step,
    first_ref, sources_ref, readers_ref, sm_ref, smt_ref, own_ref, dec_ref, y_ref, start_ref, pre_ref, carry, pre,
):
    @pl.when(pl.program_id(0) == 0)
    def _():
        carry[...] = jnp.zeros_like(carry)
        pre[...] = jnp.ones_like(pre)

    t = lax.broadcasted_iota(jnp.int32, (CHUNK, CHUNK), 0)
    s = lax.broadcasted_iota(jnp.int32, (CHUNK, CHUNK), 1)
    made = []
    states = [carry[:, lanes(j)] for j in range(PAIRS)]
    before = pre[...]
    for i in range(per_step):
        rows = slice(i * CHUNK, (i + 1) * CHUNK)
        sm = sm_ref[rows, :]
        smt = smt_ref[:, lanes(i)]
        readers = message.get(readers_ref, i, 0)
        readers_twice = twice(readers)
        scores = jnp.where(t >= s, mm_nt(readers, message.get(sources_ref, i, 0)), 0.0)
        ys = []
        for j in range(PAIRS):
            weights = []
            for h in (2 * j, 2 * j + 1):
                here = sm[:, CUM * HEADS + h : CUM * HEADS + h + 1]
                there = smt[SHIFTED * HEADS + h : SHIFTED * HEADS + h + 1, :]
                weights.append(
                    (scores * jnp.exp(jnp.minimum(here - there, CLAMP))).astype(bf16)
                )
            values = split_pair(message.get(first_ref, i, X + j))
            within = mm(jnp.concatenate(weights, axis=1), values)
            carried = mm_two(readers_twice, *two_terms(states[j]))
            ys.append(within + spread_pair(sm, ECUM, j) * carried)
        made.append((ys, list(states), before))
        for j in range(PAIRS):
            states[j] = dec_ref[i, 0:1, lanes(j)] * states[j] + own_ref[i, :, lanes(j)]
        before = before * dec_ref[i]
    for i, (ys, starts, prefix) in enumerate(made):
        pre_ref[i] = prefix
        for j in range(PAIRS):
            y_ref[i * CHUNK : (i + 1) * CHUNK, lanes(j)] = ys[j]
            start_ref[i, :, lanes(j)] = starts[j]
    pre[...] = before
    for j in range(PAIRS):
        carry[:, lanes(j)] = states[j]


def mix_kernel(
    message, per_step,
    first_ref, readers_ref, second_ref, within_ref, ecum_ref, inbound_ref, pre_ref, gain_ref, skip_ref,
    y_ref, sums_ref, second_out,
):
    second_out[...] = second_ref[...]
    inbound = inbound_ref[...].astype(bf16)
    fill = jnp.zeros((LANES - HEADS, CHUNK), f32)
    for i in range(per_step):
        rows = slice(i * CHUNK, (i + 1) * CHUNK)
        ecum = jnp.concatenate([ecum_ref[:, lanes(i)], fill], axis=0).T
        carried = mm(message.get(readers_ref, i, 0), inbound)
        power = jnp.zeros((CHUNK, LANES), f32)
        cross = jnp.zeros((CHUNK, LANES), f32)
        for j in range(PAIRS):
            at = lanes(j)
            decay = spread_pair(ecum, 0, j) * pre_ref[i, 0:1, at]
            y = within_ref[rows, at] + decay * carried[:, at]
            y_ref[rows, at] = y
            values = message.get(first_ref, i, X + j).astype(f32)
            gates = message.get(second_ref, i, Z + j).astype(f32)
            grad = message.get(second_ref, i, GRAD + j).astype(f32)
            gated = (y + skip_ref[0:1, at] * values) * (gates * sigmoid(gates))
            power = power + gated * gated
            cross = cross + grad * gain_ref[0:1, at] * gated
        sums_ref[i, 0:1, :] = jnp.sum(power.T, axis=0, keepdims=True)
        sums_ref[i, 1:2, :] = jnp.sum(cross.T, axis=0, keepdims=True)
        sums_ref[i, 2:, :] = jnp.zeros((6, LANES), f32)


def norm_factors(sums):
    sums = sums * (1.0 / GROUP_WIDTH)
    inverse = lax.rsqrt(sums[0:1] + epsilon)
    pull = inverse * inverse * inverse * sums[1:2]
    return (
        jnp.broadcast_to(inverse, (CHUNK, LANES)).T,
        jnp.broadcast_to(pull, (CHUNK, LANES)).T,
    )


def norm_kernel(
    message, per_step,
    first_ref, readers_ref, second_ref, y_ref, sm_ref, pre_ref, sums_ref, other_ref, gain_ref, skip_ref,
    mixed_ref, back_ref, slab_ref,
    back_sum,
):
    @pl.when(pl.program_id(0) == 0)
    def _():
        back_sum[...] = jnp.zeros_like(back_sum)

    sums = [back_sum[:, lanes(j)] for j in range(PAIRS)]
    for i in range(per_step):
        rows = slice(i * CHUNK, (i + 1) * CHUNK)
        sm = sm_ref[rows, :]
        readers_t = twice(message.get(readers_ref, i, 0).T)
        inverse, pull = norm_factors(sums_ref[i] + other_ref[i])
        for j in range(PAIRS):
            at = lanes(j)
            values = message.get(first_ref, i, X + j).astype(f32)
            gates = message.get(second_ref, i, Z + j).astype(f32)
            grad = message.get(second_ref, i, GRAD + j).astype(f32)
            silu = gates * sigmoid(gates)
            gated = (y_ref[rows, at] + skip_ref[0:1, at] * values) * silu
            d_mixed = (inverse * grad * gain_ref[0:1, at] - pull * gated) * silu
            back = mm_two(readers_t, *two_terms(d_mixed * spread_pair(sm, ECUM, j)))
            sums[j] = sums[j] + pre_ref[i, 0:1, at] * back
            mixed_ref[rows, at] = d_mixed.astype(bf16)
            back_ref[i, :, at] = back
    for j in range(PAIRS):
        back_sum[:, lanes(j)] = sums[j]
        slab_ref[:, lanes(j)] = sums[j].astype(bf16)


def local_kernel(
    message, per_step,
    first_ref, sources_ref, readers_ref, second_ref, y_ref, grad_ref, sm_ref, smt_ref, start_ref, pre_ref, inbound_ref,
    sums_ref, other_ref, gain_ref, skip_ref,
    values_out, sources_out, readers_out, gate_ref, e_ref, start_out, param_ref,
    gain_sum, skip_sum,
):
    c = pl.program_id(0)

    @pl.when(c == 0)
    def _():
        gain_sum[...] = jnp.zeros_like(gain_sum)
        skip_sum[...] = jnp.zeros_like(skip_sum)

    s = lax.broadcasted_iota(jnp.int32, (CHUNK, CHUNK), 0)
    t = lax.broadcasted_iota(jnp.int32, (CHUNK, CHUNK), 1)
    causal = t >= s
    ones = head_rows()
    ones_twice = twice(ones)
    gains = [gain_sum[0:1, lanes(j)] for j in range(PAIRS)]
    skips = [skip_sum[0:1, lanes(j)] for j in range(PAIRS)]
    for i in range(per_step):
        rows = slice(i * CHUNK, (i + 1) * CHUNK)
        sm = sm_ref[rows, :]
        smt = smt_ref[:, lanes(i)]
        sources = message.get(sources_ref, i, 0)
        readers = message.get(readers_ref, i, 0)
        inverse, pull = norm_factors(sums_ref[i] + other_ref[i])
        scores = jnp.where(causal, mm_nt(sources, readers), 0.0)
        total = jnp.zeros((CHUNK, CHUNK), f32)
        d_values, d_gates, highs, lows, scaleds, starts = [], [], [], [], [], []
        for j in range(PAIRS):
            at = lanes(j)
            rounded = grad_ref[rows, at]
            grads = split_pair(rounded)
            x = message.get(first_ref, i, X + j)
            weight_grads = mm_nt(x, grads)
            weights = []
            for k, h in enumerate((2 * j, 2 * j + 1)):
                there = sm[:, SHIFTED * HEADS + h : SHIFTED * HEADS + h + 1]
                here = smt[CUM * HEADS + h : CUM * HEADS + h + 1, :]
                decay = jnp.exp(jnp.minimum(here - there, CLAMP))
                weights.append((scores * decay).astype(bf16))
                total = total + weight_grads[:, lanes(k)] * decay
            d_values.append(mm(jnp.concatenate(weights, axis=1), grads))

            values = x.astype(f32)
            gates = message.get(second_ref, i, Z + j).astype(f32)
            grad = message.get(second_ref, i, GRAD + j).astype(f32)
            y = y_ref[rows, at]
            mixed = y + skip_ref[0:1, at] * values
            sig = sigmoid(gates)
            silu = gates * sig
            gated = mixed * silu
            scaled = inverse * grad
            gains[j] = gains[j] + jnp.sum(scaled * gated, axis=0, keepdims=True)
            d_gated = scaled * gain_ref[0:1, at] - pull * gated
            d_gate = d_gated * mixed * (sig + silu * (1.0 - sig))
            d_gates.append(d_gate.astype(bf16))
            skips[j] = skips[j] + jnp.sum(values * (d_gated * silu), axis=0, keepdims=True)
            d_mixed = rounded.astype(f32)
            high, low = two_terms(d_mixed * y)
            highs.append(high)
            lows.append(low)
            scaleds.append((d_mixed * spread_pair(sm, ECUM, j)).astype(bf16))
            starts.append(
                start_ref[i, :, at] + pre_ref[i, 0:1, at] * inbound_ref[:, at].astype(f32)
            )
        e = sum_heads(ones_twice, highs, lows)
        total = jnp.where(causal, total, 0.0).astype(bf16)
        start = jnp.concatenate([part.astype(bf16) for part in starts], axis=1)
        d_readers = mm_tn(total, sources) + mm_nt(jnp.concatenate(scaleds, axis=1), start)
        for j in range(PAIRS):
            values_out[rows, lanes(j)] = d_values[j]
            message.put(gate_ref, i, j, d_gates[j])
            start_out[i, :, lanes(j)] = starts[j]
        e_ref[:, lanes(i)] = e[:HEADS]
        sources_out[rows, :] = mm(total, readers)
        message.put(readers_out, i, 0, d_readers.astype(bf16))
    for j in range(PAIRS):
        gain_sum[0:1, lanes(j)] = gains[j]
        skip_sum[0:1, lanes(j)] = skips[j]

    @pl.when(c == pl.num_programs(0) - 1)
    def _():
        for j in range(PAIRS):
            param_ref[j : j + 1, :] = gain_sum[0:1, lanes(j)]
        high, low = two_terms(jnp.broadcast_to(skip_sum[0:1, :], (LANES, WIDTH)))
        skips = (mm_nt(high, ones) + mm_nt(low, ones))[0:1]
        param_ref[PAIRS : PAIRS + 1, :] = jnp.concatenate(
            [skips, jnp.zeros((1, LANES - 16), f32)], axis=1
        )
        param_ref[PAIRS + 1 :, :] = jnp.zeros((8 - PAIRS - 1, LANES), f32)


def last_kernel(
    message, per_step,
    first_ref, sources_ref, within_ref, d_sources_ref, d_readers_ref, gate_ref, grad_ref, e_ref, sm_ref, smt_ref, outer_ref,
    back_ref, start_ref, dec_ref, skip_ref, heads_ref, early_ref,
    out_ref,
    carry, sums, message_s, sent,
):
    c = pl.program_id(0)

    @pl.when(c == 0)
    def _():
        carry[...] = outer_ref[...].astype(f32)
        sums[...] = jnp.zeros_like(sums)

    r = message.rows
    ones = head_rows()
    ones_twice = twice(ones)
    before = lax.broadcasted_iota(jnp.int32, (CHUNK, CHUNK), 0)
    after = lax.broadcasted_iota(jnp.int32, (CHUNK, CHUNK), 1)
    earlier = jnp.where(before < after, 1.0, 0.0)
    decay_rate = jnp.exp(heads_ref[:HEADS, :])
    first_peer = (pl.num_programs(0) - 1 - c) * per_step * message.per_chunk
    mine = message_s.at[pl.ds(first_peer, per_step * message.per_chunk)]
    chunks = sent.shape[0] - 3

    def body_copy(chunk):
        at = (pl.ds(chunk * message.per_chunk, message.per_chunk), pl.ds(0, LAST_Z * r))
        return pltpu.make_async_copy(message_s.at[at], out_ref.at[at], sent.at[chunk])

    gates_copy = pltpu.make_async_copy(
        gate_ref, out_ref.at[:, pl.ds(LAST_Z * r, PAIRS * r)], sent.at[chunks]
    )
    readers_copy = pltpu.make_async_copy(
        d_readers_ref, out_ref.at[:, pl.ds(LAST_C * r, r)], sent.at[chunks + 1]
    )

    @pl.when(c == 0)
    def _():
        gates_copy.start()
        readers_copy.start()

    states = [carry[:, lanes(j)] for j in range(PAIRS)]
    logs_sum, steps_sum = sums[:HEADS, :], sums[HEADS:, :]
    for i in reversed(range(per_step)):
        rows = slice(i * CHUNK, (i + 1) * CHUNK)
        sm = sm_ref[rows, :]
        sources_twice = twice(message.get(sources_ref, i, 0))
        d_values, highs, lows, scaleds, rounded, fluxes = [], [], [], [], [], []
        for j in range(PAIRS):
            at = lanes(j)
            high, low = two_terms(states[j])
            rounded.append(high)
            values = message.get(first_ref, i, X + j).astype(f32)
            weight = spread_pair(sm, WEIGHT, j)
            grad = within_ref[rows, at] + weight * mm_two(sources_twice, high, low)
            skipped = skip_ref[0:1, at] * grad_ref[rows, at].astype(f32)
            d_values.append((grad + skipped).astype(bf16))
            high, low = two_terms(values * grad)
            highs.append(high)
            lows.append(low)
            scaleds.append((values * weight).astype(bf16))
            states[j] = dec_ref[i, 0:1, at] * states[j] + back_ref[i, :, at]
            fluxes.append(
                jnp.broadcast_to(
                    jnp.sum(start_ref[i, :, at] * states[j], axis=0, keepdims=True), (16, LANES)
                )
            )
        d_sources = d_sources_ref[rows, :] + mm_nt(
            jnp.concatenate(scaleds, axis=1), jnp.concatenate(rounded, axis=1)
        )
        g = sum_heads(ones_twice, highs, lows)[:HEADS]
        constant = sum_heads(ones_twice, *two_terms_each(fluxes))[:HEADS, 0:1]
        flux = constant + mm_exact(g - e_ref[:, lanes(i)], earlier)
        soft = smt_ref[DT * HEADS : (DT + 1) * HEADS, lanes(i)]
        rate = smt_ref[RATE * HEADS : (RATE + 1) * HEADS, lanes(i)]
        sig = smt_ref[SIG * HEADS : (SIG + 1) * HEADS, lanes(i)]
        steps = (g / soft - decay_rate * flux) * sig
        logs_sum = logs_sum + flux * rate
        steps_sum = steps_sum + steps
        steps = jnp.concatenate([steps, jnp.zeros_like(steps)], axis=0)
        for j in range(PAIRS):
            message.put(mine, i, LAST_X + j, d_values[j])
        message.put(mine, i, LAST_B, d_sources.astype(bf16))
        for p in range(message.per_chunk):
            part = steps if p == 0 else pltpu.roll(steps, LANES - p * r, 1)
            mine[i * message.per_chunk + p, LAST * r : LAST * r + STEP_ROWS, :] = part.astype(bf16)
        body_copy((pl.num_programs(0) - 1 - c) * per_step + i).start()
    for j in range(PAIRS):
        carry[:, lanes(j)] = states[j]
    sums[:HEADS, :] = logs_sum
    sums[HEADS:, :] = steps_sum

    @pl.when(c == pl.num_programs(0) - 1)
    def _():
        late = []
        for k in range(2):
            column = jnp.sum(sums[k * HEADS : (k + 1) * HEADS, :], axis=1, keepdims=True)
            block = jnp.broadcast_to(column, (HEADS, LANES))
            block = jnp.concatenate([block, jnp.zeros((LANES - HEADS, LANES), f32)], axis=0)
            late.append(block.T[0:1, :])
        small = [
            jnp.zeros((HEADS, LANES), f32), early_ref[: PAIRS + 1, :], *late,
            jnp.zeros((STEP_ROWS - BIAS_ROW - 1, LANES), f32),
        ]
        small = jnp.concatenate(small, axis=0).astype(bf16)
        own_rows = lax.broadcasted_iota(jnp.int32, (STEP_ROWS, LANES), 0) < HEADS

        def fill(peer, unused):
            steps_at = slice(LAST * r, LAST * r + STEP_ROWS)
            message_s[peer, steps_at, :] = jnp.where(own_rows, message_s[peer, steps_at, :], small)
            return unused

        lax.fori_loop(0, message_s.shape[0], fill, 0)
        at = (slice(None), pl.ds(LAST * r, STEP_ROWS))
        tiles = pltpu.make_async_copy(message_s.at[at], out_ref.at[at], sent.at[chunks + 2])
        tiles.start()
        for chunk in range(chunks):
            body_copy(chunk).wait()
        gates_copy.wait()
        readers_copy.wait()
        tiles.wait()


def finish(own_ref, other_ref, logs_ref, skip_ref, bias_ref, gain_ref):
    total = own_ref[...] + other_ref[...]
    count = logs_ref.shape[1]
    logs_ref[...] = total[0:1, :count]
    bias_ref[...] = total[1:2, :count]
    skip_ref[...] = total[2:3, :count]
    gain_ref[...] = total[8:]


def call(kernel, out_shape, flops, moved, grid=None, in_specs=None, out_specs=None, scratch=()):
    extra = {}
    if grid is not None:
        extra = dict(grid=grid, in_specs=in_specs, out_specs=out_specs)
    return pl.pallas_call(
        kernel,
        out_shape=out_shape,
        scratch_shapes=list(scratch),
        compiler_params=pltpu.CompilerParams(vmem_limit_bytes=28 * 1024 * 1024),
        cost_estimate=pl.CostEstimate(flops=flops, bytes_accessed=moved, transcendentals=0),
        **extra,
    )


def shifted(array, count, by):
    pairs = [(i, i + by) for i in range(count) if 0 <= i + by < count]
    return lax.ppermute(array, "slab", pairs)


def carry_over(state, decay, first_decay, count, sign):
    window, window_decay, step = state, decay, 1
    result = result_decay = None
    while step < count:
        arrived = shifted(window, count, sign * step)
        more = 2 * step < count
        if result is None:
            result = arrived
            if more:
                result_decay = first_decay
                window = (state.astype(f32) + decay[0:1] * arrived.astype(f32)).astype(bf16)
                window_decay = decay * first_decay
        else:
            if more:
                arrived_decay = shifted(window_decay, count, sign * step)
                window = (window.astype(f32) + window_decay[0:1] * arrived.astype(f32)).astype(bf16)
                window_decay = window_decay * arrived_decay
            result = result.astype(f32) + result_decay[0:1] * arrived.astype(f32)
            if more:
                result_decay = result_decay * arrived_decay
        step *= 2
    return jnp.zeros_like(state) if result is None else result


def two_parts(array, axis, count):
    step, other = 1, jnp.zeros_like(array)
    while step < count:
        array = array if step == 1 else array + other
        other = lax.ppermute(array, axis, [(i, i ^ step) for i in range(count)])
        step *= 2
    return array, other


def on_device(
    slab_count, sub_count, tensor_count,
    mixer_x, gate_z, b_matrix, c_matrix, raw_steps, decay_log, skip_gain, step_bias, norm_gain, out_grad,
):
    rows = mixer_x.shape[0]
    peers = sub_count * tensor_count
    tokens = rows * peers
    chunks = tokens // CHUNK
    message = Message(rows)
    owners = [t * sub_count + s for s in range(sub_count) for t in range(tensor_count)]
    sub = lax.axis_index("sub")

    def struct(shape, kind=f32):
        return jax.ShapeDtypeStruct(shape, kind)

    def hbm(shape, kind=f32):
        return pltpu.HBM(shape, kind)

    def in_hbm(array):
        return pltpu.with_memory_space_constraint(array, pltpu.HBM)

    def exchange(array):
        return lax.all_to_all(array, ("sub", "tensor"), split_axis=0, concat_axis=0, tiled=True)

    own_logs = lax.dynamic_slice(decay_log, (sub * HEADS,), (HEADS,))
    own_bias = lax.dynamic_slice(step_bias, (sub * HEADS,), (HEADS,))
    own_skip = lax.dynamic_slice(skip_gain, (sub * HEADS,), (HEADS,))
    own_gain = lax.dynamic_slice(norm_gain, (sub * WIDTH,), (WIDTH,)).reshape(1, WIDTH)
    heads = jnp.broadcast_to(jnp.concatenate([own_logs, own_bias])[:, None], (2 * HEADS, LANES))
    skip_row = jnp.repeat(own_skip, HEAD_DIM).reshape(1, WIDTH)

    first_rows = FIRST * rows + STEP_ROWS
    second_rows = SECOND * rows
    last_rows = LAST * rows + STEP_ROWS

    def packed(kernel, height, arrays, whole_arrays=(), scratch=()):
        out = hbm((sub_count, tensor_count, height, LANES), bf16)
        moved = 4 * peers * height * LANES
        runs = 1
        parts = tensor_count * runs
        specs = [
            pl.BlockSpec((rows, a.shape[1] // parts), lambda t, k: (0, t * runs + k)) for a in arrays
        ] + [pl.BlockSpec(a.shape, lambda t, k: (0, 0)) for a in whole_arrays]
        out_spec = pl.BlockSpec((sub_count // runs, 1, height, LANES), lambda t, k: (k, t, 0, 0))
        made = call(kernel, out, 0, moved, (tensor_count, runs), specs, out_spec, scratch)(
            *(in_hbm(a) for a in (*arrays, *whole_arrays))
        )
        return made.reshape(peers, height, LANES)

    first = exchange(
        packed(
            pack_first, first_rows, (mixer_x, b_matrix, c_matrix), (raw_steps,),
            [pltpu.VMEM((LANES, LANES), f32)],
        )
    )
    tensor_rows = lax.broadcasted_iota(jnp.int32, (tensor_count, LANES), 0)
    mine = (tensor_rows == lax.axis_index("tensor")).astype(f32)
    half = first[:, HALF * rows : (HALF + 1) * rows, :]
    other_half = lax.ppermute(half, "sub", [(i, i ^ 1) for i in range(sub_count)])
    even = sub % 2 == 0
    sources, readers = jnp.where(even, half, other_half), jnp.where(even, other_half, half)
    gate_z, heads, skip_row, own_gain, mine = lax.optimization_barrier(
        (gate_z, heads, skip_row, own_gain, mine)
    )
    second = exchange(packed(pack_second, second_rows, (gate_z, out_grad)))

    def flow(kernel, shape_specs, flops, moved, in_specs, scratch=(), per=2):
        per = min(per, chunks)

        def body(*refs):
            return kernel(message, per, *refs)

        shapes = tuple(shape for shape, _ in shape_specs)
        specs = tuple(spec for _, spec in shape_specs)
        return call(body, shapes, flops, moved, (chunks // per,), in_specs, specs, scratch)

    def specs_of(per, down=False):
        per = min(per, chunks)
        steps = chunks // per

        def spec(block, axis):
            def index(c):
                at = steps - 1 - c if down else c
                return tuple(at if k == axis else 0 for k in range(len(block)))

            return pl.BlockSpec(block, index)

        return dict(
            message=lambda height: spec((per * message.per_chunk, height, LANES), 0),
            token=lambda width: spec((per * CHUNK, width), 0),
            lane=lambda height: spec((height, per * CHUNK), 1),
            chunk=lambda *shape: spec((per,) + shape, 0),
        )

    up = specs_of(2)
    many = specs_of(4)
    all_at_once = specs_of(8)
    dn = specs_of(8, down=True)

    def whole(*shape):
        return pl.BlockSpec(shape, lambda c: (0,) * len(shape))

    unit = 2 * tokens * CHUNK * WIDTH
    size = tokens * WIDTH

    sm, smt, own, dec, state, decay = flow(
        state_kernel,
        [
            (hbm((tokens, LANES)), up["token"](LANES)),
            (hbm((KINDS * HEADS, tokens)), up["lane"](KINDS * HEADS)),
            (hbm((chunks, STATE, WIDTH)), up["chunk"](STATE, WIDTH)),
            (hbm((chunks, 8, WIDTH)), up["chunk"](8, WIDTH)),
            (struct((STATE, WIDTH), bf16), whole(STATE, WIDTH)),
            (struct((8, WIDTH)), whole(8, WIDTH)),
        ],
        2 * unit, size * 8,
        [
            up["message"](PAIRS * rows), up["message"](rows),
            pl.BlockSpec((peers, STEP_ROWS, LANES), lambda c: (0, FIRST * rows // STEP_ROWS, 0)),
            whole(2 * HEADS, LANES),
        ],
        [pltpu.VMEM((STATE, WIDTH), f32), pltpu.VMEM((chunks, KINDS * HEADS, LANES), f32)],
    )(first, sources, first, heads)

    before = after = None
    if slab_count > 2:
        before, after = shifted(decay, slab_count, 1), shifted(decay, slab_count, -1)
    inbound = carry_over(state, decay, before, slab_count, 1)

    within, starts, pre = flow(
        within_kernel,
        [
            (hbm((tokens, WIDTH)), up["token"](WIDTH)),
            (hbm((chunks, STATE, WIDTH)), up["chunk"](STATE, WIDTH)),
            (hbm((chunks, 8, WIDTH)), up["chunk"](8, WIDTH)),
        ],
        6 * unit, size * 16,
        [
            up["message"](PAIRS * rows), up["message"](rows), up["message"](rows),
            up["token"](LANES), up["lane"](KINDS * HEADS),
            up["chunk"](STATE, WIDTH), up["chunk"](8, WIDTH),
        ],
        [pltpu.VMEM((STATE, WIDTH), f32), pltpu.VMEM((8, WIDTH), f32)],
    )(first, sources, readers, in_hbm(sm), in_hbm(smt), in_hbm(own), in_hbm(dec))

    anywhere = pl.BlockSpec(memory_space=pl.ANY)
    per_mix = min(2, chunks)
    ecum_block = pl.BlockSpec((HEADS, per_mix * CHUNK), lambda c: (ECUM, c))
    y, sums, second = flow(
        mix_kernel,
        [
            (struct((tokens, WIDTH)), up["token"](WIDTH)),
            (struct((chunks, 8, LANES)), up["chunk"](8, LANES)),
            (struct((peers, second_rows, LANES), bf16), up["message"](second_rows)),
        ],
        unit, size * 16,
        [
            up["message"](PAIRS * rows), up["message"](rows), up["message"](second_rows),
            up["token"](WIDTH), ecum_block, whole(STATE, WIDTH), up["chunk"](8, WIDTH),
            whole(1, WIDTH), whole(1, WIDTH),
        ],
        per=per_mix,
    )(
        first, readers, in_hbm(second), in_hbm(within), in_hbm(smt), inbound, in_hbm(pre),
        own_gain, skip_row,
    )

    partner = lax.ppermute(sums, "sub", [(i, i ^ 1) for i in range(sub_count)])

    d_mixed, back, slab_back = flow(
        norm_kernel,
        [
            (struct((tokens, WIDTH), bf16), all_at_once["token"](WIDTH)),
            (struct((chunks, STATE, WIDTH)), all_at_once["chunk"](STATE, WIDTH)),
            (struct((STATE, WIDTH), bf16), whole(STATE, WIDTH)),
        ],
        2 * unit, size * 12,
        [
            all_at_once["message"](PAIRS * rows), all_at_once["message"](rows), all_at_once["message"](second_rows),
            all_at_once["token"](WIDTH), all_at_once["token"](LANES), all_at_once["chunk"](8, WIDTH), all_at_once["chunk"](8, LANES),
            all_at_once["chunk"](8, LANES), whole(1, WIDTH), whole(1, WIDTH),
        ],
        [pltpu.VMEM((STATE, WIDTH), f32)],
        per=8,
    )(first, readers, second, y, sm, pre, sums, partner, own_gain, skip_row)

    outer = carry_over(slab_back, decay, after, slab_count, -1)

    d_values, d_sources, d_readers, d_gates, e, starts, params = flow(
        local_kernel,
        [
            (struct((tokens, WIDTH)), many["token"](WIDTH)),
            (struct((tokens, STATE)), many["token"](STATE)),
            (struct((peers, rows, LANES), bf16), many["message"](rows)),
            (struct((peers, PAIRS * rows, LANES), bf16), many["message"](PAIRS * rows)),
            (struct((HEADS, tokens)), many["lane"](HEADS)),
            (struct((chunks, STATE, WIDTH)), many["chunk"](STATE, WIDTH)),
            (struct((8, LANES)), whole(8, LANES)),
        ],
        10 * unit, size * 16,
        [
            many["message"](PAIRS * rows), many["message"](rows), many["message"](rows),
            many["message"](second_rows), many["token"](WIDTH), many["token"](WIDTH), many["token"](LANES),
            many["lane"](KINDS * HEADS),
            many["chunk"](STATE, WIDTH), many["chunk"](8, WIDTH), whole(STATE, WIDTH),
            many["chunk"](8, LANES), many["chunk"](8, LANES), whole(1, WIDTH), whole(1, WIDTH),
        ],
        [pltpu.VMEM((8, WIDTH), f32), pltpu.VMEM((8, WIDTH), f32)],
        per=4,
    )(
        first, sources, readers, second, y, d_mixed, sm, smt, starts, pre, inbound,
        sums, partner, own_gain, skip_row,
    )

    (last,) = flow(
        last_kernel,
        [(hbm((peers, last_rows, LANES), bf16), anywhere)],
        4 * unit, size * 16,
        [
            dn["message"](PAIRS * rows), dn["message"](rows), dn["token"](WIDTH), dn["token"](STATE),
            anywhere, anywhere,
            dn["token"](WIDTH), dn["lane"](HEADS), dn["token"](LANES), dn["lane"](KINDS * HEADS),
            whole(STATE, WIDTH), dn["chunk"](STATE, WIDTH), dn["chunk"](STATE, WIDTH),
            dn["chunk"](8, WIDTH), whole(1, WIDTH), whole(2 * HEADS, LANES), whole(8, LANES),
        ],
        [
            pltpu.VMEM((STATE, WIDTH), f32), pltpu.VMEM((2 * HEADS, LANES), f32),
            pltpu.VMEM((peers, last_rows, LANES), bf16),
            pltpu.SemaphoreType.DMA((chunks + 3,)),
        ],
        per=8,
    )(
        first, sources, d_values, d_sources, d_readers, d_gates, d_mixed, e, sm, smt, outer, back,
        starts, dec, skip_row, heads, params,
    )

    last_back = exchange(last)
    tile_at = LAST * rows // STEP_ROWS
    def tile(at):
        return pl.BlockSpec((peers, STEP_ROWS, LANES), lambda c: (0, at, 0))

    params = call(
        lambda *refs: unpack_params(sub_count, tensor_count, *refs),
        struct((8 + sub_count * PAIRS, LANES)),
        0, 4 * peers * STEP_ROWS * LANES, (1,),
        [tile(tile_at), whole(tensor_count, LANES)],
        whole(8 + sub_count * PAIRS, LANES),
    )(last_back, mine)
    own_params, other_params = two_parts(params, "slab", slab_count)
    wide, narrow = struct((rows, CHANNELS), bf16), struct((rows, GROUPS * STATE), bf16)
    grad_x, grad_gates, grad_b, grad_c, grad_steps = call(
        lambda *refs: unpack(owners, *refs),
        (wide, wide, narrow, narrow, struct((rows, MIXER_HEADS), bf16)),
        0, 10 * rows * CHANNELS,
    )(last_back)
    row = struct((1, sub_count * HEADS))
    grad_logs, grad_skip, grad_bias, grad_gain = call(
        finish, (row, row, row, struct((sub_count * PAIRS, LANES))), 0, 1 << 16,
    )(own_params, other_params)
    return (
        grad_x,
        grad_gates,
        grad_b,
        grad_c,
        grad_steps,
        grad_logs.reshape(-1),
        grad_skip.reshape(-1),
        grad_bias.reshape(-1),
        grad_gain.reshape(-1),
    )


def solution(mesh):
    tensor_count = mesh.shape["tensor"]
    sub_count = OWNERS // tensor_count
    slab_count = mesh.shape["dp"] // sub_count
    devices = mesh.devices.reshape(slab_count, sub_count, tensor_count)
    split_mesh = Mesh(devices, ("slab", "sub", "tensor"))
    rows = P(("slab", "sub", "tensor"), None)
    param = P("tensor")

    def local(*arrays):
        return on_device(slab_count, sub_count, tensor_count, *arrays)

    return jax.shard_map(
        local,
        mesh=split_mesh,
        in_specs=(rows,) * 5 + (param,) * 4 + (rows,),
        out_specs=(rows,) * 5 + (param,) * 4,
        check_vma=False,
    )
```

```python
import jax
import jax.numpy as jnp
from jax import lax
from jax.experimental import pallas as pl
from jax.experimental.pallas import tpu as pltpu
from jax.sharding import Mesh
from jax.sharding import PartitionSpec as P

MIXER_HEADS = 128
HEAD_DIM = 64
STATE = 128
GROUPS = 8
CHANNELS = MIXER_HEADS * HEAD_DIM
HEADS = 8
WIDTH = HEADS * HEAD_DIM
GROUP_WIDTH = 2 * WIDTH
OWNERS = MIXER_HEADS // HEADS
LANES = 128
PAIRS = WIDTH // LANES
CHUNK = 128
STEP_ROWS = 16
epsilon = 1e-05
f32 = jnp.float32
bf16 = jnp.bfloat16

DT, CUM, WEIGHT, SHIFTED, ECUM, RATE, SIG = range(7)
KINDS = 8
CLAMP = 80.0


def mm(a, b):
    return jnp.dot(a, b, preferred_element_type=f32)


def mm_nt(a, b):
    return lax.dot_general(a, b, (((1,), (1,)), ((), ())), preferred_element_type=f32)


def mm_tn(a, b):
    return lax.dot_general(a, b, (((0,), (0,)), ((), ())), preferred_element_type=f32)


def mm_exact(a, b):
    return jnp.dot(a, b, precision=lax.Precision.HIGHEST, preferred_element_type=f32)


def two_terms(values):
    high = values.astype(bf16)
    return high, (values - high.astype(f32)).astype(bf16)


def two_terms_each(tiles):
    return zip(*(two_terms(tile) for tile in tiles))


def twice(a):
    return jnp.concatenate([a, a], axis=1)


def mm_two(a_twice, high, low):
    return mm(a_twice, jnp.concatenate([high, low], axis=0))


def sum_heads(ones_twice, highs, lows):
    return mm_nt(ones_twice, jnp.concatenate([*highs, *lows], axis=1))


def sigmoid(values):
    return 0.5 + 0.5 * jnp.tanh(0.5 * values)


def low_half(rows):
    return lax.broadcasted_iota(jnp.int32, (rows, LANES), 1) < HEAD_DIM


def spread_pair(values, kind, j):
    rows = values.shape[0]
    at = kind * HEADS + 2 * j
    return jnp.where(
        low_half(rows),
        jnp.broadcast_to(values[:, at : at + 1], (rows, LANES)),
        jnp.broadcast_to(values[:, at + 1 : at + 2], (rows, LANES)),
    )


def head_rows():
    row = lax.broadcasted_iota(jnp.int32, (16, WIDTH), 0)
    channel = lax.broadcasted_iota(jnp.int32, (16, WIDTH), 1) // HEAD_DIM
    return jnp.where(row == channel, 1.0, 0.0).astype(bf16)


def split_pair(block):
    low = low_half(block.shape[0])
    zero = jnp.zeros_like(block)
    return jnp.concatenate(
        [jnp.where(low, block, zero), jnp.where(low, zero, block)], axis=0
    )


def lanes(j):
    return slice(j * LANES, (j + 1) * LANES)


class Message:
    def __init__(self, rows):
        self.rows = rows
        self.per_chunk = CHUNK // rows

    def place(self, chunk, k):
        r = self.rows
        return (slice(chunk * self.per_chunk, (chunk + 1) * self.per_chunk), slice(k * r, (k + 1) * r))

    def get(self, ref, chunk, k):
        a, b = self.place(chunk, k)
        return ref[a, b, :].reshape(CHUNK, LANES)

    def put(self, ref, chunk, k, value):
        a, b = self.place(chunk, k)
        ref[a, b, :] = value.reshape(self.per_chunk, self.rows, LANES)


X, HALF = 0, PAIRS
FIRST = PAIRS + 1
Z, GRAD = 0, PAIRS
SECOND = 2 * PAIRS
LAST_X, LAST_B, LAST_Z, LAST_C = 0, PAIRS, PAIRS + 1, 2 * PAIRS + 1
LAST = 2 * PAIRS + 2


def pack_first(x_ref, b_ref, c_ref, steps_ref, out_ref, by_head):
    r = x_ref.shape[0]
    step = pl.program_id(0) * pl.num_programs(1) + pl.program_id(1)
    subs = out_ref.shape[0]

    @pl.when(step == 0)
    def _():
        steps = steps_ref[...].astype(f32)
        by_head[...] = jnp.concatenate([steps, jnp.zeros((LANES - r, LANES), f32)], axis=0).T

    zero = jnp.zeros((STEP_ROWS - HEADS, LANES), f32)
    for s in range(subs):
        for j in range(PAIRS):
            out_ref[s, 0, j * r : (j + 1) * r, :] = x_ref[:, lanes(s * PAIRS + j)]
        half = b_ref if s % 2 == 0 else c_ref
        out_ref[s, 0, HALF * r : (HALF + 1) * r, :] = half[:, lanes(s // 2)]
        at = pl.multiple_of((step * subs + s) * HEADS, HEADS)
        mine = jnp.concatenate([by_head[pl.ds(at, HEADS), :], zero], axis=0)
        out_ref[s, 0, FIRST * r :, :] = mine.astype(bf16)


def pack_second(z_ref, grad_ref, out_ref):
    r = z_ref.shape[0]
    for s in range(out_ref.shape[0]):
        for j in range(PAIRS):
            at = lanes(s * PAIRS + j)
            out_ref[s, 0, (Z + j) * r : (Z + j + 1) * r, :] = z_ref[:, at]
            out_ref[s, 0, (GRAD + j) * r : (GRAD + j + 1) * r, :] = grad_ref[:, at]


def add_halves(owners, in_ref, block, out_ref):
    r = out_ref.shape[0]
    peer_of = {own: peer for peer, own in enumerate(owners)}
    for g in range(GROUPS):
        halves = [
            in_ref[peer_of[2 * g + k], block * r : (block + 1) * r, :].astype(f32) for k in range(2)
        ]
        out_ref[:, lanes(g)] = (halves[0] + halves[1]).astype(bf16)


def unpack(owners, in_ref, x_ref, z_ref, b_ref, c_ref, steps_ref):
    r = x_ref.shape[0]
    peer_of = {own: peer for peer, own in enumerate(owners)}
    for peer, own in enumerate(owners):
        for j in range(PAIRS):
            for block, ref in ((LAST_X, x_ref), (LAST_Z, z_ref)):
                at = slice((block + j) * r, (block + j + 1) * r)
                ref[:, lanes(own * PAIRS + j)] = in_ref[peer, at, :]
    add_halves(owners, in_ref, LAST_B, b_ref)
    add_halves(owners, in_ref, LAST_C, c_ref)
    by_head = jnp.concatenate(
        [
            in_ref[peer_of[own], LAST * r : LAST * r + STEP_ROWS, :].astype(f32)[:HEADS]
            for own in range(OWNERS)
        ],
        axis=0,
    )
    steps_ref[...] = by_head.T[:r, :].astype(bf16)


GAIN_ROW, SKIP_ROW, LOGS_ROW, BIAS_ROW = HEADS, HEADS + PAIRS, HEADS + PAIRS + 1, HEADS + PAIRS + 2


def unpack_params(sub_count, tensor_count, tile_ref, mine_ref, out_ref):
    lane = lax.broadcasted_iota(jnp.int32, (1, LANES), 1)
    totals = [jnp.zeros((1, LANES), f32) for _ in range(3)]
    for s in range(sub_count):
        rows = jnp.zeros((STEP_ROWS, LANES), f32)
        for t in range(tensor_count):
            mine = mine_ref[t : t + 1, :] > 0.0
            rows = jnp.where(mine, tile_ref[s * tensor_count + t].astype(f32), rows)
        for k, at in enumerate((LOGS_ROW, BIAS_ROW, SKIP_ROW)):
            part = jnp.where(lane < HEADS, rows[at : at + 1], 0.0)
            totals[k] = totals[k] + (part if s == 0 else pltpu.roll(part, s * HEADS, 1))
        out_ref[8 + s * PAIRS : 8 + (s + 1) * PAIRS, :] = rows[GAIN_ROW : GAIN_ROW + PAIRS]
    out_ref[:8, :] = jnp.concatenate(totals + [jnp.zeros((5, LANES), f32)], axis=0)


def state_kernel(
    message, per_step,
    first_ref, sources_ref, steps_ref, heads_ref, sm_ref, smt_ref, own_ref, dec_ref, state_ref, whole_ref,
    carry, rows_s,
):
    c = pl.program_id(0)

    @pl.when(c == 0)
    def _():
        carry[...] = jnp.zeros_like(carry)
        whole_ref[...] = jnp.ones_like(whole_ref)
        chunks = rows_s.shape[0]
        before = lax.broadcasted_iota(jnp.int32, (CHUNK, CHUNK), 0)
        after = lax.broadcasted_iota(jnp.int32, (CHUNK, CHUNK), 1)
        raws = []
        for k in range(chunks):
            raw = heads_ref[HEADS:, :]
            for p in range(message.per_chunk):
                part = steps_ref[k * message.per_chunk + p].astype(f32)[:HEADS]
                raw = raw + (part if p == 0 else pltpu.roll(part, p * message.rows, 1))
            raws.append(raw)
        raw = jnp.concatenate(raws, axis=0)
        small = jnp.exp(-jnp.abs(raw))
        series = small * (
            1.0 - small * (0.5 - small * (1.0 / 3 - small * (0.25 - small * 0.2)))
        )
        soft = jnp.maximum(raw, 0.0) + jnp.where(small < 0.015625, series, jnp.log(1.0 + small))
        sig = jnp.where(raw >= 0.0, 1.0, small) / (1.0 + small)
        decay_rate = jnp.concatenate([jnp.exp(heads_ref[:HEADS, :])] * chunks, axis=0)
        rate = -decay_rate * soft
        cum = mm_exact(rate, jnp.where(before <= after, 1.0, 0.0))
        rest = mm_exact(rate, jnp.where(before > after, 1.0, 0.0))
        kinds = [
            soft, cum, soft * jnp.exp(rest), cum - jnp.log(soft), jnp.exp(cum), rate, sig,
            jnp.zeros_like(soft),
        ]
        for k in range(chunks):
            at = slice(k * HEADS, (k + 1) * HEADS)
            rows_s[k] = jnp.concatenate([kind[at] for kind in kinds], axis=0)

    made = []
    state = [carry[:, lanes(j)] for j in range(PAIRS)]
    decays = [whole_ref[:, lanes(j)] for j in range(PAIRS)]
    for i in range(per_step):
        rows = rows_s[c * per_step + i]
        sm = jnp.concatenate([rows, jnp.zeros_like(rows)], axis=0).T
        last = jnp.broadcast_to(sm[CHUNK - 1 : CHUNK, :], (8, LANES))
        sources_t = twice(message.get(sources_ref, i, 0).T)
        decs, owns = [], []
        for j in range(PAIRS):
            dec = spread_pair(last, ECUM, j)
            scaled = message.get(first_ref, i, X + j).astype(f32) * spread_pair(sm, WEIGHT, j)
            own = mm_two(sources_t, *two_terms(scaled))
            state[j] = dec[0:1] * state[j] + own
            decays[j] = decays[j] * dec
            decs.append(dec)
            owns.append(own)
        made.append((rows, sm, decs, owns))
    for i, (rows, sm, decs, owns) in enumerate(made):
        smt_ref[:, lanes(i)] = rows
        sm_ref[i * CHUNK : (i + 1) * CHUNK, :] = sm
        for j in range(PAIRS):
            dec_ref[i, :, lanes(j)] = decs[j]
            own_ref[i, :, lanes(j)] = owns[j]
    for j in range(PAIRS):
        carry[:, lanes(j)] = state[j]
        whole_ref[:, lanes(j)] = decays[j]
        state_ref[:, lanes(j)] = state[j].astype(bf16)


def within_kernel(
    message, per_step,
    first_ref, sources_ref, readers_ref, sm_ref, smt_ref, own_ref, dec_ref, y_ref, start_ref, pre_ref, carry, pre,
):
    @pl.when(pl.program_id(0) == 0)
    def _():
        carry[...] = jnp.zeros_like(carry)
        pre[...] = jnp.ones_like(pre)

    t = lax.broadcasted_iota(jnp.int32, (CHUNK, CHUNK), 0)
    s = lax.broadcasted_iota(jnp.int32, (CHUNK, CHUNK), 1)
    made = []
    states = [carry[:, lanes(j)] for j in range(PAIRS)]
    before = pre[...]
    for i in range(per_step):
        rows = slice(i * CHUNK, (i + 1) * CHUNK)
        sm = sm_ref[rows, :]
        smt = smt_ref[:, lanes(i)]
        readers = message.get(readers_ref, i, 0)
        readers_twice = twice(readers)
        scores = jnp.where(t >= s, mm_nt(readers, message.get(sources_ref, i, 0)), 0.0)
        ys = []
        for j in range(PAIRS):
            weights = []
            for h in (2 * j, 2 * j + 1):
                here = sm[:, CUM * HEADS + h : CUM * HEADS + h + 1]
                there = smt[SHIFTED * HEADS + h : SHIFTED * HEADS + h + 1, :]
                weights.append(
                    (scores * jnp.exp(jnp.minimum(here - there, CLAMP))).astype(bf16)
                )
            values = split_pair(message.get(first_ref, i, X + j))
            within = mm(jnp.concatenate(weights, axis=1), values)
            carried = mm_two(readers_twice, *two_terms(states[j]))
            ys.append(within + spread_pair(sm, ECUM, j) * carried)
        made.append((ys, list(states), before))
        for j in range(PAIRS):
            states[j] = dec_ref[i, 0:1, lanes(j)] * states[j] + own_ref[i, :, lanes(j)]
        before = before * dec_ref[i]
    for i, (ys, starts, prefix) in enumerate(made):
        pre_ref[i] = prefix
        for j in range(PAIRS):
            y_ref[i * CHUNK : (i + 1) * CHUNK, lanes(j)] = ys[j]
            start_ref[i, :, lanes(j)] = starts[j]
    pre[...] = before
    for j in range(PAIRS):
        carry[:, lanes(j)] = states[j]


def mix_kernel(
    message, per_step,
    first_ref, readers_ref, second_ref, within_ref, sm_ref, inbound_ref, pre_ref, gain_ref, skip_ref,
    y_ref, sums_ref, second_out,
):
    second_out[...] = second_ref[...]
    inbound = inbound_ref[...].astype(bf16)
    ones = jnp.ones((16, 2 * LANES), bf16)
    for i in range(per_step):
        rows = slice(i * CHUNK, (i + 1) * CHUNK)
        sm = sm_ref[rows, :]
        carried = mm(message.get(readers_ref, i, 0), inbound)
        power = jnp.zeros((CHUNK, LANES), f32)
        cross = jnp.zeros((CHUNK, LANES), f32)
        for j in range(PAIRS):
            at = lanes(j)
            decay = spread_pair(sm, ECUM, j) * pre_ref[i, 0:1, at]
            y = within_ref[rows, at] + decay * carried[:, at]
            y_ref[rows, at] = y
            values = message.get(first_ref, i, X + j).astype(f32)
            gates = message.get(second_ref, i, Z + j).astype(f32)
            grad = message.get(second_ref, i, GRAD + j).astype(f32)
            gated = (y + skip_ref[0:1, at] * values) * (gates * sigmoid(gates))
            power = power + gated * gated
            cross = cross + grad * gain_ref[0:1, at] * gated
        for k, tile in enumerate((power, cross)):
            terms = jnp.concatenate(two_terms(tile), axis=1)
            sums_ref[i, k : k + 1, :] = mm_nt(ones, terms)[0:1]
        sums_ref[i, 2:, :] = jnp.zeros((6, LANES), f32)


def norm_factors(sums):
    sums = sums * (1.0 / GROUP_WIDTH)
    inverse = lax.rsqrt(sums[0:1] + epsilon)
    pull = inverse * inverse * inverse * sums[1:2]
    return (
        jnp.broadcast_to(inverse, (CHUNK, LANES)).T,
        jnp.broadcast_to(pull, (CHUNK, LANES)).T,
    )


def norm_kernel(
    message, per_step,
    first_ref, readers_ref, second_ref, y_ref, sm_ref, pre_ref, sums_ref, other_ref, gain_ref, skip_ref,
    mixed_ref, back_ref, slab_ref,
    back_sum,
):
    @pl.when(pl.program_id(0) == 0)
    def _():
        back_sum[...] = jnp.zeros_like(back_sum)

    sums = [back_sum[:, lanes(j)] for j in range(PAIRS)]
    for i in range(per_step):
        rows = slice(i * CHUNK, (i + 1) * CHUNK)
        sm = sm_ref[rows, :]
        readers_t = twice(message.get(readers_ref, i, 0).T)
        inverse, pull = norm_factors(sums_ref[i] + other_ref[i])
        for j in range(PAIRS):
            at = lanes(j)
            values = message.get(first_ref, i, X + j).astype(f32)
            gates = message.get(second_ref, i, Z + j).astype(f32)
            grad = message.get(second_ref, i, GRAD + j).astype(f32)
            silu = gates * sigmoid(gates)
            gated = (y_ref[rows, at] + skip_ref[0:1, at] * values) * silu
            d_mixed = (inverse * grad * gain_ref[0:1, at] - pull * gated) * silu
            back = mm_two(readers_t, *two_terms(d_mixed * spread_pair(sm, ECUM, j)))
            sums[j] = sums[j] + pre_ref[i, 0:1, at] * back
            mixed_ref[rows, at] = d_mixed.astype(bf16)
            back_ref[i, :, at] = back
    for j in range(PAIRS):
        back_sum[:, lanes(j)] = sums[j]
        slab_ref[:, lanes(j)] = sums[j].astype(bf16)


def local_kernel(
    message, per_step,
    first_ref, sources_ref, readers_ref, second_ref, y_ref, grad_ref, sm_ref, smt_ref, start_ref, pre_ref, inbound_ref,
    sums_ref, other_ref, gain_ref, skip_ref,
    values_out, sources_out, readers_out, gate_ref, e_ref, start_out, param_ref,
    gain_sum, skip_sum,
):
    c = pl.program_id(0)

    @pl.when(c == 0)
    def _():
        gain_sum[...] = jnp.zeros_like(gain_sum)
        skip_sum[...] = jnp.zeros_like(skip_sum)

    s = lax.broadcasted_iota(jnp.int32, (CHUNK, CHUNK), 0)
    t = lax.broadcasted_iota(jnp.int32, (CHUNK, CHUNK), 1)
    causal = t >= s
    ones = head_rows()
    ones_twice = twice(ones)
    gains = [gain_sum[0:1, lanes(j)] for j in range(PAIRS)]
    skips = [skip_sum[0:1, lanes(j)] for j in range(PAIRS)]
    for i in range(per_step):
        rows = slice(i * CHUNK, (i + 1) * CHUNK)
        sm = sm_ref[rows, :]
        smt = smt_ref[:, lanes(i)]
        sources = message.get(sources_ref, i, 0)
        readers = message.get(readers_ref, i, 0)
        inverse, pull = norm_factors(sums_ref[i] + other_ref[i])
        scores = jnp.where(causal, mm_nt(sources, readers), 0.0)
        total = jnp.zeros((CHUNK, CHUNK), f32)
        d_values, d_gates, highs, lows, scaleds, starts = [], [], [], [], [], []
        for j in range(PAIRS):
            at = lanes(j)
            rounded = grad_ref[rows, at]
            grads = split_pair(rounded)
            x = message.get(first_ref, i, X + j)
            weight_grads = mm_nt(x, grads)
            weights = []
            for k, h in enumerate((2 * j, 2 * j + 1)):
                there = sm[:, SHIFTED * HEADS + h : SHIFTED * HEADS + h + 1]
                here = smt[CUM * HEADS + h : CUM * HEADS + h + 1, :]
                decay = jnp.exp(jnp.minimum(here - there, CLAMP))
                weights.append((scores * decay).astype(bf16))
                total = total + weight_grads[:, lanes(k)] * decay
            d_values.append(mm(jnp.concatenate(weights, axis=1), grads))

            values = x.astype(f32)
            gates = message.get(second_ref, i, Z + j).astype(f32)
            grad = message.get(second_ref, i, GRAD + j).astype(f32)
            y = y_ref[rows, at]
            mixed = y + skip_ref[0:1, at] * values
            sig = sigmoid(gates)
            silu = gates * sig
            gated = mixed * silu
            scaled = inverse * grad
            gains[j] = gains[j] + jnp.sum(scaled * gated, axis=0, keepdims=True)
            d_gated = scaled * gain_ref[0:1, at] - pull * gated
            d_gate = d_gated * mixed * (sig + silu * (1.0 - sig))
            d_gates.append(d_gate.astype(bf16))
            skips[j] = skips[j] + jnp.sum(values * (d_gated * silu), axis=0, keepdims=True)
            d_mixed = rounded.astype(f32)
            high, low = two_terms(d_mixed * y)
            highs.append(high)
            lows.append(low)
            scaleds.append((d_mixed * spread_pair(sm, ECUM, j)).astype(bf16))
            starts.append(
                start_ref[i, :, at] + pre_ref[i, 0:1, at] * inbound_ref[:, at].astype(f32)
            )
        e = sum_heads(ones_twice, highs, lows)
        total = jnp.where(causal, total, 0.0).astype(bf16)
        start = jnp.concatenate([part.astype(bf16) for part in starts], axis=1)
        d_readers = mm_tn(total, sources) + mm_nt(jnp.concatenate(scaleds, axis=1), start)
        for j in range(PAIRS):
            values_out[rows, lanes(j)] = d_values[j]
            message.put(gate_ref, i, j, d_gates[j])
            start_out[i, :, lanes(j)] = starts[j]
        e_ref[:, lanes(i)] = e[:HEADS]
        sources_out[rows, :] = mm(total, readers)
        message.put(readers_out, i, 0, d_readers.astype(bf16))
    for j in range(PAIRS):
        gain_sum[0:1, lanes(j)] = gains[j]
        skip_sum[0:1, lanes(j)] = skips[j]

    @pl.when(c == pl.num_programs(0) - 1)
    def _():
        for j in range(PAIRS):
            param_ref[j : j + 1, :] = gain_sum[0:1, lanes(j)]
        high, low = two_terms(jnp.broadcast_to(skip_sum[0:1, :], (LANES, WIDTH)))
        skips = (mm_nt(high, ones) + mm_nt(low, ones))[0:1]
        param_ref[PAIRS : PAIRS + 1, :] = jnp.concatenate(
            [skips, jnp.zeros((1, LANES - 16), f32)], axis=1
        )
        param_ref[PAIRS + 1 :, :] = jnp.zeros((8 - PAIRS - 1, LANES), f32)


def last_kernel(
    message, per_step,
    first_ref, sources_ref, within_ref, d_sources_ref, d_readers_ref, gate_ref, grad_ref, e_ref, sm_ref, smt_ref, outer_ref,
    back_ref, start_ref, dec_ref, skip_ref, heads_ref, early_ref,
    out_ref,
    carry, sums, message_s, sent,
):
    c = pl.program_id(0)

    @pl.when(c == 0)
    def _():
        carry[...] = outer_ref[...].astype(f32)
        sums[...] = jnp.zeros_like(sums)

    r = message.rows
    ones = head_rows()
    ones_twice = twice(ones)
    before = lax.broadcasted_iota(jnp.int32, (CHUNK, CHUNK), 0)
    after = lax.broadcasted_iota(jnp.int32, (CHUNK, CHUNK), 1)
    earlier = jnp.where(before < after, 1.0, 0.0)
    decay_rate = jnp.exp(heads_ref[:HEADS, :])
    first_peer = (pl.num_programs(0) - 1 - c) * per_step * message.per_chunk
    mine = message_s.at[pl.ds(first_peer, per_step * message.per_chunk)]
    chunks = sent.shape[0] - 3

    def body_copy(chunk):
        at = (pl.ds(chunk * message.per_chunk, message.per_chunk), pl.ds(0, LAST_Z * r))
        return pltpu.make_async_copy(message_s.at[at], out_ref.at[at], sent.at[chunk])

    gates_copy = pltpu.make_async_copy(
        gate_ref, out_ref.at[:, pl.ds(LAST_Z * r, PAIRS * r)], sent.at[chunks]
    )
    readers_copy = pltpu.make_async_copy(
        d_readers_ref, out_ref.at[:, pl.ds(LAST_C * r, r)], sent.at[chunks + 1]
    )

    @pl.when(c == 0)
    def _():
        gates_copy.start()
        readers_copy.start()

    states = [carry[:, lanes(j)] for j in range(PAIRS)]
    logs_sum, steps_sum = sums[:HEADS, :], sums[HEADS:, :]
    for i in reversed(range(per_step)):
        rows = slice(i * CHUNK, (i + 1) * CHUNK)
        sm = sm_ref[rows, :]
        sources_twice = twice(message.get(sources_ref, i, 0))
        d_values, highs, lows, scaleds, rounded, fluxes = [], [], [], [], [], []
        for j in range(PAIRS):
            at = lanes(j)
            high, low = two_terms(states[j])
            rounded.append(high)
            values = message.get(first_ref, i, X + j).astype(f32)
            weight = spread_pair(sm, WEIGHT, j)
            grad = within_ref[rows, at] + weight * mm_two(sources_twice, high, low)
            skipped = skip_ref[0:1, at] * grad_ref[rows, at].astype(f32)
            d_values.append((grad + skipped).astype(bf16))
            high, low = two_terms(values * grad)
            highs.append(high)
            lows.append(low)
            scaleds.append((values * weight).astype(bf16))
            states[j] = dec_ref[i, 0:1, at] * states[j] + back_ref[i, :, at]
            fluxes.append(
                jnp.broadcast_to(
                    jnp.sum(start_ref[i, :, at] * states[j], axis=0, keepdims=True), (16, LANES)
                )
            )
        d_sources = d_sources_ref[rows, :] + mm_nt(
            jnp.concatenate(scaleds, axis=1), jnp.concatenate(rounded, axis=1)
        )
        g = sum_heads(ones_twice, highs, lows)[:HEADS]
        constant = sum_heads(ones_twice, *two_terms_each(fluxes))[:HEADS, 0:1]
        flux = constant + mm_exact(g - e_ref[:, lanes(i)], earlier)
        soft = smt_ref[DT * HEADS : (DT + 1) * HEADS, lanes(i)]
        rate = smt_ref[RATE * HEADS : (RATE + 1) * HEADS, lanes(i)]
        sig = smt_ref[SIG * HEADS : (SIG + 1) * HEADS, lanes(i)]
        steps = (g / soft - decay_rate * flux) * sig
        logs_sum = logs_sum + flux * rate
        steps_sum = steps_sum + steps
        steps = jnp.concatenate([steps, jnp.zeros_like(steps)], axis=0)
        for j in range(PAIRS):
            message.put(mine, i, LAST_X + j, d_values[j])
        message.put(mine, i, LAST_B, d_sources.astype(bf16))
        for p in range(message.per_chunk):
            part = steps if p == 0 else pltpu.roll(steps, LANES - p * r, 1)
            mine[i * message.per_chunk + p, LAST * r : LAST * r + STEP_ROWS, :] = part.astype(bf16)
        body_copy((pl.num_programs(0) - 1 - c) * per_step + i).start()
    for j in range(PAIRS):
        carry[:, lanes(j)] = states[j]
    sums[:HEADS, :] = logs_sum
    sums[HEADS:, :] = steps_sum

    @pl.when(c == pl.num_programs(0) - 1)
    def _():
        late = []
        for k in range(2):
            column = jnp.sum(sums[k * HEADS : (k + 1) * HEADS, :], axis=1, keepdims=True)
            block = jnp.broadcast_to(column, (HEADS, LANES))
            block = jnp.concatenate([block, jnp.zeros((LANES - HEADS, LANES), f32)], axis=0)
            late.append(block.T[0:1, :])
        small = [
            jnp.zeros((HEADS, LANES), f32), early_ref[: PAIRS + 1, :], *late,
            jnp.zeros((STEP_ROWS - BIAS_ROW - 1, LANES), f32),
        ]
        small = jnp.concatenate(small, axis=0).astype(bf16)
        own_rows = lax.broadcasted_iota(jnp.int32, (STEP_ROWS, LANES), 0) < HEADS

        def fill(peer, unused):
            steps_at = slice(LAST * r, LAST * r + STEP_ROWS)
            message_s[peer, steps_at, :] = jnp.where(own_rows, message_s[peer, steps_at, :], small)
            return unused

        lax.fori_loop(0, message_s.shape[0], fill, 0)
        at = (slice(None), pl.ds(LAST * r, STEP_ROWS))
        tiles = pltpu.make_async_copy(message_s.at[at], out_ref.at[at], sent.at[chunks + 2])
        tiles.start()
        for chunk in range(chunks):
            body_copy(chunk).wait()
        gates_copy.wait()
        readers_copy.wait()
        tiles.wait()


def finish(own_ref, other_ref, logs_ref, skip_ref, bias_ref, gain_ref):
    total = own_ref[...] + other_ref[...]
    count = logs_ref.shape[1]
    logs_ref[...] = total[0:1, :count]
    bias_ref[...] = total[1:2, :count]
    skip_ref[...] = total[2:3, :count]
    gain_ref[...] = total[8:]


def call(kernel, out_shape, flops, moved, grid=None, in_specs=None, out_specs=None, scratch=()):
    extra = {}
    if grid is not None:
        extra = dict(grid=grid, in_specs=in_specs, out_specs=out_specs)
    return pl.pallas_call(
        kernel,
        out_shape=out_shape,
        scratch_shapes=list(scratch),
        compiler_params=pltpu.CompilerParams(vmem_limit_bytes=28 * 1024 * 1024),
        cost_estimate=pl.CostEstimate(flops=flops, bytes_accessed=moved, transcendentals=0),
        **extra,
    )


def shifted(array, count, by):
    pairs = [(i, i + by) for i in range(count) if 0 <= i + by < count]
    return lax.ppermute(array, "slab", pairs)


def carry_over(state, decay, first_decay, count, sign):
    window, window_decay, step = state, decay, 1
    result = result_decay = None
    while step < count:
        arrived = shifted(window, count, sign * step)
        more = 2 * step < count
        if result is None:
            result = arrived
            if more:
                result_decay = first_decay
                window = (state.astype(f32) + decay[0:1] * arrived.astype(f32)).astype(bf16)
                window_decay = decay * first_decay
        else:
            if more:
                arrived_decay = shifted(window_decay, count, sign * step)
                window = (window.astype(f32) + window_decay[0:1] * arrived.astype(f32)).astype(bf16)
                window_decay = window_decay * arrived_decay
            result = result.astype(f32) + result_decay[0:1] * arrived.astype(f32)
            if more:
                result_decay = result_decay * arrived_decay
        step *= 2
    return jnp.zeros_like(state) if result is None else result


def two_parts(array, axis, count):
    step, other = 1, jnp.zeros_like(array)
    while step < count:
        array = array if step == 1 else array + other
        other = lax.ppermute(array, axis, [(i, i ^ step) for i in range(count)])
        step *= 2
    return array, other


def on_device(
    slab_count, sub_count, tensor_count,
    mixer_x, gate_z, b_matrix, c_matrix, raw_steps, decay_log, skip_gain, step_bias, norm_gain, out_grad,
):
    rows = mixer_x.shape[0]
    peers = sub_count * tensor_count
    tokens = rows * peers
    chunks = tokens // CHUNK
    message = Message(rows)
    owners = [t * sub_count + s for s in range(sub_count) for t in range(tensor_count)]
    sub = lax.axis_index("sub")

    def struct(shape, kind=f32):
        return jax.ShapeDtypeStruct(shape, kind)

    def hbm(shape, kind=f32):
        return pltpu.HBM(shape, kind)

    def in_hbm(array):
        return pltpu.with_memory_space_constraint(array, pltpu.HBM)

    def exchange(array):
        return lax.all_to_all(array, ("sub", "tensor"), split_axis=0, concat_axis=0, tiled=True)

    own_logs = lax.dynamic_slice(decay_log, (sub * HEADS,), (HEADS,))
    own_bias = lax.dynamic_slice(step_bias, (sub * HEADS,), (HEADS,))
    own_skip = lax.dynamic_slice(skip_gain, (sub * HEADS,), (HEADS,))
    own_gain = lax.dynamic_slice(norm_gain, (sub * WIDTH,), (WIDTH,)).reshape(1, WIDTH)
    heads = jnp.broadcast_to(jnp.concatenate([own_logs, own_bias])[:, None], (2 * HEADS, LANES))
    skip_row = jnp.repeat(own_skip, HEAD_DIM).reshape(1, WIDTH)

    first_rows = FIRST * rows + STEP_ROWS
    second_rows = SECOND * rows
    last_rows = LAST * rows + STEP_ROWS

    def packed(kernel, height, arrays, whole_arrays=(), scratch=()):
        out = hbm((sub_count, tensor_count, height, LANES), bf16)
        moved = 4 * peers * height * LANES
        runs = 1
        parts = tensor_count * runs
        specs = [
            pl.BlockSpec((rows, a.shape[1] // parts), lambda t, k: (0, t * runs + k)) for a in arrays
        ] + [pl.BlockSpec(a.shape, lambda t, k: (0, 0)) for a in whole_arrays]
        out_spec = pl.BlockSpec((sub_count // runs, 1, height, LANES), lambda t, k: (k, t, 0, 0))
        made = call(kernel, out, 0, moved, (tensor_count, runs), specs, out_spec, scratch)(
            *(in_hbm(a) for a in (*arrays, *whole_arrays))
        )
        return made.reshape(peers, height, LANES)

    first = exchange(
        packed(
            pack_first, first_rows, (mixer_x, b_matrix, c_matrix), (raw_steps,),
            [pltpu.VMEM((LANES, LANES), f32)],
        )
    )
    tensor_rows = lax.broadcasted_iota(jnp.int32, (tensor_count, LANES), 0)
    mine = (tensor_rows == lax.axis_index("tensor")).astype(f32)
    half = first[:, HALF * rows : (HALF + 1) * rows, :]
    other_half = lax.ppermute(half, "sub", [(i, i ^ 1) for i in range(sub_count)])
    even = sub % 2 == 0
    sources, readers = jnp.where(even, half, other_half), jnp.where(even, other_half, half)
    gate_z, heads, skip_row, own_gain, mine = lax.optimization_barrier(
        (gate_z, heads, skip_row, own_gain, mine)
    )
    second = exchange(packed(pack_second, second_rows, (gate_z, out_grad)))

    def flow(kernel, shape_specs, flops, moved, in_specs, scratch=(), per=2):
        per = min(per, chunks)

        def body(*refs):
            return kernel(message, per, *refs)

        shapes = tuple(shape for shape, _ in shape_specs)
        specs = tuple(spec for _, spec in shape_specs)
        return call(body, shapes, flops, moved, (chunks // per,), in_specs, specs, scratch)

    def specs_of(per, down=False):
        per = min(per, chunks)
        steps = chunks // per

        def spec(block, axis):
            def index(c):
                at = steps - 1 - c if down else c
                return tuple(at if k == axis else 0 for k in range(len(block)))

            return pl.BlockSpec(block, index)

        return dict(
            message=lambda height: spec((per * message.per_chunk, height, LANES), 0),
            token=lambda width: spec((per * CHUNK, width), 0),
            lane=lambda height: spec((height, per * CHUNK), 1),
            chunk=lambda *shape: spec((per,) + shape, 0),
        )

    up = specs_of(2)
    many = specs_of(4)
    all_at_once = specs_of(8)
    dn = specs_of(8, down=True)

    def whole(*shape):
        return pl.BlockSpec(shape, lambda c: (0,) * len(shape))

    unit = 2 * tokens * CHUNK * WIDTH
    size = tokens * WIDTH

    sm, smt, own, dec, state, decay = flow(
        state_kernel,
        [
            (hbm((tokens, LANES)), up["token"](LANES)),
            (hbm((KINDS * HEADS, tokens)), up["lane"](KINDS * HEADS)),
            (hbm((chunks, STATE, WIDTH)), up["chunk"](STATE, WIDTH)),
            (hbm((chunks, 8, WIDTH)), up["chunk"](8, WIDTH)),
            (struct((STATE, WIDTH), bf16), whole(STATE, WIDTH)),
            (struct((8, WIDTH)), whole(8, WIDTH)),
        ],
        2 * unit, size * 8,
        [
            up["message"](PAIRS * rows), up["message"](rows),
            pl.BlockSpec((peers, STEP_ROWS, LANES), lambda c: (0, FIRST * rows // STEP_ROWS, 0)),
            whole(2 * HEADS, LANES),
        ],
        [pltpu.VMEM((STATE, WIDTH), f32), pltpu.VMEM((chunks, KINDS * HEADS, LANES), f32)],
    )(first, sources, first, heads)

    before = after = None
    if slab_count > 2:
        before, after = shifted(decay, slab_count, 1), shifted(decay, slab_count, -1)
    inbound = carry_over(state, decay, before, slab_count, 1)

    within, starts, pre = flow(
        within_kernel,
        [
            (hbm((tokens, WIDTH)), up["token"](WIDTH)),
            (hbm((chunks, STATE, WIDTH)), up["chunk"](STATE, WIDTH)),
            (hbm((chunks, 8, WIDTH)), up["chunk"](8, WIDTH)),
        ],
        6 * unit, size * 16,
        [
            up["message"](PAIRS * rows), up["message"](rows), up["message"](rows),
            up["token"](LANES), up["lane"](KINDS * HEADS),
            up["chunk"](STATE, WIDTH), up["chunk"](8, WIDTH),
        ],
        [pltpu.VMEM((STATE, WIDTH), f32), pltpu.VMEM((8, WIDTH), f32)],
    )(first, sources, readers, in_hbm(sm), in_hbm(smt), in_hbm(own), in_hbm(dec))

    anywhere = pl.BlockSpec(memory_space=pl.ANY)
    per_mix = min(2, chunks)
    y, sums, second = flow(
        mix_kernel,
        [
            (struct((tokens, WIDTH)), up["token"](WIDTH)),
            (struct((chunks, 8, LANES)), up["chunk"](8, LANES)),
            (struct((peers, second_rows, LANES), bf16), up["message"](second_rows)),
        ],
        unit, size * 16,
        [
            up["message"](PAIRS * rows), up["message"](rows), up["message"](second_rows),
            up["token"](WIDTH), up["token"](LANES), whole(STATE, WIDTH), up["chunk"](8, WIDTH),
            whole(1, WIDTH), whole(1, WIDTH),
        ],
        per=per_mix,
    )(
        first, readers, in_hbm(second), in_hbm(within), in_hbm(sm), inbound, in_hbm(pre),
        own_gain, skip_row,
    )

    partner = lax.ppermute(sums, "sub", [(i, i ^ 1) for i in range(sub_count)])

    d_mixed, back, slab_back = flow(
        norm_kernel,
        [
            (struct((tokens, WIDTH), bf16), all_at_once["token"](WIDTH)),
            (struct((chunks, STATE, WIDTH)), all_at_once["chunk"](STATE, WIDTH)),
            (struct((STATE, WIDTH), bf16), whole(STATE, WIDTH)),
        ],
        2 * unit, size * 12,
        [
            all_at_once["message"](PAIRS * rows), all_at_once["message"](rows), all_at_once["message"](second_rows),
            all_at_once["token"](WIDTH), all_at_once["token"](LANES), all_at_once["chunk"](8, WIDTH), all_at_once["chunk"](8, LANES),
            all_at_once["chunk"](8, LANES), whole(1, WIDTH), whole(1, WIDTH),
        ],
        [pltpu.VMEM((STATE, WIDTH), f32)],
        per=8,
    )(first, readers, second, y, sm, pre, sums, partner, own_gain, skip_row)

    outer = carry_over(slab_back, decay, after, slab_count, -1)

    d_values, d_sources, d_readers, d_gates, e, starts, params = flow(
        local_kernel,
        [
            (struct((tokens, WIDTH)), many["token"](WIDTH)),
            (struct((tokens, STATE)), many["token"](STATE)),
            (struct((peers, rows, LANES), bf16), many["message"](rows)),
            (struct((peers, PAIRS * rows, LANES), bf16), many["message"](PAIRS * rows)),
            (struct((HEADS, tokens)), many["lane"](HEADS)),
            (struct((chunks, STATE, WIDTH)), many["chunk"](STATE, WIDTH)),
            (struct((8, LANES)), whole(8, LANES)),
        ],
        10 * unit, size * 16,
        [
            many["message"](PAIRS * rows), many["message"](rows), many["message"](rows),
            many["message"](second_rows), many["token"](WIDTH), many["token"](WIDTH), many["token"](LANES),
            many["lane"](KINDS * HEADS),
            many["chunk"](STATE, WIDTH), many["chunk"](8, WIDTH), whole(STATE, WIDTH),
            many["chunk"](8, LANES), many["chunk"](8, LANES), whole(1, WIDTH), whole(1, WIDTH),
        ],
        [pltpu.VMEM((8, WIDTH), f32), pltpu.VMEM((8, WIDTH), f32)],
        per=4,
    )(
        first, sources, readers, second, y, d_mixed, sm, smt, starts, pre, inbound,
        sums, partner, own_gain, skip_row,
    )

    (last,) = flow(
        last_kernel,
        [(hbm((peers, last_rows, LANES), bf16), anywhere)],
        4 * unit, size * 16,
        [
            dn["message"](PAIRS * rows), dn["message"](rows), dn["token"](WIDTH), dn["token"](STATE),
            anywhere, anywhere,
            dn["token"](WIDTH), dn["lane"](HEADS), dn["token"](LANES), dn["lane"](KINDS * HEADS),
            whole(STATE, WIDTH), dn["chunk"](STATE, WIDTH), dn["chunk"](STATE, WIDTH),
            dn["chunk"](8, WIDTH), whole(1, WIDTH), whole(2 * HEADS, LANES), whole(8, LANES),
        ],
        [
            pltpu.VMEM((STATE, WIDTH), f32), pltpu.VMEM((2 * HEADS, LANES), f32),
            pltpu.VMEM((peers, last_rows, LANES), bf16),
            pltpu.SemaphoreType.DMA((chunks + 3,)),
        ],
        per=8,
    )(
        first, sources, d_values, d_sources, d_readers, d_gates, d_mixed, e, sm, smt, outer, back,
        starts, dec, skip_row, heads, params,
    )

    last_back = exchange(last)
    tile_at = LAST * rows // STEP_ROWS
    def tile(at):
        return pl.BlockSpec((peers, STEP_ROWS, LANES), lambda c: (0, at, 0))

    params = call(
        lambda *refs: unpack_params(sub_count, tensor_count, *refs),
        struct((8 + sub_count * PAIRS, LANES)),
        0, 4 * peers * STEP_ROWS * LANES, (1,),
        [tile(tile_at), whole(tensor_count, LANES)],
        whole(8 + sub_count * PAIRS, LANES),
    )(last_back, mine)
    own_params, other_params = two_parts(params, "slab", slab_count)
    wide, narrow = struct((rows, CHANNELS), bf16), struct((rows, GROUPS * STATE), bf16)
    grad_x, grad_gates, grad_b, grad_c, grad_steps = call(
        lambda *refs: unpack(owners, *refs),
        (wide, wide, narrow, narrow, struct((rows, MIXER_HEADS), bf16)),
        0, 10 * rows * CHANNELS,
    )(last_back)
    row = struct((1, sub_count * HEADS))
    grad_logs, grad_skip, grad_bias, grad_gain = call(
        finish, (row, row, row, struct((sub_count * PAIRS, LANES))), 0, 1 << 16,
    )(own_params, other_params)
    return (
        grad_x,
        grad_gates,
        grad_b,
        grad_c,
        grad_steps,
        grad_logs.reshape(-1),
        grad_skip.reshape(-1),
        grad_bias.reshape(-1),
        grad_gain.reshape(-1),
    )


def solution(mesh):
    tensor_count = mesh.shape["tensor"]
    sub_count = OWNERS // tensor_count
    slab_count = mesh.shape["dp"] // sub_count
    devices = mesh.devices.reshape(slab_count, sub_count, tensor_count)
    split_mesh = Mesh(devices, ("slab", "sub", "tensor"))
    rows = P(("slab", "sub", "tensor"), None)
    param = P("tensor")

    def local(*arrays):
        return on_device(slab_count, sub_count, tensor_count, *arrays)

    return jax.shard_map(
        local,
        mesh=split_mesh,
        in_specs=(rows,) * 5 + (param,) * 4 + (rows,),
        out_specs=(rows,) * 5 + (param,) * 4,
        check_vma=False,
    )
```

```python
import jax
import jax.numpy as jnp
from jax import lax
from jax.experimental import pallas as pl
from jax.experimental.pallas import tpu as pltpu
from jax.sharding import Mesh
from jax.sharding import PartitionSpec as P

MIXER_HEADS = 128
HEAD_DIM = 64
STATE = 128
GROUPS = 8
CHANNELS = MIXER_HEADS * HEAD_DIM
HEADS = 8
WIDTH = HEADS * HEAD_DIM
GROUP_WIDTH = 2 * WIDTH
OWNERS = MIXER_HEADS // HEADS
LANES = 128
PAIRS = WIDTH // LANES
CHUNK = 128
STEP_ROWS = 16
epsilon = 1e-05
f32 = jnp.float32
bf16 = jnp.bfloat16

DT, CUM, WEIGHT, SHIFTED, ECUM, RATE, SIG = range(7)
KINDS = 8
CLAMP = 80.0


def mm(a, b):
    return jnp.dot(a, b, preferred_element_type=f32)


def mm_nt(a, b):
    return lax.dot_general(a, b, (((1,), (1,)), ((), ())), preferred_element_type=f32)


def mm_tn(a, b):
    return lax.dot_general(a, b, (((0,), (0,)), ((), ())), preferred_element_type=f32)


def mm_exact(a, b):
    return jnp.dot(a, b, precision=lax.Precision.HIGHEST, preferred_element_type=f32)


def two_terms(values):
    high = values.astype(bf16)
    return high, (values - high.astype(f32)).astype(bf16)


def two_terms_each(tiles):
    return zip(*(two_terms(tile) for tile in tiles))


def twice(a):
    return jnp.concatenate([a, a], axis=1)


def mm_two(a_twice, high, low):
    return mm(a_twice, jnp.concatenate([high, low], axis=0))


def sum_heads(ones_twice, highs, lows):
    return mm_nt(ones_twice, jnp.concatenate([*highs, *lows], axis=1))


def sigmoid(values):
    return 0.5 + 0.5 * jnp.tanh(0.5 * values)


def low_half(rows):
    return lax.broadcasted_iota(jnp.int32, (rows, LANES), 1) < HEAD_DIM


def spread_pair(values, kind, j):
    rows = values.shape[0]
    at = kind * HEADS + 2 * j
    return jnp.where(
        low_half(rows),
        jnp.broadcast_to(values[:, at : at + 1], (rows, LANES)),
        jnp.broadcast_to(values[:, at + 1 : at + 2], (rows, LANES)),
    )


def head_rows():
    row = lax.broadcasted_iota(jnp.int32, (16, WIDTH), 0)
    channel = lax.broadcasted_iota(jnp.int32, (16, WIDTH), 1) // HEAD_DIM
    return jnp.where(row == channel, 1.0, 0.0).astype(bf16)


def split_pair(block):
    low = low_half(block.shape[0])
    zero = jnp.zeros_like(block)
    return jnp.concatenate(
        [jnp.where(low, block, zero), jnp.where(low, zero, block)], axis=0
    )


def lanes(j):
    return slice(j * LANES, (j + 1) * LANES)


class Message:
    def __init__(self, rows):
        self.rows = rows
        self.per_chunk = CHUNK // rows

    def place(self, chunk, k):
        r = self.rows
        return (slice(chunk * self.per_chunk, (chunk + 1) * self.per_chunk), slice(k * r, (k + 1) * r))

    def get(self, ref, chunk, k):
        a, b = self.place(chunk, k)
        return ref[a, b, :].reshape(CHUNK, LANES)

    def put(self, ref, chunk, k, value):
        a, b = self.place(chunk, k)
        ref[a, b, :] = value.reshape(self.per_chunk, self.rows, LANES)


X, HALF = 0, PAIRS
FIRST = PAIRS + 1
Z, GRAD = 0, PAIRS
SECOND = 2 * PAIRS
LAST_X, LAST_B, LAST_Z, LAST_C = 0, PAIRS, PAIRS + 1, 2 * PAIRS + 1
LAST = 2 * PAIRS + 2


def pack_first(x_ref, b_ref, c_ref, steps_ref, out_ref, by_head):
    r = x_ref.shape[0]
    step = pl.program_id(0) * pl.num_programs(1) + pl.program_id(1)
    subs = out_ref.shape[0]

    @pl.when(step == 0)
    def _():
        steps = steps_ref[...].astype(f32)
        by_head[...] = jnp.concatenate([steps, jnp.zeros((LANES - r, LANES), f32)], axis=0).T

    zero = jnp.zeros((STEP_ROWS - HEADS, LANES), f32)
    for s in range(subs):
        for j in range(PAIRS):
            out_ref[s, 0, j * r : (j + 1) * r, :] = x_ref[:, lanes(s * PAIRS + j)]
        half = b_ref if s % 2 == 0 else c_ref
        out_ref[s, 0, HALF * r : (HALF + 1) * r, :] = half[:, lanes(s // 2)]
        at = pl.multiple_of((step * subs + s) * HEADS, HEADS)
        mine = jnp.concatenate([by_head[pl.ds(at, HEADS), :], zero], axis=0)
        out_ref[s, 0, FIRST * r :, :] = mine.astype(bf16)


def pack_second(z_ref, grad_ref, out_ref):
    r = z_ref.shape[0]
    for s in range(out_ref.shape[0]):
        for j in range(PAIRS):
            at = lanes(s * PAIRS + j)
            out_ref[s, 0, (Z + j) * r : (Z + j + 1) * r, :] = z_ref[:, at]
            out_ref[s, 0, (GRAD + j) * r : (GRAD + j + 1) * r, :] = grad_ref[:, at]


def add_halves(owners, in_ref, block, out_ref):
    r = out_ref.shape[0]
    peer_of = {own: peer for peer, own in enumerate(owners)}
    for g in range(GROUPS):
        halves = [
            in_ref[peer_of[2 * g + k], block * r : (block + 1) * r, :].astype(f32) for k in range(2)
        ]
        out_ref[:, lanes(g)] = (halves[0] + halves[1]).astype(bf16)


def unpack(owners, in_ref, x_ref, z_ref, b_ref, c_ref, steps_ref):
    r = x_ref.shape[0]
    peer_of = {own: peer for peer, own in enumerate(owners)}
    for peer, own in enumerate(owners):
        for j in range(PAIRS):
            for block, ref in ((LAST_X, x_ref), (LAST_Z, z_ref)):
                at = slice((block + j) * r, (block + j + 1) * r)
                ref[:, lanes(own * PAIRS + j)] = in_ref[peer, at, :]
    add_halves(owners, in_ref, LAST_B, b_ref)
    add_halves(owners, in_ref, LAST_C, c_ref)
    by_head = jnp.concatenate(
        [
            in_ref[peer_of[own], LAST * r : LAST * r + STEP_ROWS, :].astype(f32)[:HEADS]
            for own in range(OWNERS)
        ],
        axis=0,
    )
    steps_ref[...] = by_head.T[:r, :].astype(bf16)


GAIN_ROW, SKIP_ROW, LOGS_ROW, BIAS_ROW = HEADS, HEADS + PAIRS, HEADS + PAIRS + 1, HEADS + PAIRS + 2


def unpack_params(sub_count, tensor_count, tile_ref, mine_ref, out_ref):
    lane = lax.broadcasted_iota(jnp.int32, (1, LANES), 1)
    totals = [jnp.zeros((1, LANES), f32) for _ in range(3)]
    for s in range(sub_count):
        rows = jnp.zeros((STEP_ROWS, LANES), f32)
        for t in range(tensor_count):
            mine = mine_ref[t : t + 1, :] > 0.0
            rows = jnp.where(mine, tile_ref[s * tensor_count + t].astype(f32), rows)
        for k, at in enumerate((LOGS_ROW, BIAS_ROW, SKIP_ROW)):
            part = jnp.where(lane < HEADS, rows[at : at + 1], 0.0)
            totals[k] = totals[k] + (part if s == 0 else pltpu.roll(part, s * HEADS, 1))
        out_ref[8 + s * PAIRS : 8 + (s + 1) * PAIRS, :] = rows[GAIN_ROW : GAIN_ROW + PAIRS]
    out_ref[:8, :] = jnp.concatenate(totals + [jnp.zeros((5, LANES), f32)], axis=0)


def state_kernel(
    message, per_step,
    first_ref, sources_ref, steps_ref, heads_ref, sm_ref, smt_ref, own_ref, dec_ref, state_ref, whole_ref,
    carry, rows_s,
):
    c = pl.program_id(0)

    @pl.when(c == 0)
    def _():
        carry[...] = jnp.zeros_like(carry)
        whole_ref[...] = jnp.ones_like(whole_ref)
        chunks = rows_s.shape[0]
        before = lax.broadcasted_iota(jnp.int32, (CHUNK, CHUNK), 0)
        after = lax.broadcasted_iota(jnp.int32, (CHUNK, CHUNK), 1)
        raws = []
        for k in range(chunks):
            raw = heads_ref[HEADS:, :]
            for p in range(message.per_chunk):
                part = steps_ref[k * message.per_chunk + p].astype(f32)[:HEADS]
                raw = raw + (part if p == 0 else pltpu.roll(part, p * message.rows, 1))
            raws.append(raw)
        raw = jnp.concatenate(raws, axis=0)
        small = jnp.exp(-jnp.abs(raw))
        series = small * (
            1.0 - small * (0.5 - small * (1.0 / 3 - small * (0.25 - small * 0.2)))
        )
        soft = jnp.maximum(raw, 0.0) + jnp.where(small < 0.015625, series, jnp.log(1.0 + small))
        sig = jnp.where(raw >= 0.0, 1.0, small) / (1.0 + small)
        decay_rate = jnp.concatenate([jnp.exp(heads_ref[:HEADS, :])] * chunks, axis=0)
        rate = -decay_rate * soft
        cum = mm_exact(rate, jnp.where(before <= after, 1.0, 0.0))
        rest = mm_exact(rate, jnp.where(before > after, 1.0, 0.0))
        kinds = [
            soft, cum, soft * jnp.exp(rest), cum - jnp.log(soft), jnp.exp(cum), rate, sig,
            jnp.zeros_like(soft),
        ]
        for k in range(chunks):
            at = slice(k * HEADS, (k + 1) * HEADS)
            rows_s[k] = jnp.concatenate([kind[at] for kind in kinds], axis=0)

    made = []
    state = [carry[:, lanes(j)] for j in range(PAIRS)]
    decays = [whole_ref[:, lanes(j)] for j in range(PAIRS)]
    for i in range(per_step):
        rows = rows_s[c * per_step + i]
        sm = jnp.concatenate([rows, jnp.zeros_like(rows)], axis=0).T
        last = jnp.broadcast_to(sm[CHUNK - 1 : CHUNK, :], (8, LANES))
        sources_t = twice(message.get(sources_ref, i, 0).T)
        decs, owns = [], []
        for j in range(PAIRS):
            dec = spread_pair(last, ECUM, j)
            scaled = message.get(first_ref, i, X + j).astype(f32) * spread_pair(sm, WEIGHT, j)
            own = mm_two(sources_t, *two_terms(scaled))
            state[j] = dec[0:1] * state[j] + own
            decays[j] = decays[j] * dec
            decs.append(dec)
            owns.append(own)
        made.append((rows, sm, decs, owns))
    for i, (rows, sm, decs, owns) in enumerate(made):
        smt_ref[:, lanes(i)] = rows
        sm_ref[i * CHUNK : (i + 1) * CHUNK, :] = sm
        for j in range(PAIRS):
            dec_ref[i, :, lanes(j)] = decs[j]
            own_ref[i, :, lanes(j)] = owns[j]
    for j in range(PAIRS):
        carry[:, lanes(j)] = state[j]
        whole_ref[:, lanes(j)] = decays[j]
        state_ref[:, lanes(j)] = state[j].astype(bf16)


def within_kernel(
    message, per_step,
    first_ref, sources_ref, readers_ref, sm_ref, smt_ref, own_ref, dec_ref, y_ref, start_ref, pre_ref, carry, pre,
):
    @pl.when(pl.program_id(0) == 0)
    def _():
        carry[...] = jnp.zeros_like(carry)
        pre[...] = jnp.ones_like(pre)

    t = lax.broadcasted_iota(jnp.int32, (CHUNK, CHUNK), 0)
    s = lax.broadcasted_iota(jnp.int32, (CHUNK, CHUNK), 1)
    made = []
    states = [carry[:, lanes(j)] for j in range(PAIRS)]
    before = pre[...]
    for i in range(per_step):
        rows = slice(i * CHUNK, (i + 1) * CHUNK)
        sm = sm_ref[rows, :]
        smt = smt_ref[:, lanes(i)]
        readers = message.get(readers_ref, i, 0)
        readers_twice = twice(readers)
        scores = jnp.where(t >= s, mm_nt(readers, message.get(sources_ref, i, 0)), 0.0)
        ys = []
        for j in range(PAIRS):
            weights = []
            for h in (2 * j, 2 * j + 1):
                here = sm[:, CUM * HEADS + h : CUM * HEADS + h + 1]
                there = smt[SHIFTED * HEADS + h : SHIFTED * HEADS + h + 1, :]
                weights.append(
                    (scores * jnp.exp(jnp.minimum(here - there, CLAMP))).astype(bf16)
                )
            values = split_pair(message.get(first_ref, i, X + j))
            within = mm(jnp.concatenate(weights, axis=1), values)
            carried = mm_two(readers_twice, *two_terms(states[j]))
            ys.append(within + spread_pair(sm, ECUM, j) * carried)
        made.append((ys, list(states), before))
        for j in range(PAIRS):
            states[j] = dec_ref[i, 0:1, lanes(j)] * states[j] + own_ref[i, :, lanes(j)]
        before = before * dec_ref[i]
    for i, (ys, starts, prefix) in enumerate(made):
        pre_ref[i] = prefix
        for j in range(PAIRS):
            y_ref[i * CHUNK : (i + 1) * CHUNK, lanes(j)] = ys[j]
            start_ref[i, :, lanes(j)] = starts[j]
    pre[...] = before
    for j in range(PAIRS):
        carry[:, lanes(j)] = states[j]


def mix_kernel(
    message, per_step,
    first_ref, readers_ref, second_ref, within_ref, sm_ref, inbound_ref, pre_ref, gain_ref, skip_ref,
    y_ref, sums_ref, second_out,
):
    second_out[...] = second_ref[...]
    inbound = inbound_ref[...].astype(bf16)
    for i in range(per_step):
        rows = slice(i * CHUNK, (i + 1) * CHUNK)
        sm = sm_ref[rows, :]
        carried = mm(message.get(readers_ref, i, 0), inbound)
        power = jnp.zeros((CHUNK, LANES), f32)
        cross = jnp.zeros((CHUNK, LANES), f32)
        for j in range(PAIRS):
            at = lanes(j)
            decay = spread_pair(sm, ECUM, j) * pre_ref[i, 0:1, at]
            y = within_ref[rows, at] + decay * carried[:, at]
            y_ref[rows, at] = y
            values = message.get(first_ref, i, X + j).astype(f32)
            gates = message.get(second_ref, i, Z + j).astype(f32)
            grad = message.get(second_ref, i, GRAD + j).astype(f32)
            gated = (y + skip_ref[0:1, at] * values) * (gates * sigmoid(gates))
            power = power + gated * gated
            cross = cross + grad * gain_ref[0:1, at] * gated
        sums_ref[i, 0:1, :] = jnp.sum(power.T, axis=0, keepdims=True)
        sums_ref[i, 1:2, :] = jnp.sum(cross.T, axis=0, keepdims=True)
        sums_ref[i, 2:, :] = jnp.zeros((6, LANES), f32)


def norm_factors(sums):
    sums = sums * (1.0 / GROUP_WIDTH)
    inverse = lax.rsqrt(sums[0:1] + epsilon)
    pull = inverse * inverse * inverse * sums[1:2]
    return (
        jnp.broadcast_to(inverse, (CHUNK, LANES)).T,
        jnp.broadcast_to(pull, (CHUNK, LANES)).T,
    )


def norm_kernel(
    message, per_step,
    first_ref, readers_ref, second_ref, y_ref, sm_ref, pre_ref, sums_ref, other_ref, gain_ref, skip_ref,
    mixed_ref, back_ref, slab_ref,
    back_sum,
):
    @pl.when(pl.program_id(0) == 0)
    def _():
        back_sum[...] = jnp.zeros_like(back_sum)

    sums = [back_sum[:, lanes(j)] for j in range(PAIRS)]
    for i in range(per_step):
        rows = slice(i * CHUNK, (i + 1) * CHUNK)
        sm = sm_ref[rows, :]
        readers_t = twice(message.get(readers_ref, i, 0).T)
        inverse, pull = norm_factors(sums_ref[i] + other_ref[i])
        for j in range(PAIRS):
            at = lanes(j)
            values = message.get(first_ref, i, X + j).astype(f32)
            gates = message.get(second_ref, i, Z + j).astype(f32)
            grad = message.get(second_ref, i, GRAD + j).astype(f32)
            silu = gates * sigmoid(gates)
            gated = (y_ref[rows, at] + skip_ref[0:1, at] * values) * silu
            d_mixed = (inverse * grad * gain_ref[0:1, at] - pull * gated) * silu
            back = mm_two(readers_t, *two_terms(d_mixed * spread_pair(sm, ECUM, j)))
            sums[j] = sums[j] + pre_ref[i, 0:1, at] * back
            mixed_ref[rows, at] = d_mixed.astype(bf16)
            back_ref[i, :, at] = back
    for j in range(PAIRS):
        back_sum[:, lanes(j)] = sums[j]
        slab_ref[:, lanes(j)] = sums[j].astype(bf16)


def local_kernel(
    message, per_step,
    first_ref, sources_ref, readers_ref, second_ref, y_ref, grad_ref, sm_ref, smt_ref, start_ref, pre_ref, inbound_ref,
    sums_ref, other_ref, gain_ref, skip_ref,
    values_out, sources_out, readers_out, gate_ref, e_ref, start_out, param_ref,
    gain_sum, skip_sum,
):
    c = pl.program_id(0)

    @pl.when(c == 0)
    def _():
        gain_sum[...] = jnp.zeros_like(gain_sum)
        skip_sum[...] = jnp.zeros_like(skip_sum)

    s = lax.broadcasted_iota(jnp.int32, (CHUNK, CHUNK), 0)
    t = lax.broadcasted_iota(jnp.int32, (CHUNK, CHUNK), 1)
    causal = t >= s
    ones = head_rows()
    ones_twice = twice(ones)
    gains = [gain_sum[0:1, lanes(j)] for j in range(PAIRS)]
    skips = [skip_sum[0:1, lanes(j)] for j in range(PAIRS)]
    for i in range(per_step):
        rows = slice(i * CHUNK, (i + 1) * CHUNK)
        sm = sm_ref[rows, :]
        smt = smt_ref[:, lanes(i)]
        sources = message.get(sources_ref, i, 0)
        readers = message.get(readers_ref, i, 0)
        inverse, pull = norm_factors(sums_ref[i] + other_ref[i])
        scores = jnp.where(causal, mm_nt(sources, readers), 0.0)
        total = jnp.zeros((CHUNK, CHUNK), f32)
        d_values, d_gates, highs, lows, scaleds, starts = [], [], [], [], [], []
        for j in range(PAIRS):
            at = lanes(j)
            rounded = grad_ref[rows, at]
            grads = split_pair(rounded)
            x = message.get(first_ref, i, X + j)
            weight_grads = mm_nt(x, grads)
            weights = []
            for k, h in enumerate((2 * j, 2 * j + 1)):
                there = sm[:, SHIFTED * HEADS + h : SHIFTED * HEADS + h + 1]
                here = smt[CUM * HEADS + h : CUM * HEADS + h + 1, :]
                decay = jnp.exp(jnp.minimum(here - there, CLAMP))
                weights.append((scores * decay).astype(bf16))
                total = total + weight_grads[:, lanes(k)] * decay
            d_values.append(mm(jnp.concatenate(weights, axis=1), grads))

            values = x.astype(f32)
            gates = message.get(second_ref, i, Z + j).astype(f32)
            grad = message.get(second_ref, i, GRAD + j).astype(f32)
            y = y_ref[rows, at]
            mixed = y + skip_ref[0:1, at] * values
            sig = sigmoid(gates)
            silu = gates * sig
            gated = mixed * silu
            scaled = inverse * grad
            gains[j] = gains[j] + jnp.sum(scaled * gated, axis=0, keepdims=True)
            d_gated = scaled * gain_ref[0:1, at] - pull * gated
            d_gate = d_gated * mixed * (sig + silu * (1.0 - sig))
            d_gates.append(d_gate.astype(bf16))
            skips[j] = skips[j] + jnp.sum(values * (d_gated * silu), axis=0, keepdims=True)
            d_mixed = rounded.astype(f32)
            high, low = two_terms(d_mixed * y)
            highs.append(high)
            lows.append(low)
            scaleds.append((d_mixed * spread_pair(sm, ECUM, j)).astype(bf16))
            starts.append(
                start_ref[i, :, at] + pre_ref[i, 0:1, at] * inbound_ref[:, at].astype(f32)
            )
        e = sum_heads(ones_twice, highs, lows)
        total = jnp.where(causal, total, 0.0).astype(bf16)
        start = jnp.concatenate([part.astype(bf16) for part in starts], axis=1)
        d_readers = mm_tn(total, sources) + mm_nt(jnp.concatenate(scaleds, axis=1), start)
        for j in range(PAIRS):
            values_out[rows, lanes(j)] = d_values[j]
            message.put(gate_ref, i, j, d_gates[j])
            start_out[i, :, lanes(j)] = starts[j]
        e_ref[:, lanes(i)] = e[:HEADS]
        sources_out[rows, :] = mm(total, readers)
        message.put(readers_out, i, 0, d_readers.astype(bf16))
    for j in range(PAIRS):
        gain_sum[0:1, lanes(j)] = gains[j]
        skip_sum[0:1, lanes(j)] = skips[j]

    @pl.when(c == pl.num_programs(0) - 1)
    def _():
        for j in range(PAIRS):
            param_ref[j : j + 1, :] = gain_sum[0:1, lanes(j)]
        high, low = two_terms(jnp.broadcast_to(skip_sum[0:1, :], (LANES, WIDTH)))
        skips = (mm_nt(high, ones) + mm_nt(low, ones))[0:1]
        param_ref[PAIRS : PAIRS + 1, :] = jnp.concatenate(
            [skips, jnp.zeros((1, LANES - 16), f32)], axis=1
        )
        param_ref[PAIRS + 1 :, :] = jnp.zeros((8 - PAIRS - 1, LANES), f32)


def last_kernel(
    message, per_step,
    first_ref, sources_ref, within_ref, d_sources_ref, d_readers_ref, gate_ref, grad_ref, e_ref, sm_ref, smt_ref, outer_ref,
    back_ref, start_ref, dec_ref, skip_ref, heads_ref, early_ref,
    out_ref,
    carry, sums, message_s, sent,
):
    c = pl.program_id(0)

    @pl.when(c == 0)
    def _():
        carry[...] = outer_ref[...].astype(f32)
        sums[...] = jnp.zeros_like(sums)

    r = message.rows
    ones = head_rows()
    ones_twice = twice(ones)
    before = lax.broadcasted_iota(jnp.int32, (CHUNK, CHUNK), 0)
    after = lax.broadcasted_iota(jnp.int32, (CHUNK, CHUNK), 1)
    earlier = jnp.where(before < after, 1.0, 0.0)
    decay_rate = jnp.exp(heads_ref[:HEADS, :])
    first_peer = (pl.num_programs(0) - 1 - c) * per_step * message.per_chunk
    mine = message_s.at[pl.ds(first_peer, per_step * message.per_chunk)]
    chunks = sent.shape[0] - 3

    def body_copy(chunk):
        at = (pl.ds(chunk * message.per_chunk, message.per_chunk), pl.ds(0, LAST_Z * r))
        return pltpu.make_async_copy(message_s.at[at], out_ref.at[at], sent.at[chunk])

    gates_copy = pltpu.make_async_copy(
        gate_ref, out_ref.at[:, pl.ds(LAST_Z * r, PAIRS * r)], sent.at[chunks]
    )
    readers_copy = pltpu.make_async_copy(
        d_readers_ref, out_ref.at[:, pl.ds(LAST_C * r, r)], sent.at[chunks + 1]
    )

    @pl.when(c == 0)
    def _():
        gates_copy.start()
        readers_copy.start()

    states = [carry[:, lanes(j)] for j in range(PAIRS)]
    logs_sum, steps_sum = sums[:HEADS, :], sums[HEADS:, :]
    for i in reversed(range(per_step)):
        rows = slice(i * CHUNK, (i + 1) * CHUNK)
        sm = sm_ref[rows, :]
        sources_twice = twice(message.get(sources_ref, i, 0))
        d_values, highs, lows, scaleds, rounded, fluxes = [], [], [], [], [], []
        for j in range(PAIRS):
            at = lanes(j)
            high, low = two_terms(states[j])
            rounded.append(high)
            values = message.get(first_ref, i, X + j).astype(f32)
            weight = spread_pair(sm, WEIGHT, j)
            grad = within_ref[rows, at] + weight * mm_two(sources_twice, high, low)
            skipped = skip_ref[0:1, at] * grad_ref[rows, at].astype(f32)
            d_values.append((grad + skipped).astype(bf16))
            high, low = two_terms(values * grad)
            highs.append(high)
            lows.append(low)
            scaleds.append((values * weight).astype(bf16))
            states[j] = dec_ref[i, 0:1, at] * states[j] + back_ref[i, :, at]
            fluxes.append(
                jnp.broadcast_to(
                    jnp.sum(start_ref[i, :, at] * states[j], axis=0, keepdims=True), (16, LANES)
                )
            )
        d_sources = d_sources_ref[rows, :] + mm_nt(
            jnp.concatenate(scaleds, axis=1), jnp.concatenate(rounded, axis=1)
        )
        g = sum_heads(ones_twice, highs, lows)[:HEADS]
        constant = sum_heads(ones_twice, *two_terms_each(fluxes))[:HEADS, 0:1]
        flux = constant + mm_exact(g - e_ref[:, lanes(i)], earlier)
        soft = smt_ref[DT * HEADS : (DT + 1) * HEADS, lanes(i)]
        rate = smt_ref[RATE * HEADS : (RATE + 1) * HEADS, lanes(i)]
        sig = smt_ref[SIG * HEADS : (SIG + 1) * HEADS, lanes(i)]
        steps = (g / soft - decay_rate * flux) * sig
        logs_sum = logs_sum + flux * rate
        steps_sum = steps_sum + steps
        steps = jnp.concatenate([steps, jnp.zeros_like(steps)], axis=0)
        for j in range(PAIRS):
            message.put(mine, i, LAST_X + j, d_values[j])
        message.put(mine, i, LAST_B, d_sources.astype(bf16))
        for p in range(message.per_chunk):
            part = steps if p == 0 else pltpu.roll(steps, LANES - p * r, 1)
            mine[i * message.per_chunk + p, LAST * r : LAST * r + STEP_ROWS, :] = part.astype(bf16)
        body_copy((pl.num_programs(0) - 1 - c) * per_step + i).start()
    for j in range(PAIRS):
        carry[:, lanes(j)] = states[j]
    sums[:HEADS, :] = logs_sum
    sums[HEADS:, :] = steps_sum

    @pl.when(c == pl.num_programs(0) - 1)
    def _():
        late = []
        for k in range(2):
            column = jnp.sum(sums[k * HEADS : (k + 1) * HEADS, :], axis=1, keepdims=True)
            block = jnp.broadcast_to(column, (HEADS, LANES))
            block = jnp.concatenate([block, jnp.zeros((LANES - HEADS, LANES), f32)], axis=0)
            late.append(block.T[0:1, :])
        small = [
            jnp.zeros((HEADS, LANES), f32), early_ref[: PAIRS + 1, :], *late,
            jnp.zeros((STEP_ROWS - BIAS_ROW - 1, LANES), f32),
        ]
        small = jnp.concatenate(small, axis=0).astype(bf16)
        own_rows = lax.broadcasted_iota(jnp.int32, (STEP_ROWS, LANES), 0) < HEADS

        def fill(peer, unused):
            steps_at = slice(LAST * r, LAST * r + STEP_ROWS)
            message_s[peer, steps_at, :] = jnp.where(own_rows, message_s[peer, steps_at, :], small)
            return unused

        lax.fori_loop(0, message_s.shape[0], fill, 0)
        at = (slice(None), pl.ds(LAST * r, STEP_ROWS))
        tiles = pltpu.make_async_copy(message_s.at[at], out_ref.at[at], sent.at[chunks + 2])
        tiles.start()
        for chunk in range(chunks):
            body_copy(chunk).wait()
        gates_copy.wait()
        readers_copy.wait()
        tiles.wait()


def finish(own_ref, other_ref, logs_ref, skip_ref, bias_ref, gain_ref):
    total = own_ref[...] + other_ref[...]
    count = logs_ref.shape[1]
    logs_ref[...] = total[0:1, :count]
    bias_ref[...] = total[1:2, :count]
    skip_ref[...] = total[2:3, :count]
    gain_ref[...] = total[8:]


def call(kernel, out_shape, flops, moved, grid=None, in_specs=None, out_specs=None, scratch=()):
    extra = {}
    if grid is not None:
        extra = dict(grid=grid, in_specs=in_specs, out_specs=out_specs)
    return pl.pallas_call(
        kernel,
        out_shape=out_shape,
        scratch_shapes=list(scratch),
        compiler_params=pltpu.CompilerParams(vmem_limit_bytes=28 * 1024 * 1024),
        cost_estimate=pl.CostEstimate(flops=flops, bytes_accessed=moved, transcendentals=0),
        **extra,
    )


def shifted(array, count, by):
    pairs = [(i, i + by) for i in range(count) if 0 <= i + by < count]
    return lax.ppermute(array, "slab", pairs)


def carry_over(state, decay, first_decay, count, sign):
    window, window_decay, step = state, decay, 1
    result = result_decay = None
    while step < count:
        arrived = shifted(window, count, sign * step)
        more = 2 * step < count
        if result is None:
            result = arrived
            if more:
                result_decay = first_decay
                window = (state.astype(f32) + decay[0:1] * arrived.astype(f32)).astype(bf16)
                window_decay = decay * first_decay
        else:
            if more:
                arrived_decay = shifted(window_decay, count, sign * step)
                window = (window.astype(f32) + window_decay[0:1] * arrived.astype(f32)).astype(bf16)
                window_decay = window_decay * arrived_decay
            result = result.astype(f32) + result_decay[0:1] * arrived.astype(f32)
            if more:
                result_decay = result_decay * arrived_decay
        step *= 2
    return jnp.zeros_like(state) if result is None else result


def two_parts(array, axis, count):
    step, other = 1, jnp.zeros_like(array)
    while step < count:
        array = array if step == 1 else array + other
        other = lax.ppermute(array, axis, [(i, i ^ step) for i in range(count)])
        step *= 2
    return array, other


def on_device(
    slab_count, sub_count, tensor_count,
    mixer_x, gate_z, b_matrix, c_matrix, raw_steps, decay_log, skip_gain, step_bias, norm_gain, out_grad,
):
    rows = mixer_x.shape[0]
    peers = sub_count * tensor_count
    tokens = rows * peers
    chunks = tokens // CHUNK
    message = Message(rows)
    owners = [t * sub_count + s for s in range(sub_count) for t in range(tensor_count)]
    sub = lax.axis_index("sub")

    def struct(shape, kind=f32):
        return jax.ShapeDtypeStruct(shape, kind)

    def hbm(shape, kind=f32):
        return pltpu.HBM(shape, kind)

    def in_hbm(array):
        return pltpu.with_memory_space_constraint(array, pltpu.HBM)

    def exchange(array):
        return lax.all_to_all(array, ("sub", "tensor"), split_axis=0, concat_axis=0, tiled=True)

    own_logs = lax.dynamic_slice(decay_log, (sub * HEADS,), (HEADS,))
    own_bias = lax.dynamic_slice(step_bias, (sub * HEADS,), (HEADS,))
    own_skip = lax.dynamic_slice(skip_gain, (sub * HEADS,), (HEADS,))
    own_gain = lax.dynamic_slice(norm_gain, (sub * WIDTH,), (WIDTH,)).reshape(1, WIDTH)
    heads = jnp.broadcast_to(jnp.concatenate([own_logs, own_bias])[:, None], (2 * HEADS, LANES))
    skip_row = jnp.repeat(own_skip, HEAD_DIM).reshape(1, WIDTH)

    first_rows = FIRST * rows + STEP_ROWS
    second_rows = SECOND * rows
    last_rows = LAST * rows + STEP_ROWS

    def packed(kernel, height, arrays, whole_arrays=(), scratch=()):
        out = hbm((sub_count, tensor_count, height, LANES), bf16)
        moved = 4 * peers * height * LANES
        runs = 1
        parts = tensor_count * runs
        specs = [
            pl.BlockSpec((rows, a.shape[1] // parts), lambda t, k: (0, t * runs + k)) for a in arrays
        ] + [pl.BlockSpec(a.shape, lambda t, k: (0, 0)) for a in whole_arrays]
        out_spec = pl.BlockSpec((sub_count // runs, 1, height, LANES), lambda t, k: (k, t, 0, 0))
        made = call(kernel, out, 0, moved, (tensor_count, runs), specs, out_spec, scratch)(
            *(in_hbm(a) for a in (*arrays, *whole_arrays))
        )
        return made.reshape(peers, height, LANES)

    first = exchange(
        packed(
            pack_first, first_rows, (mixer_x, b_matrix, c_matrix), (raw_steps,),
            [pltpu.VMEM((LANES, LANES), f32)],
        )
    )
    tensor_rows = lax.broadcasted_iota(jnp.int32, (tensor_count, LANES), 0)
    mine = (tensor_rows == lax.axis_index("tensor")).astype(f32)
    half = first[:, HALF * rows : (HALF + 1) * rows, :]
    other_half = lax.ppermute(half, "sub", [(i, i ^ 1) for i in range(sub_count)])
    even = sub % 2 == 0
    sources, readers = jnp.where(even, half, other_half), jnp.where(even, other_half, half)
    gate_z, heads, skip_row, own_gain, mine = lax.optimization_barrier(
        (gate_z, heads, skip_row, own_gain, mine)
    )
    second = exchange(packed(pack_second, second_rows, (gate_z, out_grad)))

    def flow(kernel, shape_specs, flops, moved, in_specs, scratch=(), per=2):
        per = min(per, chunks)

        def body(*refs):
            return kernel(message, per, *refs)

        shapes = tuple(shape for shape, _ in shape_specs)
        specs = tuple(spec for _, spec in shape_specs)
        return call(body, shapes, flops, moved, (chunks // per,), in_specs, specs, scratch)

    def specs_of(per, down=False):
        per = min(per, chunks)
        steps = chunks // per

        def spec(block, axis):
            def index(c):
                at = steps - 1 - c if down else c
                return tuple(at if k == axis else 0 for k in range(len(block)))

            return pl.BlockSpec(block, index)

        return dict(
            message=lambda height: spec((per * message.per_chunk, height, LANES), 0),
            token=lambda width: spec((per * CHUNK, width), 0),
            lane=lambda height: spec((height, per * CHUNK), 1),
            chunk=lambda *shape: spec((per,) + shape, 0),
        )

    up = specs_of(2)
    many = specs_of(4)
    all_at_once = specs_of(8)
    dn = specs_of(8, down=True)

    def whole(*shape):
        return pl.BlockSpec(shape, lambda c: (0,) * len(shape))

    unit = 2 * tokens * CHUNK * WIDTH
    size = tokens * WIDTH

    sm, smt, own, dec, state, decay = flow(
        state_kernel,
        [
            (hbm((tokens, LANES)), up["token"](LANES)),
            (hbm((KINDS * HEADS, tokens)), up["lane"](KINDS * HEADS)),
            (hbm((chunks, STATE, WIDTH)), up["chunk"](STATE, WIDTH)),
            (hbm((chunks, 8, WIDTH)), up["chunk"](8, WIDTH)),
            (struct((STATE, WIDTH), bf16), whole(STATE, WIDTH)),
            (struct((8, WIDTH)), whole(8, WIDTH)),
        ],
        2 * unit, size * 8,
        [
            up["message"](PAIRS * rows), up["message"](rows),
            pl.BlockSpec((peers, STEP_ROWS, LANES), lambda c: (0, FIRST * rows // STEP_ROWS, 0)),
            whole(2 * HEADS, LANES),
        ],
        [pltpu.VMEM((STATE, WIDTH), f32), pltpu.VMEM((chunks, KINDS * HEADS, LANES), f32)],
    )(first, sources, first, heads)

    before = after = None
    if slab_count > 2:
        before, after = shifted(decay, slab_count, 1), shifted(decay, slab_count, -1)
    inbound = carry_over(state, decay, before, slab_count, 1)

    within, starts, pre = flow(
        within_kernel,
        [
            (hbm((tokens, WIDTH)), up["token"](WIDTH)),
            (hbm((chunks, STATE, WIDTH)), up["chunk"](STATE, WIDTH)),
            (hbm((chunks, 8, WIDTH)), up["chunk"](8, WIDTH)),
        ],
        6 * unit, size * 16,
        [
            up["message"](PAIRS * rows), up["message"](rows), up["message"](rows),
            up["token"](LANES), up["lane"](KINDS * HEADS),
            up["chunk"](STATE, WIDTH), up["chunk"](8, WIDTH),
        ],
        [pltpu.VMEM((STATE, WIDTH), f32), pltpu.VMEM((8, WIDTH), f32)],
    )(first, sources, readers, in_hbm(sm), in_hbm(smt), in_hbm(own), in_hbm(dec))

    anywhere = pl.BlockSpec(memory_space=pl.ANY)
    per_mix = min(2, chunks)
    y, sums, second = flow(
        mix_kernel,
        [
            (struct((tokens, WIDTH)), up["token"](WIDTH)),
            (struct((chunks, 8, LANES)), up["chunk"](8, LANES)),
            (struct((peers, second_rows, LANES), bf16), up["message"](second_rows)),
        ],
        unit, size * 16,
        [
            up["message"](PAIRS * rows), up["message"](rows), up["message"](second_rows),
            up["token"](WIDTH), up["token"](LANES), whole(STATE, WIDTH), up["chunk"](8, WIDTH),
            whole(1, WIDTH), whole(1, WIDTH),
        ],
        per=per_mix,
    )(
        first, readers, in_hbm(second), in_hbm(within), in_hbm(sm), inbound, in_hbm(pre),
        own_gain, skip_row,
    )

    partner = lax.ppermute(sums, "sub", [(i, i ^ 1) for i in range(sub_count)])

    d_mixed, back, slab_back = flow(
        norm_kernel,
        [
            (struct((tokens, WIDTH), bf16), all_at_once["token"](WIDTH)),
            (struct((chunks, STATE, WIDTH)), all_at_once["chunk"](STATE, WIDTH)),
            (struct((STATE, WIDTH), bf16), whole(STATE, WIDTH)),
        ],
        2 * unit, size * 12,
        [
            all_at_once["message"](PAIRS * rows), all_at_once["message"](rows), all_at_once["message"](second_rows),
            all_at_once["token"](WIDTH), all_at_once["token"](LANES), all_at_once["chunk"](8, WIDTH), all_at_once["chunk"](8, LANES),
            all_at_once["chunk"](8, LANES), whole(1, WIDTH), whole(1, WIDTH),
        ],
        [pltpu.VMEM((STATE, WIDTH), f32)],
        per=8,
    )(first, readers, second, y, sm, pre, sums, partner, own_gain, skip_row)

    outer = carry_over(slab_back, decay, after, slab_count, -1)

    d_values, d_sources, d_readers, d_gates, e, starts, params = flow(
        local_kernel,
        [
            (struct((tokens, WIDTH)), many["token"](WIDTH)),
            (struct((tokens, STATE)), many["token"](STATE)),
            (struct((peers, rows, LANES), bf16), many["message"](rows)),
            (struct((peers, PAIRS * rows, LANES), bf16), many["message"](PAIRS * rows)),
            (struct((HEADS, tokens)), many["lane"](HEADS)),
            (struct((chunks, STATE, WIDTH)), many["chunk"](STATE, WIDTH)),
            (struct((8, LANES)), whole(8, LANES)),
        ],
        10 * unit, size * 16,
        [
            many["message"](PAIRS * rows), many["message"](rows), many["message"](rows),
            many["message"](second_rows), many["token"](WIDTH), many["token"](WIDTH), many["token"](LANES),
            many["lane"](KINDS * HEADS),
            many["chunk"](STATE, WIDTH), many["chunk"](8, WIDTH), whole(STATE, WIDTH),
            many["chunk"](8, LANES), many["chunk"](8, LANES), whole(1, WIDTH), whole(1, WIDTH),
        ],
        [pltpu.VMEM((8, WIDTH), f32), pltpu.VMEM((8, WIDTH), f32)],
        per=4,
    )(
        first, sources, readers, second, y, d_mixed, sm, smt, starts, pre, inbound,
        sums, partner, own_gain, skip_row,
    )

    (last,) = flow(
        last_kernel,
        [(hbm((peers, last_rows, LANES), bf16), anywhere)],
        4 * unit, size * 16,
        [
            dn["message"](PAIRS * rows), dn["message"](rows), dn["token"](WIDTH), dn["token"](STATE),
            anywhere, anywhere,
            dn["token"](WIDTH), dn["lane"](HEADS), dn["token"](LANES), dn["lane"](KINDS * HEADS),
            whole(STATE, WIDTH), dn["chunk"](STATE, WIDTH), dn["chunk"](STATE, WIDTH),
            dn["chunk"](8, WIDTH), whole(1, WIDTH), whole(2 * HEADS, LANES), whole(8, LANES),
        ],
        [
            pltpu.VMEM((STATE, WIDTH), f32), pltpu.VMEM((2 * HEADS, LANES), f32),
            pltpu.VMEM((peers, last_rows, LANES), bf16),
            pltpu.SemaphoreType.DMA((chunks + 3,)),
        ],
        per=8,
    )(
        first, sources, d_values, d_sources, d_readers, d_gates, d_mixed, e, sm, smt, outer, back,
        starts, dec, skip_row, heads, params,
    )

    last_back = exchange(last)
    tile_at = LAST * rows // STEP_ROWS
    def tile(at):
        return pl.BlockSpec((peers, STEP_ROWS, LANES), lambda c: (0, at, 0))

    params = call(
        lambda *refs: unpack_params(sub_count, tensor_count, *refs),
        struct((8 + sub_count * PAIRS, LANES)),
        0, 4 * peers * STEP_ROWS * LANES, (1,),
        [tile(tile_at), whole(tensor_count, LANES)],
        whole(8 + sub_count * PAIRS, LANES),
    )(last_back, mine)
    own_params, other_params = two_parts(params, "slab", slab_count)
    wide, narrow = struct((rows, CHANNELS), bf16), struct((rows, GROUPS * STATE), bf16)
    grad_x, grad_gates, grad_b, grad_c, grad_steps = call(
        lambda *refs: unpack(owners, *refs),
        (wide, wide, narrow, narrow, struct((rows, MIXER_HEADS), bf16)),
        0, 10 * rows * CHANNELS,
    )(last_back)
    row = struct((1, sub_count * HEADS))
    grad_logs, grad_skip, grad_bias, grad_gain = call(
        finish, (row, row, row, struct((sub_count * PAIRS, LANES))), 0, 1 << 16,
    )(own_params, other_params)
    return (
        grad_x,
        grad_gates,
        grad_b,
        grad_c,
        grad_steps,
        grad_logs.reshape(-1),
        grad_skip.reshape(-1),
        grad_bias.reshape(-1),
        grad_gain.reshape(-1),
    )


def solution(mesh):
    tensor_count = mesh.shape["tensor"]
    sub_count = OWNERS // tensor_count
    slab_count = mesh.shape["dp"] // sub_count
    devices = mesh.devices.reshape(slab_count, sub_count, tensor_count)
    split_mesh = Mesh(devices, ("slab", "sub", "tensor"))
    rows = P(("slab", "sub", "tensor"), None)
    param = P("tensor")

    def local(*arrays):
        return on_device(slab_count, sub_count, tensor_count, *arrays)

    return jax.shard_map(
        local,
        mesh=split_mesh,
        in_specs=(rows,) * 5 + (param,) * 4 + (rows,),
        out_specs=(rows,) * 5 + (param,) * 4,
        check_vma=False,
    )
```
